32 devices in a mesh: dp: 8 (over z, x), seq: 4 (over y, core).
Axes of the slice: x: 2, y: 2, z: 4, core: 2. Of those that a mesh axis runs over, the one named last changes fastest.
Arguments:
- stream: float32 [8, 2048, 1024], P('dp', 'seq'), may hold values from -6 to 6
- cotangent: float32 [8, 2048, 1024], P('dp', 'seq'), may hold values from -6 to 6
- positions: int32 [8, 2048], P('dp', 'seq'), may hold values from 0 to 2047
- mixing_weight: float32 [2, 1024, 3072], P(None, ('dp', 'seq')), may hold values from -0.1875 to 0.1875
- mixing_first: float32 [2, 1024, 3072], P(None, ('dp', 'seq')), may hold values from -0.0012207031 to 0.0012207031
- mixing_second: float32 [2, 1024, 3072], P(None, ('dp', 'seq')), may hold values from 3.9694434e-08 to 1.5877774e-07
- mixing_average: float32 [2, 1024, 3072], P(None, ('dp', 'seq')), may hold values from -0.00036621094 to 0.00036621094
- output_weight: float32 [2, 1024, 1024], P(None, ('dp', 'seq')), may hold values from -1.5 to 1.5
- output_first: float32 [2, 1024, 1024], P(None, ('dp', 'seq')), may hold values from -0.0012207031 to 0.0012207031
- output_second: float32 [2, 1024, 1024], P(None, ('dp', 'seq')), may hold values from 3.9694434e-08 to 1.5877774e-07
- output_average: float32 [2, 1024, 1024], P(None, ('dp', 'seq')), may hold values from -0.0029296875 to 0.0029296875
- expand_weight: float32 [2, 1024, 4096], P(None, ('dp', 'seq')), may hold values from -0.1875 to 0.1875
- expand_first: float32 [2, 1024, 4096], P(None, ('dp', 'seq')), may hold values from -0.0012207031 to 0.0012207031
- expand_second: float32 [2, 1024, 4096], P(None, ('dp', 'seq')), may hold values from 9.923609e-09 to 3.9694434e-08
- expand_average: float32 [2, 1024, 4096], P(None, ('dp', 'seq')), may hold values from -0.00036621094 to 0.00036621094
- shrink_weight: float32 [2, 4096, 1024], P(None, ('dp', 'seq')), may hold values from -0.09375 to 0.09375
- shrink_first: float32 [2, 4096, 1024], P(None, ('dp', 'seq')), may hold values from -0.0012207031 to 0.0012207031
- shrink_second: float32 [2, 4096, 1024], P(None, ('dp', 'seq')), may hold values from 3.9694434e-08 to 1.5877774e-07
- shrink_average: float32 [2, 4096, 1024], P(None, ('dp', 'seq')), may hold values from -0.00018310547 to 0.00018310547
- affine_weight: float32 [2, 13312], P(None, ('dp', 'seq')), may hold values from -0.3 to 1.5, as said below
- affine_first: float32 [2, 13312], P(None, ('dp', 'seq')), may hold values from -0.0048828125 to 0.0048828125
- affine_second: float32 [2, 13312], P(None, ('dp', 'seq')), may hold values from 6.3511095e-07 to 2.5404438e-06
- affine_average: float32 [2, 13312], P(None, ('dp', 'seq')), may hold values from -0.001 to 0.002
Outputs:
- result: float32 [8, 2048, 1024], P('dp', 'seq')
- stream_grad: float32 [8, 2048, 1024], P('dp', 'seq')
- gradient_norm: float32 [], replicated
- mixing_master: float32 [2, 1024, 3072], P(None, ('dp', 'seq'))
- mixing_moment: float32 [2, 1024, 3072], P(None, ('dp', 'seq'))
- mixing_square: float32 [2, 1024, 3072], P(None, ('dp', 'seq'))
- mixing_smooth: float32 [2, 1024, 3072], P(None, ('dp', 'seq'))
- output_master: float32 [2, 1024, 1024], P(None, ('dp', 'seq'))
- output_moment: float32 [2, 1024, 1024], P(None, ('dp', 'seq'))
- output_square: float32 [2, 1024, 1024], P(None, ('dp', 'seq'))
- output_smooth: float32 [2, 1024, 1024], P(None, ('dp', 'seq'))
- expand_master: float32 [2, 1024, 4096], P(None, ('dp', 'seq'))
- expand_moment: float32 [2, 1024, 4096], P(None, ('dp', 'seq'))
- expand_square: float32 [2, 1024, 4096], P(None, ('dp', 'seq'))
- expand_smooth: float32 [2, 1024, 4096], P(None, ('dp', 'seq'))
- shrink_master: float32 [2, 4096, 1024], P(None, ('dp', 'seq'))
- shrink_moment: float32 [2, 4096, 1024], P(None, ('dp', 'seq'))
- shrink_square: float32 [2, 4096, 1024], P(None, ('dp', 'seq'))
- shrink_smooth: float32 [2, 4096, 1024], P(None, ('dp', 'seq'))
- affine_master: float32 [2, 13312], P(None, ('dp', 'seq'))
- affine_moment: float32 [2, 13312], P(None, ('dp', 'seq'))
- affine_square: float32 [2, 13312], P(None, ('dp', 'seq'))
- affine_smooth: float32 [2, 13312], P(None, ('dp', 'seq'))
The draws below stay inside these ranges and needn't reach their ends.
Inputs may be any that keep to these rules, and one draw needn't show every extreme that they name: `affine_weight`: the entries of the two norms' gains lie between 0.5 and 1.5, those of the biases between -0.3 and 0.3.
All inputs are finite; a program needn't handle non-finite values.
Results may differ from the reference program's by a relative error of at most 0.012.
Values may be sent and summed in bfloat16 or wider, within the bound.
No kernel may reach another device: no remote copies, remote signals or barrier semaphores. Data moves between devices by JAX's collectives and lax.ppermute only.
A program may use at most 384 MiB of HBM per device.

```python
import math
import jax
import jax.numpy as jnp
from jax import lax

D = 1024
H = 16
HD = 64
ROT = 16
FF = 4096
LEN = 2048
LAYERS = 2
STEP = 3
SEQS = 8
NSMALL = 13312
NPARAMS = 25192448


def draw_affine_weight(key, part):
    key = jax.random.fold_in(key, 5)
    columns_all = 9 * D + FF
    column = jnp.arange(columns_all)
    gain_slot = (column < D) | (column >= 2 * D) & (column < 3 * D)
    feature_frac = (column % D).astype(jnp.float32) / (D - 1)
    gain_key = jax.random.fold_in(key, 11)
    shift_key = jax.random.fold_in(key, 12)
    gain_draw = (0.56 + 0.8 * feature_frac)[None, :] * (1.0 + 0.1 * jax.random.truncated_normal(gain_key, -1.0, 1.0, (LAYERS, columns_all), jnp.float32))
    shifts = 0.1 * jax.random.truncated_normal(shift_key, -3.0, 3.0, (LAYERS, columns_all), jnp.float32)
    return jnp.where(gain_slot[None, :], gain_draw, shifts).astype(jnp.float32)


def with_ends(entries, stream_key, low, largest):
    index_at = [jax.random.randint(jax.random.fold_in(stream_key, axis), (), 0, length) for axis, length in enumerate(entries.shape)]
    longest = entries.shape.index(max(entries.shape))
    neighbour = index_at[:longest] + [(index_at[longest] + 1) % entries.shape[longest]] + index_at[longest + 1:]
    return entries.at[tuple(index_at)].set(low).at[tuple(neighbour)].set(largest)


def level_of(rng, dims, split, low, largest):
    level = 1.0
    for dim, shards_of in split:
        draws = jax.random.uniform(jax.random.fold_in(jax.random.fold_in(rng, 6), dim), (shards_of,), jnp.float32, low / len(split), largest / len(split))
        level = level * jnp.repeat(jnp.exp(draws), dims[dim] // shards_of).reshape((-1,) + (1,) * (len(dims) - 1 - dim))
    return level


def gaussian(rng, extent, deviation, limit, cuts=(), dtype=jnp.bfloat16):
    entries = deviation * jax.random.normal(rng, extent, jnp.float32)
    if cuts:
        entries = entries * level_of(rng, extent, cuts, -0.22, 0.18)
    return jnp.clip(entries, -limit, limit).astype(dtype)


def setup_inputs(seed: int = 0) -> dict:
    keys = jax.random.split(jax.random.key(seed), 24)
    stream = gaussian(keys[0], (SEQS, LEN, D), 1.0, 6.0, ((0, 8), (1, 4)), jnp.float32)
    cotangent = gaussian(keys[1], (SEQS, LEN, D), 1.0, 6.0, ((0, 8), (1, 4)), jnp.float32)
    positions = with_ends(jax.random.randint(keys[2], (SEQS, LEN), 0, LEN), jax.random.fold_in(keys[2], 1), 0, LEN - 1).astype(jnp.int32)
    mixing_weight = gaussian(keys[3], (LAYERS, D, 3 * D), D ** -0.5, 0.1875, ((1, 32),), jnp.float32)
    mixing_first = gaussian(keys[4], (LAYERS, D, 3 * D), (1.0 / NPARAMS ** 0.5), 0.0012207031, ((1, 32),), jnp.float32)
    mixing_second = jnp.clip(jnp.exp(math.log(1.5877773762440484e-07) - 1.3862944 * jax.random.uniform(keys[5], (LAYERS, D, 3 * D), jnp.float32) ** level_of(keys[5], (LAYERS, D, 3 * D), ((1, 32),), -0.2, 0.2)), 3.969443440610121e-08, 1.5877773762440484e-07)
    mixing_average = gaussian(keys[6], (LAYERS, D, 3 * D), (0.002 / D ** 0.5), 0.00036621094, ((1, 32),), jnp.float32)
    output_weight = gaussian(keys[7], (LAYERS, D, D), (D * 32 // LEN) ** -0.5, 1.5, ((1, 32),), jnp.float32)
    output_first = gaussian(keys[8], (LAYERS, D, D), (1.0 / NPARAMS ** 0.5), 0.0012207031, ((1, 32),), jnp.float32)
    output_second = jnp.clip(jnp.exp(math.log(1.5877773762440484e-07) - 1.3862944 * jax.random.uniform(keys[9], (LAYERS, D, D), jnp.float32) ** level_of(keys[9], (LAYERS, D, D), ((1, 32),), -0.2, 0.2)), 3.969443440610121e-08, 1.5877773762440484e-07)
    output_average = gaussian(keys[10], (LAYERS, D, D), (0.002 / (D * 32 // LEN) ** 0.5), 0.0029296875, ((1, 32),), jnp.float32)
    expand_weight = gaussian(keys[11], (LAYERS, D, FF), D ** -0.5, 0.1875, ((1, 32),), jnp.float32)
    expand_first = gaussian(keys[12], (LAYERS, D, FF), (1.0 / NPARAMS ** 0.5), 0.0012207031, ((1, 32),), jnp.float32)
    expand_second = jnp.clip(jnp.exp(math.log(3.969443440610121e-08) - 1.3862944 * jax.random.uniform(keys[13], (LAYERS, D, FF), jnp.float32) ** level_of(keys[13], (LAYERS, D, FF), ((1, 32),), -0.2, 0.2)), 9.923608601525302e-09, 3.969443440610121e-08)
    expand_average = gaussian(keys[14], (LAYERS, D, FF), (0.002 / D ** 0.5), 0.00036621094, ((1, 32),), jnp.float32)
    shrink_weight = gaussian(keys[15], (LAYERS, FF, D), FF ** -0.5, 0.09375, ((1, 32),), jnp.float32)
    shrink_first = gaussian(keys[16], (LAYERS, FF, D), (1.0 / NPARAMS ** 0.5), 0.0012207031, ((1, 32),), jnp.float32)
    shrink_second = jnp.clip(jnp.exp(math.log(1.5877773762440484e-07) - 1.3862944 * jax.random.uniform(keys[17], (LAYERS, FF, D), jnp.float32) ** level_of(keys[17], (LAYERS, FF, D), ((1, 32),), -0.2, 0.2)), 3.969443440610121e-08, 1.5877773762440484e-07)
    shrink_average = gaussian(keys[18], (LAYERS, FF, D), (0.002 / FF ** 0.5), 0.00018310547, ((1, 32),), jnp.float32)
    affine_weight = draw_affine_weight(jax.random.fold_in(keys[23], 71), 0)
    affine_first = gaussian(keys[20], (LAYERS, NSMALL), (4.0 / NPARAMS ** 0.5), 0.0048828125, ((1, 32),), jnp.float32)
    affine_second = jnp.clip(jnp.exp(math.log(2.5404438019904774e-06) - 1.3862944 * jax.random.uniform(keys[21], (LAYERS, NSMALL), jnp.float32) ** level_of(keys[21], (LAYERS, NSMALL), ((1, 32),), -0.2, 0.2)), 6.351109504976193e-07, 2.5404438019904774e-06)
    affine_average = jnp.clip(-0.001 + 0.003 * jax.random.uniform(keys[22], (LAYERS, NSMALL), jnp.float32) ** level_of(keys[22], (LAYERS, NSMALL), ((1, 32),), -0.2, 0.2), -0.001, 0.002)
    return dict(stream=stream, cotangent=cotangent, positions=positions, mixing_weight=mixing_weight, mixing_first=mixing_first, mixing_second=mixing_second, mixing_average=mixing_average, output_weight=output_weight, output_first=output_first, output_second=output_second, output_average=output_average, expand_weight=expand_weight, expand_first=expand_first, expand_second=expand_second, expand_average=expand_average, shrink_weight=shrink_weight, shrink_first=shrink_first, shrink_second=shrink_second, shrink_average=shrink_average, affine_weight=affine_weight, affine_first=affine_first, affine_second=affine_second, affine_average=affine_average)


@jax.custom_vjp
def low(v):
    return lax.optimization_barrier(v.astype(jnp.bfloat16)).astype(jnp.float32)

@jax.custom_vjp
def low_back(v):
    return v

def low_keep(v):
    return (low(v), None)

def low_pass(kept, grad):
    return (grad,)

def back_keep(v):
    return (v, None)

def back_low(kept, grad):
    return (low(grad),)
low.defvjp(low_keep, low_pass)
low_back.defvjp(back_keep, back_low)
HIGHEST = lax.Precision.HIGHEST
NORM_EPS = 1e-05
CLIP_LIMIT = 1.0
BETA_FIRST = 0.5
BETA_SECOND = 0.5
ADAM_EPS = 1e-08
WEIGHT_DECAY = 0.01
EMA_DECAY = 0.999
SMALL_RATE = 0.1
MASK_VALUE = -1e+30

def layer_norm(values, norm_gain, norm_shift):
    centre = values - lax.optimization_barrier(jnp.mean(values, -1, keepdims=True))
    spread = lax.optimization_barrier(jnp.mean(centre * centre, -1, keepdims=True))
    return centre * lax.rsqrt(spread + NORM_EPS) * norm_gain + norm_shift

def phases(positions, rotary):
    steps_half = jnp.arange(rotary // 2).astype(jnp.float32)
    frequency = 10000.0 ** (-2.0 * steps_half / rotary)
    angles = positions.astype(jnp.float32)[..., None] * frequency
    angles = jnp.concatenate([angles, angles], -1)
    return (jnp.cos(angles), jnp.sin(angles))

def rotate(values, cosine_table, sine_table, rotary):
    halfway = rotary // 2
    turning = values[..., :rotary]
    swapped = jnp.concatenate([-turning[..., halfway:], turning[..., :halfway]], -1)
    return jnp.concatenate([turning * cosine_table + swapped * sine_table, values[..., rotary:]], -1)

def split_affine(affine):
    bounds = [D, D, D, D, 3 * D, D, FF, D]
    pieces = []
    offset = 0
    for length in bounds:
        pieces.append(affine[offset:offset + length])
        offset = offset + length
    return pieces

def attention(query_rows, key_rows, value_rows):
    group_size = query_rows.shape[0]
    block_rows = min(512, LEN)
    block_count = LEN // block_rows
    key_index = jnp.arange(LEN).astype(jnp.int32)

    def one_block(packed):
        query_block, start_row = packed
        scores = low_back(jnp.einsum('gqhd,gkhd->ghqk', query_block, key_rows, precision=HIGHEST))
        row_index = start_row + jnp.arange(block_rows).astype(jnp.int32)
        allowed = key_index[None, :] <= row_index[:, None]
        scores = jnp.where(allowed, scores, MASK_VALUE)
        exponent = jnp.exp(scores - lax.optimization_barrier(jnp.max(scores, -1, keepdims=True)))
        attend_weights = low(exponent / lax.optimization_barrier(jnp.sum(exponent, -1, keepdims=True)))
        return jnp.einsum('ghqk,gkhd->gqhd', attend_weights, value_rows, precision=HIGHEST)
    split_query = query_rows.reshape(group_size, block_count, block_rows, H, HD).transpose(1, 0, 2, 3, 4)
    starts = (jnp.arange(block_count) * block_rows).astype(jnp.int32)
    outcome = lax.map(jax.checkpoint(one_block), (split_query, starts))
    return outcome.transpose(1, 0, 2, 3, 4).reshape(group_size, LEN, D)

def layer_forward(stream, cosine_table, sine_table, mixing, output, expand, shrink, affine):
    group_size = stream.shape[0]
    gain_one, shift_one, gain_two, shift_two, mixing_bias, output_bias, expand_bias, shrink_bias = split_affine(affine)
    normed_one = low(layer_norm(stream, gain_one, shift_one))
    mixed_rows = low_back(jnp.einsum('gtd,de->gte', normed_one, mixing, precision=HIGHEST)) + mixing_bias
    mixed_rows = mixed_rows.reshape(group_size, LEN, 3, H, HD)
    query_scale = 1.0 / math.sqrt(HD)
    query_rows = low_back(low(rotate(mixed_rows[:, :, 0], cosine_table, sine_table, ROT) * query_scale))
    key_rows = low_back(low(rotate(mixed_rows[:, :, 1], cosine_table, sine_table, ROT)))
    value_rows = low_back(low(mixed_rows[:, :, 2]))
    attended = low_back(low(attention(query_rows, key_rows, value_rows)))
    branch_one = low_back(jnp.einsum('gtd,de->gte', attended, output, precision=HIGHEST)) + output_bias
    normed_two = low(layer_norm(stream, gain_two, shift_two))
    hidden = low_back(jnp.einsum('gtd,df->gtf', normed_two, expand, precision=HIGHEST)) + expand_bias
    activated = low(jax.nn.gelu(hidden, approximate=False))
    branch_two = low_back(jnp.einsum('gtf,fd->gtd', activated, shrink, precision=HIGHEST)) + shrink_bias
    return stream + branch_one + branch_two

def network(stream, params, cosine_table, sine_table):
    mixing_all, output_all, expand_all, shrink_all, affine_all = params
    for layer_index in range(LAYERS):
        stream = layer_forward(stream, cosine_table, sine_table, low(mixing_all[layer_index]), low(output_all[layer_index]), low(expand_all[layer_index]), low(shrink_all[layer_index]), low(affine_all[layer_index]))
    return stream

def adamw_update(weight, first_moment, second, average, gradient, clip_scale, step_rate, decay_rate):
    clipped = gradient * clip_scale
    first_new = BETA_FIRST * first_moment + (1.0 - BETA_FIRST) * clipped
    second_new = BETA_SECOND * second + (1.0 - BETA_SECOND) * clipped * clipped
    first_hat = first_new / (1.0 - BETA_FIRST ** STEP)
    second_hat = second_new / (1.0 - BETA_SECOND ** STEP)
    weight_new = weight - step_rate * (first_hat / (jnp.sqrt(second_hat) + ADAM_EPS) + decay_rate * weight)
    average_new = EMA_DECAY * average + (1.0 - EMA_DECAY) * weight_new
    return (weight_new, first_new, second_new, average_new)

def reference(stream, cotangent, positions, mixing_weight, mixing_first, mixing_second, mixing_average, output_weight, output_first, output_second, output_average, expand_weight, expand_first, expand_second, expand_average, shrink_weight, shrink_first, shrink_second, shrink_average, affine_weight, affine_first, affine_second, affine_average):
    params = (mixing_weight, output_weight, expand_weight, shrink_weight, affine_weight)
    group_size = math.gcd(SEQS, max(1, 4096 // LEN))
    group_count = SEQS // group_size
    stream_groups = stream.reshape(group_count, group_size, LEN, D)
    cotangent_groups = cotangent.reshape(group_count, group_size, LEN, D)
    position_groups = positions.reshape(group_count, group_size, LEN)

    def one_group(totals, packed):
        stream_part, cotangent_part, position_part = packed
        cosine_table, sine_table = phases(position_part, ROT)
        cosine_table = cosine_table[:, :, None, :]
        sine_table = sine_table[:, :, None, :]
        outcome, pullback = jax.vjp(lambda values, weights: network(values, weights, cosine_table, sine_table), stream_part, params)
        stream_part_grad, param_grads = pullback(cotangent_part)
        return (jax.tree.map(jnp.add, totals, param_grads), (outcome, stream_part_grad))
    zero_grads = jax.tree.map(jnp.zeros_like, params)
    gradients, (outcomes, stream_grads) = lax.scan(one_group, zero_grads, (stream_groups, cotangent_groups, position_groups))
    squares = jnp.float32(0.0)
    for gradient_piece in gradients:
        squares = squares + jnp.sum(gradient_piece * gradient_piece)
    gradient_norm = jnp.sqrt(squares)
    clip_scale = jnp.minimum(1.0, CLIP_LIMIT / (gradient_norm + 1e-06))
    step_rates = (D ** (-0.5), (D * 32 // LEN) ** (-0.5), D ** (-0.5), FF ** (-0.5), SMALL_RATE)
    decays = (WEIGHT_DECAY, WEIGHT_DECAY, WEIGHT_DECAY, WEIGHT_DECAY, 0.0)
    states = ((mixing_weight, mixing_first, mixing_second, mixing_average), (output_weight, output_first, output_second, output_average), (expand_weight, expand_first, expand_second, expand_average), (shrink_weight, shrink_first, shrink_second, shrink_average), (affine_weight, affine_first, affine_second, affine_average))
    updated = ()
    for kind_index in range(5):
        weight, first_moment, second, average = states[kind_index]
        updated = updated + adamw_update(weight, first_moment, second, average, gradients[kind_index], clip_scale, step_rates[kind_index], decays[kind_index])
    return (outcomes.reshape(SEQS, LEN, D), stream_grads.reshape(SEQS, LEN, D), gradient_norm) + updated
```

```python
from functools import partial
import math

import jax
import jax.numpy as jnp
from jax import lax
from jax.experimental import pallas as pl
from jax.experimental.pallas import tpu as pltpu
from jax.sharding import PartitionSpec as P

D = 1024
H = 16
HD = 64
ROT = 16
FF = 4096
LEN = 2048
LAYERS = 2
STEP = 3

NORM_EPS = 1e-05
CLIP_LIMIT = 1.0
BETA_FIRST = 0.5
BETA_SECOND = 0.5
ADAM_EPS = 1e-08
WEIGHT_DECAY = 0.01
EMA_DECAY = 0.999
SMALL_RATE = 0.1
MASK_VALUE = -1e30
ROWS = 256
BLOCK = 512
QUERY_SCALE = 1.0 / math.sqrt(HD)
BF = jnp.bfloat16
F32 = jnp.float32
VMEM_LIMIT = 48 * 1024 * 1024


def dp_parts():
    size = lax.axis_size("dp")
    outer = 4 if size % 4 == 0 else size
    return outer, size // outer


def outer_ring(value):
    outer, inner = dp_parts()
    size = outer * inner
    return lax.ppermute(value, "dp", [(i, (i + inner) % size) for i in range(size)])


def inner_ring(value):
    outer, inner = dp_parts()
    moves = [
        (a * inner + b, a * inner + (b + 1) % inner) for a in range(outer) for b in range(inner)
    ]
    return lax.ppermute(value, "dp", moves)


def chip_ring(value):
    size = lax.axis_size("seq")
    return lax.ppermute(value, "seq", [(i, (i + 2) % size) for i in range(size)])


def core_swap(value):
    size = lax.axis_size("seq")
    return lax.ppermute(value, "seq", [(i, i ^ 1) for i in range(size)])


def put(total, piece, first, second):
    start = (first, second) + (0,) * (total.ndim - 2)
    return lax.dynamic_update_slice(total, piece[None, None], start)


def pick(total, first, second):
    sizes = (1, 1) + total.shape[2:]
    start = (first, second) + (0,) * (total.ndim - 2)
    return lax.dynamic_slice(total, start, sizes)[0, 0]


def dp_gather(value):
    outer, inner = dp_parts()
    me = lax.axis_index("dp")
    a, b = me // inner, me % inner
    total = jnp.zeros((outer, inner) + value.shape, value.dtype)
    piece = value
    for step in range(outer):
        passing = piece
        for turn in range(inner):
            total = put(total, passing, (a - step) % outer, (b - turn) % inner)
            if turn < inner - 1:
                passing = inner_ring(passing)
        if step < outer - 1:
            piece = outer_ring(piece)
    return total.reshape((outer * inner * value.shape[0],) + value.shape[1:])


def dp_scatter(value):
    outer, inner = dp_parts()
    me = lax.axis_index("dp")
    a, b = me // inner, me % inner
    rows = value.shape[0] // (outer * inner)
    value = value.reshape((outer, inner, rows) + value.shape[1:])

    def inner_sum(at):
        arrived = None
        for turn in range(1, inner):
            own = pick(value, at, (b - turn) % inner)
            if arrived is not None:
                own = (own.astype(F32) + arrived.astype(F32)).astype(BF)
            arrived = inner_ring(own)
        own = pick(value, at, b).astype(F32)
        return own if arrived is None else own + arrived.astype(F32)

    arrived = None
    for step in range(1, outer):
        part = inner_sum((a - step) % outer)
        if arrived is not None:
            part = part + arrived.astype(F32)
        arrived = outer_ring(part.astype(BF))
    part = inner_sum(a)
    return part if arrived is None else part + arrived.astype(F32)


def seq_gather(value):
    chips = lax.axis_size("seq") // 2
    me = lax.axis_index("seq")
    y, c = me // 2, me % 2
    total = jnp.zeros((chips, 2) + value.shape, value.dtype)
    piece = value
    for step in range(chips):
        at = (y - step) % chips
        total = put(total, piece, at, c)
        total = put(total, core_swap(piece), at, 1 - c)
        if step < chips - 1:
            piece = chip_ring(piece)
    return total.reshape((chips * 2 * value.shape[0],) + value.shape[1:])


def seq_scatter(value):
    chips = lax.axis_size("seq") // 2
    me = lax.axis_index("seq")
    y, c = me // 2, me % 2
    rows = value.shape[0] // (2 * chips)
    value = value.reshape((chips, 2, rows) + value.shape[1:])

    def core_sum(at):
        arrived = core_swap(pick(value, at, 1 - c))
        return pick(value, at, c).astype(F32) + arrived.astype(F32)

    arrived = None
    for step in range(1, chips):
        part = core_sum((y - step) % chips)
        if arrived is not None:
            part = part + arrived.astype(F32)
        arrived = chip_ring(part.astype(BF))
    part = core_sum(y)
    return part if arrived is None else part + arrived.astype(F32)


def seq_exchange(value):
    return lax.all_to_all(value, "seq", split_axis=0, concat_axis=0, tiled=True)


def head_masks(width, dtype):
    lane = lax.broadcasted_iota(jnp.int32, (1, width), 1) // HD
    return [(lane == h).astype(F32).astype(dtype) for h in range(width // HD)]


def swap_halves(values):
    width = values.shape[1]
    lane = lax.broadcasted_iota(jnp.int32, values.shape, 1) % HD
    return jnp.where(
        lane < ROT // 2,
        pltpu.roll(values, width - ROT // 2, 1),
        pltpu.roll(values, ROT // 2, 1),
    )


def widen(table, width):
    return jnp.concatenate([table] * (width // 128), axis=1) if width > 128 else table


def matmul(left, right):
    return lax.dot_general(left, right, (((1,), (0,)), ((), ())), preferred_element_type=F32)


def matmul_nt(left, right):
    return lax.dot_general(left, right, (((1,), (1,)), ((), ())), preferred_element_type=F32)


def matmul_tn(left, right):
    return lax.dot_general(left, right, (((0,), (0,)), ((), ())), preferred_element_type=F32)


def mix_kernel(x_ref, w_ref, c_ref, cos_ref, sin_ref, out_ref):
    width = w_ref.shape[1] // 3
    mixed = matmul(x_ref[...], w_ref[...]) + c_ref[...]
    cosine = widen(cos_ref[...], width)
    sine = widen(sin_ref[...], width)
    query = mixed[:, :width]
    key = mixed[:, width : 2 * width]
    query = (query * cosine + swap_halves(query) * sine) * QUERY_SCALE
    key = key * cosine + swap_halves(key) * sine
    out_ref[:, :width] = query.astype(BF)
    out_ref[:, width : 2 * width] = key.astype(BF)
    out_ref[:, 2 * width :] = mixed[:, 2 * width :].astype(BF)


def mix(x, weight, shift, cosine, sine):
    length, columns = x.shape[0], weight.shape[1]
    return pl.pallas_call(
        mix_kernel,
        grid=(length // ROWS,),
        in_specs=[
            pl.BlockSpec((ROWS, D), lambda i: (i, 0)),
            pl.BlockSpec((D, columns), lambda i: (0, 0)),
            pl.BlockSpec((1, columns), lambda i: (0, 0)),
            pl.BlockSpec((ROWS, 128), lambda i: (i, 0)),
            pl.BlockSpec((ROWS, 128), lambda i: (i, 0)),
        ],
        out_specs=pl.BlockSpec((ROWS, columns), lambda i: (i, 0)),
        out_shape=jax.ShapeDtypeStruct((length, columns), BF),
        compiler_params=pltpu.CompilerParams(vmem_limit_bytes=VMEM_LIMIT),
        cost_estimate=pl.CostEstimate(
            flops=2 * length * D * columns,
            bytes_accessed=2 * (length * D + D * columns + length * columns),
            transcendentals=0,
        ),
        name="mix",
    )(x, weight, shift, cosine, sine)


def attend_kernel(q_ref, k_ref, v_ref, o_ref, lse_ref, acc_ref, high_ref, sum_ref):
    block, width = q_ref.shape
    heads = width // HD
    i = pl.program_id(0)
    masks = head_masks(width, BF)
    query = q_ref[...]
    queries = [query * mask for mask in masks]
    acc_ref[...] = jnp.zeros(acc_ref.shape, F32)
    sum_ref[...] = jnp.zeros(sum_ref.shape, F32)
    high_ref[...] = jnp.full(high_ref.shape, MASK_VALUE, F32)

    def tile(j, diagonal):
        rows = pl.ds(pl.multiple_of(j * block, block), block)
        key = k_ref[rows, :]
        value = v_ref[rows, :]
        for h in range(heads):
            scores = matmul_nt(queries[h], key)
            if diagonal:
                row = lax.broadcasted_iota(jnp.int32, scores.shape, 0)
                column = lax.broadcasted_iota(jnp.int32, scores.shape, 1)
                scores = jnp.where(column <= row, scores, MASK_VALUE)
            old = high_ref[h]
            new = jnp.maximum(old, jnp.max(scores, 1, keepdims=True))
            weights = jnp.exp(scores - new[:, :1])
            shrink = jnp.exp(old - new)
            sum_ref[h] = sum_ref[h] * shrink + jnp.sum(weights, 1, keepdims=True)
            acc_ref[h] = acc_ref[h] * shrink[:, :1] + matmul(weights.astype(BF), value)
            high_ref[h] = new

    def step(j, carry):
        tile(j, False)
        return carry

    lax.fori_loop(0, i, step, 0)
    tile(i, True)
    lane = lax.broadcasted_iota(jnp.int32, (block, width), 1) // HD
    small_lane = lax.broadcasted_iota(jnp.int32, (block, 128), 1)
    total = jnp.zeros((block, width), F32)
    log_total = jnp.zeros((block, 128), F32)
    for h in range(heads):
        total = jnp.where(lane == h, acc_ref[h] / sum_ref[h][:, :1], total)
        log_total = jnp.where(small_lane == h, high_ref[h] + jnp.log(sum_ref[h]), log_total)
    o_ref[...] = total.astype(BF)
    lse_ref[...] = log_total


def attend(mixed):
    length, width = mixed.shape[0], mixed.shape[1] // 3
    heads = width // HD
    block = min(BLOCK, length)
    flops = 2 * length * length * width * 2
    return pl.pallas_call(
        attend_kernel,
        grid=(length // block,),
        in_specs=[
            pl.BlockSpec((block, width), lambda i: (i, 0)),
            pl.BlockSpec((length, width), lambda i: (0, 1)),
            pl.BlockSpec((length, width), lambda i: (0, 2)),
        ],
        out_specs=[
            pl.BlockSpec((block, width), lambda i: (i, 0)),
            pl.BlockSpec((block, 128), lambda i: (i, 0)),
        ],
        out_shape=[
            jax.ShapeDtypeStruct((length, width), BF),
            jax.ShapeDtypeStruct((length, 128), F32),
        ],
        scratch_shapes=[
            pltpu.VMEM((heads, block, width), F32),
            pltpu.VMEM((heads, block, 128), F32),
            pltpu.VMEM((heads, block, 128), F32),
        ],
        compiler_params=pltpu.CompilerParams(vmem_limit_bytes=VMEM_LIMIT),
        cost_estimate=pl.CostEstimate(
            flops=flops, bytes_accessed=8 * length * width, transcendentals=length * length * heads
        ),
        name="attend",
    )(mixed, mixed, mixed)


def attend_back_kernel(
    q_ref,
    k_ref,
    v_ref,
    do_ref,
    lse_ref,
    inner_ref,
    cos_ref,
    sin_ref,
    out_ref,
    total_ref,
    dq_ref,
    dk_ref,
    dv_ref,
):
    block, width = k_ref.shape
    length = q_ref.shape[0]
    heads = width // HD
    steps = length // block
    j = pl.program_id(0)
    masks = head_masks(width, BF)
    key = k_ref[...]
    value = v_ref[...]
    keys = [key * mask for mask in masks]

    @pl.when(j == 0)
    def _():
        dq_ref[...] = jnp.zeros(dq_ref.shape, F32)
        total_ref[...] = jnp.zeros(total_ref.shape, F32)

    dk_ref[...] = jnp.zeros(dk_ref.shape, F32)
    dv_ref[...] = jnp.zeros(dv_ref.shape, F32)

    def tile(i, diagonal):
        rows = pl.ds(pl.multiple_of(i * block, block), block)
        query = q_ref[rows, :]
        grad = do_ref[rows, :]
        log_total = lse_ref[:, rows]
        inner = inner_ref[:, rows]
        for h in range(heads):
            query_head = query * masks[h]
            grad_head = grad * masks[h]
            scores = matmul_nt(key, query_head) - log_total[h : h + 1, :]
            if diagonal:
                row = lax.broadcasted_iota(jnp.int32, scores.shape, 0)
                column = lax.broadcasted_iota(jnp.int32, scores.shape, 1)
                scores = jnp.where(row <= column, scores, MASK_VALUE)
            weights = jnp.exp(scores)
            dv_ref[...] += matmul(weights.astype(BF), grad_head)
            weight_grad = matmul_nt(value, grad_head)
            score_grad = (weights * (weight_grad - inner[h : h + 1, :])).astype(BF)
            dk_ref[...] += matmul(score_grad, query_head)
            dq_ref[rows, :] += matmul_tn(score_grad, keys[h])

    def step(i, carry):
        tile(i, False)
        return carry

    tile(j, True)
    lax.fori_loop(j + 1, steps, step, 0)

    own = pl.ds(pl.multiple_of(j * block, block), block)
    key_grad = dk_ref[...]
    cosine = widen(cos_ref[own, :], width)
    sine = widen(sin_ref[own, :], width)
    key_grad = key_grad * cosine - swap_halves(key_grad) * sine
    value_grad = dv_ref[...]
    out_ref[own, width : 2 * width] = key_grad.astype(BF)
    out_ref[own, 2 * width :] = value_grad.astype(BF)
    total_ref[:, width : 2 * width] += jnp.sum(key_grad, 0, keepdims=True)
    total_ref[:, 2 * width :] += jnp.sum(value_grad, 0, keepdims=True)
    query_grad = dq_ref[own, :] * QUERY_SCALE
    query_grad = query_grad * cosine - swap_halves(query_grad) * sine
    out_ref[own, :width] = query_grad.astype(BF)
    total_ref[:, :width] += jnp.sum(query_grad, 0, keepdims=True)


def attend_back(mixed, grads, log_total, inner, cosine, sine):
    length, width = mixed.shape[0], mixed.shape[1] // 3
    heads = width // HD
    block = min(BLOCK, length)
    flops = 2 * length * length * width * 5
    return pl.pallas_call(
        attend_back_kernel,
        grid=(length // block,),
        in_specs=[
            pl.BlockSpec((length, width), lambda j: (0, 0)),
            pl.BlockSpec((block, width), lambda j: (j, 1)),
            pl.BlockSpec((block, width), lambda j: (j, 2)),
            pl.BlockSpec((length, width), lambda j: (0, 0)),
            pl.BlockSpec((heads, length), lambda j: (0, 0)),
            pl.BlockSpec((heads, length), lambda j: (0, 0)),
            pl.BlockSpec((length, 128), lambda j: (0, 0)),
            pl.BlockSpec((length, 128), lambda j: (0, 0)),
        ],
        out_specs=[
            pl.BlockSpec((length, 3 * width), lambda j: (0, 0)),
            pl.BlockSpec((1, 3 * width), lambda j: (0, 0)),
        ],
        out_shape=[
            jax.ShapeDtypeStruct((length, 3 * width), BF),
            jax.ShapeDtypeStruct((1, 3 * width), F32),
        ],
        scratch_shapes=[
            pltpu.VMEM((length, width), F32),
            pltpu.VMEM((block, width), F32),
            pltpu.VMEM((block, width), F32),
        ],
        compiler_params=pltpu.CompilerParams(vmem_limit_bytes=VMEM_LIMIT),
        cost_estimate=pl.CostEstimate(
            flops=flops, bytes_accessed=16 * length * width, transcendentals=length * length * heads
        ),
        name="attend_back",
    )(mixed, mixed, mixed, grads, log_total, inner, cosine, sine)


def gelu_pair(values):
    size = jnp.abs(values) * (1.0 / math.sqrt(2.0))
    bell = jnp.exp(-size * size)
    turn = 1.0 / (1.0 + 0.3275911 * size)
    series = turn * (
        0.254829592
        + turn * (-0.284496736 + turn * (1.421413741 + turn * (-1.453152027 + turn * 1.061405429)))
    )
    tail = 0.5 * series * bell
    below = jnp.where(values < 0.0, tail, 1.0 - tail)
    slope = below + values * bell * (1.0 / math.sqrt(2.0 * math.pi))
    return values * below, slope


def feed_kernel(x_ref, wi_ref, ci_ref, wd_ref, o_ref, wo_ref, act_ref, slope_ref, out_ref):
    hidden = matmul(x_ref[...], wi_ref[...]) + ci_ref[...]
    activated, slope = gelu_pair(hidden)
    activated = activated.astype(BF)
    act_ref[...] = activated
    slope_ref[...] = slope.astype(BF)
    out = matmul(activated, wd_ref[...]) + matmul(o_ref[...], wo_ref[...])
    out_ref[...] = out.astype(BF)


def feed(x, expand, shift, shrink, attended, output):
    length, units, width = x.shape[0], expand.shape[1], attended.shape[1]
    return pl.pallas_call(
        feed_kernel,
        grid=(length // ROWS,),
        in_specs=[
            pl.BlockSpec((ROWS, D), lambda i: (i, 0)),
            pl.BlockSpec((D, units), lambda i: (0, 0)),
            pl.BlockSpec((1, units), lambda i: (0, 0)),
            pl.BlockSpec((units, D), lambda i: (0, 0)),
            pl.BlockSpec((ROWS, width), lambda i: (i, 0)),
            pl.BlockSpec((width, D), lambda i: (0, 0)),
        ],
        out_specs=[
            pl.BlockSpec((ROWS, units), lambda i: (i, 0)),
            pl.BlockSpec((ROWS, units), lambda i: (i, 0)),
            pl.BlockSpec((ROWS, D), lambda i: (i, 0)),
        ],
        out_shape=[
            jax.ShapeDtypeStruct((length, units), BF),
            jax.ShapeDtypeStruct((length, units), BF),
            jax.ShapeDtypeStruct((length, D), BF),
        ],
        compiler_params=pltpu.CompilerParams(vmem_limit_bytes=VMEM_LIMIT),
        cost_estimate=pl.CostEstimate(
            flops=2 * length * D * (2 * units + width),
            bytes_accessed=2 * (2 * D * units + 2 * length * D + 2 * length * units),
            transcendentals=length * units,
        ),
        name="feed",
    )(x, expand, shift, shrink, attended, output)


def rotary_tables(positions):
    steps_half = jnp.arange(ROT // 2).astype(F32)
    frequency = 10000.0 ** (-2.0 * steps_half / ROT)
    angles = positions.astype(F32)[:, None] * frequency
    cosine, sine = jnp.cos(angles), jnp.sin(angles)
    rest = jnp.zeros((positions.shape[0], HD - ROT), F32)
    cosine = jnp.concatenate([cosine, cosine, rest + 1.0] * 2, -1)
    sine = jnp.concatenate([-sine, sine, rest] * 2, -1)
    return cosine, sine


def split_affine(affine):
    bounds = [D, D, D, D, 3 * D, D, FF, D]
    pieces = []
    offset = 0
    for length in bounds:
        pieces.append(affine[offset : offset + length])
        offset = offset + length
    return pieces


def adamw_update(
    weight, first_moment, second, average, gradient, clip_scale, step_rate, decay_rate
):
    clipped = gradient * clip_scale
    first_new = BETA_FIRST * first_moment + (1.0 - BETA_FIRST) * clipped
    second_new = BETA_SECOND * second + (1.0 - BETA_SECOND) * clipped * clipped
    first_hat = first_new / (1.0 - BETA_FIRST**STEP)
    second_hat = second_new / (1.0 - BETA_SECOND**STEP)
    weight_new = weight - step_rate * (
        first_hat / (jnp.sqrt(second_hat) + ADAM_EPS) + decay_rate * weight
    )
    average_new = EMA_DECAY * average + (1.0 - EMA_DECAY) * weight_new
    return (weight_new, first_new, second_new, average_new)


def normalize(values):
    centre = values - jnp.mean(values, -1, keepdims=True)
    spread = jnp.mean(centre * centre, -1, keepdims=True)
    scale = lax.rsqrt(spread + NORM_EPS)
    return centre * scale, scale


def local(
    stream,
    cotangent,
    positions,
    mixing_weight,
    mixing_first,
    mixing_second,
    mixing_average,
    output_weight,
    output_first,
    output_second,
    output_average,
    expand_weight,
    expand_first,
    expand_second,
    expand_average,
    shrink_weight,
    shrink_first,
    shrink_second,
    shrink_average,
    affine_weight,
    affine_first,
    affine_second,
    affine_average,
):
    parts = lax.axis_size("seq")
    copies = lax.axis_size("dp")
    devices = parts * copies
    part = lax.axis_index("seq")
    width = D // parts
    units = FF // parts
    rows_d = D // devices
    rows_f = FF // devices
    rows = stream.shape[0] * stream.shape[1]
    small = affine_weight.shape[1]

    def part_of(vector, before):
        view = vector.reshape(before, parts, -1)
        return lax.dynamic_index_in_dim(view, part, 1, keepdims=False).reshape(-1)

    def spread_part(vector, before):
        view = jnp.zeros((before, parts, vector.shape[0] // before), F32)
        view = lax.dynamic_update_slice(view, vector.reshape(before, 1, -1), (0, part, 0))
        return view.reshape(-1)

    affine_low = affine_weight.astype(BF).reshape(1, LAYERS * small)
    affine_all = lax.all_to_all(
        jnp.broadcast_to(affine_low, (devices, LAYERS * small)),
        ("dp", "seq"),
        split_axis=0,
        concat_axis=0,
        tiled=True,
    )
    affine_all = affine_all.reshape(devices, LAYERS, small).transpose(1, 0, 2)
    affine_all = affine_all.reshape(LAYERS, devices * small).astype(F32)

    current = stream.reshape(rows, D)
    lane_positions = positions.reshape(rows // 128, 128)
    cosine, sine = rotary_tables(seq_gather(lane_positions).reshape(-1))
    gradient = cotangent.reshape(rows, D)

    def weights_of(layer):
        mixing = mixing_weight[layer].astype(BF).reshape(rows_d, 3, parts, width)
        mixing = mixing.transpose(2, 0, 1, 3).reshape(parts, rows_d, 3 * width)
        expand = expand_weight[layer].astype(BF).reshape(rows_d, copies, parts, rows_f)
        expand = expand.transpose(2, 0, 1, 3).reshape(parts, rows_d, units)
        both = seq_exchange(jnp.concatenate([mixing, expand], -1))
        both = both.reshape(parts * rows_d, 3 * width + units)
        mixing = dp_gather(both[:, : 3 * width])
        output = dp_gather(output_weight[layer].astype(BF))
        expand = dp_gather(both[:, 3 * width :])
        shrink = dp_gather(shrink_weight[layer].astype(BF))
        output = seq_exchange(output.reshape(parts, -1, D)).reshape(
            parts, copies // parts, rows_d, D
        )
        output = output.transpose(1, 0, 2, 3).reshape(width, D)
        return mixing, output, expand, shrink

    stored = []
    for layer in range(LAYERS):
        mixing, output, expand, shrink = weights_of(layer)
        (
            gain_one,
            shift_one,
            gain_two,
            shift_two,
            mixing_bias,
            output_bias,
            expand_bias,
            shrink_bias,
        ) = split_affine(affine_all[layer])
        mixing_scaled = (mixing.astype(F32) * gain_one[:, None]).astype(BF)
        expand_scaled = (expand.astype(F32) * gain_two[:, None]).astype(BF)
        mixing_shift = jnp.sum(mixing.astype(F32) * shift_one[:, None], 0)
        mixing_shift = mixing_shift + part_of(mixing_bias, 3)
        expand_shift = jnp.sum(expand.astype(F32) * shift_two[:, None], 0)
        expand_shift = expand_shift + part_of(expand_bias, copies)
        own_normed, scale = normalize(current)
        normed = seq_gather(own_normed.astype(BF))
        mixed = mix(normed, mixing_scaled, mixing_shift[None], cosine, sine)
        attended, log_total = attend(mixed)
        activated, slope, branch = feed(
            normed, expand_scaled, expand_shift[None], shrink, attended, output
        )
        stored.append(
            (
                own_normed,
                scale,
                normed,
                mixed,
                attended,
                log_total,
                activated,
                slope,
                mixing,
                mixing_scaled,
                output,
                expand,
                expand_scaled,
                shrink,
                (gain_one, shift_one, gain_two, shift_two),
            )
        )
        current = current + seq_scatter(branch) + output_bias + shrink_bias
    result = current.reshape(stream.shape)

    reduced = [None] * LAYERS
    for layer in reversed(range(LAYERS)):
        (
            own_normed,
            scale,
            normed,
            mixed,
            attended,
            log_total,
            activated,
            slope,
            mixing,
            mixing_scaled,
            output,
            expand,
            expand_scaled,
            shrink,
            (gain_one, shift_one, gain_two, shift_two),
        ) = stored[layer]
        heads = width // HD
        grads = seq_gather(gradient.astype(BF))
        attended_grad = matmul_nt(grads, output).astype(BF)
        hidden_grad = matmul_nt(grads, shrink) * slope.astype(F32)
        hidden_total = jnp.sum(hidden_grad, 0)
        hidden_low = hidden_grad.astype(BF)
        shrink_grad = dp_scatter(matmul_tn(activated, grads).astype(BF))
        output_grad = matmul_tn(attended, grads).astype(BF)
        output_grad = output_grad.reshape(copies // parts, parts, rows_d, D).transpose(1, 0, 2, 3)
        output_grad = seq_exchange(output_grad.reshape(parts, copies // parts * rows_d, D))
        output_grad = dp_scatter(output_grad.reshape(copies * rows_d, D))
        inner = attended_grad.astype(F32) * attended.astype(F32)
        inner = jnp.sum(inner.reshape(-1, heads, HD), -1).T
        mixed_low, mixed_total = attend_back(
            mixed, attended_grad, log_total[:, :heads].T, inner, cosine, sine
        )
        mixed_total = mixed_total[0]
        normed_grad = matmul_nt(hidden_low, expand_scaled) + matmul_nt(mixed_low, mixing_scaled)
        normed_grad = seq_scatter(normed_grad.astype(BF))
        expand_raw = matmul_tn(normed, hidden_low)
        mixing_raw = matmul_tn(normed, mixed_low)
        expand_grad = expand_raw * gain_two[:, None] + shift_two[:, None] * hidden_total
        mixing_grad = mixing_raw * gain_one[:, None] + shift_one[:, None] * mixed_total
        gain_two_grad = jnp.sum(expand_raw * expand.astype(F32), 1)
        gain_one_grad = jnp.sum(mixing_raw * mixing.astype(F32), 1)
        shift_two_grad = jnp.sum(expand.astype(F32) * hidden_total, 1)
        shift_one_grad = jnp.sum(mixing.astype(F32) * mixed_total, 1)
        expand_grad = dp_scatter(expand_grad.astype(BF))
        mixing_grad = dp_scatter(mixing_grad.astype(BF))
        both = jnp.concatenate([mixing_grad, expand_grad], -1).astype(BF)
        both = seq_exchange(both.reshape(parts, rows_d, 3 * width + units)).astype(F32)
        mixing_grad = both[..., : 3 * width].reshape(parts, rows_d, 3, width)
        mixing_grad = mixing_grad.transpose(1, 2, 0, 3).reshape(rows_d, 3 * D)
        expand_grad = both[..., 3 * width :].reshape(parts, rows_d, copies, rows_f)
        expand_grad = expand_grad.transpose(1, 2, 0, 3).reshape(rows_d, FF)
        output_sum = jnp.sum(gradient, 0)
        affine_grad = jnp.concatenate(
            [
                gain_one_grad,
                shift_one_grad,
                gain_two_grad,
                shift_two_grad,
                spread_part(mixed_total, 3),
                output_sum,
                spread_part(hidden_total, copies),
                output_sum,
            ]
        )
        affine_grad = lax.all_to_all(
            affine_grad.reshape(devices, small),
            ("dp", "seq"),
            split_axis=0,
            concat_axis=0,
            tiled=True,
        )
        affine_grad = jnp.sum(affine_grad, 0)
        reduced[layer] = (mixing_grad, output_grad, expand_grad, shrink_grad, affine_grad)
        projected = jnp.mean(normed_grad * own_normed, -1, keepdims=True)
        middle = jnp.mean(normed_grad, -1, keepdims=True)
        gradient = gradient + scale * (normed_grad - middle - own_normed * projected)
    stream_grad = gradient.reshape(stream.shape)

    stacked = []
    squares = jnp.float32(0.0)
    for kind in range(5):
        kind_grad = jnp.stack([reduced[layer][kind] for layer in range(LAYERS)])
        stacked.append(kind_grad)
        squares = squares + jnp.sum(kind_grad * kind_grad)
    squares = lax.all_to_all(
        jnp.broadcast_to(squares, (devices, 128)),
        ("dp", "seq"),
        split_axis=0,
        concat_axis=0,
        tiled=True,
    )
    gradient_norm = jnp.sqrt(jnp.sum(squares[:, 0]))
    clip_scale = jnp.minimum(1.0, CLIP_LIMIT / (gradient_norm + 1e-06))
    step_rates = (D ** (-0.5), (D * 32 // LEN) ** (-0.5), D ** (-0.5), FF ** (-0.5), SMALL_RATE)
    decays = (WEIGHT_DECAY, WEIGHT_DECAY, WEIGHT_DECAY, WEIGHT_DECAY, 0.0)
    states = (
        (mixing_weight, mixing_first, mixing_second, mixing_average),
        (output_weight, output_first, output_second, output_average),
        (expand_weight, expand_first, expand_second, expand_average),
        (shrink_weight, shrink_first, shrink_second, shrink_average),
        (affine_weight, affine_first, affine_second, affine_average),
    )
    updated = ()
    for kind in range(5):
        weight, first_moment, second, average = states[kind]
        updated = updated + adamw_update(
            weight,
            first_moment,
            second,
            average,
            stacked[kind],
            clip_scale,
            step_rates[kind],
            decays[kind],
        )
    return (result, stream_grad, gradient_norm) + updated


def solution(mesh):
    tokens = P("dp", "seq", None)
    matrix = P(None, ("dp", "seq"), None)
    vector = P(None, ("dp", "seq"))
    states = (matrix,) * 16 + (vector,) * 4
    return jax.shard_map(
        local,
        mesh=mesh,
        in_specs=(tokens, tokens, P("dp", "seq")) + states,
        out_specs=(tokens, tokens, P()) + states,
        check_vma=False,
    )
```

```python
from functools import partial
import math

import jax
import jax.numpy as jnp
from jax import lax
from jax.experimental import pallas as pl
from jax.experimental.pallas import tpu as pltpu
from jax.sharding import PartitionSpec as P

D = 1024
H = 16
HD = 64
ROT = 16
FF = 4096
LEN = 2048
LAYERS = 2
STEP = 3

NORM_EPS = 1e-05
CLIP_LIMIT = 1.0
BETA_FIRST = 0.5
BETA_SECOND = 0.5
ADAM_EPS = 1e-08
WEIGHT_DECAY = 0.01
EMA_DECAY = 0.999
SMALL_RATE = 0.1
MASK_VALUE = -1e30
ROWS = 256
BLOCK = 512
QUERY_SCALE = 1.0 / math.sqrt(HD)
BF = jnp.bfloat16
F32 = jnp.float32
VMEM_LIMIT = 48 * 1024 * 1024


def dp_parts():
    size = lax.axis_size("dp")
    outer = 4 if size % 4 == 0 else size
    return outer, size // outer


def outer_ring(value):
    outer, inner = dp_parts()
    size = outer * inner
    return lax.ppermute(value, "dp", [(i, (i + inner) % size) for i in range(size)])


def inner_ring(value):
    outer, inner = dp_parts()
    moves = [
        (a * inner + b, a * inner + (b + 1) % inner) for a in range(outer) for b in range(inner)
    ]
    return lax.ppermute(value, "dp", moves)


def chip_ring(value):
    size = lax.axis_size("seq")
    return lax.ppermute(value, "seq", [(i, (i + 2) % size) for i in range(size)])


def core_swap(value):
    size = lax.axis_size("seq")
    return lax.ppermute(value, "seq", [(i, i ^ 1) for i in range(size)])


def assemble_kernel(slots_ref, *refs):
    n = pl.program_id(0)
    for step, piece_ref in enumerate(refs[:-1]):

        @pl.when(n == step)
        def _(piece_ref=piece_ref):
            refs[-1][...] = piece_ref[...][None]


def assemble(pieces, slots):
    count, piece = len(pieces), pieces[0]
    total = pl.pallas_call(
        assemble_kernel,
        grid_spec=pltpu.PrefetchScalarGridSpec(
            num_scalar_prefetch=1,
            grid=(count,),
            in_specs=[pl.BlockSpec(memory_space=pltpu.VMEM)] * count,
            out_specs=pl.BlockSpec((1,) + piece.shape, lambda n, slots: (slots[n], 0, 0)),
        ),
        out_shape=jax.ShapeDtypeStruct((count,) + piece.shape, piece.dtype),
        compiler_params=pltpu.CompilerParams(vmem_limit_bytes=VMEM_LIMIT),
        cost_estimate=pl.CostEstimate(
            flops=0, bytes_accessed=4 * count * piece.size, transcendentals=0
        ),
        name="assemble",
    )(jnp.stack(slots).astype(jnp.int32), *pieces)
    return total.reshape((count * piece.shape[0],) + piece.shape[1:])


def pick(total, first, second):
    sizes = (1, 1) + total.shape[2:]
    start = (first, second) + (0,) * (total.ndim - 2)
    return lax.dynamic_slice(total, start, sizes)[0, 0]


class Gather:
    def __init__(self, value):
        self.pieces = [value]
        self.chains = []

    def forward(self):
        self.pieces.append(outer_ring(self.pieces[-1]))

    def cross(self):
        chain = [self.pieces[len(self.chains)]]
        for turn in range(1, dp_parts()[1]):
            chain.append(inner_ring(chain[-1]))
        self.chains.append(chain)

    def hold(self, *values):
        held = lax.optimization_barrier((values, self.pieces, self.chains))
        self.pieces, self.chains = held[1], held[2]
        return held[0]

    def done(self):
        outer, inner = dp_parts()
        me = lax.axis_index("dp")
        a, b = me // inner, me % inner
        pieces, slots = [], []
        for step, chain in enumerate(self.chains):
            for turn, piece in enumerate(chain):
                pieces.append(piece)
                slots.append((a - step) % outer * inner + (b - turn) % inner)
        return assemble(pieces, slots)


class Scatter:
    def __init__(self, *values):
        outer, inner = dp_parts()
        me = lax.axis_index("dp")
        self.a, self.b = me // inner, me % inner
        self.values = [
            value.reshape((outer, inner, -1) + value.shape[1:]) for value in values
        ]
        self.parts = []
        self.arrived = None
        self.steps = 0

    def own(self, at, turn):
        inner = dp_parts()[1]
        taken = [pick(value, at, (self.b - turn) % inner) for value in self.values]
        return taken[0] if len(taken) == 1 else jnp.concatenate(taken, -1)

    def cross(self):
        outer, inner = dp_parts()
        at = (self.a - len(self.parts) - 1) % outer
        arrived = None
        for turn in range(1, inner):
            own = self.own(at, turn)
            if arrived is not None:
                own = (own.astype(F32) + arrived.astype(F32)).astype(BF)
            arrived = inner_ring(own)
        self.parts.append((self.own(at, 0), arrived))

    def part(self):
        own, arrived = self.parts[self.steps]
        total = own.astype(F32)
        if arrived is not None:
            total = total + arrived.astype(F32)
        if self.arrived is not None:
            total = total + self.arrived.astype(F32)
        return total

    def forward(self):
        self.arrived = outer_ring(self.part().astype(BF))
        self.steps += 1

    def hold(self, *values):
        held = lax.optimization_barrier((values, self.values, self.parts, self.arrived))
        self.values, self.parts, self.arrived = held[1], held[2], held[3]
        return held[0]

    def done(self):
        return self.part()


def seq_gather(value):
    chips = lax.axis_size("seq") // 2
    me = lax.axis_index("seq")
    y, c = me // 2, me % 2
    pieces, slots = [], []
    piece = value
    for step in range(chips):
        at = (y - step) % chips
        pieces += [piece, core_swap(piece)]
        slots += [2 * at + c, 2 * at + 1 - c]
        if step < chips - 1:
            piece = chip_ring(piece)
    return assemble(pieces, slots)


class SeqScatter:
    def __init__(self, others, own):
        chips = lax.axis_size("seq") // 2
        self.core = lax.axis_index("seq") % 2
        rows = own.shape[0] // 2
        others = others.reshape((chips - 1, 2, rows) + own.shape[1:])
        self.values = [others[n] for n in range(chips - 1)]
        self.values.append(own.reshape((2, rows) + own.shape[1:]))
        self.sending = self.cores(0).astype(BF)

    def cores(self, n):
        value = self.values[n]
        kept = lax.dynamic_index_in_dim(value, self.core, 0, keepdims=False)
        passed = lax.dynamic_index_in_dim(value, 1 - self.core, 0, keepdims=False)
        return kept.astype(F32) + core_swap(passed).astype(F32)

    def hold(self, *values):
        held = lax.optimization_barrier((values, self.sending))
        self.sending = held[1]
        return held[0]

    def done(self):
        for n in range(1, len(self.values)):
            arrived = chip_ring(self.sending)
            total = self.cores(n) + arrived.astype(F32)
            self.sending = total.astype(BF)
        return total


def seq_exchange(value):
    return lax.all_to_all(value, "seq", split_axis=0, concat_axis=0, tiled=True)


def head_masks(width, dtype):
    lane = lax.broadcasted_iota(jnp.int32, (1, width), 1) // HD
    return [(lane == h).astype(F32).astype(dtype) for h in range(width // HD)]


def swap_halves(values):
    width = values.shape[1]
    lane = lax.broadcasted_iota(jnp.int32, values.shape, 1) % HD
    return jnp.where(
        lane < ROT // 2,
        pltpu.roll(values, width - ROT // 2, 1),
        pltpu.roll(values, ROT // 2, 1),
    )


def matmul(left, right):
    return lax.dot_general(left, right, (((1,), (0,)), ((), ())), preferred_element_type=F32)


def matmul_nt(left, right):
    return lax.dot_general(left, right, (((1,), (1,)), ((), ())), preferred_element_type=F32)


def matmul_tn(left, right):
    return lax.dot_general(left, right, (((0,), (0,)), ((), ())), preferred_element_type=F32)


def mix_kernel(x_ref, w_ref, c_ref, cos_ref, sin_ref, out_ref):
    mixed = matmul(x_ref[...], w_ref[...]) + c_ref[...]
    cosine, sine = cos_ref[...], sin_ref[...]
    for start in range(0, w_ref.shape[1], 3 * 128):
        query = mixed[:, start : start + 128]
        key = mixed[:, start + 128 : start + 256]
        query = (query * cosine + swap_halves(query) * sine) * QUERY_SCALE
        key = key * cosine + swap_halves(key) * sine
        out_ref[:, start : start + 128] = query.astype(BF)
        out_ref[:, start + 128 : start + 256] = key.astype(BF)
        out_ref[:, start + 256 : start + 384] = mixed[:, start + 256 : start + 384].astype(BF)


def mix(x, weight, shift, cosine, sine):
    length, columns = x.shape[0], weight.shape[1]
    return pl.pallas_call(
        mix_kernel,
        grid=(length // ROWS,),
        in_specs=[
            pl.BlockSpec((ROWS, D), lambda i: (i, 0)),
            pl.BlockSpec((D, columns), lambda i: (0, 0)),
            pl.BlockSpec((1, columns), lambda i: (0, 0)),
            pl.BlockSpec((ROWS, 128), lambda i: (i, 0)),
            pl.BlockSpec((ROWS, 128), lambda i: (i, 0)),
        ],
        out_specs=pl.BlockSpec((ROWS, columns), lambda i: (i, 0)),
        out_shape=jax.ShapeDtypeStruct((length, columns), BF),
        compiler_params=pltpu.CompilerParams(vmem_limit_bytes=VMEM_LIMIT),
        cost_estimate=pl.CostEstimate(
            flops=2 * length * D * columns,
            bytes_accessed=2 * (length * D + D * columns + length * columns),
            transcendentals=0,
        ),
        name="mix",
    )(x, weight, shift, cosine, sine)


def attend_kernel(q_ref, k_ref, v_ref, o_ref, lse_ref, acc_ref, turned_ref):
    block, width = q_ref.shape
    heads = width // HD
    i = pl.program_id(0)
    query = q_ref[...]
    queries = [query * mask for mask in head_masks(width, BF)]

    @pl.when(i == 0)
    def _():
        turned_ref[...] = v_ref[...].T

    acc_ref[...] = jnp.zeros(acc_ref.shape, F32)

    def tile(j, diagonal, carry):
        rows = pl.ds(pl.multiple_of(j * block, block), block)
        key = k_ref[rows, :]
        scores = [matmul_nt(key, queries[h]) for h in range(heads)]
        if diagonal:
            row = lax.broadcasted_iota(jnp.int32, (block, block), 0)
            column = lax.broadcasted_iota(jnp.int32, (block, block), 1)
            allowed = row <= column
            scores = [jnp.where(allowed, score, MASK_VALUE) for score in scores]
        highs = [
            jnp.maximum(carry[h][0], jnp.max(scores[h], 0, keepdims=True)) for h in range(heads)
        ]
        weights = [jnp.exp(scores[h] - highs[h]) for h in range(heads)]
        fades = [jnp.exp(carry[h][0] - highs[h]) for h in range(heads)]
        sums = [
            carry[h][1] * fades[h] + jnp.sum(weights[h], 0, keepdims=True) for h in range(heads)
        ]
        for h in range(heads):
            part = slice(h * HD, (h + 1) * HD)
            product = matmul(turned_ref[part, rows], weights[h].astype(BF))
            acc_ref[part, :] = acc_ref[part, :] * fades[h] + product
        return [(highs[h], sums[h]) for h in range(heads)]

    empty = (jnp.full((1, block), MASK_VALUE, F32), jnp.zeros((1, block), F32))
    carry = lax.fori_loop(0, i, lambda j, carry: tile(j, False, carry), [empty] * heads)
    carry = tile(i, True, carry)
    for h in range(heads):
        part = slice(h * HD, (h + 1) * HD)
        acc_ref[part, :] = acc_ref[part, :] / carry[h][1]
        lse_ref[h : h + 1, :] = carry[h][0] + jnp.log(carry[h][1])
    o_ref[...] = acc_ref[...].T.astype(BF)


def attend(mixed, half):
    length, width = mixed.shape[0], 128
    heads = width // HD
    block = min(BLOCK, length)
    return pl.pallas_call(
        attend_kernel,
        grid=(length // block,),
        in_specs=[
            pl.BlockSpec((block, width), lambda i: (i, 3 * half)),
            pl.BlockSpec((length, width), lambda i: (0, 3 * half + 1)),
            pl.BlockSpec((length, width), lambda i: (0, 3 * half + 2)),
        ],
        out_specs=[
            pl.BlockSpec((block, width), lambda i: (i, 0)),
            pl.BlockSpec((heads, block), lambda i: (0, i)),
        ],
        out_shape=[
            jax.ShapeDtypeStruct((length, width), BF),
            jax.ShapeDtypeStruct((heads, length), F32),
        ],
        scratch_shapes=[
            pltpu.VMEM((width, block), F32),
            pltpu.VMEM((width, length), BF),
        ],
        compiler_params=pltpu.CompilerParams(vmem_limit_bytes=VMEM_LIMIT),
        cost_estimate=pl.CostEstimate(
            flops=8 * length * length * width,
            bytes_accessed=8 * length * width,
            transcendentals=length * length * heads,
        ),
        name="attend",
    )(mixed, mixed, mixed)


def attend_back_kernel(
    q_ref,
    k_ref,
    v_ref,
    do_ref,
    o_ref,
    lse_ref,
    cos_ref,
    sin_ref,
    out_ref,
    total_ref,
    inner_ref,
    dq_ref,
    dk_ref,
    dv_ref,
):
    block, width = k_ref.shape
    length = q_ref.shape[0]
    heads = width // HD
    steps = length // block
    j = pl.program_id(0)
    masks = head_masks(width, BF)
    key = k_ref[...]
    value = v_ref[...]
    keys = [key * mask for mask in masks]
    values = [value * mask for mask in masks]

    @pl.when(j == 0)
    def _():
        dq_ref[...] = jnp.zeros(dq_ref.shape, F32)
        total_ref[...] = jnp.zeros(total_ref.shape, F32)
        product = do_ref[...].astype(F32) * o_ref[...].astype(F32)
        coarse = product.astype(BF)
        fine = (product - coarse.astype(F32)).astype(BF)
        row = lax.broadcasted_iota(jnp.int32, (8, width), 0)
        lane = lax.broadcasted_iota(jnp.int32, (8, width), 1) // HD
        chosen = (row == lane).astype(F32).astype(BF)
        inner_ref[...] = matmul_nt(chosen, coarse) + matmul_nt(chosen, fine)

    dk_ref[...] = jnp.zeros(dk_ref.shape, F32)
    dv_ref[...] = jnp.zeros(dv_ref.shape, F32)

    def tile(i, diagonal):
        rows = pl.ds(pl.multiple_of(i * block, block), block)
        query = q_ref[rows, :]
        grad = do_ref[rows, :]
        log_total = lse_ref[:, rows]
        inner = inner_ref[:, rows]
        scores = [matmul_nt(keys[h], query) for h in range(heads)]
        weight_grads = [matmul_nt(values[h], grad) for h in range(heads)]
        if diagonal:
            row = lax.broadcasted_iota(jnp.int32, (block, block), 0)
            column = lax.broadcasted_iota(jnp.int32, (block, block), 1)
            allowed = row <= column
            scores = [jnp.where(allowed, score, MASK_VALUE) for score in scores]
        weights = [jnp.exp(scores[h] - log_total[h : h + 1, :]) for h in range(heads)]
        low = [weight.astype(BF) for weight in weights]
        score_grads = [
            (weights[h] * (weight_grads[h] - inner[h : h + 1, :])).astype(BF)
            for h in range(heads)
        ]
        dv_ref[...] += matmul(
            jnp.concatenate(low, 1), jnp.concatenate([grad * mask for mask in masks], 0)
        )
        dk_ref[...] += matmul(
            jnp.concatenate(score_grads, 1),
            jnp.concatenate([query * mask for mask in masks], 0),
        )
        dq_ref[rows, :] += matmul_tn(
            jnp.concatenate(score_grads, 0), jnp.concatenate(keys, 0)
        )

    def step(i, carry):
        tile(i, False)
        return carry

    tile(j, True)
    lax.fori_loop(j + 1, steps, step, 0)

    own = pl.ds(pl.multiple_of(j * block, block), block)
    cosine = cos_ref[own, :]
    sine = sin_ref[own, :]
    key_grad = dk_ref[...]
    key_grad = key_grad * cosine - swap_halves(key_grad) * sine
    value_grad = dv_ref[...]
    query_grad = dq_ref[own, :] * QUERY_SCALE
    query_grad = query_grad * cosine - swap_halves(query_grad) * sine
    out_ref[:, :width] = query_grad.astype(BF)
    out_ref[:, width : 2 * width] = key_grad.astype(BF)
    out_ref[:, 2 * width :] = value_grad.astype(BF)
    total_ref[:, :width] += jnp.sum(query_grad, 0, keepdims=True)
    total_ref[:, width : 2 * width] += jnp.sum(key_grad, 0, keepdims=True)
    total_ref[:, 2 * width :] += jnp.sum(value_grad, 0, keepdims=True)


def attend_back(mixed, grads, attended, log_total, cosine, sine, half):
    length, width = mixed.shape[0], 128
    heads = width // HD
    block = min(BLOCK, length)
    return pl.pallas_call(
        attend_back_kernel,
        grid=(length // block,),
        in_specs=[
            pl.BlockSpec((length, width), lambda j: (0, 3 * half)),
            pl.BlockSpec((block, width), lambda j: (j, 3 * half + 1)),
            pl.BlockSpec((block, width), lambda j: (j, 3 * half + 2)),
            pl.BlockSpec((length, width), lambda j: (0, half)),
            pl.BlockSpec((length, width), lambda j: (0, 0)),
            pl.BlockSpec((heads, length), lambda j: (0, 0)),
            pl.BlockSpec((length, 128), lambda j: (0, 0)),
            pl.BlockSpec((length, 128), lambda j: (0, 0)),
        ],
        out_specs=[
            pl.BlockSpec((block, 3 * width), lambda j: (j, 0)),
            pl.BlockSpec((1, 3 * width), lambda j: (0, 0)),
        ],
        out_shape=[
            jax.ShapeDtypeStruct((length, 3 * width), BF),
            jax.ShapeDtypeStruct((1, 3 * width), F32),
        ],
        scratch_shapes=[
            pltpu.VMEM((8, length), F32),
            pltpu.VMEM((length, width), F32),
            pltpu.VMEM((block, width), F32),
            pltpu.VMEM((block, width), F32),
        ],
        compiler_params=pltpu.CompilerParams(vmem_limit_bytes=VMEM_LIMIT),
        cost_estimate=pl.CostEstimate(
            flops=20 * length * length * width,
            bytes_accessed=16 * length * width,
            transcendentals=length * length * heads,
        ),
        name="attend_back",
    )(mixed, mixed, mixed, grads, attended, log_total, cosine, sine)


def gelu_pair(values):
    size = jnp.abs(values) * (1.0 / math.sqrt(2.0))
    bell = jnp.exp(-size * size)
    turn = 1.0 / (1.0 + 0.3275911 * size)
    series = turn * (
        0.254829592
        + turn * (-0.284496736 + turn * (1.421413741 + turn * (-1.453152027 + turn * 1.061405429)))
    )
    tail = 0.5 * series * bell
    below = jnp.where(values < 0.0, tail, 1.0 - tail)
    slope = below + values * bell * (1.0 / math.sqrt(2.0 * math.pi))
    return values * below, slope


def chip_rows(own, length):
    chips = lax.axis_size("seq") // 2
    y = lax.axis_index("seq") // 2
    per = length // ROWS // chips
    if own:
        return per, lambda i, y_ref: y_ref[0] * per + i, y
    return (
        (chips - 1) * per,
        lambda i, y_ref: (y_ref[0] + chips - 1 - i // per) % chips * per + i % per,
        y,
    )


def feed_kernel(y_ref, x_ref, wi_ref, ci_ref, wd_ref, wo_ref, *refs):
    attended = refs[: wo_ref.shape[0] // 128]
    act_ref, slope_ref, out_ref = refs[-3:]
    hidden = matmul(x_ref[...], wi_ref[...]) + ci_ref[...]
    activated, slope = gelu_pair(hidden)
    activated = activated.astype(BF)
    act_ref[...] = activated
    slope_ref[...] = slope.astype(BF)
    out = matmul(activated, wd_ref[...])
    for half, o_ref in enumerate(attended):
        out = out + matmul(o_ref[...], wo_ref[half * 128 : (half + 1) * 128, :])
    out_ref[...] = out.astype(BF)


def feed(x, expand, shift, shrink, output, attended, own, kept=()):
    length, units, width = x.shape[0], expand.shape[1], output.shape[0]
    steps, row, y = chip_rows(own, length)

    def rows(columns):
        return pl.BlockSpec((ROWS, columns), lambda i, y_ref: (row(i, y_ref), 0))

    def whole(shape):
        return pl.BlockSpec(shape, lambda i, y_ref: (0, 0))

    first = 6 + len(attended)
    return pl.pallas_call(
        feed_kernel,
        grid_spec=pltpu.PrefetchScalarGridSpec(
            num_scalar_prefetch=1,
            grid=(steps,),
            in_specs=[rows(D), whole((D, units)), whole((1, units)), whole((units, D))]
            + [whole((width, D))]
            + [rows(128)] * len(attended)
            + [pl.BlockSpec(memory_space=pl.ANY)] * len(kept),
            out_specs=[
                rows(units),
                rows(units),
                pl.BlockSpec((ROWS, D), lambda i, y_ref: (i, 0)),
            ],
        ),
        out_shape=[
            jax.ShapeDtypeStruct((length, units), BF),
            jax.ShapeDtypeStruct((length, units), BF),
            jax.ShapeDtypeStruct((steps * ROWS, D), BF),
        ],
        input_output_aliases={first: 0, first + 1: 1} if kept else {},
        compiler_params=pltpu.CompilerParams(vmem_limit_bytes=VMEM_LIMIT),
        cost_estimate=pl.CostEstimate(
            flops=2 * steps * ROWS * D * (2 * units + width),
            bytes_accessed=2 * (2 * D * units + 2 * steps * ROWS * (D + units)),
            transcendentals=steps * ROWS * units,
        ),
        name="feed",
    )(y.reshape(1), x, expand, shift, shrink, output, *attended, *kept)


def norm_grad_kernel(y_ref, h_ref, wi_ref, wm_ref, *refs):
    out = matmul_nt(h_ref[...], wi_ref[...])
    for half, m_ref in enumerate(refs[:-1]):
        out = out + matmul_nt(m_ref[...], wm_ref[:, half * 384 : (half + 1) * 384])
    refs[-1][...] = out.astype(BF)


def norm_grad(hidden, expand, mixed, mixing, own):
    length, units, columns = hidden.shape[0], expand.shape[1], mixing.shape[1]
    steps, row, y = chip_rows(own, length)

    def rows(count):
        return pl.BlockSpec((ROWS, count), lambda i, y_ref: (row(i, y_ref), 0))

    def whole(shape):
        return pl.BlockSpec(shape, lambda i, y_ref: (0, 0))

    return pl.pallas_call(
        norm_grad_kernel,
        grid_spec=pltpu.PrefetchScalarGridSpec(
            num_scalar_prefetch=1,
            grid=(steps,),
            in_specs=[rows(units), whole((D, units)), whole((D, columns))]
            + [rows(384)] * len(mixed),
            out_specs=pl.BlockSpec((ROWS, D), lambda i, y_ref: (i, 0)),
        ),
        out_shape=jax.ShapeDtypeStruct((steps * ROWS, D), BF),
        compiler_params=pltpu.CompilerParams(vmem_limit_bytes=VMEM_LIMIT),
        cost_estimate=pl.CostEstimate(
            flops=2 * steps * ROWS * D * (units + columns),
            bytes_accessed=2 * (D + steps * ROWS) * (units + columns),
            transcendentals=0,
        ),
        name="norm_grad",
    )(y.reshape(1), hidden, expand, mixing, *mixed)


def home_spans(parts, copies, width, units):
    mixing, expand = [], []
    size = units // copies
    for p in range(parts):
        for half in range(width // 128):
            for kind in range(3):
                at = kind * parts * width + p * width + half * 128
                mixing.append((p, half * 384 + kind * 128, at, 128))
        for d in range(copies):
            expand.append((p, 3 * width + d * size, (d * parts + p) * size, size))
    return mixing, expand


def adam(grad, weight, first, second, average, rate, decay):
    first_new = BETA_FIRST * first + (1.0 - BETA_FIRST) * grad
    second_new = BETA_SECOND * second + (1.0 - BETA_SECOND) * grad * grad
    first_hat = first_new / (1.0 - BETA_FIRST**STEP)
    second_hat = second_new / (1.0 - BETA_SECOND**STEP)
    weight_new = weight - rate * (
        first_hat / (jnp.sqrt(second_hat) + ADAM_EPS) + decay * weight
    )
    return weight_new, first_new, second_new, EMA_DECAY * average + (1.0 - EMA_DECAY) * weight_new


def adam_kernel(spans, rates, clip_ref, exchanged_ref, output_ref, shrink_ref, *refs):
    clip = clip_ref[0]
    states, news = refs[:16], refs[16:]

    def step(kind, grad, columns):
        old = [ref[0, :, columns] for ref in states[4 * kind : 4 * kind + 4]]
        new = adam(grad.astype(F32) * clip, *old, rates[kind], WEIGHT_DECAY)
        for ref, value in zip(news[4 * kind : 4 * kind + 4], new):
            ref[0, :, columns] = value

    for kind, part in ((0, spans[0]), (2, spans[1])):
        for source, start, at, count in part:
            grad = exchanged_ref[0, source, :, start : start + count]
            step(kind, grad, slice(at, at + count))
    step(1, output_ref[0], slice(None))
    step(3, shrink_ref[0], slice(None))


def update(clip, exchanged, output, shrink, states, spans, rates):
    layers, parts, rows, columns = exchanged.shape
    chunk = 16 if rows % 16 == 0 else rows
    chunks = rows // chunk

    def block(array):
        size = array.shape[1] // chunks
        return pl.BlockSpec((1, size, array.shape[2]), lambda l, n: (l, n, 0))

    return pl.pallas_call(
        partial(adam_kernel, spans, rates),
        grid=(layers, chunks),
        in_specs=[
            pl.BlockSpec(memory_space=pltpu.SMEM),
            pl.BlockSpec((1, parts, chunk, columns), lambda l, n: (l, 0, n, 0)),
            block(output),
            block(shrink),
        ]
        + [block(state) for state in states],
        out_specs=[block(state) for state in states],
        out_shape=[jax.ShapeDtypeStruct(state.shape, F32) for state in states],
        compiler_params=pltpu.CompilerParams(vmem_limit_bytes=VMEM_LIMIT),
        name="update",
    )(clip, exchanged, output, shrink, *states)


def rotary_tables(positions):
    half = ROT // 2
    steps_half = jnp.arange(half).astype(F32)
    frequency = 10000.0 ** (-2.0 * steps_half / ROT)
    angles = positions.astype(F32)[None, :] * frequency[:, None]
    cosine = jnp.concatenate([jnp.cos(angles), jnp.ones_like(angles)], 0)
    entry = jnp.arange(128)[None, :] % HD
    index = jnp.arange(half)[:, None]
    turning = (entry < ROT) & (entry % half == index)
    still = (entry >= ROT) & (index == 0)
    sign = jnp.where(entry < half, -1.0, 1.0)
    spread_cosine = jnp.concatenate([turning, still], 0).astype(F32)
    spread_sine = turning.astype(F32) * sign

    def lay(table, spread):
        return lax.dot_general(
            table, spread, (((0,), (0,)), ((), ())), precision=lax.Precision.HIGHEST
        )

    return lay(cosine, spread_cosine), lay(jnp.sin(angles), spread_sine)


def split_affine(affine):
    bounds = [D, D, D, D, 3 * D, D, FF, D]
    pieces = []
    offset = 0
    for length in bounds:
        pieces.append(affine[offset : offset + length])
        offset = offset + length
    return pieces


def normalize(values):
    centre = values - jnp.mean(values, -1, keepdims=True)
    spread = jnp.mean(centre * centre, -1, keepdims=True)
    scale = lax.rsqrt(spread + NORM_EPS)
    return centre * scale, scale


def local(
    stream,
    cotangent,
    positions,
    mixing_weight,
    mixing_first,
    mixing_second,
    mixing_average,
    output_weight,
    output_first,
    output_second,
    output_average,
    expand_weight,
    expand_first,
    expand_second,
    expand_average,
    shrink_weight,
    shrink_first,
    shrink_second,
    shrink_average,
    affine_weight,
    affine_first,
    affine_second,
    affine_average,
):
    parts = lax.axis_size("seq")
    copies = lax.axis_size("dp")
    devices = parts * copies
    part = lax.axis_index("seq")
    width = D // parts
    units = FF // parts
    rows_d = D // devices
    rows_f = FF // devices
    rows = stream.shape[0] * stream.shape[1]
    small = affine_weight.shape[1]

    halves = width // 128
    outer = dp_parts()[0]

    def mixing_part(vector):
        view = vector.reshape(3, parts, halves, 128)
        view = lax.dynamic_index_in_dim(view, part, 1, keepdims=False)
        return view.transpose(1, 0, 2).reshape(-1)

    def expand_part(vector):
        view = vector.reshape(copies, parts, -1)
        return lax.dynamic_index_in_dim(view, part, 1, keepdims=False).reshape(-1)

    def spread_mixing(vector):
        view = jnp.zeros((3, parts, width), F32)
        vector = vector.reshape(halves, 3, 128).transpose(1, 0, 2).reshape(3, 1, width)
        return lax.dynamic_update_slice(view, vector, (0, part, 0)).reshape(-1)

    def spread_expand(vector):
        view = jnp.zeros((copies, parts, rows_f), F32)
        return lax.dynamic_update_slice(view, vector.reshape(copies, 1, rows_f), (0, part, 0)).reshape(-1)

    def arrange(mixing, expand):
        mixing = mixing.astype(BF).reshape(rows_d, 3, parts, halves, 128)
        mixing = mixing.transpose(2, 0, 3, 1, 4).reshape(parts, rows_d, 3 * width)
        expand = expand.astype(BF).reshape(rows_d, copies, parts, rows_f)
        expand = expand.transpose(2, 0, 1, 3).reshape(parts, rows_d, units)
        return [mixing, expand]

    def settle_output(gathered):
        gathered = gathered.reshape(parts, copies // parts * rows_d, D)
        output = seq_exchange(gathered).reshape(parts, copies // parts, rows_d, D)
        return output.transpose(1, 0, 2, 3).reshape(width, D)

    def scaled(weight, gain, shift, bias):
        wide = weight.astype(F32)
        return (wide * gain[:, None]).astype(BF), (jnp.sum(wide * shift[:, None], 0) + bias)[None]

    def shift_grads(raw, weight, total, gain, shift):
        wide = weight.astype(F32)
        return (
            (raw * gain[:, None] + shift[:, None] * total).astype(BF),
            jnp.sum(raw * wide, 1),
            jnp.sum(wide * total, 1),
        )

    def norm_back(gradient, normed_grad, own_normed, scale):
        projected = jnp.mean(normed_grad * own_normed, -1, keepdims=True)
        middle = jnp.mean(normed_grad, -1, keepdims=True)
        return gradient + scale * (normed_grad - middle - own_normed * projected)

    def outgoing_output(attended, grads):
        output_grad = jnp.concatenate([matmul_tn(out, grads).astype(BF) for out in attended], 0)
        output_grad = output_grad.reshape(copies // parts, parts, rows_d, D).transpose(1, 0, 2, 3)
        output_grad = seq_exchange(output_grad.reshape(parts, copies // parts * rows_d, D))
        return output_grad.reshape(-1, width)

    def affine_home(pieces):
        affine_grad = lax.all_to_all(
            jnp.concatenate(pieces).reshape(devices, small),
            ("dp", "seq"),
            split_axis=0,
            concat_axis=0,
            tiled=True,
        )
        return jnp.sum(affine_grad, 0)

    def sum_squares(*values):
        return sum(jnp.sum(value.astype(F32) * value.astype(F32)) for value in values)

    current = stream.reshape(rows, D)
    gradient = cotangent.reshape(rows, D)

    pair = jnp.stack([positions.reshape(-1) // 16, positions.reshape(-1) % 16]).astype(BF)
    pair = jnp.broadcast_to(pair.reshape(1, rows_d, -1), (parts, rows_d, 2 * rows // rows_d))
    both = jnp.concatenate(arrange(mixing_weight[0], expand_weight[0]) + [pair], -1)
    both = seq_exchange(both)
    pair = both[..., 3 * width + units :].astype(F32).reshape(parts, 2, rows)
    places = (pair[:, 0] * 16.0 + pair[:, 1]).reshape(-1)
    both = both.reshape(parts * rows_d, -1)
    near = Gather(
        jnp.concatenate(
            [both[:, : 3 * width], output_weight[0].astype(BF).reshape(-1, width)], -1
        )
    )
    affine_low, near.pieces = lax.optimization_barrier((affine_weight.astype(BF), near.pieces))
    affine_low = affine_low.reshape(1, LAYERS * small)
    affine_all = lax.all_to_all(
        jnp.broadcast_to(affine_low, (devices, LAYERS * small)),
        ("dp", "seq"),
        split_axis=0,
        concat_axis=0,
        tiled=True,
    )
    affine_all = affine_all.reshape(devices, LAYERS, small).transpose(1, 0, 2)
    affine_all = affine_all.reshape(LAYERS, devices * small).astype(F32)
    vectors = [split_affine(affine_all[layer]) for layer in range(LAYERS)]
    own_normed, scale = normalize(current)
    normed = seq_gather(own_normed.astype(BF))
    for step in range(outer - 1):
        near.forward()
        near.cross()
    expand_own, shrink_own, places = near.hold(
        both[:, 3 * width : 3 * width + units], shrink_weight[0], places
    )
    near.cross()
    far = Gather(
        jnp.concatenate([expand_own, shrink_own.astype(BF).reshape(-1, units)], -1)
    )
    far.forward()
    far.cross()
    cosine, sine = rotary_tables(places)
    gathered = near.done()
    mixing = gathered[:, : 3 * width]
    output = settle_output(gathered[:, 3 * width :].reshape(copies * rows_d, D))

    later = far.hold(
        *(weight[1] for weight in (mixing_weight, expand_weight, output_weight, shrink_weight))
    )
    later_both = seq_exchange(jnp.concatenate(arrange(later[0], later[1]), -1))
    later_both = later_both.reshape(parts * rows_d, -1)
    later_own = jnp.concatenate(
        [
            later_both[:, : 3 * width],
            later[2].astype(BF).reshape(-1, width),
            later_both[:, 3 * width :],
            later[3].astype(BF).reshape(-1, units),
        ],
        -1,
    )
    later_all = lax.all_gather(later_own, "dp", axis=0, tiled=True)

    gain_one, shift_one, gain_two, shift_two = vectors[0][:4]
    mixing_scaled, mixing_shift = scaled(mixing, gain_one, shift_one, mixing_part(vectors[0][4]))
    mixed = mix(normed, mixing_scaled, mixing_shift, cosine, sine)
    mixed, low_gradient = far.hold(mixed, gradient.astype(BF))
    grads = seq_gather(low_gradient)
    attended, logs = [], []
    for half in range(halves):
        if len(far.pieces) < outer:
            far.forward()
            far.cross()
        out, log_total = attend(mixed, half)
        mixed, out, log_total, grads = far.hold(mixed, out, log_total, grads)
        attended.append(out)
        logs.append(log_total)
    while len(far.pieces) < outer:
        far.forward()
    while len(far.chains) < outer:
        far.cross()
    gathered = far.done()
    expand, shrink = gathered[:, :units], gathered[:, units:].reshape(-1, D)
    expand_scaled, expand_shift = scaled(
        expand, gain_two, shift_two, expand_part(vectors[0][6])
    )
    weight_set = (normed, expand_scaled, expand_shift, shrink, output, attended)
    activated, slope, others = feed(*weight_set, False)
    activated, slope, own = feed(*weight_set, True, (activated, slope))
    stored = [(own_normed, scale, normed, mixed, attended, logs, activated, slope)]
    weights = [(mixing, mixing_scaled, output, expand, expand_scaled, shrink)]
    current = current + SeqScatter(others, own).done() + vectors[0][5] + vectors[0][7]

    own_normed, scale = normalize(current)
    normed = seq_gather(own_normed.astype(BF))
    mixing = later_all[:, : 3 * width]
    output = settle_output(later_all[:, 3 * width : 4 * width].reshape(copies * rows_d, D))
    expand = later_all[:, 4 * width : 4 * width + units]
    shrink = later_all[:, 4 * width + units :].reshape(-1, D)
    gain_one, shift_one, gain_two, shift_two = vectors[1][:4]
    mixing_scaled, mixing_shift = scaled(mixing, gain_one, shift_one, mixing_part(vectors[1][4]))
    expand_scaled, expand_shift = scaled(
        expand, gain_two, shift_two, expand_part(vectors[1][6])
    )
    mixed = mix(normed, mixing_scaled, mixing_shift, cosine, sine)
    attended, logs = [], []
    for half in range(halves):
        out, log_total = attend(mixed, half)
        attended.append(out)
        logs.append(log_total)
    weight_set = (normed, expand_scaled, expand_shift, shrink, output, attended)
    activated, slope, others = feed(*weight_set, False)
    activated, slope, own = feed(*weight_set, True, (activated, slope))
    result = current + SeqScatter(others, own).done() + vectors[1][5] + vectors[1][7]
    result = result.reshape(stream.shape)

    attended_grad = matmul_nt(grads, output).astype(BF)
    shrink_grad = matmul_tn(activated, grads).astype(BF).reshape(-1, units)
    output_grad = outgoing_output(attended, grads)
    later_first = lax.psum_scatter(
        jnp.concatenate([shrink_grad, output_grad], -1), "dp", scatter_dimension=0, tiled=True
    )
    hidden_grad = matmul_nt(grads, shrink) * slope.astype(F32)
    hidden_total = jnp.sum(hidden_grad, 0)
    hidden_low = hidden_grad.astype(BF)
    lows, totals = [], []
    for half in range(halves):
        low, total = attend_back(
            mixed, attended_grad, attended[half], logs[half], cosine, sine, half
        )
        lows.append(low)
        totals.append(total[0])
    mixed_total = jnp.concatenate(totals)
    output_sum = jnp.sum(gradient, 0)
    others = norm_grad(hidden_low, expand_scaled, lows, mixing_scaled, False)
    own = norm_grad(hidden_low, expand_scaled, lows, mixing_scaled, True)
    travel = SeqScatter(others, own)
    hidden_low, lows = travel.hold(hidden_low, lows)
    expand_raw = matmul_tn(normed, hidden_low)
    mixing_raw = jnp.concatenate([matmul_tn(normed, low) for low in lows], -1)
    expand_grad, gain_two_grad, shift_two_grad = shift_grads(
        expand_raw, expand, hidden_total, gain_two, shift_two
    )
    mixing_grad, gain_one_grad, shift_one_grad = shift_grads(
        mixing_raw, mixing, mixed_total, gain_one, shift_one
    )
    pieces = [gain_one_grad, shift_one_grad, gain_two_grad, shift_two_grad]
    pieces += [spread_mixing(mixed_total), output_sum, spread_expand(hidden_total), output_sum]
    normed_grad, expand_grad, mixing_grad, pieces = lax.optimization_barrier(
        (travel.done(), expand_grad, mixing_grad, pieces)
    )
    gradient = norm_back(gradient, normed_grad, own_normed, scale)
    low_gradient, expand_grad, mixing_grad, pieces = lax.optimization_barrier(
        (gradient.astype(BF), expand_grad, mixing_grad, pieces)
    )
    grads = seq_gather(low_gradient)
    later_second = lax.psum_scatter(
        jnp.concatenate([mixing_grad, expand_grad], -1), "dp", scatter_dimension=0, tiled=True
    )
    later_affine = affine_home(pieces)

    own_normed, scale, normed, mixed, attended, logs, activated, slope = stored[0]
    mixing, mixing_scaled, output, expand, expand_scaled, shrink = weights[0]
    gain_one, shift_one, gain_two, shift_two = vectors[0][:4]
    shrink_grad = matmul_tn(activated, grads).astype(BF).reshape(-1, units)
    hidden_grad = matmul_nt(grads, shrink) * slope.astype(F32)
    hidden_total = jnp.sum(hidden_grad, 0)
    hidden_low = hidden_grad.astype(BF)
    expand_raw = matmul_tn(normed, hidden_low)
    expand_grad, gain_two_grad, shift_two_grad = shift_grads(
        expand_raw, expand, hidden_total, gain_two, shift_two
    )
    attended_grad = matmul_nt(grads, output).astype(BF)
    far = Scatter(expand_grad, shrink_grad)
    (attended_grad,) = far.hold(attended_grad)
    far.cross()
    output_grad = outgoing_output(attended, grads)
    lows, totals = [], []
    for half in range(halves):
        low, total = attend_back(
            mixed, attended_grad, attended[half], logs[half], cosine, sine, half
        )
        mixed, low, total = far.hold(mixed, low, total)
        if len(far.parts) < outer:
            far.forward()
            far.cross()
        lows.append(low)
        totals.append(total[0])
    mixed_total = jnp.concatenate(totals)
    mixing_raw = jnp.concatenate([matmul_tn(normed, low) for low in lows], -1)
    mixing_grad, gain_one_grad, shift_one_grad = shift_grads(
        mixing_raw, mixing, mixed_total, gain_one, shift_one
    )
    mixing_grad, lows = far.hold(mixing_grad, lows)
    while len(far.parts) < outer:
        far.forward()
        far.cross()
    near = Scatter(mixing_grad, output_grad)
    near.cross()
    while far.steps < outer - 1:
        far.forward()
    others = norm_grad(hidden_low, expand_scaled, lows, mixing_scaled, False)
    own = norm_grad(hidden_low, expand_scaled, lows, mixing_scaled, True)
    travel = SeqScatter(others, own)
    for step in range(outer - 1):
        near.forward()
        near.cross()
    output_sum = jnp.sum(gradient, 0)
    pieces = [gain_one_grad, shift_one_grad, gain_two_grad, shift_two_grad]
    pieces += [spread_mixing(mixed_total), output_sum, spread_expand(hidden_total), output_sum]
    affine_grad = jnp.stack([affine_home(pieces), later_affine])
    gradient = norm_back(gradient, travel.done(), own_normed, scale)
    stream_grad = gradient.reshape(stream.shape)

    later_home = seq_exchange(later_second.reshape(parts, rows_d, -1))
    far_grad = far.done()
    near_grad = near.done()
    home = jnp.concatenate([near_grad[:, : 3 * width], far_grad[:, :units]], -1).astype(BF)
    home = seq_exchange(home.reshape(parts, rows_d, -1))
    squares = sum_squares(near_grad, far_grad, later_first, later_second, affine_grad)
    squares = lax.all_to_all(
        jnp.broadcast_to(squares, (devices, 128)),
        ("dp", "seq"),
        split_axis=0,
        concat_axis=0,
        tiled=True,
    )
    gradient_norm = jnp.sqrt(jnp.sum(squares[:, 0]))
    clip_scale = jnp.minimum(1.0, CLIP_LIMIT / (gradient_norm + 1e-06))
    exchanged = jnp.stack([home, later_home])
    output_grad = jnp.stack(
        [near_grad[:, 3 * width :].astype(BF), later_first[:, units:]]
    ).reshape(LAYERS, rows_d, D)
    shrink_grad = jnp.stack([far_grad[:, units:].astype(BF), later_first[:, :units]])
    shrink_grad = shrink_grad.reshape(LAYERS, rows_f, D)
    spans = home_spans(parts, copies, width, units)
    if rows_f % 128 or rows_d % 16:
        mixing_view = exchanged[..., : 3 * width].reshape(LAYERS, parts, rows_d, halves, 3, 128)
        mixing_view = mixing_view.transpose(0, 2, 4, 1, 3, 5).reshape(LAYERS, rows_d, 3 * D)
        expand_view = exchanged[..., 3 * width :].reshape(LAYERS, parts, rows_d, copies, rows_f)
        expand_view = expand_view.transpose(0, 2, 3, 1, 4).reshape(LAYERS, rows_d, FF)
        exchanged = jnp.concatenate([mixing_view, expand_view], -1)[:, None]
        spans = ([(0, 0, 0, 3 * D)], [(0, 3 * D, 0, FF)])
    states = (
        (mixing_weight, mixing_first, mixing_second, mixing_average)
        + (output_weight, output_first, output_second, output_average)
        + (expand_weight, expand_first, expand_second, expand_average)
        + (shrink_weight, shrink_first, shrink_second, shrink_average)
    )
    rates = (D ** (-0.5), (D * 32 // LEN) ** (-0.5), D ** (-0.5), FF ** (-0.5))
    updated = update(
        clip_scale.reshape(1), exchanged, output_grad, shrink_grad, states, spans, rates
    )
    affine_new = adam(
        affine_grad * clip_scale,
        affine_weight,
        affine_first,
        affine_second,
        affine_average,
        SMALL_RATE,
        0.0,
    )
    return (result, stream_grad, gradient_norm) + tuple(updated) + tuple(affine_new)


def solution(mesh):
    tokens = P("dp", "seq", None)
    matrix = P(None, ("dp", "seq"), None)
    vector = P(None, ("dp", "seq"))
    states = (matrix,) * 16 + (vector,) * 4
    return jax.shard_map(
        local,
        mesh=mesh,
        in_specs=(tokens, tokens, P("dp", "seq")) + states,
        out_specs=(tokens, tokens, P()) + states,
        check_vma=False,
    )
```

```python
from functools import partial
import math

import jax
import jax.numpy as jnp
from jax import lax
from jax.experimental import pallas as pl
from jax.experimental.pallas import tpu as pltpu
from jax.sharding import PartitionSpec as P

D = 1024
H = 16
HD = 64
ROT = 16
FF = 4096
LEN = 2048
LAYERS = 2
STEP = 3

NORM_EPS = 1e-05
CLIP_LIMIT = 1.0
BETA_FIRST = 0.5
BETA_SECOND = 0.5
ADAM_EPS = 1e-08
WEIGHT_DECAY = 0.01
EMA_DECAY = 0.999
SMALL_RATE = 0.1
MASK_VALUE = -1e30
ROWS = 256
BLOCK = 512
QUERY_SCALE = 1.0 / math.sqrt(HD)
BF = jnp.bfloat16
F32 = jnp.float32
VMEM_LIMIT = 48 * 1024 * 1024
LIGHT = pl.CostEstimate(flops=1000, bytes_accessed=1000, transcendentals=0)


def dp_parts():
    size = lax.axis_size("dp")
    outer = 4 if size % 4 == 0 else size
    return outer, size // outer


def outer_ring(value):
    outer, inner = dp_parts()
    size = outer * inner
    return lax.ppermute(value, "dp", [(i, (i + inner) % size) for i in range(size)])


def inner_ring(value):
    outer, inner = dp_parts()
    moves = [
        (a * inner + b, a * inner + (b + 1) % inner) for a in range(outer) for b in range(inner)
    ]
    return lax.ppermute(value, "dp", moves)


def chip_ring(value):
    size = lax.axis_size("seq")
    return lax.ppermute(value, "seq", [(i, (i + 2) % size) for i in range(size)])


def core_swap(value):
    size = lax.axis_size("seq")
    return lax.ppermute(value, "seq", [(i, i ^ 1) for i in range(size)])


def assemble_kernel(slots_ref, *refs):
    n = pl.program_id(0)
    for step, piece_ref in enumerate(refs[:-1]):

        @pl.when(n == step)
        def _(piece_ref=piece_ref):
            refs[-1][...] = piece_ref[...][None]


def assemble(pieces, slots):
    count, piece = len(pieces), pieces[0]
    total = pl.pallas_call(
        assemble_kernel,
        grid_spec=pltpu.PrefetchScalarGridSpec(
            num_scalar_prefetch=1,
            grid=(count,),
            in_specs=[pl.BlockSpec(memory_space=pltpu.VMEM)] * count,
            out_specs=pl.BlockSpec((1,) + piece.shape, lambda n, slots: (slots[n], 0, 0)),
        ),
        out_shape=jax.ShapeDtypeStruct((count,) + piece.shape, piece.dtype),
        compiler_params=pltpu.CompilerParams(vmem_limit_bytes=VMEM_LIMIT),
        cost_estimate=LIGHT,
        name="assemble",
    )(jnp.stack(slots).astype(jnp.int32), *pieces)
    return total.reshape((count * piece.shape[0],) + piece.shape[1:])


def pick(total, first, second):
    sizes = (1, 1) + total.shape[2:]
    start = (first, second) + (0,) * (total.ndim - 2)
    return lax.dynamic_slice(total, start, sizes)[0, 0]


class Gather:
    def __init__(self, value):
        self.pieces = [value]
        self.chains = []

    def forward(self):
        self.pieces.append(outer_ring(self.pieces[-1]))

    def cross(self):
        chain = [self.pieces[len(self.chains)]]
        for turn in range(1, dp_parts()[1]):
            chain.append(inner_ring(chain[-1]))
        self.chains.append(chain)

    def hold(self, *values):
        held = lax.optimization_barrier((values, self.pieces, self.chains))
        self.pieces, self.chains = held[1], held[2]
        return held[0]

    def done(self):
        outer, inner = dp_parts()
        me = lax.axis_index("dp")
        a, b = me // inner, me % inner
        pieces, slots = [], []
        for step, chain in enumerate(self.chains):
            for turn, piece in enumerate(chain):
                pieces.append(piece)
                slots.append((a - step) % outer * inner + (b - turn) % inner)
        return pieces, slots


class Scatter:
    def __init__(self, *values):
        outer, inner = dp_parts()
        me = lax.axis_index("dp")
        self.a, self.b = me // inner, me % inner
        self.values = [
            value.reshape((outer, inner, -1) + value.shape[1:]) for value in values
        ]
        self.parts = []
        self.arrived = None
        self.steps = 0

    def own(self, at, turn):
        inner = dp_parts()[1]
        taken = [pick(value, at, (self.b - turn) % inner) for value in self.values]
        return taken[0] if len(taken) == 1 else jnp.concatenate(taken, -1)

    def cross(self):
        outer, inner = dp_parts()
        at = (self.a - len(self.parts) - 1) % outer
        arrived = None
        for turn in range(1, inner):
            own = self.own(at, turn)
            if arrived is not None:
                own = (own.astype(F32) + arrived.astype(F32)).astype(BF)
            arrived = inner_ring(own)
        self.parts.append((self.own(at, 0), arrived))

    def part(self):
        own, arrived = self.parts[self.steps]
        total = own.astype(F32)
        if arrived is not None:
            total = total + arrived.astype(F32)
        if self.arrived is not None:
            total = total + self.arrived.astype(F32)
        return total

    def forward(self):
        self.arrived = outer_ring(self.part().astype(BF))
        self.steps += 1

    def hold(self, *values):
        held = lax.optimization_barrier((values, self.values, self.parts, self.arrived))
        self.values, self.parts, self.arrived = held[1], held[2], held[3]
        return held[0]

    def done(self):
        return self.part()


class SeqGather:
    def __init__(self, value):
        self.pieces = [value]
        for step in range(1, lax.axis_size("seq") // 2):
            self.pieces.append(chip_ring(self.pieces[-1]))

    def hold(self, *values):
        held = lax.optimization_barrier((values, self.pieces))
        self.pieces = held[1]
        return held[0]

    def done(self):
        chips = lax.axis_size("seq") // 2
        me = lax.axis_index("seq")
        y, c = me // 2, me % 2
        pieces, slots = [], []
        for step, piece in enumerate(self.pieces):
            at = (y - step) % chips
            pieces += [piece, core_swap(piece)]
            slots += [2 * at + c, 2 * at + 1 - c]
        return assemble(pieces, slots)


class SeqScatter:
    def __init__(self, others):
        self.chips = lax.axis_size("seq") // 2
        self.core = lax.axis_index("seq") % 2
        rows = others.shape[0] // (2 * (self.chips - 1))
        others = others.reshape((self.chips - 1, 2, rows) + others.shape[1:])
        self.values = [others[n] for n in range(self.chips - 1)]
        self.sending = self.cores(self.values[0]).astype(BF)

    def cores(self, value):
        kept = lax.dynamic_index_in_dim(value, self.core, 0, keepdims=False)
        passed = lax.dynamic_index_in_dim(value, 1 - self.core, 0, keepdims=False)
        return kept.astype(F32) + core_swap(passed).astype(F32)

    def hold(self, *values):
        held = lax.optimization_barrier((values, self.sending))
        self.sending = held[1]
        return held[0]

    def done(self, own, others=()):
        own = own.reshape((2, own.shape[0] // 2) + own.shape[1:])
        for value in self.values[1:] + [own]:
            arrived = chip_ring(self.sending)
            arrived, value, others = lax.optimization_barrier((arrived, value, others))
            total = self.cores(value) + arrived.astype(F32)
            self.sending = total.astype(BF)
        return total, others


def sum_exchange(value):
    copies, parts = lax.axis_size("dp"), lax.axis_size("seq")
    rows = value.shape[0] // (copies * parts)
    value = value.reshape((copies * parts, rows) + value.shape[1:])
    value = lax.all_to_all(value, ("dp", "seq"), split_axis=0, concat_axis=0, tiled=True)
    return value.reshape((copies, parts) + value.shape[1:])


def seq_exchange(value):
    return lax.all_to_all(value, "seq", split_axis=0, concat_axis=0, tiled=True)


def head_masks(width, dtype):
    lane = lax.broadcasted_iota(jnp.int32, (1, width), 1) // HD
    return [(lane == h).astype(F32).astype(dtype) for h in range(width // HD)]


def swap_halves(values):
    width = values.shape[1]
    lane = lax.broadcasted_iota(jnp.int32, values.shape, 1) % HD
    return jnp.where(
        lane < ROT // 2,
        pltpu.roll(values, width - ROT // 2, 1),
        pltpu.roll(values, ROT // 2, 1),
    )


def as_column(row):
    return jnp.broadcast_to(row, (128, row.shape[1])).T[:, :1]


def as_row(column):
    return jnp.broadcast_to(column, (column.shape[0], 128)).T[:1, :]


def matmul(left, right):
    return lax.dot_general(left, right, (((1,), (0,)), ((), ())), preferred_element_type=F32)


def matmul_nt(left, right):
    return lax.dot_general(left, right, (((1,), (1,)), ((), ())), preferred_element_type=F32)


def matmul_tn(left, right):
    return lax.dot_general(left, right, (((0,), (0,)), ((), ())), preferred_element_type=F32)


def mix_kernel(slots_ref, x_ref, gain_ref, low_ref, bias_ref, cos_ref, sin_ref, *refs):
    out_ref, scaled_ref = refs[-3], refs[-2]
    shift_ref = refs[-1]
    columns = scaled_ref.shape[1]

    @pl.when(pl.program_id(0) == 0)
    def _():
        if len(refs) == 4:
            raw_ref = refs[0]
        else:
            pieces, raw_ref, rest_ref = refs[:-5], refs[-5], refs[-4]
            for n, piece_ref in enumerate(pieces):
                size = piece_ref.shape[0]
                rows = pl.ds(pl.multiple_of(slots_ref[n] * size, size), size)
                raw_ref[rows, :] = piece_ref[:, :columns]
                rest_ref[rows, :] = piece_ref[:, columns:]
        raw = raw_ref[...]
        scaled_ref[...] = (raw.astype(F32) * as_column(gain_ref[...])).astype(BF)
        low = jnp.broadcast_to(low_ref[...], (8, D)).astype(BF)
        shift_ref[...] = matmul(low, raw) + bias_ref[...]

    mixed = matmul(x_ref[...], scaled_ref[...]) + shift_ref[0:1, :]
    cosine, sine = cos_ref[...], sin_ref[...]
    for start in range(0, columns, 3 * 128):
        query = mixed[:, start : start + 128]
        key = mixed[:, start + 128 : start + 256]
        query = (query * cosine + swap_halves(query) * sine) * QUERY_SCALE
        key = key * cosine + swap_halves(key) * sine
        out_ref[:, start : start + 128] = query.astype(BF)
        out_ref[:, start + 128 : start + 256] = key.astype(BF)
        out_ref[:, start + 256 : start + 384] = mixed[:, start + 256 : start + 384].astype(BF)


def mix(x, weight, gain, low, bias, cosine, sine, slots=None):
    length, columns = x.shape[0], bias.shape[0]

    def whole(shape):
        return pl.BlockSpec(shape, lambda i, slots_ref: (0, 0))

    def rows(count):
        return pl.BlockSpec((ROWS, count), lambda i, slots_ref: (i, 0))

    out_specs = [rows(columns), whole((D, columns))]
    out_shape = [
        jax.ShapeDtypeStruct((length, columns), BF),
        jax.ShapeDtypeStruct((D, columns), BF),
    ]
    if slots is None:
        slots, weight_specs = jnp.zeros((1,), jnp.int32), [whole((D, columns))]
    else:
        slots = jnp.stack(slots).astype(jnp.int32)
        weight_specs = [pl.BlockSpec(memory_space=pltpu.VMEM)] * len(weight)
        rest = weight[0].shape[1] - columns
        out_specs = [whole((D, columns)), whole((D, rest))] + out_specs
        out_shape = [
            jax.ShapeDtypeStruct((D, columns), BF),
            jax.ShapeDtypeStruct((D, rest), BF),
        ] + out_shape
    return pl.pallas_call(
        mix_kernel,
        grid_spec=pltpu.PrefetchScalarGridSpec(
            num_scalar_prefetch=1,
            grid=(length // ROWS,),
            in_specs=[rows(D), whole((1, D)), whole((1, D)), whole((1, columns))]
            + [rows(128), rows(128)]
            + weight_specs,
            out_specs=out_specs,
            scratch_shapes=[pltpu.VMEM((8, columns), F32)],
        ),
        out_shape=out_shape,
        compiler_params=pltpu.CompilerParams(vmem_limit_bytes=VMEM_LIMIT),
        cost_estimate=LIGHT,
        name="mix",
    )(slots, x, gain[None], low[None], bias[None], cosine, sine, *weight)


def attend_kernel(q_ref, k_ref, v_ref, o_ref, lse_ref, acc_ref, turned_ref):
    block, width = q_ref.shape
    heads = width // HD
    i = pl.program_id(0)
    query = q_ref[...]
    queries = [query * mask for mask in head_masks(width, BF)]

    @pl.when(i == 0)
    def _():
        turned_ref[...] = v_ref[...].T

    acc_ref[...] = jnp.zeros(acc_ref.shape, F32)

    def tile(j, diagonal, carry):
        rows = pl.ds(pl.multiple_of(j * block, block), block)
        key = k_ref[rows, :]
        scores = [matmul_nt(key, queries[h]) for h in range(heads)]
        if diagonal:
            row = lax.broadcasted_iota(jnp.int32, (block, block), 0)
            column = lax.broadcasted_iota(jnp.int32, (block, block), 1)
            allowed = row <= column
            scores = [jnp.where(allowed, score, MASK_VALUE) for score in scores]
        highs = [
            jnp.maximum(carry[h][0], jnp.max(scores[h], 0, keepdims=True)) for h in range(heads)
        ]
        weights = [jnp.exp(scores[h] - highs[h]) for h in range(heads)]
        fades = [jnp.exp(carry[h][0] - highs[h]) for h in range(heads)]
        sums = [
            carry[h][1] * fades[h] + jnp.sum(weights[h], 0, keepdims=True) for h in range(heads)
        ]
        for h in range(heads):
            part = slice(h * HD, (h + 1) * HD)
            product = matmul(turned_ref[part, rows], weights[h].astype(BF))
            acc_ref[part, :] = acc_ref[part, :] * fades[h] + product
        return [(highs[h], sums[h]) for h in range(heads)]

    empty = (jnp.full((1, block), MASK_VALUE, F32), jnp.zeros((1, block), F32))
    carry = lax.fori_loop(0, i, lambda j, carry: tile(j, False, carry), [empty] * heads)
    carry = tile(i, True, carry)
    for h in range(heads):
        part = slice(h * HD, (h + 1) * HD)
        acc_ref[part, :] = acc_ref[part, :] / carry[h][1]
        lse_ref[h : h + 1, :] = carry[h][0] + jnp.log(carry[h][1])
    o_ref[...] = acc_ref[...].T.astype(BF)


def attend(mixed, half):
    length, width = mixed.shape[0], 128
    heads = width // HD
    block = min(BLOCK, length)
    return pl.pallas_call(
        attend_kernel,
        grid=(length // block,),
        in_specs=[
            pl.BlockSpec((block, width), lambda i: (i, 3 * half)),
            pl.BlockSpec((length, width), lambda i: (0, 3 * half + 1)),
            pl.BlockSpec((length, width), lambda i: (0, 3 * half + 2)),
        ],
        out_specs=[
            pl.BlockSpec((block, width), lambda i: (i, 0)),
            pl.BlockSpec((heads, block), lambda i: (0, i)),
        ],
        out_shape=[
            jax.ShapeDtypeStruct((length, width), BF),
            jax.ShapeDtypeStruct((heads, length), F32),
        ],
        scratch_shapes=[
            pltpu.VMEM((width, block), F32),
            pltpu.VMEM((width, length), BF),
        ],
        compiler_params=pltpu.CompilerParams(vmem_limit_bytes=VMEM_LIMIT),
        cost_estimate=LIGHT,
        name="attend",
    )(mixed, mixed, mixed)


def attend_back_kernel(
    q_ref,
    k_ref,
    v_ref,
    do_ref,
    o_ref,
    lse_ref,
    cos_ref,
    sin_ref,
    out_ref,
    total_ref,
    inner_ref,
    dq_ref,
    dk_ref,
    dv_ref,
):
    block, width = k_ref.shape
    length = q_ref.shape[0]
    heads = width // HD
    steps = length // block
    j = pl.program_id(0)
    masks = head_masks(width, BF)
    key = k_ref[...]
    value = v_ref[...]
    keys = [key * mask for mask in masks]
    values = [value * mask for mask in masks]

    @pl.when(j == 0)
    def _():
        dq_ref[...] = jnp.zeros(dq_ref.shape, F32)
        total_ref[...] = jnp.zeros(total_ref.shape, F32)
        product = do_ref[...].astype(F32) * o_ref[...].astype(F32)
        coarse = product.astype(BF)
        fine = (product - coarse.astype(F32)).astype(BF)
        row = lax.broadcasted_iota(jnp.int32, (8, width), 0)
        lane = lax.broadcasted_iota(jnp.int32, (8, width), 1) // HD
        chosen = (row == lane).astype(F32).astype(BF)
        inner_ref[...] = matmul_nt(chosen, coarse) + matmul_nt(chosen, fine)

    dk_ref[...] = jnp.zeros(dk_ref.shape, F32)
    dv_ref[...] = jnp.zeros(dv_ref.shape, F32)

    def tile(i, diagonal):
        rows = pl.ds(pl.multiple_of(i * block, block), block)
        query = q_ref[rows, :]
        grad = do_ref[rows, :]
        log_total = lse_ref[:, rows]
        inner = inner_ref[:, rows]
        scores = [matmul_nt(keys[h], query) for h in range(heads)]
        weight_grads = [matmul_nt(values[h], grad) for h in range(heads)]
        if diagonal:
            row = lax.broadcasted_iota(jnp.int32, (block, block), 0)
            column = lax.broadcasted_iota(jnp.int32, (block, block), 1)
            allowed = row <= column
            scores = [jnp.where(allowed, score, MASK_VALUE) for score in scores]
        weights = [jnp.exp(scores[h] - log_total[h : h + 1, :]) for h in range(heads)]
        low = [weight.astype(BF) for weight in weights]
        score_grads = [
            (weights[h] * (weight_grads[h] - inner[h : h + 1, :])).astype(BF)
            for h in range(heads)
        ]
        dv_ref[...] += matmul(
            jnp.concatenate(low, 1), jnp.concatenate([grad * mask for mask in masks], 0)
        )
        dk_ref[...] += matmul(
            jnp.concatenate(score_grads, 1),
            jnp.concatenate([query * mask for mask in masks], 0),
        )
        dq_ref[rows, :] += matmul_tn(
            jnp.concatenate(score_grads, 0), jnp.concatenate(keys, 0)
        )

    def step(i, carry):
        tile(i, False)
        return carry

    tile(j, True)
    lax.fori_loop(j + 1, steps, step, 0)

    own = pl.ds(pl.multiple_of(j * block, block), block)
    cosine = cos_ref[own, :]
    sine = sin_ref[own, :]
    key_grad = dk_ref[...]
    key_grad = key_grad * cosine - swap_halves(key_grad) * sine
    value_grad = dv_ref[...]
    query_grad = dq_ref[own, :] * QUERY_SCALE
    query_grad = query_grad * cosine - swap_halves(query_grad) * sine
    out_ref[:, :width] = query_grad.astype(BF)
    out_ref[:, width : 2 * width] = key_grad.astype(BF)
    out_ref[:, 2 * width :] = value_grad.astype(BF)
    total_ref[:, :width] += jnp.sum(query_grad, 0, keepdims=True)
    total_ref[:, width : 2 * width] += jnp.sum(key_grad, 0, keepdims=True)
    total_ref[:, 2 * width :] += jnp.sum(value_grad, 0, keepdims=True)


def attend_back(mixed, grads, attended, log_total, cosine, sine, half):
    length, width = mixed.shape[0], 128
    heads = width // HD
    block = min(BLOCK, length)
    return pl.pallas_call(
        attend_back_kernel,
        grid=(length // block,),
        in_specs=[
            pl.BlockSpec((length, width), lambda j: (0, 3 * half)),
            pl.BlockSpec((block, width), lambda j: (j, 3 * half + 1)),
            pl.BlockSpec((block, width), lambda j: (j, 3 * half + 2)),
            pl.BlockSpec((length, width), lambda j: (0, half)),
            pl.BlockSpec((length, width), lambda j: (0, 0)),
            pl.BlockSpec((heads, length), lambda j: (0, 0)),
            pl.BlockSpec((length, 128), lambda j: (0, 0)),
            pl.BlockSpec((length, 128), lambda j: (0, 0)),
        ],
        out_specs=[
            pl.BlockSpec((block, 3 * width), lambda j: (j, 0)),
            pl.BlockSpec((1, 3 * width), lambda j: (0, 0)),
        ],
        out_shape=[
            jax.ShapeDtypeStruct((length, 3 * width), BF),
            jax.ShapeDtypeStruct((1, 3 * width), F32),
        ],
        scratch_shapes=[
            pltpu.VMEM((8, length), F32),
            pltpu.VMEM((length, width), F32),
            pltpu.VMEM((block, width), F32),
            pltpu.VMEM((block, width), F32),
        ],
        compiler_params=pltpu.CompilerParams(vmem_limit_bytes=VMEM_LIMIT),
        cost_estimate=LIGHT,
        name="attend_back",
    )(mixed, mixed, mixed, grads, attended, log_total, cosine, sine)


def gelu_pair(values):
    size = jnp.abs(values) * (1.0 / math.sqrt(2.0))
    bell = jnp.exp(-size * size)
    turn = 1.0 / (1.0 + 0.3275911 * size)
    series = turn * (
        0.254829592
        + turn * (-0.284496736 + turn * (1.421413741 + turn * (-1.453152027 + turn * 1.061405429)))
    )
    tail = 0.5 * series * bell
    below = jnp.where(values < 0.0, tail, 1.0 - tail)
    slope = below + values * bell * (1.0 / math.sqrt(2.0 * math.pi))
    return values * below, slope


def chip_rows(own, length):
    chips = lax.axis_size("seq") // 2
    y = lax.axis_index("seq") // 2
    per = length // ROWS // chips
    if own is None:
        return length // ROWS, lambda i, y_ref: i, y
    if own:
        return per, lambda i, y_ref: y_ref[0] * per + i, y
    return (
        (chips - 1) * per,
        lambda i, y_ref: (y_ref[0] + chips - 1 - i // per) % chips * per + i % per,
        y,
    )


def feed_kernel(first, last, halves, count, y_ref, slots_ref, x_ref, *refs):
    refs = list(refs)
    if first:
        gain_ref, low_ref, bias_ref = refs[:3]
        del refs[:3]
        if count:
            pieces = refs[:count]
            del refs[:count]
        else:
            raw_ref = refs.pop(0)
    else:
        scaled_ref, shift_ref = refs[:2]
        del refs[:2]
    if last:
        out_ref = refs.pop()
        if count:
            shrink_ref = refs.pop()
        else:
            shrink_ref = refs.pop(0)
        output_ref = refs.pop(0)
        attended = refs[:halves]
    if first:
        if count:
            raw_ref = refs.pop()
        act_ref, slope_ref, scaled_ref, shift_ref = refs[-4:]
        units = scaled_ref.shape[1]

        @pl.when(pl.program_id(0) == 0)
        def _():
            if count:
                for n, piece_ref in enumerate(pieces):
                    size = piece_ref.shape[0]
                    rows = pl.ds(pl.multiple_of(slots_ref[n] * size, size), size)
                    raw_ref[rows, :] = piece_ref[:, :units]
                    shrink_ref[rows, :] = piece_ref[:, units:]
            raw = raw_ref[...]
            scaled_ref[...] = (raw.astype(F32) * as_column(gain_ref[...])).astype(BF)
            low = jnp.broadcast_to(low_ref[...], (8, D)).astype(BF)
            shift_ref[...] = matmul(low, raw) + bias_ref[...]

    else:
        act_ref, slope_ref = refs[-2:]
    hidden = matmul(x_ref[...], scaled_ref[...]) + shift_ref[0:1, :]
    activated, slope = gelu_pair(hidden)
    activated = activated.astype(BF)
    act_ref[...] = activated
    slope_ref[...] = slope.astype(BF)
    if last:
        out = matmul(activated, shrink_ref[...])
        for half, o_ref in enumerate(attended):
            out = out + matmul(o_ref[...], output_ref[half * 128 : (half + 1) * 128, :])
        out_ref[...] = out.astype(BF)


def feed(rows_of, x, units, first=None, scaled=None, last=None, kept=(), slots=None):
    length = x.shape[0]
    steps, row, y = chip_rows(rows_of, length)

    def rows(columns):
        return pl.BlockSpec((ROWS, columns), lambda i, *_: (row(i, _[0]), 0))

    def whole(shape, column=0):
        return pl.BlockSpec(shape, lambda i, *_: (0, column))

    specs, values, halves, count = [rows(D)], [x], 0, 0
    out_specs = [rows(units), rows(units)]
    out_shape = [jax.ShapeDtypeStruct((length, units), BF)] * 2
    if first is not None:
        gain, low, bias, weight = first
        values += [gain[None], low[None], bias[None]]
        specs += [whole((1, D)), whole((1, D)), whole((1, units))]
        out_specs += [whole((D, units)), whole((8, units))]
        out_shape += [
            jax.ShapeDtypeStruct((D, units), BF),
            jax.ShapeDtypeStruct((8, units), F32),
        ]
        if slots is not None:
            count = len(weight)
            values += weight
            specs += [pl.BlockSpec(memory_space=pltpu.VMEM)] * count
            out_specs += [whole((D, units))]
            out_shape += [jax.ShapeDtypeStruct((D, units), BF)]
        else:
            values.append(weight[0])
            specs.append(whole((D, units), weight[1]))
    else:
        values += list(scaled)
        specs += [whole((D, units)), whole((8, units))]
    if last is not None:
        shrink, output, attended = last
        halves = len(attended)
        if count:
            out_specs.append(whole((units, D)))
            out_shape.append(jax.ShapeDtypeStruct((units, D), BF))
        else:
            values.append(shrink[0])
            specs.append(whole((units, D), shrink[1]))
        values += [output, *attended]
        specs += [whole(output.shape)] + [rows(128)] * halves
        out_specs.append(pl.BlockSpec((ROWS, D), lambda i, *_: (i, 0)))
        out_shape.append(jax.ShapeDtypeStruct((steps * ROWS, D), BF))
    aliases = {2 + len(values) + n: n for n in range(len(kept))}
    values += list(kept)
    specs += [pl.BlockSpec(memory_space=pl.ANY)] * len(kept)
    slots = jnp.zeros((1,), jnp.int32) if slots is None else jnp.stack(slots).astype(jnp.int32)
    return pl.pallas_call(
        partial(feed_kernel, first is not None, last is not None, halves, count),
        grid_spec=pltpu.PrefetchScalarGridSpec(
            num_scalar_prefetch=2, grid=(steps,), in_specs=specs, out_specs=out_specs
        ),
        out_shape=out_shape,
        input_output_aliases=aliases,
        compiler_params=pltpu.CompilerParams(vmem_limit_bytes=VMEM_LIMIT),
        cost_estimate=LIGHT,
        name="feed",
    )(y.reshape(1), slots, *values)


def branch_kernel(y_ref, act_ref, shrink_ref, output_ref, *refs):
    out = matmul(act_ref[...], shrink_ref[...])
    for half, o_ref in enumerate(refs[:-1]):
        out = out + matmul(o_ref[...], output_ref[half * 128 : (half + 1) * 128, :])
    refs[-1][...] = out.astype(BF)


def branch(rows_of, activated, shrink, output, attended):
    length, units = activated.shape
    steps, row, y = chip_rows(rows_of, length)

    def rows(columns):
        return pl.BlockSpec((ROWS, columns), lambda i, y_ref: (row(i, y_ref), 0))

    return pl.pallas_call(
        branch_kernel,
        grid_spec=pltpu.PrefetchScalarGridSpec(
            num_scalar_prefetch=1,
            grid=(steps,),
            in_specs=[
                rows(units),
                pl.BlockSpec((units, D), lambda i, y_ref: (0, shrink[1])),
                pl.BlockSpec(output.shape, lambda i, y_ref: (0, 0)),
            ]
            + [rows(128)] * len(attended),
            out_specs=pl.BlockSpec((ROWS, D), lambda i, y_ref: (i, 0)),
        ),
        out_shape=jax.ShapeDtypeStruct((steps * ROWS, D), BF),
        compiler_params=pltpu.CompilerParams(vmem_limit_bytes=VMEM_LIMIT),
        cost_estimate=LIGHT,
        name="branch",
    )(y.reshape(1), activated, shrink[0], output, *attended)


def norm_grad_kernel(y_ref, h_ref, wi_ref, wm_ref, *refs):
    out = matmul_nt(h_ref[...], wi_ref[...])
    for half, m_ref in enumerate(refs[:-1]):
        out = out + matmul_nt(m_ref[...], wm_ref[:, half * 384 : (half + 1) * 384])
    refs[-1][...] = out.astype(BF)


def norm_grad(hidden, expand, mixed, mixing, own):
    length, units, columns = hidden.shape[0], expand.shape[1], mixing.shape[1]
    steps, row, y = chip_rows(own, length)

    def rows(count):
        return pl.BlockSpec((ROWS, count), lambda i, y_ref: (row(i, y_ref), 0))

    def whole(shape):
        return pl.BlockSpec(shape, lambda i, y_ref: (0, 0))

    return pl.pallas_call(
        norm_grad_kernel,
        grid_spec=pltpu.PrefetchScalarGridSpec(
            num_scalar_prefetch=1,
            grid=(steps,),
            in_specs=[rows(units), whole((D, units)), whole((D, columns))]
            + [rows(384)] * len(mixed),
            out_specs=pl.BlockSpec((ROWS, D), lambda i, y_ref: (i, 0)),
        ),
        out_shape=jax.ShapeDtypeStruct((steps * ROWS, D), BF),
        compiler_params=pltpu.CompilerParams(vmem_limit_bytes=VMEM_LIMIT),
        cost_estimate=LIGHT,
        name="norm_grad",
    )(y.reshape(1), hidden, expand, mixing, *mixed)


def hidden_back_kernel(grad_ref, shrink_ref, slope_ref, output_ref, low_ref, total_ref, do_ref):
    grads = grad_ref[...]
    hidden = matmul_nt(grads, shrink_ref[...]) * slope_ref[...].astype(F32)
    low_ref[...] = hidden.astype(BF)

    @pl.when(pl.program_id(0) == 0)
    def _():
        total_ref[...] = jnp.zeros(total_ref.shape, F32)

    total_ref[...] += jnp.sum(hidden, 0, keepdims=True)
    do_ref[...] = matmul_nt(grads, output_ref[...]).astype(BF)


def hidden_back(grads, shrink, slope, output):
    length, units = slope.shape
    width = output.shape[0]
    array, column = shrink
    return pl.pallas_call(
        hidden_back_kernel,
        grid=(length // BLOCK,),
        in_specs=[
            pl.BlockSpec((BLOCK, D), lambda i: (i, 0)),
            pl.BlockSpec((units, D), lambda i: (0, column)),
            pl.BlockSpec((BLOCK, units), lambda i: (i, 0)),
            pl.BlockSpec((width, D), lambda i: (0, 0)),
        ],
        out_specs=[
            pl.BlockSpec((BLOCK, units), lambda i: (i, 0)),
            pl.BlockSpec((1, units), lambda i: (0, 0)),
            pl.BlockSpec((BLOCK, width), lambda i: (i, 0)),
        ],
        out_shape=[
            jax.ShapeDtypeStruct((length, units), BF),
            jax.ShapeDtypeStruct((1, units), F32),
            jax.ShapeDtypeStruct((length, width), BF),
        ],
        compiler_params=pltpu.CompilerParams(vmem_limit_bytes=VMEM_LIMIT),
        cost_estimate=LIGHT,
        name="hidden_back",
    )(grads, array, slope, output)


def product_kernel(x_ref, g_ref, out_ref):
    out_ref[...] = matmul_tn(x_ref[...], g_ref[...]).astype(BF)


def product(x, grads, block=BLOCK):
    length, count = x.shape
    block = min(block, count)
    return pl.pallas_call(
        product_kernel,
        grid=(count // block,),
        in_specs=[
            pl.BlockSpec((length, block), lambda i: (0, i)),
            pl.BlockSpec((length, D), lambda i: (0, 0)),
        ],
        out_specs=pl.BlockSpec((block, D), lambda i: (i, 0)),
        out_shape=jax.ShapeDtypeStruct((count, D), BF),
        compiler_params=pltpu.CompilerParams(vmem_limit_bytes=VMEM_LIMIT),
        cost_estimate=LIGHT,
        name="product",
    )(x, grads)


def weight_grad_kernel(x_ref, weight_ref, gain_ref, shift_ref, total_ref, *refs):
    lows, (out_ref, gain_out_ref, shift_out_ref) = refs[:-3], refs[-3:]
    gain, shift = as_column(gain_ref[...]), as_column(shift_ref[...])
    x = x_ref[...]
    start, gain_sum, shift_sum = 0, 0.0, 0.0
    for low_ref in lows:
        columns = slice(start, start + low_ref.shape[1])
        start += low_ref.shape[1]
        raw = matmul_tn(x, low_ref[...])
        weight = weight_ref[:, columns].astype(F32)
        total = total_ref[:, columns]
        out_ref[:, columns] = (raw * gain + shift * total).astype(BF)
        gain_sum = gain_sum + jnp.sum(raw * weight, 1, keepdims=True)
        shift_sum = shift_sum + jnp.sum(weight * total, 1, keepdims=True)
    gain_out_ref[...] = as_row(gain_sum)
    shift_out_ref[...] = as_row(shift_sum)


def weight_grad(x, lows, weight, gain, shift, total):
    length, columns = x.shape[0], total.shape[1]
    array, column = weight
    row = pl.BlockSpec((1, ROWS), lambda i: (0, i))
    return pl.pallas_call(
        weight_grad_kernel,
        grid=(D // ROWS,),
        in_specs=[
            pl.BlockSpec((length, ROWS), lambda i: (0, i)),
            pl.BlockSpec((ROWS, columns), lambda i: (i, column)),
            row,
            row,
            pl.BlockSpec((1, columns), lambda i: (0, 0)),
        ]
        + [pl.BlockSpec(low.shape, lambda i: (0, 0)) for low in lows],
        out_specs=[pl.BlockSpec((ROWS, columns), lambda i: (i, 0)), row, row],
        out_shape=[
            jax.ShapeDtypeStruct((D, columns), BF),
            jax.ShapeDtypeStruct((1, D), F32),
            jax.ShapeDtypeStruct((1, D), F32),
        ],
        compiler_params=pltpu.CompilerParams(vmem_limit_bytes=VMEM_LIMIT),
        cost_estimate=LIGHT,
        name="weight_grad",
    )(x, array, gain[None], shift[None], total, *lows)


def pack_kernel(spans, mixing_ref, expand_ref, *refs):
    out_ref = refs[-1]
    for source_ref, part in ((mixing_ref, spans[0]), (expand_ref, spans[1])):
        for p, start, at, count in part:
            out_ref[p, :, start : start + count] = source_ref[0, :, at : at + count].astype(BF)
    for pair_ref in refs[:-1]:
        end = out_ref.shape[2] - pair_ref.shape[1]
        for p in range(out_ref.shape[0]):
            out_ref[p, :, end:] = pair_ref[...]


def pack(mixing, expand, layer, spans, columns, pair=()):
    parts, rows = lax.axis_size("seq"), mixing.shape[1]
    columns = columns + sum(value.shape[1] for value in pair)
    return pl.pallas_call(
        partial(pack_kernel, spans),
        grid=(1,),
        in_specs=[
            pl.BlockSpec((1,) + mixing.shape[1:], lambda i: (layer, 0, 0)),
            pl.BlockSpec((1,) + expand.shape[1:], lambda i: (layer, 0, 0)),
        ]
        + [pl.BlockSpec(value.shape, lambda i: (0, 0)) for value in pair],
        out_specs=pl.BlockSpec((parts, rows, columns), lambda i: (0, 0, 0)),
        out_shape=jax.ShapeDtypeStruct((parts, rows, columns), BF),
        compiler_params=pltpu.CompilerParams(vmem_limit_bytes=VMEM_LIMIT),
        cost_estimate=LIGHT,
        name="pack",
    )(mixing, expand, *pair)


def home_spans(parts, copies, width, units):
    mixing, expand = [], []
    size = units // copies
    for p in range(parts):
        for half in range(width // 128):
            for kind in range(3):
                at = kind * parts * width + p * width + half * 128
                mixing.append((p, half * 384 + kind * 128, at, 128))
        for d in range(copies):
            expand.append((p, 3 * width + d * size, (d * parts + p) * size, size))
    return mixing, expand


def adam(grad, weight, first, second, average, rate, decay):
    first_new = BETA_FIRST * first + (1.0 - BETA_FIRST) * grad
    second_new = BETA_SECOND * second + (1.0 - BETA_SECOND) * grad * grad
    first_hat = first_new / (1.0 - BETA_FIRST**STEP)
    second_hat = second_new / (1.0 - BETA_SECOND**STEP)
    weight_new = weight - rate * (
        first_hat / (jnp.sqrt(second_hat) + ADAM_EPS) + decay * weight
    )
    return weight_new, first_new, second_new, EMA_DECAY * average + (1.0 - EMA_DECAY) * weight_new


def adam_kernel(spans, rates, clip_ref, exchanged_ref, output_ref, shrink_ref, *refs):
    clip = clip_ref[0]
    states, news = refs[:16], refs[16:]

    def step(kind, grad, columns):
        old = [ref[0, :, columns] for ref in states[4 * kind : 4 * kind + 4]]
        new = adam(grad.astype(F32) * clip, *old, rates[kind], WEIGHT_DECAY)
        for ref, value in zip(news[4 * kind : 4 * kind + 4], new):
            ref[0, :, columns] = value

    for kind, part in ((0, spans[0]), (2, spans[1])):
        for source, start, at, count in part:
            grad = exchanged_ref[0, source, :, start : start + count]
            step(kind, grad, slice(at, at + count))
    step(1, output_ref[0], slice(None))
    step(3, shrink_ref[0], slice(None))


def update(clip, exchanged, output, shrink, states, spans, rates):
    layers, parts, rows, columns = exchanged.shape
    chunk = 16 if rows % 16 == 0 else rows
    chunks = rows // chunk

    def block(array):
        size = array.shape[1] // chunks
        return pl.BlockSpec((1, size, array.shape[2]), lambda l, n: (l, n, 0))

    return pl.pallas_call(
        partial(adam_kernel, spans, rates),
        grid=(layers, chunks),
        in_specs=[
            pl.BlockSpec(memory_space=pltpu.SMEM),
            pl.BlockSpec((1, parts, chunk, columns), lambda l, n: (l, 0, n, 0)),
            block(output),
            block(shrink),
        ]
        + [block(state) for state in states],
        out_specs=[block(state) for state in states],
        out_shape=[jax.ShapeDtypeStruct(state.shape, F32) for state in states],
        compiler_params=pltpu.CompilerParams(vmem_limit_bytes=VMEM_LIMIT),
        cost_estimate=LIGHT,
        name="update",
    )(clip, exchanged, output, shrink, *states)


def rotary_tables(positions):
    half = ROT // 2
    steps_half = jnp.arange(half).astype(F32)
    frequency = 10000.0 ** (-2.0 * steps_half / ROT)
    angles = positions.astype(F32)[None, :] * frequency[:, None]
    cosine = jnp.concatenate([jnp.cos(angles), jnp.ones_like(angles)], 0)
    entry = jnp.arange(128)[None, :] % HD
    index = jnp.arange(half)[:, None]
    turning = (entry < ROT) & (entry % half == index)
    still = (entry >= ROT) & (index == 0)
    sign = jnp.where(entry < half, -1.0, 1.0)
    spread_cosine = jnp.concatenate([turning, still], 0).astype(F32)
    spread_sine = turning.astype(F32) * sign

    def lay(table, spread):
        return lax.dot_general(
            table, spread, (((0,), (0,)), ((), ())), precision=lax.Precision.HIGHEST
        )

    return lay(cosine, spread_cosine), lay(jnp.sin(angles), spread_sine)


def split_affine(affine):
    bounds = [D, D, D, D, 3 * D, D, FF, D]
    pieces = []
    offset = 0
    for length in bounds:
        pieces.append(affine[offset : offset + length])
        offset = offset + length
    return pieces


def normalize(values):
    centre = values - jnp.mean(values, -1, keepdims=True)
    spread = jnp.mean(centre * centre, -1, keepdims=True)
    scale = lax.rsqrt(spread + NORM_EPS)
    return centre * scale, scale


def local(
    stream,
    cotangent,
    positions,
    mixing_weight,
    mixing_first,
    mixing_second,
    mixing_average,
    output_weight,
    output_first,
    output_second,
    output_average,
    expand_weight,
    expand_first,
    expand_second,
    expand_average,
    shrink_weight,
    shrink_first,
    shrink_second,
    shrink_average,
    affine_weight,
    affine_first,
    affine_second,
    affine_average,
):
    parts = lax.axis_size("seq")
    copies = lax.axis_size("dp")
    devices = parts * copies
    part = lax.axis_index("seq")
    width = D // parts
    units = FF // parts
    rows_d = D // devices
    rows_f = FF // devices
    rows = stream.shape[0] * stream.shape[1]
    small = affine_weight.shape[1]

    halves = width // 128
    outer = dp_parts()[0]

    def mixing_part(vector):
        view = vector.reshape(3, parts, halves, 128)
        view = lax.dynamic_index_in_dim(view, part, 1, keepdims=False)
        return view.transpose(1, 0, 2).reshape(-1)

    def expand_part(vector):
        view = vector.reshape(copies, parts, -1)
        return lax.dynamic_index_in_dim(view, part, 1, keepdims=False).reshape(-1)

    def spread_mixing(vector):
        view = jnp.zeros((3, parts, width), F32)
        vector = vector.reshape(halves, 3, 128).transpose(1, 0, 2).reshape(3, 1, width)
        return lax.dynamic_update_slice(view, vector, (0, part, 0)).reshape(-1)

    def spread_expand(vector):
        view = jnp.zeros((copies, parts, rows_f), F32)
        return lax.dynamic_update_slice(view, vector.reshape(copies, 1, rows_f), (0, part, 0)).reshape(-1)

    spans = home_spans(parts, copies, width, units)
    aligned = rows_f % 128 == 0 and rows_d % 16 == 0

    def arrange(layer, mixing, expand, pair=()):
        if aligned:
            return pack(mixing, expand, layer, spans, 3 * width + units, pair)
        mixing = mixing[layer].astype(BF).reshape(rows_d, 3, parts, halves, 128)
        mixing = mixing.transpose(2, 0, 3, 1, 4).reshape(parts, rows_d, 3 * width)
        expand = expand[layer].astype(BF).reshape(rows_d, copies, parts, rows_f)
        expand = expand.transpose(2, 0, 1, 3).reshape(parts, rows_d, units)
        pair = [jnp.broadcast_to(value, (parts,) + value.shape) for value in pair]
        return jnp.concatenate([mixing, expand] + pair, -1)

    def settle_output(exchanged):
        output = exchanged.reshape(parts, copies // parts, rows_d, D)
        return output.transpose(1, 0, 2, 3).reshape(width, D)

    def norm_back(gradient, normed_grad, own_normed, scale):
        projected = jnp.mean(normed_grad * own_normed, -1, keepdims=True)
        middle = jnp.mean(normed_grad, -1, keepdims=True)
        return gradient + scale * (normed_grad - middle - own_normed * projected)

    def outgoing_output(attended, grads):
        output_grad = jnp.concatenate([product(out, grads) for out in attended], 0)
        output_grad = output_grad.reshape(copies // parts, parts, rows_d, D).transpose(1, 0, 2, 3)
        output_grad = seq_exchange(output_grad.reshape(parts, copies // parts * rows_d, D))
        return output_grad.reshape(-1, width)

    def exchange_affine(pieces):
        grads = jnp.concatenate(pieces).reshape(devices, 1, small)
        return lax.all_to_all(grads, ("dp", "seq"), split_axis=0, concat_axis=0, tiled=True)

    def sum_squares(*values):
        return sum(jnp.sum(value.astype(F32) * value.astype(F32)) for value in values)

    tie = lax.optimization_barrier
    current = stream.reshape(rows, D)
    gradient = cotangent.reshape(rows, D)

    def view(array, column):
        if units == D:
            return array, column
        return array[:, column * units : (column + 1) * units].reshape(-1, D), 0

    pair = jnp.stack([positions.reshape(-1) // 16, positions.reshape(-1) % 16]).astype(BF)
    pair = pair.reshape(rows_d, 2 * rows // rows_d)
    both = arrange(0, mixing_weight, expand_weight, (pair,))
    both, current = tie((both, current))
    both = seq_exchange(both)
    own_normed, scale = normalize(current)
    travel = SeqGather(own_normed.astype(BF))
    pair = both[..., 3 * width + units :].astype(F32).reshape(parts, 2, rows)
    places = (pair[:, 0] * 16.0 + pair[:, 1]).reshape(-1)
    both = both.reshape(parts * rows_d, -1)
    near = Gather(
        jnp.concatenate(
            [both[:, : 3 * width], output_weight[0].astype(BF).reshape(-1, width)], -1
        )
    )
    places, affine_low, layer_mixing, layer_expand = near.hold(
        places, affine_weight, mixing_weight, expand_weight
    )
    near.forward()
    affine_low = affine_low.astype(BF).reshape(1, LAYERS * small)
    affine_all = lax.all_to_all(
        jnp.broadcast_to(affine_low, (devices, LAYERS * small)),
        ("dp", "seq"),
        split_axis=0,
        concat_axis=0,
        tiled=True,
    )
    cosine, sine = rotary_tables(places)
    later_both = arrange(1, layer_mixing, layer_expand)
    cosine, sine, later_both, expand_own, shrink_own = near.hold(
        cosine, sine, later_both, both[:, 3 * width : 3 * width + units], shrink_weight[0]
    )
    near.forward()
    near.cross()
    far_own = jnp.concatenate([expand_own, shrink_own.astype(BF).reshape(-1, units)], -1)
    affine_all, far_own, near.pieces, near.chains, travel.pieces, later_both, low_gradient = tie(
        (
            affine_all,
            far_own,
            near.pieces,
            near.chains,
            travel.pieces,
            later_both,
            gradient,
        )
    )
    normed = travel.done()
    near.forward()
    near.cross()
    travel = SeqGather(low_gradient.astype(BF))
    affine_all = affine_all.reshape(devices, LAYERS, small).transpose(1, 0, 2)
    affine_all = affine_all.reshape(LAYERS, devices * small).astype(F32)
    vectors = [split_affine(affine_all[layer]) for layer in range(LAYERS)]
    vectors, normed = near.hold(vectors, normed)
    for step in range(3, outer - 1):
        near.forward()
        near.cross()
    while len(near.chains) < outer:
        near.cross()
    far = Gather(far_own)
    far.pieces[0], near.pieces, near.chains = tie((far.pieces[0], near.pieces, near.chains))
    far.forward()
    far.cross()
    pieces, slots = near.done()
    later_both = seq_exchange(later_both)

    gain_one, shift_one, gain_two, shift_two = vectors[0][:4]
    mixing, output, mixed, mixing_scaled = mix(
        normed, pieces, gain_one, shift_one, mixing_part(vectors[0][4]), cosine, sine, slots
    )
    mixed, output, later_both, later_shrink, later_output = far.hold(
        mixed, output, later_both, shrink_weight[1], output_weight[1]
    )
    far.forward()
    far.cross()
    output = seq_exchange(output.reshape(parts, -1, D))

    later_both = later_both.reshape(parts * rows_d, -1)
    later_own = jnp.concatenate(
        [
            later_both[:, 3 * width :],
            later_shrink.astype(BF).reshape(-1, units),
            later_both[:, : 3 * width],
            later_output.astype(BF).reshape(-1, width),
        ],
        -1,
    )
    (later_own,) = travel.hold(later_own)
    later_all = lax.all_gather(later_own, "dp", axis=0, tiled=True)
    attended, logs = [], []
    for half in range(halves):
        out, log_total = attend(mixed, half)
        attended.append(out)
        logs.append(log_total)
        if half == 0:
            mixed, out, output = far.hold(mixed, out, output)
            far.forward()
            far.cross()
    output = settle_output(output)
    attended, logs = far.hold(attended, logs)
    while len(far.pieces) < outer:
        far.forward()
    while len(far.chains) < outer:
        far.cross()
    grads = travel.done()
    attended, logs, grads = far.hold(attended, logs, grads)
    pieces, slots = far.done()
    first = (gain_two, shift_two, expand_part(vectors[0][6]))
    if units == D:
        activated, slope, expand_scaled, expand_shift, expand, shrink, others = feed(
            False,
            normed,
            units,
            first=first + (pieces,),
            last=(None, output, attended),
            slots=slots,
        )
    else:
        far_all = assemble(pieces, slots)
        expand, shrink = far_all[:, :units], view(far_all, 1)[0]
        activated, slope, expand_scaled, expand_shift, others = feed(
            False,
            normed,
            units,
            first=first + ((expand, 0),),
            last=((shrink, 0), output, attended),
        )
    shrink = (shrink, 0)
    travel = SeqScatter(others)
    activated, slope = travel.hold(activated, slope)
    activated, slope, own = feed(
        True,
        normed,
        units,
        scaled=(expand_scaled, expand_shift),
        last=(shrink, output, attended),
        kept=(activated, slope),
    )
    stored = [(own_normed, scale, normed, mixed, attended, logs, activated, slope)]
    weights = [(mixing, mixing_scaled, output, expand, expand_scaled, shrink)]
    current = current + travel.done(own)[0] + vectors[0][5] + vectors[0][7]

    own_normed, scale = normalize(current)
    travel = SeqGather(own_normed.astype(BF))
    mixing = later_all[:, 2 * units : 2 * units + 3 * width]
    later_output = later_all[:, 2 * units + 3 * width :].reshape(copies * rows_d, D)
    mixing, later_output, later_all = travel.hold(mixing, later_output, later_all)
    normed = travel.done()
    expand, shrink = later_all, view(later_all, 1)
    gain_one, shift_one, gain_two, shift_two = vectors[1][:4]
    mixed, mixing_scaled = mix(
        normed, [mixing], gain_one, shift_one, mixing_part(vectors[1][4]), cosine, sine
    )
    mixed, later_output = tie((mixed, later_output))
    output = seq_exchange(later_output.reshape(parts, -1, D))
    attended, logs = [], []
    for half in range(halves):
        out, log_total = attend(mixed, half)
        attended.append(out)
        logs.append(log_total)
    activated, slope, expand_scaled, expand_shift = feed(
        None,
        normed,
        units,
        first=(gain_two, shift_two, expand_part(vectors[1][6]), (later_all, 0)),
    )

    grads, attended, logs, activated, output = tie((grads, attended, logs, activated, output))
    output = settle_output(output)
    output_grad = outgoing_output(attended, grads)
    hidden_low, hidden_total, attended_grad = hidden_back(grads, shrink, slope, output)
    shrink_grad = product(activated, grads).reshape(-1, units)
    expand_grad, gain_two_grad, shift_two_grad = weight_grad(
        normed, [hidden_low], (expand, 0), gain_two, shift_two, hidden_total
    )
    later_grad = jnp.concatenate([expand_grad, shrink_grad, output_grad], -1)
    later_grad, attended_grad = tie((later_grad, attended_grad))
    later_first = lax.psum_scatter(later_grad, "dp", scatter_dimension=0, tiled=True)
    lows, totals = [], []
    for half in range(halves):
        low, total = attend_back(
            mixed, attended_grad, attended[half], logs[half], cosine, sine, half
        )
        lows.append(low)
        totals.append(total)
    mixed_total = jnp.concatenate(totals, -1)
    others = norm_grad(hidden_low, expand_scaled, lows, mixing_scaled, False)
    travel = SeqScatter(others)
    hidden_low, lows, activated = travel.hold(hidden_low, lows, activated)
    own = norm_grad(hidden_low, expand_scaled, lows, mixing_scaled, True)
    last = (shrink, output, attended)
    result_others = branch(False, activated, *last)
    result_own = branch(True, activated, *last)
    normed_grad, (result_others, result_own) = travel.done(own, (result_others, result_own))
    normed_grad, lows = tie((normed_grad, lows))
    gradient = norm_back(gradient, normed_grad, own_normed, scale)
    travel = SeqGather(gradient.astype(BF))
    lows, own_piece = tie((lows, travel.pieces[0]))
    mixing_grad, gain_one_grad, shift_one_grad = weight_grad(
        normed, lows, (mixing, 0), gain_one, shift_one, mixed_total
    )
    (mixing_grad,) = travel.hold(mixing_grad)
    grads = travel.done()
    later_mixing = sum_exchange(mixing_grad)
    output_sum = jnp.sum(cotangent.reshape(rows, D), 0)

    def small_grads(*pieces):
        gains, mixed_total, output_sum, hidden_total = pieces
        pieces = [piece[0] for piece in gains]
        pieces += [spread_mixing(mixed_total[0]), output_sum]
        return pieces + [spread_expand(hidden_total[0]), output_sum]

    gains = (gain_one_grad, shift_one_grad, gain_two_grad, shift_two_grad)
    later_pieces = small_grads(gains, mixed_total, output_sum, hidden_total)

    later_current, later_vectors = current, vectors[1]
    current = stream.reshape(rows, D)
    own_normed, scale, normed, mixed, attended, logs, activated, slope = stored[0]
    mixing, mixing_scaled, output, expand, expand_scaled, shrink = weights[0]
    gain_one, shift_one, gain_two, shift_two = vectors[0][:4]
    far = Scatter(product(activated, grads).reshape(-1, units))
    (grads,) = far.hold(grads)
    far.cross()
    hidden_low, hidden_total, attended_grad = hidden_back(grads, shrink, slope, output)
    hidden_low, attended_grad, result_others, later_pieces = far.hold(
        hidden_low, attended_grad, result_others, later_pieces
    )
    far.forward()
    far.cross()
    expand_grad, gain_two_grad, shift_two_grad = weight_grad(
        normed, [hidden_low], (expand, 0), gain_two, shift_two, hidden_total
    )
    output_grad = outgoing_output(attended, grads)
    attended_grad, expand_grad, output_grad = far.hold(attended_grad, expand_grad, output_grad)
    far_grad = lax.psum_scatter(
        jnp.concatenate([expand_grad, output_grad], -1), "dp", scatter_dimension=0, tiled=True
    )
    travel = SeqScatter(result_others)
    lows, totals = [], []
    for half in range(halves):
        if len(far.parts) < outer:
            far.forward()
            far.cross()
        low, total = attend_back(
            mixed, attended_grad, attended[half], logs[half], cosine, sine, half
        )
        mixed, low, total, later_mixing = far.hold(mixed, low, total, later_mixing)
        if half == 0:
            result, (mixed, low) = travel.done(result_own, (mixed, low))
            exchanged = exchange_affine(later_pieces)
        lows.append(low)
        totals.append(total)
    exchanged, lows = tie((exchanged, lows))
    later_affine = jnp.sum(exchanged, 0)
    mixed_total = jnp.concatenate(totals, -1)
    mixing_grad, gain_one_grad, shift_one_grad = weight_grad(
        normed, lows, (mixing, 0), gain_one, shift_one, mixed_total
    )
    output_sum = jnp.sum(gradient, 0)
    gains = (gain_one_grad, shift_one_grad, gain_two_grad, shift_two_grad)
    pieces = small_grads(gains, mixed_total, output_sum, hidden_total)
    pieces = jnp.concatenate(pieces).reshape(devices, small)
    coarse = pieces.astype(BF)
    fine = (pieces - coarse.astype(F32)).astype(BF)
    pieces = jnp.concatenate([coarse, fine], -1)
    extra = 128 * pl.cdiv(2 * small, 128 * rows_d)
    pieces = jnp.pad(pieces, ((0, 0), (0, extra * rows_d - 2 * small)))
    mixing_grad = jnp.concatenate([mixing_grad, pieces.reshape(D, extra)], -1)
    mixing_grad, lows, result, later_first = tie((mixing_grad, lows, result, later_first))
    mixing_grad = sum_exchange(mixing_grad)
    result = later_current + result + later_vectors[5] + later_vectors[7]
    result = result.reshape(stream.shape)
    others = norm_grad(hidden_low, expand_scaled, lows, mixing_scaled, False)
    travel = SeqScatter(others)
    (lows,) = travel.hold(lows)
    own = norm_grad(hidden_low, expand_scaled, lows, mixing_scaled, True)
    while len(far.parts) < outer:
        far.forward()
        far.cross()
    while far.steps < outer - 1:
        far.forward()
    shrink_grad = far.done()
    later_mixing = jnp.sum(later_mixing.astype(F32), 0)
    squares = sum_squares(shrink_grad, later_first, later_mixing, later_affine)
    shrink_grad, later_mixing = shrink_grad.astype(BF), later_mixing.astype(BF)
    normed_grad, (mixing_grad, squares, shrink_grad, later_mixing) = travel.done(
        own, (mixing_grad, squares, shrink_grad, later_mixing)
    )

    home = jnp.stack([far_grad[:, :units], later_first[:, :units]], 1)
    home = seq_exchange(home.reshape(parts, rows_d, 2, units))
    output_grad = far_grad[:, units:]
    pieces = mixing_grad[..., 3 * width :].reshape(devices, -1)[:, : 2 * small].astype(F32)
    affine_grad = jnp.sum(pieces[:, :small] + pieces[:, small:], 0, keepdims=True)
    mixing_grad = jnp.sum(mixing_grad[..., : 3 * width].astype(F32), 0)
    squares = squares + sum_squares(mixing_grad, affine_grad, far_grad)
    mixing_grad = mixing_grad.astype(BF)
    affine_grad = jnp.stack([affine_grad[0], later_affine[0]])
    squares, home = tie((squares, home))
    expand_grad, later_expand = home[:, :, 0], home[:, :, 1]
    squares = lax.all_to_all(
        jnp.broadcast_to(squares, (devices, 128)),
        ("dp", "seq"),
        split_axis=0,
        concat_axis=0,
        tiled=True,
    )
    squares, normed_grad = tie((squares, normed_grad))
    gradient = norm_back(gradient, normed_grad, own_normed, scale)
    stream_grad = gradient.reshape(stream.shape)
    gradient_norm = jnp.sqrt(jnp.sum(squares[:, 0]))
    clip_scale = jnp.minimum(1.0, CLIP_LIMIT / (gradient_norm + 1e-06))
    output_grad = jnp.stack([output_grad, later_first[:, 2 * units :]])
    output_grad = output_grad.reshape(LAYERS, rows_d, D)
    shrink_grad = jnp.stack([shrink_grad, later_first[:, units : 2 * units]])
    shrink_grad = shrink_grad.reshape(LAYERS, rows_f, D)
    mixing_grad = jnp.stack([mixing_grad, later_mixing])
    expand_grad = jnp.stack([expand_grad, later_expand])
    exchanged = jnp.concatenate([mixing_grad, expand_grad], -1)
    if not aligned:
        mixing_view = exchanged[..., : 3 * width].reshape(LAYERS, parts, rows_d, halves, 3, 128)
        mixing_view = mixing_view.transpose(0, 2, 4, 1, 3, 5).reshape(LAYERS, rows_d, 3 * D)
        expand_view = exchanged[..., 3 * width :].reshape(LAYERS, parts, rows_d, copies, rows_f)
        expand_view = expand_view.transpose(0, 2, 3, 1, 4).reshape(LAYERS, rows_d, FF)
        exchanged = jnp.concatenate([mixing_view, expand_view], -1)[:, None]
        spans = ([(0, 0, 0, 3 * D)], [(0, 3 * D, 0, FF)])
    states = (
        (mixing_weight, mixing_first, mixing_second, mixing_average)
        + (output_weight, output_first, output_second, output_average)
        + (expand_weight, expand_first, expand_second, expand_average)
        + (shrink_weight, shrink_first, shrink_second, shrink_average)
    )
    rates = (D ** (-0.5), (D * 32 // LEN) ** (-0.5), D ** (-0.5), FF ** (-0.5))
    updated = update(
        clip_scale.reshape(1), exchanged, output_grad, shrink_grad, states, spans, rates
    )
    affine_new = adam(
        affine_grad * clip_scale,
        affine_weight,
        affine_first,
        affine_second,
        affine_average,
        SMALL_RATE,
        0.0,
    )
    return (result, stream_grad, gradient_norm) + tuple(updated) + tuple(affine_new)


def solution(mesh):
    tokens = P("dp", "seq", None)
    matrix = P(None, ("dp", "seq"), None)
    vector = P(None, ("dp", "seq"))
    states = (matrix,) * 16 + (vector,) * 4
    return jax.shard_map(
        local,
        mesh=mesh,
        in_specs=(tokens, tokens, P("dp", "seq")) + states,
        out_specs=(tokens, tokens, P()) + states,
        check_vma=False,
    )
```

```python
from functools import partial
import math

import jax
import jax.numpy as jnp
from jax import lax
from jax.experimental import pallas as pl
from jax.experimental.pallas import tpu as pltpu
from jax.sharding import PartitionSpec as P

D = 1024
H = 16
HD = 64
ROT = 16
FF = 4096
LEN = 2048
LAYERS = 2
STEP = 3

NORM_EPS = 1e-05
CLIP_LIMIT = 1.0
BETA_FIRST = 0.5
BETA_SECOND = 0.5
ADAM_EPS = 1e-08
WEIGHT_DECAY = 0.01
EMA_DECAY = 0.999
SMALL_RATE = 0.1
MASK_VALUE = -1e30
ROWS = 256
BLOCK = 512
QUERY_SCALE = 1.0 / math.sqrt(HD)
BF = jnp.bfloat16
F32 = jnp.float32
VMEM_LIMIT = 60 * 1024 * 1024
LIGHT = pl.CostEstimate(flops=1000, bytes_accessed=1000, transcendentals=0)


def dp_parts():
    size = lax.axis_size("dp")
    outer = 4 if size % 4 == 0 else size
    return outer, size // outer


def outer_ring(value):
    outer, inner = dp_parts()
    size = outer * inner
    return lax.ppermute(value, "dp", [(i, (i + inner) % size) for i in range(size)])


def inner_ring(value):
    outer, inner = dp_parts()
    moves = [
        (a * inner + b, a * inner + (b + 1) % inner) for a in range(outer) for b in range(inner)
    ]
    return lax.ppermute(value, "dp", moves)


def chip_ring(value):
    size = lax.axis_size("seq")
    return lax.ppermute(value, "seq", [(i, (i + 2) % size) for i in range(size)])


def core_swap(value):
    size = lax.axis_size("seq")
    return lax.ppermute(value, "seq", [(i, i ^ 1) for i in range(size)])


def assemble_kernel(slots_ref, *refs):
    n = pl.program_id(0)
    for step, piece_ref in enumerate(refs[:-1]):

        @pl.when(n == step)
        def _(piece_ref=piece_ref):
            refs[-1][...] = piece_ref[...][None]


def assemble(pieces, slots):
    count, piece = len(pieces), pieces[0]
    total = pl.pallas_call(
        assemble_kernel,
        grid_spec=pltpu.PrefetchScalarGridSpec(
            num_scalar_prefetch=1,
            grid=(count,),
            in_specs=[pl.BlockSpec(memory_space=pltpu.VMEM)] * count,
            out_specs=pl.BlockSpec((1,) + piece.shape, lambda n, slots: (slots[n], 0, 0)),
        ),
        out_shape=jax.ShapeDtypeStruct((count,) + piece.shape, piece.dtype),
        compiler_params=pltpu.CompilerParams(vmem_limit_bytes=VMEM_LIMIT),
        cost_estimate=LIGHT,
        name="assemble",
    )(jnp.stack(slots).astype(jnp.int32), *pieces)
    return total.reshape((count * piece.shape[0],) + piece.shape[1:])


def pick(total, first, second):
    sizes = (1, 1) + total.shape[2:]
    start = (first, second) + (0,) * (total.ndim - 2)
    return lax.dynamic_slice(total, start, sizes)[0, 0]


class Gather:
    def __init__(self, value):
        self.pieces = [value]
        self.chains = []

    def forward(self):
        self.pieces.append(outer_ring(self.pieces[-1]))

    def cross(self):
        chain = [self.pieces[len(self.chains)]]
        for turn in range(1, dp_parts()[1]):
            chain.append(inner_ring(chain[-1]))
        self.chains.append(chain)

    def hold(self, *values):
        held = lax.optimization_barrier((values, self.pieces, self.chains))
        self.pieces, self.chains = held[1], held[2]
        return held[0]

    def done(self):
        outer, inner = dp_parts()
        me = lax.axis_index("dp")
        a, b = me // inner, me % inner
        pieces, slots = [], []
        for step, chain in enumerate(self.chains):
            for turn, piece in enumerate(chain):
                pieces.append(piece)
                slots.append((a - step) % outer * inner + (b - turn) % inner)
        return pieces, slots


class Scatter:
    def __init__(self, *values):
        outer, inner = dp_parts()
        me = lax.axis_index("dp")
        self.a, self.b = me // inner, me % inner
        self.values = [
            value.reshape((outer, inner, -1) + value.shape[1:]) for value in values
        ]
        self.parts = []
        self.arrived = None
        self.steps = 0

    def own(self, at, turn):
        inner = dp_parts()[1]
        taken = [pick(value, at, (self.b - turn) % inner) for value in self.values]
        return taken[0] if len(taken) == 1 else jnp.concatenate(taken, -1)

    def cross(self):
        outer, inner = dp_parts()
        at = (self.a - len(self.parts) - 1) % outer
        arrived = None
        for turn in range(1, inner):
            own = self.own(at, turn)
            if arrived is not None:
                own = (own.astype(F32) + arrived.astype(F32)).astype(BF)
            arrived = inner_ring(own)
        self.parts.append((self.own(at, 0), arrived))

    def part(self):
        own, arrived = self.parts[self.steps]
        total = own.astype(F32)
        if arrived is not None:
            total = total + arrived.astype(F32)
        if self.arrived is not None:
            total = total + self.arrived.astype(F32)
        return total

    def forward(self):
        self.arrived = outer_ring(self.part().astype(BF))
        self.steps += 1

    def hold(self, *values):
        held = lax.optimization_barrier((values, self.values, self.parts, self.arrived))
        self.values, self.parts, self.arrived = held[1], held[2], held[3]
        return held[0]

    def done(self):
        return self.part()


class SeqGather:
    def __init__(self, value):
        self.pieces = [value]
        for step in range(1, lax.axis_size("seq") // 2):
            self.pieces.append(chip_ring(self.pieces[-1]))

    def hold(self, *values):
        held = lax.optimization_barrier((values, self.pieces))
        self.pieces = held[1]
        return held[0]

    def take(self, start, stop):
        chips = lax.axis_size("seq") // 2
        me = lax.axis_index("seq")
        y, c = me // 2, me % 2
        pieces, slots = [], []
        for step in range(start, stop):
            at = (y - step) % chips
            pieces += [self.pieces[step], core_swap(self.pieces[step])]
            slots += [2 * at + c, 2 * at + 1 - c]
        return pieces, slots

    def done(self):
        return assemble(*self.take(0, len(self.pieces)))


class SeqScatter:
    def __init__(self, others):
        self.chips = lax.axis_size("seq") // 2
        self.core = lax.axis_index("seq") % 2
        rows = others.shape[0] // (2 * (self.chips - 1))
        others = others.reshape((self.chips - 1, 2, rows) + others.shape[1:])
        self.values = [others[n] for n in range(self.chips - 1)]
        self.sending = self.cores(self.values[0]).astype(BF)

    def cores(self, value):
        kept = lax.dynamic_index_in_dim(value, self.core, 0, keepdims=False)
        passed = lax.dynamic_index_in_dim(value, 1 - self.core, 0, keepdims=False)
        return kept.astype(F32) + core_swap(passed).astype(F32)

    def hold(self, *values):
        held = lax.optimization_barrier((values, self.sending))
        self.sending = held[1]
        return held[0]

    def done(self, own, others=()):
        own = own.reshape((2, own.shape[0] // 2) + own.shape[1:])
        for value in self.values[1:] + [own]:
            arrived = chip_ring(self.sending)
            arrived, value, others = lax.optimization_barrier((arrived, value, others))
            total = self.cores(value) + arrived.astype(F32)
            self.sending = total.astype(BF)
        return total, others


def sum_exchange(value):
    copies, parts = lax.axis_size("dp"), lax.axis_size("seq")
    rows = value.shape[0] // (copies * parts)
    value = value.reshape((copies * parts, rows) + value.shape[1:])
    value = lax.all_to_all(value, ("dp", "seq"), split_axis=0, concat_axis=0, tiled=True)
    return value.reshape((copies, parts) + value.shape[1:])


def seq_swap(value):
    size = lax.axis_size("seq")
    chips = size // 2
    me = lax.axis_index("seq")
    y, c = me // 2, me % 2
    value = value.reshape((chips, 2) + value.shape[1:])
    kept = lax.dynamic_index_in_dim(value, c, 1, keepdims=False)
    arrived = core_swap(lax.dynamic_index_in_dim(value, 1 - c, 1, keepdims=False))
    pair = jnp.where(c == 0, jnp.stack([kept, arrived], 1), jnp.stack([arrived, kept], 1))
    parts = []
    for step in range(chips):
        part = lax.dynamic_index_in_dim(pair, (y + step) % chips, 0, keepdims=False)
        if step:
            part = lax.ppermute(part, "seq", [(i, (i + 2 * step) % size) for i in range(size)])
        parts.append(part)
    if chips == 2:
        total = jnp.where(y == 0, jnp.stack(parts), jnp.stack(parts[::-1]))
    else:
        total = jnp.zeros_like(pair)
        for step, part in enumerate(parts):
            total = lax.dynamic_update_index_in_dim(total, part, (y - step) % chips, 0)
    return total.reshape((size,) + value.shape[2:])


def seq_exchange(value):
    return lax.all_to_all(value, "seq", split_axis=0, concat_axis=0, tiled=True)


def head_masks(width, dtype):
    lane = lax.broadcasted_iota(jnp.int32, (1, width), 1) // HD
    return [(lane == h).astype(F32).astype(dtype) for h in range(width // HD)]


def swap_halves(values):
    width = values.shape[1]
    lane = lax.broadcasted_iota(jnp.int32, values.shape, 1) % HD
    return jnp.where(
        lane < ROT // 2,
        pltpu.roll(values, width - ROT // 2, 1),
        pltpu.roll(values, ROT // 2, 1),
    )


def as_column(row):
    return jnp.broadcast_to(row, (128, row.shape[1])).T[:, :1]


def as_row(column):
    return jnp.broadcast_to(column, (column.shape[0], 128)).T[:1, :]


def matmul(left, right):
    return lax.dot_general(left, right, (((1,), (0,)), ((), ())), preferred_element_type=F32)


def matmul_nt(left, right):
    return lax.dot_general(left, right, (((1,), (1,)), ((), ())), preferred_element_type=F32)


def matmul_tn(left, right):
    return lax.dot_general(left, right, (((0,), (0,)), ((), ())), preferred_element_type=F32)


def mix_kernel(count, pieces, x_slots_ref, slots_ref, *refs):
    refs = list(refs)
    inputs = refs[:count]
    del refs[:count]
    cos_ref, sin_ref = refs[:2]
    i = pl.program_id(0)
    if pieces:
        gain_ref, low_ref, bias_ref = refs[2:5]
        normed_ref, out_ref, raw_ref, scaled_ref, shift_ref = refs[-5:]
        columns = scaled_ref.shape[1]

        @pl.when(i == 0)
        def _():
            for n, piece_ref in enumerate(refs[5 : 5 + pieces]):
                size = piece_ref.shape[0]
                rows = pl.ds(pl.multiple_of(slots_ref[n] * size, size), size)
                raw_ref[rows, :] = piece_ref[...]
            raw = raw_ref[...]
            scaled_ref[...] = (raw.astype(F32) * as_column(gain_ref[...])).astype(BF)
            low = jnp.broadcast_to(low_ref[...], (8, D)).astype(BF)
            shift_ref[...] = matmul(low, raw) + bias_ref[...]

    else:
        scaled_ref, shift_ref = refs[2:4]
        normed_ref, out_ref = refs[-2:]
        columns = scaled_ref.shape[1]
    for n, x_ref in enumerate(inputs):

        @pl.when(i == n)
        def _(x_ref=x_ref):
            normed_ref[...] = x_ref[...]

    mixed = matmul(normed_ref[...], scaled_ref[...]) + shift_ref[0:1, :]
    cosine, sine = cos_ref[...], sin_ref[...]
    for start in range(0, columns, 3 * 128):
        query = mixed[:, start : start + 128]
        key = mixed[:, start + 128 : start + 256]
        query = (query * cosine + swap_halves(query) * sine) * QUERY_SCALE
        key = key * cosine + swap_halves(key) * sine
        out_ref[:, start : start + 128] = query.astype(BF)
        out_ref[:, start + 128 : start + 256] = key.astype(BF)
        out_ref[:, start + 256 : start + 384] = mixed[:, start + 256 : start + 384].astype(BF)


def mix(inputs, x_slots, cosine, sine, first=None, scaled=None, kept=()):
    count, size, length = len(inputs), inputs[0].shape[0], cosine.shape[0]
    columns = (first[2].shape[0] if scaled is None else scaled[0].shape[1])

    def whole(shape):
        return pl.BlockSpec(shape, lambda i, *_: (0, 0))

    def rows(width):
        return pl.BlockSpec((size, width), lambda i, *_: (_[0][i], 0))

    held = pl.BlockSpec(memory_space=pltpu.VMEM)
    values = [*inputs, cosine, sine]
    specs = [held] * count + [rows(128), rows(128)]
    out_specs = [rows(D), rows(columns)]
    out_shape = [
        jax.ShapeDtypeStruct((length, D), BF),
        jax.ShapeDtypeStruct((length, columns), BF),
    ]
    pieces, slots = (), [jnp.int32(0)]
    if first is not None:
        gain, low, bias, pieces, slots = first
        values += [gain[None], low[None], bias[None], *pieces]
        specs += [whole((1, D)), whole((1, D)), whole((1, columns))] + [held] * len(pieces)
        out_specs += [whole((D, columns)), whole((D, columns)), whole((8, columns))]
        out_shape += [
            jax.ShapeDtypeStruct((D, columns), BF),
            jax.ShapeDtypeStruct((D, columns), BF),
            jax.ShapeDtypeStruct((8, columns), F32),
        ]
    else:
        values += list(scaled)
        specs += [whole((D, columns)), whole((8, columns))]
    aliases = {2 + len(values) + n: n for n in range(len(kept))}
    values += list(kept)
    specs += [pl.BlockSpec(memory_space=pl.ANY)] * len(kept)
    return pl.pallas_call(
        partial(mix_kernel, count, len(pieces)),
        grid_spec=pltpu.PrefetchScalarGridSpec(
            num_scalar_prefetch=2, grid=(count,), in_specs=specs, out_specs=out_specs
        ),
        out_shape=out_shape,
        input_output_aliases=aliases,
        compiler_params=pltpu.CompilerParams(vmem_limit_bytes=VMEM_LIMIT),
        cost_estimate=LIGHT,
        name="mix",
    )(jnp.stack(x_slots).astype(jnp.int32), jnp.stack(slots).astype(jnp.int32), *values)


def attend_kernel(q_ref, k_ref, v_ref, o_ref, lse_ref, acc_ref, turned_ref):
    block, width = q_ref.shape
    heads = width // HD
    i = pl.program_id(0)
    query = q_ref[...]
    queries = [query * mask for mask in head_masks(width, BF)]

    @pl.when(i == 0)
    def _():
        turned_ref[...] = v_ref[...].T

    acc_ref[...] = jnp.zeros(acc_ref.shape, F32)

    def tile(j, diagonal, carry):
        rows = pl.ds(pl.multiple_of(j * block, block), block)
        key = k_ref[rows, :]
        scores = [matmul_nt(key, queries[h]) for h in range(heads)]
        if diagonal:
            row = lax.broadcasted_iota(jnp.int32, (block, block), 0)
            column = lax.broadcasted_iota(jnp.int32, (block, block), 1)
            allowed = row <= column
            scores = [jnp.where(allowed, score, MASK_VALUE) for score in scores]
        highs = [
            jnp.maximum(carry[h][0], jnp.max(scores[h], 0, keepdims=True)) for h in range(heads)
        ]
        weights = [jnp.exp(scores[h] - highs[h]) for h in range(heads)]
        fades = [jnp.exp(carry[h][0] - highs[h]) for h in range(heads)]
        sums = [
            carry[h][1] * fades[h] + jnp.sum(weights[h], 0, keepdims=True) for h in range(heads)
        ]
        for h in range(heads):
            part = slice(h * HD, (h + 1) * HD)
            product = matmul(turned_ref[part, rows], weights[h].astype(BF))
            acc_ref[part, :] = acc_ref[part, :] * fades[h] + product
        return [(highs[h], sums[h]) for h in range(heads)]

    empty = (jnp.full((1, block), MASK_VALUE, F32), jnp.zeros((1, block), F32))
    carry = lax.fori_loop(0, i, lambda j, carry: tile(j, False, carry), [empty] * heads)
    carry = tile(i, True, carry)
    for h in range(heads):
        part = slice(h * HD, (h + 1) * HD)
        acc_ref[part, :] = acc_ref[part, :] / carry[h][1]
        lse_ref[h : h + 1, :] = carry[h][0] + jnp.log(carry[h][1])
    o_ref[...] = acc_ref[...].T.astype(BF)


def attend(mixed, half):
    length, width = mixed.shape[0], 128
    heads = width // HD
    block = min(BLOCK, length)
    return pl.pallas_call(
        attend_kernel,
        grid=(length // block,),
        in_specs=[
            pl.BlockSpec((block, width), lambda i: (i, 3 * half)),
            pl.BlockSpec((length, width), lambda i: (0, 3 * half + 1)),
            pl.BlockSpec((length, width), lambda i: (0, 3 * half + 2)),
        ],
        out_specs=[
            pl.BlockSpec((block, width), lambda i: (i, 0)),
            pl.BlockSpec((heads, block), lambda i: (0, i)),
        ],
        out_shape=[
            jax.ShapeDtypeStruct((length, width), BF),
            jax.ShapeDtypeStruct((heads, length), F32),
        ],
        scratch_shapes=[
            pltpu.VMEM((width, block), F32),
            pltpu.VMEM((width, length), BF),
        ],
        compiler_params=pltpu.CompilerParams(vmem_limit_bytes=VMEM_LIMIT),
        cost_estimate=LIGHT,
        name="attend",
    )(mixed, mixed, mixed)


def attend_back_kernel(
    q_ref,
    k_ref,
    v_ref,
    do_ref,
    o_ref,
    lse_ref,
    cos_ref,
    sin_ref,
    out_ref,
    total_ref,
    inner_ref,
    dq_ref,
    dk_ref,
    dv_ref,
):
    block, width = k_ref.shape
    length = q_ref.shape[0]
    heads = width // HD
    steps = length // block
    j = pl.program_id(0)
    masks = head_masks(width, BF)
    key = k_ref[...]
    value = v_ref[...]
    keys = [key * mask for mask in masks]
    values = [value * mask for mask in masks]

    @pl.when(j == 0)
    def _():
        dq_ref[...] = jnp.zeros(dq_ref.shape, F32)
        total_ref[...] = jnp.zeros(total_ref.shape, F32)
        product = do_ref[...].astype(F32) * o_ref[...].astype(F32)
        coarse = product.astype(BF)
        fine = (product - coarse.astype(F32)).astype(BF)
        row = lax.broadcasted_iota(jnp.int32, (8, width), 0)
        lane = lax.broadcasted_iota(jnp.int32, (8, width), 1) // HD
        chosen = (row == lane).astype(F32).astype(BF)
        inner_ref[...] = matmul_nt(chosen, coarse) + matmul_nt(chosen, fine)

    dk_ref[...] = jnp.zeros(dk_ref.shape, F32)
    dv_ref[...] = jnp.zeros(dv_ref.shape, F32)

    def tile(i, diagonal):
        rows = pl.ds(pl.multiple_of(i * block, block), block)
        query = q_ref[rows, :]
        grad = do_ref[rows, :]
        log_total = lse_ref[:, rows]
        inner = inner_ref[:, rows]
        scores = [matmul_nt(keys[h], query) for h in range(heads)]
        weight_grads = [matmul_nt(values[h], grad) for h in range(heads)]
        if diagonal:
            row = lax.broadcasted_iota(jnp.int32, (block, block), 0)
            column = lax.broadcasted_iota(jnp.int32, (block, block), 1)
            allowed = row <= column
            scores = [jnp.where(allowed, score, MASK_VALUE) for score in scores]
        weights = [jnp.exp(scores[h] - log_total[h : h + 1, :]) for h in range(heads)]
        low = [weight.astype(BF) for weight in weights]
        score_grads = [
            (weights[h] * (weight_grads[h] - inner[h : h + 1, :])).astype(BF)
            for h in range(heads)
        ]
        dv_ref[...] += matmul(
            jnp.concatenate(low, 1), jnp.concatenate([grad * mask for mask in masks], 0)
        )
        dk_ref[...] += matmul(
            jnp.concatenate(score_grads, 1),
            jnp.concatenate([query * mask for mask in masks], 0),
        )
        dq_ref[rows, :] += matmul_tn(
            jnp.concatenate(score_grads, 0), jnp.concatenate(keys, 0)
        )

    def step(i, carry):
        tile(i, False)
        return carry

    tile(j, True)
    lax.fori_loop(j + 1, steps, step, 0)

    own = pl.ds(pl.multiple_of(j * block, block), block)
    cosine = cos_ref[own, :]
    sine = sin_ref[own, :]
    key_grad = dk_ref[...]
    key_grad = key_grad * cosine - swap_halves(key_grad) * sine
    value_grad = dv_ref[...]
    query_grad = dq_ref[own, :] * QUERY_SCALE
    query_grad = query_grad * cosine - swap_halves(query_grad) * sine
    out_ref[:, :width] = query_grad.astype(BF)
    out_ref[:, width : 2 * width] = key_grad.astype(BF)
    out_ref[:, 2 * width :] = value_grad.astype(BF)
    total_ref[:, :width] += jnp.sum(query_grad, 0, keepdims=True)
    total_ref[:, width : 2 * width] += jnp.sum(key_grad, 0, keepdims=True)
    total_ref[:, 2 * width :] += jnp.sum(value_grad, 0, keepdims=True)


def attend_back(mixed, grads, attended, log_total, cosine, sine, half):
    length, width = mixed.shape[0], 128
    heads = width // HD
    block = min(BLOCK, length)
    return pl.pallas_call(
        attend_back_kernel,
        grid=(length // block,),
        in_specs=[
            pl.BlockSpec((length, width), lambda j: (0, 3 * half)),
            pl.BlockSpec((block, width), lambda j: (j, 3 * half + 1)),
            pl.BlockSpec((block, width), lambda j: (j, 3 * half + 2)),
            pl.BlockSpec((length, width), lambda j: (0, half)),
            pl.BlockSpec((length, width), lambda j: (0, 0)),
            pl.BlockSpec((heads, length), lambda j: (0, 0)),
            pl.BlockSpec((length, 128), lambda j: (0, 0)),
            pl.BlockSpec((length, 128), lambda j: (0, 0)),
        ],
        out_specs=[
            pl.BlockSpec((block, 3 * width), lambda j: (j, 0)),
            pl.BlockSpec((1, 3 * width), lambda j: (0, 0)),
        ],
        out_shape=[
            jax.ShapeDtypeStruct((length, 3 * width), BF),
            jax.ShapeDtypeStruct((1, 3 * width), F32),
        ],
        scratch_shapes=[
            pltpu.VMEM((8, length), F32),
            pltpu.VMEM((length, width), F32),
            pltpu.VMEM((block, width), F32),
            pltpu.VMEM((block, width), F32),
        ],
        compiler_params=pltpu.CompilerParams(vmem_limit_bytes=VMEM_LIMIT),
        cost_estimate=LIGHT,
        name="attend_back",
    )(mixed, mixed, mixed, grads, attended, log_total, cosine, sine)


def gelu_pair(values):
    size = jnp.abs(values) * (1.0 / math.sqrt(2.0))
    bell = jnp.exp(-size * size)
    turn = 1.0 / (1.0 + 0.3275911 * size)
    series = turn * (
        0.254829592
        + turn * (-0.284496736 + turn * (1.421413741 + turn * (-1.453152027 + turn * 1.061405429)))
    )
    tail = 0.5 * series * bell
    below = jnp.where(values < 0.0, tail, 1.0 - tail)
    slope = below + values * bell * (1.0 / math.sqrt(2.0 * math.pi))
    return values * below, slope


def chip_rows(own, length):
    chips = lax.axis_size("seq") // 2
    y = lax.axis_index("seq") // 2
    per = length // ROWS // chips
    if own is None:
        return length // ROWS, lambda i, y_ref: i, y
    if own:
        return per, lambda i, y_ref: y_ref[0] * per + i, y
    return (
        (chips - 1) * per,
        lambda i, y_ref: (y_ref[0] + chips - 1 - i // per) % chips * per + i % per,
        y,
    )


def feed_kernel(first, last, halves, count, y_ref, slots_ref, x_ref, *refs):
    refs = list(refs)
    if first:
        gain_ref, low_ref, bias_ref = refs[:3]
        del refs[:3]
        if count:
            pieces = refs[:count]
            del refs[:count]
        else:
            raw_ref = refs.pop(0)
    else:
        scaled_ref, shift_ref = refs[:2]
        del refs[:2]
    if last:
        out_ref = refs.pop()
        if count:
            shrink_ref = refs.pop()
        else:
            shrink_ref = refs.pop(0)
        output_ref = refs.pop(0)
        attended = refs[:halves]
    if first:
        if count:
            raw_ref = refs.pop()
        act_ref, slope_ref, scaled_ref, shift_ref = refs[-4:]
        units = scaled_ref.shape[1]

        @pl.when(pl.program_id(0) == 0)
        def _():
            if count:
                for n, piece_ref in enumerate(pieces):
                    size = piece_ref.shape[0]
                    rows = pl.ds(pl.multiple_of(slots_ref[n] * size, size), size)
                    raw_ref[rows, :] = piece_ref[:, :units]
                    shrink_ref[rows, :] = piece_ref[:, units:]
            raw = raw_ref[...]
            scaled_ref[...] = (raw.astype(F32) * as_column(gain_ref[...])).astype(BF)
            low = jnp.broadcast_to(low_ref[...], (8, D)).astype(BF)
            shift_ref[...] = matmul(low, raw) + bias_ref[...]

    else:
        act_ref, slope_ref = refs[-2:]
    hidden = matmul(x_ref[...], scaled_ref[...]) + shift_ref[0:1, :]
    activated, slope = gelu_pair(hidden)
    activated = activated.astype(BF)
    act_ref[...] = activated
    slope_ref[...] = slope.astype(BF)
    if last:
        out = matmul(activated, shrink_ref[...])
        for half, o_ref in enumerate(attended):
            out = out + matmul(o_ref[...], output_ref[half * 128 : (half + 1) * 128, :])
        out_ref[...] = out.astype(BF)


def feed(rows_of, x, units, first=None, scaled=None, last=None, kept=(), slots=None):
    length = x.shape[0]
    steps, row, y = chip_rows(rows_of, length)

    def rows(columns):
        return pl.BlockSpec((ROWS, columns), lambda i, *_: (row(i, _[0]), 0))

    def whole(shape, column=0):
        return pl.BlockSpec(shape, lambda i, *_: (0, column))

    specs, values, halves, count = [rows(D)], [x], 0, 0
    out_specs = [rows(units), rows(units)]
    out_shape = [jax.ShapeDtypeStruct((length, units), BF)] * 2
    if first is not None:
        gain, low, bias, weight = first
        values += [gain[None], low[None], bias[None]]
        specs += [whole((1, D)), whole((1, D)), whole((1, units))]
        out_specs += [whole((D, units)), whole((8, units))]
        out_shape += [
            jax.ShapeDtypeStruct((D, units), BF),
            jax.ShapeDtypeStruct((8, units), F32),
        ]
        if slots is not None:
            count = len(weight)
            values += weight
            specs += [pl.BlockSpec(memory_space=pltpu.VMEM)] * count
            out_specs += [whole((D, units))]
            out_shape += [jax.ShapeDtypeStruct((D, units), BF)]
        else:
            values.append(weight[0])
            specs.append(whole((D, units), weight[1]))
    else:
        values += list(scaled)
        specs += [whole((D, units)), whole((8, units))]
    if last is not None:
        shrink, output, attended = last
        halves = len(attended)
        if count:
            out_specs.append(whole((units, D)))
            out_shape.append(jax.ShapeDtypeStruct((units, D), BF))
        else:
            values.append(shrink[0])
            specs.append(whole((units, D), shrink[1]))
        values += [output, *attended]
        specs += [whole(output.shape)] + [rows(128)] * halves
        out_specs.append(pl.BlockSpec((ROWS, D), lambda i, *_: (i, 0)))
        out_shape.append(jax.ShapeDtypeStruct((steps * ROWS, D), BF))
    aliases = {2 + len(values) + n: n for n in range(len(kept))}
    values += list(kept)
    specs += [pl.BlockSpec(memory_space=pl.ANY)] * len(kept)
    slots = jnp.zeros((1,), jnp.int32) if slots is None else jnp.stack(slots).astype(jnp.int32)
    return pl.pallas_call(
        partial(feed_kernel, first is not None, last is not None, halves, count),
        grid_spec=pltpu.PrefetchScalarGridSpec(
            num_scalar_prefetch=2, grid=(steps,), in_specs=specs, out_specs=out_specs
        ),
        out_shape=out_shape,
        input_output_aliases=aliases,
        compiler_params=pltpu.CompilerParams(vmem_limit_bytes=VMEM_LIMIT),
        cost_estimate=LIGHT,
        name="feed",
    )(y.reshape(1), slots, *values)


def branch_kernel(y_ref, act_ref, shrink_ref, output_ref, *refs):
    out = matmul(act_ref[...], shrink_ref[...])
    for half, o_ref in enumerate(refs[:-1]):
        out = out + matmul(o_ref[...], output_ref[half * 128 : (half + 1) * 128, :])
    refs[-1][...] = out.astype(BF)


def branch(rows_of, activated, shrink, output, attended):
    length, units = activated.shape
    steps, row, y = chip_rows(rows_of, length)

    def rows(columns):
        return pl.BlockSpec((ROWS, columns), lambda i, y_ref: (row(i, y_ref), 0))

    return pl.pallas_call(
        branch_kernel,
        grid_spec=pltpu.PrefetchScalarGridSpec(
            num_scalar_prefetch=1,
            grid=(steps,),
            in_specs=[
                rows(units),
                pl.BlockSpec((units, D), lambda i, y_ref: (0, shrink[1])),
                pl.BlockSpec(output.shape, lambda i, y_ref: (0, 0)),
            ]
            + [rows(128)] * len(attended),
            out_specs=pl.BlockSpec((ROWS, D), lambda i, y_ref: (i, 0)),
        ),
        out_shape=jax.ShapeDtypeStruct((steps * ROWS, D), BF),
        compiler_params=pltpu.CompilerParams(vmem_limit_bytes=VMEM_LIMIT),
        cost_estimate=LIGHT,
        name="branch",
    )(y.reshape(1), activated, shrink[0], output, *attended)


def norm_grad_kernel(y_ref, h_ref, wi_ref, wm_ref, *refs):
    out = matmul_nt(h_ref[...], wi_ref[...])
    for half, m_ref in enumerate(refs[:-1]):
        out = out + matmul_nt(m_ref[...], wm_ref[:, half * 384 : (half + 1) * 384])
    refs[-1][...] = out.astype(BF)


def norm_grad(hidden, expand, mixed, mixing, own):
    length, units, columns = hidden.shape[0], expand.shape[1], mixing.shape[1]
    steps, row, y = chip_rows(own, length)

    def rows(count):
        return pl.BlockSpec((ROWS, count), lambda i, y_ref: (row(i, y_ref), 0))

    def whole(shape):
        return pl.BlockSpec(shape, lambda i, y_ref: (0, 0))

    return pl.pallas_call(
        norm_grad_kernel,
        grid_spec=pltpu.PrefetchScalarGridSpec(
            num_scalar_prefetch=1,
            grid=(steps,),
            in_specs=[rows(units), whole((D, units)), whole((D, columns))]
            + [rows(384)] * len(mixed),
            out_specs=pl.BlockSpec((ROWS, D), lambda i, y_ref: (i, 0)),
        ),
        out_shape=jax.ShapeDtypeStruct((steps * ROWS, D), BF),
        compiler_params=pltpu.CompilerParams(vmem_limit_bytes=VMEM_LIMIT),
        cost_estimate=LIGHT,
        name="norm_grad",
    )(y.reshape(1), hidden, expand, mixing, *mixed)


def hidden_back_kernel(grad_ref, shrink_ref, slope_ref, output_ref, low_ref, total_ref, do_ref):
    grads = grad_ref[...]
    hidden = matmul_nt(grads, shrink_ref[...]) * slope_ref[...].astype(F32)
    low_ref[...] = hidden.astype(BF)

    @pl.when(pl.program_id(0) == 0)
    def _():
        total_ref[...] = jnp.zeros(total_ref.shape, F32)

    total_ref[...] += jnp.sum(hidden, 0, keepdims=True)
    do_ref[...] = matmul_nt(grads, output_ref[...]).astype(BF)


def hidden_back(grads, shrink, slope, output):
    length, units = slope.shape
    width = output.shape[0]
    array, column = shrink
    return pl.pallas_call(
        hidden_back_kernel,
        grid=(length // BLOCK,),
        in_specs=[
            pl.BlockSpec((BLOCK, D), lambda i: (i, 0)),
            pl.BlockSpec((units, D), lambda i: (0, column)),
            pl.BlockSpec((BLOCK, units), lambda i: (i, 0)),
            pl.BlockSpec((width, D), lambda i: (0, 0)),
        ],
        out_specs=[
            pl.BlockSpec((BLOCK, units), lambda i: (i, 0)),
            pl.BlockSpec((1, units), lambda i: (0, 0)),
            pl.BlockSpec((BLOCK, width), lambda i: (i, 0)),
        ],
        out_shape=[
            jax.ShapeDtypeStruct((length, units), BF),
            jax.ShapeDtypeStruct((1, units), F32),
            jax.ShapeDtypeStruct((length, width), BF),
        ],
        compiler_params=pltpu.CompilerParams(vmem_limit_bytes=VMEM_LIMIT),
        cost_estimate=LIGHT,
        name="hidden_back",
    )(grads, array, slope, output)


def product_kernel(x_ref, g_ref, out_ref):
    out_ref[...] = matmul_tn(x_ref[...], g_ref[...]).astype(BF)


def product(x, grads, column=0, wide=D):
    length, count = x.shape
    block = min(BLOCK, count)
    return pl.pallas_call(
        product_kernel,
        grid=(count // block,),
        in_specs=[
            pl.BlockSpec((length, block), lambda i: (0, i)),
            pl.BlockSpec((length, D), lambda i: (0, 0)),
        ],
        out_specs=pl.BlockSpec((block, D), lambda i: (i, column)),
        out_shape=jax.ShapeDtypeStruct((count, wide), BF),
        compiler_params=pltpu.CompilerParams(vmem_limit_bytes=VMEM_LIMIT),
        cost_estimate=LIGHT,
        name="product",
    )(x, grads)


def weight_grad_kernel(count, x_ref, weight_ref, gain_ref, shift_ref, total_ref, *refs):
    lows, (out_ref, gain_out_ref, shift_out_ref) = refs[:count], refs[-3:]
    gain, shift = as_column(gain_ref[...]), as_column(shift_ref[...])
    x = x_ref[...]
    start, gain_sum, shift_sum = 0, 0.0, 0.0
    for low_ref in lows:
        columns = slice(start, start + low_ref.shape[1])
        start += low_ref.shape[1]
        raw = matmul_tn(x, low_ref[...])
        weight = weight_ref[:, columns].astype(F32)
        total = total_ref[:, columns]
        out_ref[:, columns] = (raw * gain + shift * total).astype(BF)
        gain_sum = gain_sum + jnp.sum(raw * weight, 1, keepdims=True)
        shift_sum = shift_sum + jnp.sum(weight * total, 1, keepdims=True)
    gain_out_ref[...] = as_row(gain_sum)
    shift_out_ref[...] = as_row(shift_sum)


def weight_grad(x, lows, weight, gain, shift, total, kept=()):
    length, columns = x.shape[0], total.shape[1]
    array, column = weight
    row = pl.BlockSpec((1, ROWS), lambda i: (0, i))
    return pl.pallas_call(
        partial(weight_grad_kernel, len(lows)),
        grid=(D // ROWS,),
        in_specs=[
            pl.BlockSpec((length, ROWS), lambda i: (0, i)),
            pl.BlockSpec((ROWS, columns), lambda i: (i, column)),
            row,
            row,
            pl.BlockSpec((1, columns), lambda i: (0, 0)),
        ]
        + [pl.BlockSpec(low.shape, lambda i: (0, 0)) for low in lows]
        + [pl.BlockSpec(memory_space=pl.ANY)] * len(kept),
        out_specs=[pl.BlockSpec((ROWS, columns), lambda i: (i, 0)), row, row],
        out_shape=[
            jax.ShapeDtypeStruct((D, kept[0].shape[1] if kept else columns), BF),
            jax.ShapeDtypeStruct((1, D), F32),
            jax.ShapeDtypeStruct((1, D), F32),
        ],
        input_output_aliases={5 + len(lows): 0} if kept else {},
        compiler_params=pltpu.CompilerParams(vmem_limit_bytes=VMEM_LIMIT),
        cost_estimate=LIGHT,
        name="weight_grad",
    )(x, array, gain[None], shift[None], total, *lows, *kept)


def pack_kernel(spans, mixing_ref, expand_ref, *refs):
    out_ref = refs[-1]
    for source_ref, part in ((mixing_ref, spans[0]), (expand_ref, spans[1])):
        for p, start, at, count in part:
            out_ref[p, :, start : start + count] = source_ref[0, :, at : at + count].astype(BF)
    for pair_ref in refs[:-1]:
        end = out_ref.shape[2] - pair_ref.shape[1]
        for p in range(out_ref.shape[0]):
            out_ref[p, :, end:] = pair_ref[...]


def pack(mixing, expand, layer, spans, columns, pair=()):
    parts, rows = lax.axis_size("seq"), mixing.shape[1]
    columns = columns + sum(value.shape[1] for value in pair)
    return pl.pallas_call(
        partial(pack_kernel, spans),
        grid=(1,),
        in_specs=[
            pl.BlockSpec((1,) + mixing.shape[1:], lambda i: (layer, 0, 0)),
            pl.BlockSpec((1,) + expand.shape[1:], lambda i: (layer, 0, 0)),
        ]
        + [pl.BlockSpec(value.shape, lambda i: (0, 0)) for value in pair],
        out_specs=pl.BlockSpec((parts, rows, columns), lambda i: (0, 0, 0)),
        out_shape=jax.ShapeDtypeStruct((parts, rows, columns), BF),
        compiler_params=pltpu.CompilerParams(vmem_limit_bytes=VMEM_LIMIT),
        cost_estimate=LIGHT,
        name="pack",
    )(mixing, expand, *pair)


def home_spans(parts, copies, width, units):
    mixing, expand = [], []
    size = units // copies
    for p in range(parts):
        for half in range(width // 128):
            for kind in range(3):
                at = kind * parts * width + p * width + half * 128
                mixing.append((p, half * 384 + kind * 128, at, 128))
        for d in range(copies):
            expand.append((p, 3 * width + d * size, (d * parts + p) * size, size))
    return mixing, expand


def adam(grad, weight, first, second, average, rate, decay):
    first_new = BETA_FIRST * first + (1.0 - BETA_FIRST) * grad
    second_new = BETA_SECOND * second + (1.0 - BETA_SECOND) * grad * grad
    first_hat = first_new / (1.0 - BETA_FIRST**STEP)
    second_hat = second_new / (1.0 - BETA_SECOND**STEP)
    weight_new = weight - rate * (
        first_hat / (jnp.sqrt(second_hat) + ADAM_EPS) + decay * weight
    )
    return weight_new, first_new, second_new, EMA_DECAY * average + (1.0 - EMA_DECAY) * weight_new


def adam_kernel(spans, rates, clip_ref, exchanged_ref, output_ref, shrink_ref, *refs):
    clip = clip_ref[0]
    states, news = refs[:16], refs[16:]

    def step(kind, grad, columns):
        old = [ref[0, :, columns] for ref in states[4 * kind : 4 * kind + 4]]
        new = adam(grad.astype(F32) * clip, *old, rates[kind], WEIGHT_DECAY)
        for ref, value in zip(news[4 * kind : 4 * kind + 4], new):
            ref[0, :, columns] = value

    for kind, part in ((0, spans[0]), (2, spans[1])):
        for source, start, at, count in part:
            grad = exchanged_ref[0, source, :, start : start + count]
            step(kind, grad, slice(at, at + count))
    step(1, output_ref[0], slice(None))
    step(3, shrink_ref[0], slice(None))


def update(clip, exchanged, output, shrink, states, spans, rates):
    layers, parts, rows, columns = exchanged.shape
    chunk = 16 if rows % 16 == 0 else rows
    chunks = rows // chunk

    def block(array):
        size = array.shape[1] // chunks
        return pl.BlockSpec((1, size, array.shape[2]), lambda l, n: (l, n, 0))

    return pl.pallas_call(
        partial(adam_kernel, spans, rates),
        grid=(layers, chunks),
        in_specs=[
            pl.BlockSpec(memory_space=pltpu.SMEM),
            pl.BlockSpec((1, parts, chunk, columns), lambda l, n: (l, 0, n, 0)),
            block(output),
            block(shrink),
        ]
        + [block(state) for state in states],
        out_specs=[block(state) for state in states],
        out_shape=[jax.ShapeDtypeStruct(state.shape, F32) for state in states],
        compiler_params=pltpu.CompilerParams(vmem_limit_bytes=VMEM_LIMIT),
        cost_estimate=LIGHT,
        name="update",
    )(clip, exchanged, output, shrink, *states)


def rotary_tables(positions):
    half = ROT // 2
    steps_half = jnp.arange(half).astype(F32)
    frequency = 10000.0 ** (-2.0 * steps_half / ROT)
    angles = positions.astype(F32)[None, :] * frequency[:, None]
    cosine = jnp.concatenate([jnp.cos(angles), jnp.ones_like(angles)], 0)
    entry = jnp.arange(128)[None, :] % HD
    index = jnp.arange(half)[:, None]
    turning = (entry < ROT) & (entry % half == index)
    still = (entry >= ROT) & (index == 0)
    sign = jnp.where(entry < half, -1.0, 1.0)
    spread_cosine = jnp.concatenate([turning, still], 0).astype(F32)
    spread_sine = turning.astype(F32) * sign

    def lay(table, spread):
        return lax.dot_general(
            table, spread, (((0,), (0,)), ((), ())), precision=lax.Precision.HIGHEST
        )

    return lay(cosine, spread_cosine), lay(jnp.sin(angles), spread_sine)


def split_affine(affine):
    bounds = [D, D, D, D, 3 * D, D, FF, D]
    pieces = []
    offset = 0
    for length in bounds:
        pieces.append(affine[offset : offset + length])
        offset = offset + length
    return pieces


def normalize(values):
    centre = values - jnp.mean(values, -1, keepdims=True)
    spread = jnp.mean(centre * centre, -1, keepdims=True)
    scale = lax.rsqrt(spread + NORM_EPS)
    return centre * scale, scale


def local(
    stream,
    cotangent,
    positions,
    mixing_weight,
    mixing_first,
    mixing_second,
    mixing_average,
    output_weight,
    output_first,
    output_second,
    output_average,
    expand_weight,
    expand_first,
    expand_second,
    expand_average,
    shrink_weight,
    shrink_first,
    shrink_second,
    shrink_average,
    affine_weight,
    affine_first,
    affine_second,
    affine_average,
):
    parts = lax.axis_size("seq")
    copies = lax.axis_size("dp")
    devices = parts * copies
    part = lax.axis_index("seq")
    width = D // parts
    units = FF // parts
    rows_d = D // devices
    rows_f = FF // devices
    rows = stream.shape[0] * stream.shape[1]
    small = affine_weight.shape[1]

    halves = width // 128
    outer = dp_parts()[0]

    def mixing_part(vector):
        view = vector.reshape(3, parts, halves, 128)
        view = lax.dynamic_index_in_dim(view, part, 1, keepdims=False)
        return view.transpose(1, 0, 2).reshape(-1)

    def expand_part(vector):
        view = vector.reshape(copies, parts, -1)
        return lax.dynamic_index_in_dim(view, part, 1, keepdims=False).reshape(-1)

    def spread_mixing(vector):
        view = jnp.zeros((3, parts, width), F32)
        vector = vector.reshape(halves, 3, 128).transpose(1, 0, 2).reshape(3, 1, width)
        return lax.dynamic_update_slice(view, vector, (0, part, 0)).reshape(-1)

    def spread_expand(vector):
        view = jnp.zeros((copies, parts, rows_f), F32)
        return lax.dynamic_update_slice(view, vector.reshape(copies, 1, rows_f), (0, part, 0)).reshape(-1)

    spans = home_spans(parts, copies, width, units)
    aligned = rows_f % 128 == 0 and rows_d % 16 == 0

    def arrange(layer, mixing, expand, pair=()):
        if aligned:
            return pack(mixing, expand, layer, spans, 3 * width + units, pair)
        mixing = mixing[layer].astype(BF).reshape(rows_d, 3, parts, halves, 128)
        mixing = mixing.transpose(2, 0, 3, 1, 4).reshape(parts, rows_d, 3 * width)
        expand = expand[layer].astype(BF).reshape(rows_d, copies, parts, rows_f)
        expand = expand.transpose(2, 0, 1, 3).reshape(parts, rows_d, units)
        pair = [jnp.broadcast_to(value, (parts,) + value.shape) for value in pair]
        return jnp.concatenate([mixing, expand] + pair, -1)

    def settle_output(exchanged):
        output = exchanged.reshape(parts, copies // parts, rows_d, D)
        return output.transpose(1, 0, 2, 3).reshape(width, D)

    def norm_back(gradient, normed_grad, own_normed, scale):
        projected = jnp.mean(normed_grad * own_normed, -1, keepdims=True)
        middle = jnp.mean(normed_grad, -1, keepdims=True)
        return gradient + scale * (normed_grad - middle - own_normed * projected)

    def outgoing_output(attended, grads):
        output_grad = jnp.concatenate([product(out, grads) for out in attended], 0)
        output_grad = output_grad.reshape(copies // parts, parts, rows_d, D).transpose(1, 0, 2, 3)
        return seq_swap(output_grad.reshape(parts, copies // parts * rows_d, D))

    def beside(grads, *pieces):
        pieces = [jnp.concatenate(piece).reshape(devices, small) for piece in pieces]
        pieces = jnp.concatenate(pieces, -1)
        coarse = pieces.astype(BF)
        fine = (pieces - coarse.astype(F32)).astype(BF)
        pieces = jnp.concatenate([coarse, fine], -1)
        extra = 128 * pl.cdiv(pieces.shape[1], 128 * rows_d)
        pieces = jnp.pad(pieces, ((0, 0), (0, extra * rows_d - pieces.shape[1])))
        return jnp.concatenate([grads, pieces.reshape(D, extra)], -1)

    def apart(summed, columns, count):
        pieces = summed[..., columns:].reshape(devices, -1).astype(F32)
        size = count * small
        pieces = jnp.sum(pieces[:, :size] + pieces[:, size : 2 * size], 0).reshape(count, small)
        return jnp.sum(summed[..., :columns].astype(F32), 0), list(pieces)

    def sum_squares(*values):
        return sum(jnp.sum(value.astype(F32) * value.astype(F32)) for value in values)

    tie = lax.optimization_barrier
    chips = parts // 2
    current = stream.reshape(rows, D)
    gradient = cotangent.reshape(rows, D)

    def view(array, column):
        if units == D:
            return array, column
        return array[:, column * units : (column + 1) * units].reshape(-1, D), 0

    pair = jnp.stack([positions.reshape(-1) // 16, positions.reshape(-1) % 16]).astype(BF)
    pair = pair.reshape(rows_d, 2 * rows // rows_d)
    both = arrange(0, mixing_weight, expand_weight, (pair,))
    both, current = tie((both, current))
    both = seq_exchange(both)
    own_normed, scale = normalize(current)
    travel = SeqGather(own_normed.astype(BF))
    pair = both[..., 3 * width + units :].astype(F32).reshape(parts, 2, rows)
    places = (pair[:, 0] * 16.0 + pair[:, 1]).reshape(-1)
    both = both.reshape(parts * rows_d, -1)
    near = Gather(both[:, : 3 * width])
    places, affine_low, layer_mixing, layer_expand, first_output, later_output = near.hold(
        places,
        affine_weight,
        mixing_weight,
        expand_weight,
        output_weight[0],
        output_weight[1],
    )
    near.forward()
    affine_low = affine_low.astype(BF).reshape(1, LAYERS * small)
    affine_all = lax.all_to_all(
        jnp.broadcast_to(affine_low, (devices, LAYERS * small)),
        ("dp", "seq"),
        split_axis=0,
        concat_axis=0,
        tiled=True,
    )
    outputs = jnp.concatenate(
        [value.astype(BF).reshape(-1, width) for value in (first_output, later_output)], -1
    )
    outputs = lax.all_gather(outputs, "dp", axis=0, tiled=True)
    cosine, sine = rotary_tables(places)
    later_both = arrange(1, layer_mixing, layer_expand)
    cosine, sine, later_both, expand_own, shrink_own, low_gradient = near.hold(
        cosine,
        sine,
        later_both,
        both[:, 3 * width : 3 * width + units],
        shrink_weight[0],
        gradient.astype(BF),
    )
    near.forward()
    near.cross()
    far_own = jnp.concatenate([expand_own, shrink_own.astype(BF).reshape(-1, units)], -1)
    affine_all, far_own, near.pieces, near.chains, travel.pieces = tie(
        (affine_all, far_own, near.pieces, near.chains, travel.pieces)
    )
    inputs, x_slots = travel.take(0, chips)
    near.forward()
    near.cross()
    affine_all = affine_all.reshape(devices, LAYERS, small).transpose(1, 0, 2)
    affine_all = affine_all.reshape(LAYERS, devices * small).astype(F32)
    vectors = [split_affine(affine_all[layer]) for layer in range(LAYERS)]
    vectors, inputs = near.hold(vectors, inputs)
    for step in range(3, outer - 1):
        near.forward()
        near.cross()
    while len(near.chains) < outer:
        near.cross()
    far = Gather(far_own)
    far.pieces[0], near.pieces, near.chains = tie((far.pieces[0], near.pieces, near.chains))
    far.forward()
    far.cross()
    pieces, slots = near.done()

    gain_one, shift_one, gain_two, shift_two = vectors[0][:4]
    normed, mixed, mixing, mixing_scaled, _ = mix(
        inputs,
        x_slots,
        cosine,
        sine,
        first=(gain_one, shift_one, mixing_part(vectors[0][4]), pieces, slots),
    )
    mixed, later_both, later_shrink, outputs, low_gradient = far.hold(
        mixed, later_both, shrink_weight[1], outputs, low_gradient
    )
    far.forward()
    far.cross()
    travel = SeqGather(low_gradient)
    later_both = seq_exchange(later_both)
    outputs = jnp.stack(
        [outputs[:, layer * width : (layer + 1) * width].reshape(parts, -1, D) for layer in (0, 1)],
        1,
    )
    attended, logs = [], []
    for half in range(halves):
        out, log_total = attend(mixed, half)
        attended.append(out)
        logs.append(log_total)
        if half == 0:
            mixed, out, later_both, outputs = far.hold(mixed, out, later_both, outputs)
            far.forward()
            far.cross()
            outputs = seq_exchange(outputs)
            later_both = later_both.reshape(parts * rows_d, -1)
            later_far = jnp.concatenate(
                [later_both[:, 3 * width :], later_shrink.astype(BF).reshape(-1, units)], -1
            )
            later_near = later_both[:, : 3 * width]
    attended, logs, later_far, later_near, outputs, travel.pieces = far.hold(
        attended, logs, later_far, later_near, outputs, travel.pieces
    )
    output, later_output = (settle_output(outputs[:, layer]) for layer in (0, 1))
    later_all = lax.all_gather(later_far, "dp", axis=0, tiled=True)
    while len(far.pieces) < outer:
        far.forward()
    while len(far.chains) < outer:
        far.cross()
    attended, logs, later_near = far.hold(attended, logs, later_near)
    near = Gather(later_near)
    near.forward()
    near.cross()
    pieces, slots = far.done()
    first = (gain_two, shift_two, expand_part(vectors[0][6]))
    if units == D:
        activated, slope, expand_scaled, expand_shift, expand, shrink, others = feed(
            False,
            normed,
            units,
            first=first + (pieces,),
            last=(None, output, attended),
            slots=slots,
        )
    else:
        far_all = assemble(pieces, slots)
        expand, shrink = far_all[:, :units], view(far_all, 1)[0]
        activated, slope, expand_scaled, expand_shift, others = feed(
            False,
            normed,
            units,
            first=first + ((expand, 0),),
            last=((shrink, 0), output, attended),
        )
    shrink = (shrink, 0)
    (others,) = near.hold(others)
    near.forward()
    near.cross()
    cotangents, travel = travel, SeqScatter(others)
    activated, slope, cotangents.pieces = travel.hold(activated, slope, cotangents.pieces)
    activated, slope, own = feed(
        True,
        normed,
        units,
        scaled=(expand_scaled, expand_shift),
        last=(shrink, output, attended),
        kept=(activated, slope),
    )
    (own,) = near.hold(own)
    grads = cotangents.done()
    for step in range(2, outer - 1):
        near.forward()
        near.cross()
    stored = [(own_normed, scale, normed, mixed, attended, logs, activated, slope)]
    weights = [(mixing, mixing_scaled, output, expand, expand_scaled, shrink)]
    total, (near.pieces, near.chains, grads) = travel.done(
        own, (near.pieces, near.chains, grads)
    )
    while len(near.chains) < outer:
        near.cross()
    current = current + total + vectors[0][5] + vectors[0][7]

    own_normed, scale = normalize(current)
    travel = SeqGather(own_normed.astype(BF))
    pieces, slots = near.done()
    gain_one, shift_one, gain_two, shift_two = vectors[1][:4]
    inputs, x_slots = travel.take(0, 1)
    normed, mixed, mixing, mixing_scaled, mixing_shift = mix(
        inputs,
        x_slots,
        cosine,
        sine,
        first=(gain_one, shift_one, mixing_part(vectors[1][4]), pieces, slots),
    )
    normed, mixed = travel.hold(normed, mixed)
    inputs, x_slots = travel.take(1, chips)
    normed, mixed = mix(
        inputs,
        x_slots,
        cosine,
        sine,
        scaled=(mixing_scaled, mixing_shift),
        kept=(normed, mixed),
    )
    output = later_output
    attended, logs = [], []
    for half in range(halves):
        out, log_total = attend(mixed, half)
        attended.append(out)
        logs.append(log_total)
    attended, logs, later_all = tie((attended, logs, later_all))
    expand, shrink = later_all, view(later_all, 1)
    activated, slope, expand_scaled, expand_shift = feed(
        None,
        normed,
        units,
        first=(gain_two, shift_two, expand_part(vectors[1][6]), (later_all, 0)),
    )

    grads, attended, logs, activated = tie((grads, attended, logs, activated))
    output_grad = outgoing_output(attended, grads)
    hidden_low, hidden_total, attended_grad = hidden_back(grads, shrink, slope, output)
    if units == D:
        later_grad = product(activated, grads, 1, 2 * units + width)
        later_grad, gain_two_grad, shift_two_grad = weight_grad(
            normed, [hidden_low], (expand, 0), gain_two, shift_two, hidden_total, (later_grad,)
        )
        output_grad = output_grad.reshape(-1, width)
        later_grad = lax.dynamic_update_slice(later_grad, output_grad, (0, 2 * units))
    else:
        shrink_grad = product(activated, grads).reshape(-1, units)
        expand_grad, gain_two_grad, shift_two_grad = weight_grad(
            normed, [hidden_low], (expand, 0), gain_two, shift_two, hidden_total
        )
        output_grad = output_grad.reshape(-1, width)
        later_grad = jnp.concatenate([expand_grad, shrink_grad, output_grad], -1)
    later_grad, attended_grad = tie((later_grad, attended_grad))
    later_first = lax.psum_scatter(later_grad, "dp", scatter_dimension=0, tiled=True)
    lows, totals = [], []
    for half in range(halves):
        low, total = attend_back(
            mixed, attended_grad, attended[half], logs[half], cosine, sine, half
        )
        lows.append(low)
        totals.append(total)
    mixed_total = jnp.concatenate(totals, -1)
    others = norm_grad(hidden_low, expand_scaled, lows, mixing_scaled, False)
    travel = SeqScatter(others)
    hidden_low, lows, activated = travel.hold(hidden_low, lows, activated)
    own = norm_grad(hidden_low, expand_scaled, lows, mixing_scaled, True)
    last = (shrink, output, attended)
    result_others = branch(False, activated, *last)
    result_own = branch(True, activated, *last)
    normed_grad, (result_others, result_own) = travel.done(own, (result_others, result_own))
    normed_grad, lows = tie((normed_grad, lows))
    gradient = norm_back(gradient, normed_grad, own_normed, scale)
    travel = SeqGather(gradient.astype(BF))
    lows, own_piece = tie((lows, travel.pieces[0]))
    mixing_grad, gain_one_grad, shift_one_grad = weight_grad(
        normed, lows, (mixing, 0), gain_one, shift_one, mixed_total
    )
    (mixing_grad,) = travel.hold(mixing_grad)
    grads = travel.done()
    later_mixing = sum_exchange(mixing_grad)
    output_sum = jnp.sum(cotangent.reshape(rows, D), 0)

    def small_grads(*pieces):
        gains, mixed_total, output_sum, hidden_total = pieces
        pieces = [piece[0] for piece in gains]
        pieces += [spread_mixing(mixed_total[0]), output_sum]
        return pieces + [spread_expand(hidden_total[0]), output_sum]

    gains = (gain_one_grad, shift_one_grad, gain_two_grad, shift_two_grad)
    later_pieces = small_grads(gains, mixed_total, output_sum, hidden_total)

    later_current, later_vectors = current, vectors[1]
    current = stream.reshape(rows, D)
    own_normed, scale, normed, mixed, attended, logs, activated, slope = stored[0]
    mixing, mixing_scaled, output, expand, expand_scaled, shrink = weights[0]
    gain_one, shift_one, gain_two, shift_two = vectors[0][:4]
    far = Scatter(product(activated, grads).reshape(-1, units))
    (grads,) = far.hold(grads)
    far.cross()
    hidden_low, hidden_total, attended_grad = hidden_back(grads, shrink, slope, output)
    hidden_low, attended_grad, grads, result_others, later_pieces = far.hold(
        hidden_low, attended_grad, grads, result_others, later_pieces
    )
    far.forward()
    far.cross()
    output_grad = outgoing_output(attended, grads)
    expand_grad, gain_two_grad, shift_two_grad = weight_grad(
        normed, [hidden_low], (expand, 0), gain_two, shift_two, hidden_total
    )
    attended_grad, expand_grad, output_grad, later_mixing = far.hold(
        attended_grad, expand_grad, output_grad, later_mixing
    )
    far_grad = lax.psum_scatter(expand_grad, "dp", scatter_dimension=0, tiled=True)
    output_grad = lax.all_to_all(
        output_grad.reshape(copies, parts * rows_d, width), "dp", 0, 0, tiled=True
    )
    travel = SeqScatter(result_others)
    lows, totals, mixing_grads, gain_grads, shift_grads = [], [], [], [], []
    arrived = output_grad
    for half in range(halves):
        if len(far.parts) < outer:
            far.forward()
            far.cross()
        low, total = attend_back(
            mixed, attended_grad, attended[half], logs[half], cosine, sine, half
        )
        if half == 0:
            mixed, low, total, arrived, later_first = far.hold(
                mixed, low, total, arrived, later_first
            )
        else:
            mixed, low, total, arrived = far.hold(mixed, low, total, arrived)
        if half == 0:
            output_grad = arrived
            result, (mixed, low) = travel.done(result_own, (mixed, low))
        else:
            mixing_grads[-1] = arrived
        mixing_grad, gain_one_grad, shift_one_grad = weight_grad(
            normed,
            [low],
            (mixing, half),
            gain_one,
            shift_one,
            total,
        )
        lows.append(low)
        totals.append(total)
        gain_grads.append(gain_one_grad)
        shift_grads.append(shift_one_grad)
        pieces = [later_pieces] if half == 0 else []
        if half == halves - 1:
            output_sum = jnp.sum(gradient, 0)
            gains = (sum(gain_grads), sum(shift_grads), gain_two_grad, shift_two_grad)
            pieces.append(
                small_grads(gains, jnp.concatenate(totals, -1), output_sum, hidden_total)
            )
        mixing_grad = beside(mixing_grad, *pieces) if pieces else mixing_grad
        if half == halves - 1:
            mixing_grad, far_grad = tie((mixing_grad, far_grad))
            home = jnp.stack([far_grad, later_first[:, :units]], 1)
            home = seq_swap(home.reshape(parts, rows_d, 2, units))
        mixing_grad, lows, mixed, attended_grad = tie((mixing_grad, lows, mixed, attended_grad))
        arrived = sum_exchange(mixing_grad)
        mixing_grads.append(arrived)
    result = later_current + result + later_vectors[5] + later_vectors[7]
    result = result.reshape(stream.shape)
    others = norm_grad(hidden_low, expand_scaled, lows, mixing_scaled, False)
    travel = SeqScatter(others)
    (lows,) = travel.hold(lows)
    own = norm_grad(hidden_low, expand_scaled, lows, mixing_scaled, True)
    while len(far.parts) < outer:
        far.forward()
        far.cross()
    while far.steps < outer - 1:
        far.forward()
    shrink_grad = far.done()
    later_mixing = jnp.sum(later_mixing.astype(F32), 0)
    output_grad = jnp.sum(output_grad.astype(F32), 0)
    squares = sum_squares(shrink_grad, output_grad, later_first, later_mixing)
    shrink_grad, later_mixing, output_grad = (
        value.astype(BF) for value in (shrink_grad, later_mixing, output_grad)
    )
    others = (mixing_grads[-1], own, squares, shrink_grad, later_mixing, output_grad, home)
    others = tie(others)
    mixing_grads[-1], own, squares, shrink_grad, later_mixing, output_grad, home = others

    affine, parts_of_mixing = [], []
    for half in range(halves):
        count = (half == 0) + (half == halves - 1)
        summed, pieces = apart(mixing_grads[half], 3 * 128, count)
        parts_of_mixing.append(summed)
        affine += pieces
    affine_grad = jnp.stack(affine[::-1])
    squares = squares + sum_squares(*parts_of_mixing, affine_grad, far_grad)
    mixing_grad = jnp.concatenate(parts_of_mixing, -1).astype(BF)
    expand_grad, later_expand = home[:, :, 0], home[:, :, 1]
    squares, own = tie((squares, own))
    squares = lax.all_to_all(
        jnp.broadcast_to(squares, (devices, 128)),
        ("dp", "seq"),
        split_axis=0,
        concat_axis=0,
        tiled=True,
    )
    normed_grad = travel.done(own)[0]
    gradient = norm_back(gradient, normed_grad, own_normed, scale)
    gradient, squares = tie((gradient, squares))
    stream_grad = gradient.reshape(stream.shape)
    gradient_norm = jnp.sqrt(jnp.sum(squares[:, 0]))
    clip_scale = jnp.minimum(1.0, CLIP_LIMIT / (gradient_norm + 1e-06))
    output_grad = jnp.stack([output_grad, later_first[:, 2 * units :]])
    output_grad = output_grad.reshape(LAYERS, rows_d, D)
    shrink_grad = jnp.stack([shrink_grad, later_first[:, units : 2 * units]])
    shrink_grad = shrink_grad.reshape(LAYERS, rows_f, D)
    mixing_grad = jnp.stack([mixing_grad, later_mixing])
    expand_grad = jnp.stack([expand_grad, later_expand])
    exchanged = jnp.concatenate([mixing_grad, expand_grad], -1)
    if not aligned:
        mixing_view = exchanged[..., : 3 * width].reshape(LAYERS, parts, rows_d, halves, 3, 128)
        mixing_view = mixing_view.transpose(0, 2, 4, 1, 3, 5).reshape(LAYERS, rows_d, 3 * D)
        expand_view = exchanged[..., 3 * width :].reshape(LAYERS, parts, rows_d, copies, rows_f)
        expand_view = expand_view.transpose(0, 2, 3, 1, 4).reshape(LAYERS, rows_d, FF)
        exchanged = jnp.concatenate([mixing_view, expand_view], -1)[:, None]
        spans = ([(0, 0, 0, 3 * D)], [(0, 3 * D, 0, FF)])
    states = (
        (mixing_weight, mixing_first, mixing_second, mixing_average)
        + (output_weight, output_first, output_second, output_average)
        + (expand_weight, expand_first, expand_second, expand_average)
        + (shrink_weight, shrink_first, shrink_second, shrink_average)
    )
    rates = (D ** (-0.5), (D * 32 // LEN) ** (-0.5), D ** (-0.5), FF ** (-0.5))
    updated = update(
        clip_scale.reshape(1), exchanged, output_grad, shrink_grad, states, spans, rates
    )
    affine_new = adam(
        affine_grad * clip_scale,
        affine_weight,
        affine_first,
        affine_second,
        affine_average,
        SMALL_RATE,
        0.0,
    )
    return (result, stream_grad, gradient_norm) + tuple(updated) + tuple(affine_new)


def solution(mesh):
    tokens = P("dp", "seq", None)
    matrix = P(None, ("dp", "seq"), None)
    vector = P(None, ("dp", "seq"))
    states = (matrix,) * 16 + (vector,) * 4
    return jax.shard_map(
        local,
        mesh=mesh,
        in_specs=(tokens, tokens, P("dp", "seq")) + states,
        out_specs=(tokens, tokens, P()) + states,
        check_vma=False,
    )
```

```python
from functools import partial
import math

import jax
import jax.numpy as jnp
from jax import lax
from jax.experimental import pallas as pl
from jax.experimental.pallas import tpu as pltpu
from jax.sharding import PartitionSpec as P

D = 1024
H = 16
HD = 64
ROT = 16
FF = 4096
LEN = 2048
LAYERS = 2
STEP = 3

NORM_EPS = 1e-05
CLIP_LIMIT = 1.0
BETA_FIRST = 0.5
BETA_SECOND = 0.5
ADAM_EPS = 1e-08
WEIGHT_DECAY = 0.01
EMA_DECAY = 0.999
SMALL_RATE = 0.1
MASK_VALUE = -1e30
ROWS = 256
BLOCK = 512
QUERY_SCALE = 1.0 / math.sqrt(HD)
BF = jnp.bfloat16
F32 = jnp.float32
VMEM_LIMIT = 60 * 1024 * 1024
LIGHT = pl.CostEstimate(flops=1000, bytes_accessed=1000, transcendentals=0)


def dp_parts():
    size = lax.axis_size("dp")
    outer = 4 if size % 4 == 0 else size
    return outer, size // outer


def outer_ring(value):
    outer, inner = dp_parts()
    size = outer * inner
    return lax.ppermute(value, "dp", [(i, (i + inner) % size) for i in range(size)])


def inner_ring(value):
    outer, inner = dp_parts()
    moves = [
        (a * inner + b, a * inner + (b + 1) % inner) for a in range(outer) for b in range(inner)
    ]
    return lax.ppermute(value, "dp", moves)


def chip_ring(value):
    size = lax.axis_size("seq")
    return lax.ppermute(value, "seq", [(i, (i + 2) % size) for i in range(size)])


def core_swap(value):
    size = lax.axis_size("seq")
    return lax.ppermute(value, "seq", [(i, i ^ 1) for i in range(size)])


def assemble_kernel(slots_ref, *refs):
    n = pl.program_id(0)
    for step, piece_ref in enumerate(refs[:-1]):

        @pl.when(n == step)
        def _(piece_ref=piece_ref):
            refs[-1][...] = piece_ref[...][None]


def assemble(pieces, slots):
    count, piece = len(pieces), pieces[0]
    total = pl.pallas_call(
        assemble_kernel,
        grid_spec=pltpu.PrefetchScalarGridSpec(
            num_scalar_prefetch=1,
            grid=(count,),
            in_specs=[pl.BlockSpec(memory_space=pltpu.VMEM)] * count,
            out_specs=pl.BlockSpec((1,) + piece.shape, lambda n, slots: (slots[n], 0, 0)),
        ),
        out_shape=jax.ShapeDtypeStruct((count,) + piece.shape, piece.dtype),
        compiler_params=pltpu.CompilerParams(vmem_limit_bytes=VMEM_LIMIT),
        cost_estimate=LIGHT,
        name="assemble",
    )(jnp.stack(slots).astype(jnp.int32), *pieces)
    return total.reshape((count * piece.shape[0],) + piece.shape[1:])


class Gather:
    def __init__(self, value):
        self.pieces = [value]
        self.chains = []

    def forward(self):
        self.pieces.append(outer_ring(self.pieces[-1]))

    def cross(self):
        chain = [self.pieces[len(self.chains)]]
        for turn in range(1, dp_parts()[1]):
            chain.append(inner_ring(chain[-1]))
        self.chains.append(chain)

    def hold(self, *values):
        held = lax.optimization_barrier((values, self.pieces, self.chains))
        self.pieces, self.chains = held[1], held[2]
        return held[0]

    def done(self):
        outer, inner = dp_parts()
        me = lax.axis_index("dp")
        a, b = me // inner, me % inner
        pieces, slots = [], []
        for step, chain in enumerate(self.chains):
            for turn, piece in enumerate(chain):
                pieces.append(piece)
                slots.append((a - step) % outer * inner + (b - turn) % inner)
        return pieces, slots


class SeqGather:
    def __init__(self, value):
        self.pieces = [value]
        for step in range(1, lax.axis_size("seq") // 2):
            self.pieces.append(chip_ring(self.pieces[-1]))

    def hold(self, *values):
        held = lax.optimization_barrier((values, self.pieces))
        self.pieces = held[1]
        return held[0]

    def take(self, start, stop):
        chips = lax.axis_size("seq") // 2
        me = lax.axis_index("seq")
        y, c = me // 2, me % 2
        pieces, slots = [], []
        for step in range(start, stop):
            at = (y - step) % chips
            pieces += [self.pieces[step], core_swap(self.pieces[step])]
            slots += [2 * at + c, 2 * at + 1 - c]
        return pieces, slots

    def done(self):
        return assemble(*self.take(0, len(self.pieces)))


class SeqScatter:
    def __init__(self, others):
        self.chips = lax.axis_size("seq") // 2
        self.core = lax.axis_index("seq") % 2
        rows = others.shape[0] // (2 * (self.chips - 1))
        others = others.reshape((self.chips - 1, 2, rows) + others.shape[1:])
        self.values = [others[n] for n in range(self.chips - 1)]
        self.sending = self.cores(self.values[0]).astype(BF)

    def cores(self, value):
        kept = lax.dynamic_index_in_dim(value, self.core, 0, keepdims=False)
        passed = lax.dynamic_index_in_dim(value, 1 - self.core, 0, keepdims=False)
        return kept.astype(F32) + core_swap(passed).astype(F32)

    def hold(self, *values):
        held = lax.optimization_barrier((values, self.sending))
        self.sending = held[1]
        return held[0]

    def done(self, own, others=()):
        own = own.reshape((2, own.shape[0] // 2) + own.shape[1:])
        for value in self.values[1:] + [own]:
            arrived = chip_ring(self.sending)
            arrived, value, others = lax.optimization_barrier((arrived, value, others))
            total = self.cores(value) + arrived.astype(F32)
            self.sending = total.astype(BF)
        return total, others


def sum_exchange(value):
    copies, parts = lax.axis_size("dp"), lax.axis_size("seq")
    rows = value.shape[0] // (copies * parts)
    value = value.reshape((copies * parts, rows) + value.shape[1:])
    value = lax.all_to_all(value, ("dp", "seq"), split_axis=0, concat_axis=0, tiled=True)
    return value.reshape((copies, parts) + value.shape[1:])


def flipped(values, index):
    bit = 1
    while bit < len(values):
        chosen = (index & bit) > 0
        values = [
            jnp.where(chosen, values[n ^ bit], values[n]) for n in range(len(values))
        ]
        bit *= 2
    return values


class SeqSwap:
    def __init__(self, value):
        size = lax.axis_size("seq")
        chunks = flipped([value[n] for n in range(size)], lax.axis_index("seq"))
        self.value = [
            lax.ppermute(chunk, "seq", [(i, i ^ n) for i in range(size)]) if n else chunk
            for n, chunk in enumerate(chunks)
        ]

    def hold(self, *values):
        held = lax.optimization_barrier((values, self.value))
        self.value = held[1]
        return held[0]

    def done(self):
        return jnp.stack(flipped(self.value, lax.axis_index("seq")))


def seq_exchange(value):
    return lax.all_to_all(value, "seq", split_axis=0, concat_axis=0, tiled=True)


def head_masks(width, dtype):
    lane = lax.broadcasted_iota(jnp.int32, (1, width), 1) // HD
    return [(lane == h).astype(F32).astype(dtype) for h in range(width // HD)]


def swap_halves(values):
    width = values.shape[1]
    lane = lax.broadcasted_iota(jnp.int32, values.shape, 1) % HD
    return jnp.where(
        lane < ROT // 2,
        pltpu.roll(values, width - ROT // 2, 1),
        pltpu.roll(values, ROT // 2, 1),
    )


def as_column(row):
    return jnp.broadcast_to(row, (128, row.shape[1])).T[:, :1]


def as_row(column):
    return jnp.broadcast_to(column, (column.shape[0], 128)).T[:1, :]


def matmul(left, right):
    return lax.dot_general(left, right, (((1,), (0,)), ((), ())), preferred_element_type=F32)


def matmul_nt(left, right):
    return lax.dot_general(left, right, (((1,), (1,)), ((), ())), preferred_element_type=F32)


def matmul_tn(left, right):
    return lax.dot_general(left, right, (((0,), (0,)), ((), ())), preferred_element_type=F32)


def mix_kernel(count, pieces, x_slots_ref, slots_ref, *refs):
    refs = list(refs)
    inputs = refs[:count]
    del refs[:count]
    cos_ref, sin_ref = refs[:2]
    i = pl.program_id(0)
    if pieces:
        gain_ref, low_ref, bias_ref = refs[2:5]
        normed_ref, out_ref, raw_ref, scaled_ref, shift_ref = refs[-5:]
        columns = scaled_ref.shape[1]

        @pl.when(i == 0)
        def _():
            for n, piece_ref in enumerate(refs[5 : 5 + pieces]):
                size = piece_ref.shape[0]
                rows = pl.ds(pl.multiple_of(slots_ref[n] * size, size), size)
                raw_ref[rows, :] = piece_ref[...]
            raw = raw_ref[...]
            scaled_ref[...] = (raw.astype(F32) * as_column(gain_ref[...])).astype(BF)
            low = jnp.broadcast_to(low_ref[...], (8, D)).astype(BF)
            shift_ref[...] = matmul(low, raw) + bias_ref[...]

    else:
        scaled_ref, shift_ref = refs[2:4]
        normed_ref, out_ref = refs[-2:]
        columns = scaled_ref.shape[1]
    for n, x_ref in enumerate(inputs):

        @pl.when(i == n)
        def _(x_ref=x_ref):
            normed_ref[...] = x_ref[...]

    mixed = matmul(normed_ref[...], scaled_ref[...]) + shift_ref[0:1, :]
    cosine, sine = cos_ref[...], sin_ref[...]
    for start in range(0, columns, 3 * 128):
        query = mixed[:, start : start + 128]
        key = mixed[:, start + 128 : start + 256]
        query = (query * cosine + swap_halves(query) * sine) * QUERY_SCALE
        key = key * cosine + swap_halves(key) * sine
        out_ref[:, start : start + 128] = query.astype(BF)
        out_ref[:, start + 128 : start + 256] = key.astype(BF)
        out_ref[:, start + 256 : start + 384] = mixed[:, start + 256 : start + 384].astype(BF)


def mix(inputs, x_slots, cosine, sine, first=None, scaled=None, kept=()):
    count, size, length = len(inputs), inputs[0].shape[0], cosine.shape[0]
    columns = (first[2].shape[0] if scaled is None else scaled[0].shape[1])

    def whole(shape):
        return pl.BlockSpec(shape, lambda i, *_: (0, 0))

    def rows(width):
        return pl.BlockSpec((size, width), lambda i, *_: (_[0][i], 0))

    held = pl.BlockSpec(memory_space=pltpu.VMEM)
    values = [*inputs, cosine, sine]
    specs = [held] * count + [rows(128), rows(128)]
    out_specs = [rows(D), rows(columns)]
    out_shape = [
        jax.ShapeDtypeStruct((length, D), BF),
        jax.ShapeDtypeStruct((length, columns), BF),
    ]
    pieces, slots = (), [jnp.int32(0)]
    if first is not None:
        gain, low, bias, pieces, slots = first
        values += [gain[None], low[None], bias[None], *pieces]
        specs += [whole((1, D)), whole((1, D)), whole((1, columns))] + [held] * len(pieces)
        out_specs += [whole((D, columns)), whole((D, columns)), whole((8, columns))]
        out_shape += [
            jax.ShapeDtypeStruct((D, columns), BF),
            jax.ShapeDtypeStruct((D, columns), BF),
            jax.ShapeDtypeStruct((8, columns), F32),
        ]
    else:
        values += list(scaled)
        specs += [whole((D, columns)), whole((8, columns))]
    aliases = {2 + len(values) + n: n for n in range(len(kept))}
    values += list(kept)
    specs += [pl.BlockSpec(memory_space=pl.ANY)] * len(kept)
    return pl.pallas_call(
        partial(mix_kernel, count, len(pieces)),
        grid_spec=pltpu.PrefetchScalarGridSpec(
            num_scalar_prefetch=2, grid=(count,), in_specs=specs, out_specs=out_specs
        ),
        out_shape=out_shape,
        input_output_aliases=aliases,
        compiler_params=pltpu.CompilerParams(vmem_limit_bytes=VMEM_LIMIT),
        cost_estimate=LIGHT,
        name="mix",
    )(jnp.stack(x_slots).astype(jnp.int32), jnp.stack(slots).astype(jnp.int32), *values)


def attend_kernel(q_ref, k_ref, v_ref, o_ref, lse_ref, acc_ref, turned_ref):
    block, width = q_ref.shape
    heads = width // HD
    i = pl.program_id(0)
    query = q_ref[...]
    queries = [query * mask for mask in head_masks(width, BF)]

    @pl.when(i == 0)
    def _():
        turned_ref[...] = v_ref[...].T

    acc_ref[...] = jnp.zeros(acc_ref.shape, F32)

    def tile(j, diagonal, carry):
        rows = pl.ds(pl.multiple_of(j * block, block), block)
        key = k_ref[rows, :]
        scores = [matmul_nt(key, queries[h]) for h in range(heads)]
        if diagonal:
            row = lax.broadcasted_iota(jnp.int32, (block, block), 0)
            column = lax.broadcasted_iota(jnp.int32, (block, block), 1)
            allowed = row <= column
            scores = [jnp.where(allowed, score, MASK_VALUE) for score in scores]
        highs = [
            jnp.maximum(carry[h][0], jnp.max(scores[h], 0, keepdims=True)) for h in range(heads)
        ]
        weights = [jnp.exp(scores[h] - highs[h]) for h in range(heads)]
        fades = [jnp.exp(carry[h][0] - highs[h]) for h in range(heads)]
        sums = [
            carry[h][1] * fades[h] + jnp.sum(weights[h], 0, keepdims=True) for h in range(heads)
        ]
        for h in range(heads):
            part = slice(h * HD, (h + 1) * HD)
            product = matmul(turned_ref[part, rows], weights[h].astype(BF))
            acc_ref[part, :] = acc_ref[part, :] * fades[h] + product
        return [(highs[h], sums[h]) for h in range(heads)]

    empty = (jnp.full((1, block), MASK_VALUE, F32), jnp.zeros((1, block), F32))
    carry = lax.fori_loop(0, i, lambda j, carry: tile(j, False, carry), [empty] * heads)
    carry = tile(i, True, carry)
    for h in range(heads):
        part = slice(h * HD, (h + 1) * HD)
        acc_ref[part, :] = acc_ref[part, :] / carry[h][1]
        lse_ref[h : h + 1, :] = carry[h][0] + jnp.log(carry[h][1])
    o_ref[...] = acc_ref[...].T.astype(BF)


def attend(mixed, half):
    length, width = mixed.shape[0], 128
    heads = width // HD
    block = min(BLOCK, length)
    return pl.pallas_call(
        attend_kernel,
        grid=(length // block,),
        in_specs=[
            pl.BlockSpec((block, width), lambda i: (i, 3 * half)),
            pl.BlockSpec((length, width), lambda i: (0, 3 * half + 1)),
            pl.BlockSpec((length, width), lambda i: (0, 3 * half + 2)),
        ],
        out_specs=[
            pl.BlockSpec((block, width), lambda i: (i, 0)),
            pl.BlockSpec((heads, block), lambda i: (0, i)),
        ],
        out_shape=[
            jax.ShapeDtypeStruct((length, width), BF),
            jax.ShapeDtypeStruct((heads, length), F32),
        ],
        scratch_shapes=[
            pltpu.VMEM((width, block), F32),
            pltpu.VMEM((width, length), BF),
        ],
        compiler_params=pltpu.CompilerParams(vmem_limit_bytes=VMEM_LIMIT),
        cost_estimate=LIGHT,
        name="attend",
    )(mixed, mixed, mixed)


def attend_back_kernel(
    q_ref,
    k_ref,
    v_ref,
    do_ref,
    o_ref,
    lse_ref,
    cos_ref,
    sin_ref,
    out_ref,
    total_ref,
    inner_ref,
    dq_ref,
    dk_ref,
    dv_ref,
):
    block, width = k_ref.shape
    length = q_ref.shape[0]
    heads = width // HD
    steps = length // block
    j = pl.program_id(0)
    masks = head_masks(width, BF)
    key = k_ref[...]
    value = v_ref[...]
    keys = [key * mask for mask in masks]
    values = [value * mask for mask in masks]

    @pl.when(j == 0)
    def _():
        dq_ref[...] = jnp.zeros(dq_ref.shape, F32)
        total_ref[...] = jnp.zeros(total_ref.shape, F32)
        product = do_ref[...].astype(F32) * o_ref[...].astype(F32)
        coarse = product.astype(BF)
        fine = (product - coarse.astype(F32)).astype(BF)
        row = lax.broadcasted_iota(jnp.int32, (8, width), 0)
        lane = lax.broadcasted_iota(jnp.int32, (8, width), 1) // HD
        chosen = (row == lane).astype(F32).astype(BF)
        inner_ref[...] = matmul_nt(chosen, coarse) + matmul_nt(chosen, fine)

    dk_ref[...] = jnp.zeros(dk_ref.shape, F32)
    dv_ref[...] = jnp.zeros(dv_ref.shape, F32)

    def tile(start, count, at, number, diagonal):
        rows = pl.ds(pl.multiple_of(start, count), count)
        part = slice(at, at + number)
        query = q_ref[rows, :]
        grad = do_ref[rows, :]
        log_total = lse_ref[:, rows]
        inner = inner_ref[:, rows]
        scores = [matmul_nt(keys[h][part, :], query) for h in range(heads)]
        weight_grads = [matmul_nt(values[h][part, :], grad) for h in range(heads)]
        if diagonal:
            row = lax.broadcasted_iota(jnp.int32, scores[0].shape, 0)
            column = lax.broadcasted_iota(jnp.int32, scores[0].shape, 1)
            allowed = row <= column
            scores = [jnp.where(allowed, score, MASK_VALUE) for score in scores]
        weights = [jnp.exp(scores[h] - log_total[h : h + 1, :]) for h in range(heads)]
        low = [weight.astype(BF) for weight in weights]
        score_grads = [
            (weights[h] * (weight_grads[h] - inner[h : h + 1, :])).astype(BF)
            for h in range(heads)
        ]
        dv_ref[part, :] += matmul(
            jnp.concatenate(low, 1), jnp.concatenate([grad * mask for mask in masks], 0)
        )
        dk_ref[part, :] += matmul(
            jnp.concatenate(score_grads, 1),
            jnp.concatenate([query * mask for mask in masks], 0),
        )
        dq_ref[rows, :] += matmul_tn(
            jnp.concatenate(score_grads, 0),
            jnp.concatenate([keys[h][part, :] for h in range(heads)], 0),
        )

    def step(i, carry):
        tile(i * block, block, 0, block, False)
        return carry

    part_size = block // 2
    tile(j * block, block, 0, part_size, True)
    tile(j * block + part_size, part_size, part_size, part_size, True)
    lax.fori_loop(j + 1, steps, step, 0)

    own = pl.ds(pl.multiple_of(j * block, block), block)
    cosine = cos_ref[own, :]
    sine = sin_ref[own, :]
    key_grad = dk_ref[...]
    key_grad = key_grad * cosine - swap_halves(key_grad) * sine
    value_grad = dv_ref[...]
    query_grad = dq_ref[own, :] * QUERY_SCALE
    query_grad = query_grad * cosine - swap_halves(query_grad) * sine
    out_ref[:, :width] = query_grad.astype(BF)
    out_ref[:, width : 2 * width] = key_grad.astype(BF)
    out_ref[:, 2 * width :] = value_grad.astype(BF)
    total_ref[:, :width] += jnp.sum(query_grad, 0, keepdims=True)
    total_ref[:, width : 2 * width] += jnp.sum(key_grad, 0, keepdims=True)
    total_ref[:, 2 * width :] += jnp.sum(value_grad, 0, keepdims=True)


def attend_back(mixed, grads, attended, log_total, cosine, sine, half):
    length, width = mixed.shape[0], 128
    heads = width // HD
    block = min(BLOCK, length)
    return pl.pallas_call(
        attend_back_kernel,
        grid=(length // block,),
        in_specs=[
            pl.BlockSpec((length, width), lambda j: (0, 3 * half)),
            pl.BlockSpec((block, width), lambda j: (j, 3 * half + 1)),
            pl.BlockSpec((block, width), lambda j: (j, 3 * half + 2)),
            pl.BlockSpec((length, width), lambda j: (0, half)),
            pl.BlockSpec((length, width), lambda j: (0, 0)),
            pl.BlockSpec((heads, length), lambda j: (0, 0)),
            pl.BlockSpec((length, 128), lambda j: (0, 0)),
            pl.BlockSpec((length, 128), lambda j: (0, 0)),
        ],
        out_specs=[
            pl.BlockSpec((block, 3 * width), lambda j: (j, 0)),
            pl.BlockSpec((1, 3 * width), lambda j: (0, 0)),
        ],
        out_shape=[
            jax.ShapeDtypeStruct((length, 3 * width), BF),
            jax.ShapeDtypeStruct((1, 3 * width), F32),
        ],
        scratch_shapes=[
            pltpu.VMEM((8, length), F32),
            pltpu.VMEM((length, width), F32),
            pltpu.VMEM((block, width), F32),
            pltpu.VMEM((block, width), F32),
        ],
        compiler_params=pltpu.CompilerParams(vmem_limit_bytes=VMEM_LIMIT),
        cost_estimate=LIGHT,
        name="attend_back",
    )(mixed, mixed, mixed, grads, attended, log_total, cosine, sine)


def gelu_pair(values):
    size = jnp.abs(values) * (1.0 / math.sqrt(2.0))
    bell = jnp.exp(-size * size)
    turn = 1.0 / (1.0 + 0.3275911 * size)
    series = turn * (
        0.254829592
        + turn * (-0.284496736 + turn * (1.421413741 + turn * (-1.453152027 + turn * 1.061405429)))
    )
    tail = 0.5 * series * bell
    below = jnp.where(values < 0.0, tail, 1.0 - tail)
    slope = below + values * bell * (1.0 / math.sqrt(2.0 * math.pi))
    return values * below, slope


def chip_rows(own, length, size=ROWS):
    chips = lax.axis_size("seq") // 2
    y = lax.axis_index("seq") // 2
    per = length // size // chips
    if own is None:
        return length // size, lambda i, y_ref: i, y
    if own:
        return per, lambda i, y_ref: y_ref[0] * per + i, y
    return (
        (chips - 1) * per,
        lambda i, y_ref: (y_ref[0] + chips - 1 - i // per) % chips * per + i % per,
        y,
    )


def feed_kernel(first, last, halves, count, y_ref, slots_ref, x_ref, *refs):
    refs = list(refs)
    if first:
        gain_ref, low_ref, bias_ref = refs[:3]
        del refs[:3]
        if count:
            pieces = refs[:count]
            del refs[:count]
        else:
            raw_ref = refs.pop(0)
    else:
        scaled_ref, shift_ref = refs[:2]
        del refs[:2]
    if last:
        out_ref = refs.pop()
        if count:
            shrink_ref = refs.pop()
        else:
            shrink_ref = refs.pop(0)
        output_ref = refs.pop(0)
        attended = refs[:halves]
    if first:
        if count:
            raw_ref = refs.pop()
        act_ref, slope_ref, scaled_ref, shift_ref = refs[-4:]
        units = scaled_ref.shape[1]

        @pl.when(pl.program_id(0) == 0)
        def _():
            if count:
                for n, piece_ref in enumerate(pieces):
                    size = piece_ref.shape[0]
                    rows = pl.ds(pl.multiple_of(slots_ref[n] * size, size), size)
                    raw_ref[rows, :] = piece_ref[:, :units]
                    shrink_ref[rows, :] = piece_ref[:, units:]
            raw = raw_ref[...]
            scaled_ref[...] = (raw.astype(F32) * as_column(gain_ref[...])).astype(BF)
            low = jnp.broadcast_to(low_ref[...], (8, D)).astype(BF)
            shift_ref[...] = matmul(low, raw) + bias_ref[...]

    else:
        act_ref, slope_ref = refs[-2:]
    size = x_ref.shape[0] // 4
    spans = [slice(n * size, (n + 1) * size) for n in range(4)]
    hidden = [matmul(x_ref[span, :], scaled_ref[...]) + shift_ref[0:1, :] for span in spans]
    for n, span in enumerate(spans):
        activated, slope = gelu_pair(hidden[n])
        act_ref[span, :] = activated.astype(BF)
        slope_ref[span, :] = slope.astype(BF)
    if last:
        for span in spans:
            out = matmul(act_ref[span, :], shrink_ref[...])
            for half, o_ref in enumerate(attended):
                weight = output_ref[half * 128 : (half + 1) * 128, :]
                out = out + matmul(o_ref[span, :], weight)
            out_ref[span, :] = out.astype(BF)


def feed(rows_of, x, units, first=None, scaled=None, last=None, kept=(), slots=None):
    length = x.shape[0]
    steps, row, y = chip_rows(rows_of, length, BLOCK)

    def rows(columns):
        return pl.BlockSpec((BLOCK, columns), lambda i, *_: (row(i, _[0]), 0))

    def whole(shape, column=0):
        return pl.BlockSpec(shape, lambda i, *_: (0, column))

    specs, values, halves, count = [rows(D)], [x], 0, 0
    out_specs = [rows(units), rows(units)]
    out_shape = [jax.ShapeDtypeStruct((length, units), BF)] * 2
    if first is not None:
        gain, low, bias, weight = first
        values += [gain[None], low[None], bias[None]]
        specs += [whole((1, D)), whole((1, D)), whole((1, units))]
        out_specs += [whole((D, units)), whole((8, units))]
        out_shape += [
            jax.ShapeDtypeStruct((D, units), BF),
            jax.ShapeDtypeStruct((8, units), F32),
        ]
        if slots is not None:
            count = len(weight)
            values += weight
            specs += [pl.BlockSpec(memory_space=pltpu.VMEM)] * count
            out_specs += [whole((D, units))]
            out_shape += [jax.ShapeDtypeStruct((D, units), BF)]
        else:
            values.append(weight[0])
            specs.append(whole((D, units), weight[1]))
    else:
        values += list(scaled)
        specs += [whole((D, units)), whole((8, units))]
    if last is not None:
        shrink, output, attended = last
        halves = len(attended)
        if count:
            out_specs.append(whole((units, D)))
            out_shape.append(jax.ShapeDtypeStruct((units, D), BF))
        else:
            values.append(shrink[0])
            specs.append(whole((units, D), shrink[1]))
        values += [output, *attended]
        specs += [whole(output.shape)] + [rows(128)] * halves
        out_specs.append(pl.BlockSpec((BLOCK, D), lambda i, *_: (i, 0)))
        out_shape.append(jax.ShapeDtypeStruct((steps * BLOCK, D), BF))
    aliases = {2 + len(values) + n: n for n in range(len(kept))}
    values += list(kept)
    specs += [pl.BlockSpec(memory_space=pl.ANY)] * len(kept)
    slots = jnp.zeros((1,), jnp.int32) if slots is None else jnp.stack(slots).astype(jnp.int32)
    return pl.pallas_call(
        partial(feed_kernel, first is not None, last is not None, halves, count),
        grid_spec=pltpu.PrefetchScalarGridSpec(
            num_scalar_prefetch=2, grid=(steps,), in_specs=specs, out_specs=out_specs
        ),
        out_shape=out_shape,
        input_output_aliases=aliases,
        compiler_params=pltpu.CompilerParams(vmem_limit_bytes=VMEM_LIMIT),
        cost_estimate=LIGHT,
        name="feed",
    )(y.reshape(1), slots, *values)


def branch_kernel(y_ref, act_ref, shrink_ref, output_ref, *refs):
    out = matmul(act_ref[...], shrink_ref[...])
    for half, o_ref in enumerate(refs[:-1]):
        out = out + matmul(o_ref[...], output_ref[half * 128 : (half + 1) * 128, :])
    refs[-1][...] = out.astype(BF)


def branch(rows_of, activated, shrink, output, attended):
    length, units = activated.shape
    steps, row, y = chip_rows(rows_of, length)

    def rows(columns):
        return pl.BlockSpec((ROWS, columns), lambda i, y_ref: (row(i, y_ref), 0))

    return pl.pallas_call(
        branch_kernel,
        grid_spec=pltpu.PrefetchScalarGridSpec(
            num_scalar_prefetch=1,
            grid=(steps,),
            in_specs=[
                rows(units),
                pl.BlockSpec((units, D), lambda i, y_ref: (0, shrink[1])),
                pl.BlockSpec(output.shape, lambda i, y_ref: (0, 0)),
            ]
            + [rows(128)] * len(attended),
            out_specs=pl.BlockSpec((ROWS, D), lambda i, y_ref: (i, 0)),
        ),
        out_shape=jax.ShapeDtypeStruct((steps * ROWS, D), BF),
        compiler_params=pltpu.CompilerParams(vmem_limit_bytes=VMEM_LIMIT),
        cost_estimate=LIGHT,
        name="branch",
    )(y.reshape(1), activated, shrink[0], output, *attended)


def norm_grad_kernel(y_ref, h_ref, wi_ref, wm_ref, *refs):
    out = matmul_nt(h_ref[...], wi_ref[...])
    for half, m_ref in enumerate(refs[:-1]):
        out = out + matmul_nt(m_ref[...], wm_ref[:, half * 384 : (half + 1) * 384])
    refs[-1][...] = out.astype(BF)


def norm_grad(hidden, expand, mixed, mixing, own):
    length, units, columns = hidden.shape[0], expand.shape[1], mixing.shape[1]
    steps, row, y = chip_rows(own, length)

    def rows(count):
        return pl.BlockSpec((ROWS, count), lambda i, y_ref: (row(i, y_ref), 0))

    def whole(shape):
        return pl.BlockSpec(shape, lambda i, y_ref: (0, 0))

    return pl.pallas_call(
        norm_grad_kernel,
        grid_spec=pltpu.PrefetchScalarGridSpec(
            num_scalar_prefetch=1,
            grid=(steps,),
            in_specs=[rows(units), whole((D, units)), whole((D, columns))]
            + [rows(384)] * len(mixed),
            out_specs=pl.BlockSpec((ROWS, D), lambda i, y_ref: (i, 0)),
        ),
        out_shape=jax.ShapeDtypeStruct((steps * ROWS, D), BF),
        compiler_params=pltpu.CompilerParams(vmem_limit_bytes=VMEM_LIMIT),
        cost_estimate=LIGHT,
        name="norm_grad",
    )(y.reshape(1), hidden, expand, mixing, *mixed)


def product_kernel(g_ref, *refs):
    for half, x_ref in enumerate(refs[:-1]):
        product = matmul_tn(x_ref[...], g_ref[...])
        refs[-1][half * 128 : (half + 1) * 128, :] = product.astype(BF)


def product(inputs, grads):
    rows = 128 * len(inputs)
    block = D // 2
    return pl.pallas_call(
        product_kernel,
        grid=(D // block,),
        in_specs=[pl.BlockSpec((grads.shape[0], block), lambda i: (0, i))]
        + [pl.BlockSpec(x.shape, lambda i: (0, 0)) for x in inputs],
        out_specs=pl.BlockSpec((rows, block), lambda i: (0, i)),
        out_shape=jax.ShapeDtypeStruct((rows, D), BF),
        compiler_params=pltpu.CompilerParams(vmem_limit_bytes=VMEM_LIMIT),
        cost_estimate=LIGHT,
        name="product",
    )(grads, *inputs)


def weight_grad_kernel(count, x_ref, weight_ref, gain_ref, shift_ref, total_ref, *refs):
    lows, (out_ref, gain_out_ref, shift_out_ref) = refs[:count], refs[-3:]
    gain, shift = as_column(gain_ref[...]), as_column(shift_ref[...])
    x = x_ref[...]
    start, gain_sum, shift_sum = 0, 0.0, 0.0
    for low_ref in lows:
        columns = slice(start, start + low_ref.shape[1])
        start += low_ref.shape[1]
        raw = matmul_tn(x, low_ref[...])
        weight = weight_ref[:, columns].astype(F32)
        total = total_ref[:, columns]
        out_ref[:, columns] = (raw * gain + shift * total).astype(BF)
        gain_sum = gain_sum + jnp.sum(raw * weight, 1, keepdims=True)
        shift_sum = shift_sum + jnp.sum(weight * total, 1, keepdims=True)
    gain_out_ref[...] = as_row(gain_sum)
    shift_out_ref[...] = as_row(shift_sum)


def weight_grad(x, lows, weight, gain, shift, total, wide=None):
    length, columns = x.shape[0], total.shape[1]
    array, column = weight
    wide = wide or (0, columns)
    row = pl.BlockSpec((1, ROWS), lambda i: (0, i))
    return pl.pallas_call(
        partial(weight_grad_kernel, len(lows)),
        grid=(D // ROWS,),
        in_specs=[
            pl.BlockSpec((length, ROWS), lambda i: (0, i)),
            pl.BlockSpec((ROWS, columns), lambda i: (i, column)),
            row,
            row,
            pl.BlockSpec((1, columns), lambda i: (0, 0)),
        ]
        + [pl.BlockSpec(low.shape, lambda i: (0, 0)) for low in lows],
        out_specs=[pl.BlockSpec((ROWS, columns), lambda i: (i, wide[0])), row, row],
        out_shape=[
            jax.ShapeDtypeStruct((D, wide[1]), BF),
            jax.ShapeDtypeStruct((1, D), F32),
            jax.ShapeDtypeStruct((1, D), F32),
        ],
        compiler_params=pltpu.CompilerParams(vmem_limit_bytes=VMEM_LIMIT),
        cost_estimate=LIGHT,
        name="weight_grad",
    )(x, array, gain[None], shift[None], total, *lows)


def pack_kernel(spans, split, mixing_ref, expand_ref, *refs):
    outs = refs[-2:] if split else (refs[-1], refs[-1])
    shift = split or 0
    for source_ref, part, out_ref, back in (
        (mixing_ref, spans[0], outs[0], 0),
        (expand_ref, spans[1], outs[1], shift),
    ):
        for p, start, at, count in part:
            columns = slice(start - back, start - back + count)
            out_ref[p, :, columns] = source_ref[0, :, at : at + count].astype(BF)
    for pair_ref in refs[: -2 if split else -1]:
        end = outs[1].shape[2] - pair_ref.shape[1]
        for p in range(outs[1].shape[0]):
            outs[1][p, :, end:] = pair_ref[...]


def pack(mixing, expand, layer, spans, columns, pair=(), split=0):
    parts, rows = lax.axis_size("seq"), mixing.shape[1]
    columns = columns + sum(value.shape[1] for value in pair)
    widths = [split, columns - split] if split else [columns]
    made = pl.pallas_call(
        partial(pack_kernel, spans, split),
        grid=(1,),
        in_specs=[
            pl.BlockSpec((1,) + mixing.shape[1:], lambda i: (layer, 0, 0)),
            pl.BlockSpec((1,) + expand.shape[1:], lambda i: (layer, 0, 0)),
        ]
        + [pl.BlockSpec(value.shape, lambda i: (0, 0)) for value in pair],
        out_specs=[pl.BlockSpec((parts, rows, w), lambda i: (0, 0, 0)) for w in widths],
        out_shape=[jax.ShapeDtypeStruct((parts, rows, w), BF) for w in widths],
        compiler_params=pltpu.CompilerParams(vmem_limit_bytes=VMEM_LIMIT),
        cost_estimate=LIGHT,
        name="pack",
    )(mixing, expand, *pair)
    return made if split else made[0]


def feed_back_kernel(joined, kept, *refs):
    grad_ref, shrink_ref, slope_ref, act_ref, x_ref, output_ref = refs[:6]
    weight_ref, gain_ref, shift_ref = refs[6:9]
    low_ref, total_ref, do_ref, gain_out_ref, shift_out_ref = refs[kept : kept + 5]
    outs = refs[kept + 5 : -2]
    expand_ref, shrink_acc_ref = refs[-2:]
    i = pl.program_id(0)

    @pl.when(i == 0)
    def _():
        total_ref[...] = jnp.zeros(total_ref.shape, F32)
        expand_ref[...] = jnp.zeros(expand_ref.shape, F32)
        shrink_acc_ref[...] = jnp.zeros(shrink_acc_ref.shape, F32)

    grads = grad_ref[...]
    hidden = matmul_nt(grads, shrink_ref[...]) * slope_ref[...].astype(F32)
    low = hidden.astype(BF)
    low_ref[...] = low
    total_ref[...] += jnp.sum(hidden, 0, keepdims=True)
    shrink_acc_ref[...] += matmul_tn(act_ref[...], grads)
    do_ref[...] = matmul_nt(grads, output_ref[...]).astype(BF)
    expand_ref[...] += matmul_tn(x_ref[...], low)

    @pl.when(i == pl.num_programs(0) - 1)
    def _():
        gain, shift, total = as_column(gain_ref[...]), as_column(shift_ref[...]), total_ref[...]
        units = total.shape[1]
        raw = expand_ref[...]
        weight = weight_ref[...].astype(F32)
        outs[0][:, :units] = (raw * gain + shift * total).astype(BF)
        if joined:
            outs[0][:, units:] = shrink_acc_ref[...].astype(BF)
        else:
            outs[1][...] = shrink_acc_ref[...].astype(BF)
        gain_out_ref[...] = as_row(jnp.sum(raw * weight, 1, keepdims=True))
        shift_out_ref[...] = as_row(jnp.sum(weight * total, 1, keepdims=True))


def feed_back(grads, shrink, slope, activated, x, output, weight, gain, shift, kept=()):
    length, units = slope.shape
    width, joined = output.shape[0], units == D

    def rows(count):
        return pl.BlockSpec((BLOCK, count), lambda i: (i, 0))

    def whole(shape, column=0):
        return pl.BlockSpec(shape, lambda i: (0, column))

    out_specs = [rows(units), whole((1, units)), rows(width), whole((1, D)), whole((1, D))]
    out_shape = [
        jax.ShapeDtypeStruct((length, units), BF),
        jax.ShapeDtypeStruct((1, units), F32),
        jax.ShapeDtypeStruct((length, width), BF),
        jax.ShapeDtypeStruct((1, D), F32),
        jax.ShapeDtypeStruct((1, D), F32),
    ]
    if joined:
        out_specs.append(whole((D, 2 * units)))
        wide = kept[0].shape[1] if kept else 2 * units + width
        out_shape.append(jax.ShapeDtypeStruct((D, wide), BF))
    else:
        out_specs += [whole((D, units)), whole((units, D))]
        out_shape += [
            jax.ShapeDtypeStruct((D, units), BF),
            jax.ShapeDtypeStruct((units, D), BF),
        ]
    return pl.pallas_call(
        partial(feed_back_kernel, joined, 9 + len(kept)),
        grid=(length // BLOCK,),
        in_specs=[
            rows(D),
            whole((units, D), shrink[1]),
            rows(units),
            rows(units),
            rows(D),
            whole((width, D)),
            whole((D, units), weight[1]),
            whole((1, D)),
            whole((1, D)),
        ]
        + [pl.BlockSpec(memory_space=pl.ANY)] * len(kept),
        out_specs=out_specs,
        out_shape=out_shape,
        input_output_aliases={9: 5} if kept else {},
        scratch_shapes=[
            pltpu.VMEM((D, units), F32),
            pltpu.VMEM((units, D), F32),
        ],
        compiler_params=pltpu.CompilerParams(vmem_limit_bytes=VMEM_LIMIT),
        cost_estimate=LIGHT,
        name="feed_back",
    )(
        grads,
        shrink[0],
        slope,
        activated,
        x,
        output,
        weight[0],
        gain[None],
        shift[None],
        *kept,
    )


def home_spans(parts, copies, width, units):
    mixing, expand = [], []
    size = units // copies
    for p in range(parts):
        for half in range(width // 128):
            for kind in range(3):
                at = kind * parts * width + p * width + half * 128
                mixing.append((p, half * 384 + kind * 128, at, 128))
        for d in range(copies):
            expand.append((p, 3 * width + d * size, (d * parts + p) * size, size))
    return mixing, expand


def adam(grad, weight, first, second, average, rate, decay):
    first_new = BETA_FIRST * first + (1.0 - BETA_FIRST) * grad
    second_new = BETA_SECOND * second + (1.0 - BETA_SECOND) * grad * grad
    first_hat = first_new / (1.0 - BETA_FIRST**STEP)
    second_hat = second_new / (1.0 - BETA_SECOND**STEP)
    weight_new = weight - rate * (
        first_hat / (jnp.sqrt(second_hat) + ADAM_EPS) + decay * weight
    )
    return weight_new, first_new, second_new, EMA_DECAY * average + (1.0 - EMA_DECAY) * weight_new


def adam_kernel(spans, rates, clip_ref, mixing_ref, expand_ref, output_ref, shrink_ref, *refs):
    clip = clip_ref[0]
    states, news = refs[:16], refs[16:]

    def step(kind, grad, columns):
        old = [ref[0, :, columns] for ref in states[4 * kind : 4 * kind + 4]]
        new = adam(grad.astype(F32) * clip, *old, rates[kind], WEIGHT_DECAY)
        for ref, value in zip(news[4 * kind : 4 * kind + 4], new):
            ref[0, :, columns] = value

    for kind, part, grad_ref in ((0, spans[0], mixing_ref), (2, spans[1], expand_ref)):
        back = part[0][1]
        for source, start, at, count in part:
            grad = grad_ref[0, source, :, start - back : start - back + count]
            step(kind, grad, slice(at, at + count))
    step(1, output_ref[0], slice(None))
    step(3, shrink_ref[0], slice(None))


def update(clip, mixing, expand, output, shrink, states, spans, rates):
    layers, parts, rows = mixing.shape[:3]
    chunk = 16 if rows % 16 == 0 else rows
    chunks = rows // chunk

    def block(array):
        size = array.shape[1] // chunks
        return pl.BlockSpec((1, size, array.shape[2]), lambda l, n: (l, n, 0))

    return pl.pallas_call(
        partial(adam_kernel, spans, rates),
        grid=(layers, chunks),
        in_specs=[
            pl.BlockSpec(memory_space=pltpu.SMEM),
            pl.BlockSpec((1, parts, chunk, mixing.shape[3]), lambda l, n: (l, 0, n, 0)),
            pl.BlockSpec((1, parts, chunk, expand.shape[3]), lambda l, n: (l, 0, n, 0)),
            block(output),
            block(shrink),
        ]
        + [block(state) for state in states],
        out_specs=[block(state) for state in states],
        out_shape=[jax.ShapeDtypeStruct(state.shape, F32) for state in states],
        compiler_params=pltpu.CompilerParams(vmem_limit_bytes=VMEM_LIMIT),
        cost_estimate=LIGHT,
        name="update",
    )(clip, mixing, expand, output, shrink, *states)


def rotary_tables(positions):
    half = ROT // 2
    steps_half = jnp.arange(half).astype(F32)
    frequency = 10000.0 ** (-2.0 * steps_half / ROT)
    angles = positions.astype(F32)[None, :] * frequency[:, None]
    cosine = jnp.concatenate([jnp.cos(angles), jnp.ones_like(angles)], 0)
    entry = jnp.arange(128)[None, :] % HD
    index = jnp.arange(half)[:, None]
    turning = (entry < ROT) & (entry % half == index)
    still = (entry >= ROT) & (index == 0)
    sign = jnp.where(entry < half, -1.0, 1.0)
    spread_cosine = jnp.concatenate([turning, still], 0).astype(F32)
    spread_sine = turning.astype(F32) * sign

    def lay(table, spread):
        return lax.dot_general(
            table, spread, (((0,), (0,)), ((), ())), precision=lax.Precision.HIGHEST
        )

    return lay(cosine, spread_cosine), lay(jnp.sin(angles), spread_sine)


def split_affine(affine):
    bounds = [D, D, D, D, 3 * D, D, FF, D]
    pieces = []
    offset = 0
    for length in bounds:
        pieces.append(affine[offset : offset + length])
        offset = offset + length
    return pieces


def normalize(values):
    centre = values - jnp.mean(values, -1, keepdims=True)
    spread = jnp.mean(centre * centre, -1, keepdims=True)
    scale = lax.rsqrt(spread + NORM_EPS)
    return centre * scale, scale


def local(
    stream,
    cotangent,
    positions,
    mixing_weight,
    mixing_first,
    mixing_second,
    mixing_average,
    output_weight,
    output_first,
    output_second,
    output_average,
    expand_weight,
    expand_first,
    expand_second,
    expand_average,
    shrink_weight,
    shrink_first,
    shrink_second,
    shrink_average,
    affine_weight,
    affine_first,
    affine_second,
    affine_average,
):
    parts = lax.axis_size("seq")
    copies = lax.axis_size("dp")
    devices = parts * copies
    part = lax.axis_index("seq")
    width = D // parts
    units = FF // parts
    rows_d = D // devices
    rows_f = FF // devices
    rows = stream.shape[0] * stream.shape[1]
    small = affine_weight.shape[1]

    halves = width // 128
    outer = dp_parts()[0]

    def mixing_part(vector):
        view = vector.reshape(3, parts, halves, 128)
        view = lax.dynamic_index_in_dim(view, part, 1, keepdims=False)
        return view.transpose(1, 0, 2).reshape(-1)

    def expand_part(vector):
        view = vector.reshape(copies, parts, -1)
        return lax.dynamic_index_in_dim(view, part, 1, keepdims=False).reshape(-1)

    def spread_mixing(vector):
        view = jnp.zeros((3, parts, width), F32)
        vector = vector.reshape(halves, 3, 128).transpose(1, 0, 2).reshape(3, 1, width)
        return lax.dynamic_update_slice(view, vector, (0, part, 0)).reshape(-1)

    def spread_expand(vector):
        view = jnp.zeros((copies, parts, rows_f), F32)
        return lax.dynamic_update_slice(view, vector.reshape(copies, 1, rows_f), (0, part, 0)).reshape(-1)

    spans = home_spans(parts, copies, width, units)
    aligned = rows_f % 128 == 0 and rows_d % 16 == 0

    def arrange(layer, mixing, expand, pair=(), split=False):
        if aligned:
            return pack(
                mixing, expand, layer, spans, 3 * width + units, pair, 3 * width * split
            )
        mixing = mixing[layer].astype(BF).reshape(rows_d, 3, parts, halves, 128)
        mixing = mixing.transpose(2, 0, 3, 1, 4).reshape(parts, rows_d, 3 * width)
        expand = expand[layer].astype(BF).reshape(rows_d, copies, parts, rows_f)
        expand = expand.transpose(2, 0, 1, 3).reshape(parts, rows_d, units)
        pair = [jnp.broadcast_to(value, (parts,) + value.shape) for value in pair]
        if split:
            return mixing, jnp.concatenate([expand] + pair, -1)
        return jnp.concatenate([mixing, expand] + pair, -1)

    def settle_output(exchanged):
        output = exchanged.reshape(parts, copies // parts, rows_d, D)
        return output.transpose(1, 0, 2, 3).reshape(width, D)

    def norm_back(gradient, normed_grad, own_normed, scale):
        projected = jnp.mean(normed_grad * own_normed, -1, keepdims=True)
        middle = jnp.mean(normed_grad, -1, keepdims=True)
        return gradient + scale * (normed_grad - middle - own_normed * projected)

    def beside(grads, *pieces):
        pieces = [jnp.concatenate(piece).reshape(devices, small) for piece in pieces]
        pieces = jnp.concatenate(pieces, -1)
        coarse = pieces.astype(BF)
        fine = (pieces - coarse.astype(F32)).astype(BF)
        pieces = jnp.concatenate([coarse, fine], -1)
        extra = 128 * pl.cdiv(pieces.shape[1], 128 * rows_d)
        pieces = jnp.pad(pieces, ((0, 0), (0, extra * rows_d - pieces.shape[1])))
        return jnp.concatenate([grads, pieces.reshape(D, extra)], -1)

    def apart(summed, columns, count):
        pieces = summed[..., columns:].reshape(devices, -1).astype(F32)
        size = count * small
        pieces = jnp.sum(pieces[:, :size] + pieces[:, size : 2 * size], 0).reshape(count, small)
        return jnp.sum(summed[..., :columns].astype(F32), 0), list(pieces)

    def sum_squares(*values):
        return sum(jnp.sum(value.astype(F32) * value.astype(F32)) for value in values)

    tie = lax.optimization_barrier
    chips = parts // 2
    current = stream.reshape(rows, D)
    gradient = cotangent.reshape(rows, D)

    def view(array, column):
        if units == D:
            return array, column
        return array[:, column * units : (column + 1) * units].reshape(-1, D), 0

    pair = jnp.stack([positions.reshape(-1) // 16, positions.reshape(-1) % 16]).astype(BF)
    pair = pair.reshape(rows_d, 2 * rows // rows_d)
    both = arrange(0, mixing_weight, expand_weight, (pair,))
    both, current = tie((both, current))
    both = seq_exchange(both)
    own_normed, scale = normalize(current)
    travel = SeqGather(own_normed.astype(BF))
    pair = both[..., 3 * width + units :].astype(F32).reshape(parts, 2, rows)
    places = (pair[:, 0] * 16.0 + pair[:, 1]).reshape(-1)
    both = both.reshape(parts * rows_d, -1)
    near = Gather(both[:, : 3 * width])
    places, affine_low, layer_mixing, layer_expand, first_output, later_output = near.hold(
        places,
        affine_weight,
        mixing_weight,
        expand_weight,
        output_weight[0],
        output_weight[1],
    )
    near.forward()
    outputs = jnp.concatenate(
        [value.astype(BF).reshape(-1, width) for value in (first_output, later_output)], -1
    )
    outputs = lax.all_gather(outputs, "dp", axis=0, tiled=True)
    cosine, sine = rotary_tables(places)
    later_both = arrange(1, layer_mixing, layer_expand)
    affine_low, cosine, sine, later_both, expand_own, shrink_own, low_gradient = near.hold(
        affine_low,
        cosine,
        sine,
        later_both,
        both[:, 3 * width : 3 * width + units],
        shrink_weight[0],
        gradient.astype(BF),
    )
    near.forward()
    near.cross()
    affine_low = affine_low.astype(BF).reshape(1, LAYERS * small)
    affine_all = lax.all_to_all(
        jnp.broadcast_to(affine_low, (devices, LAYERS * small)),
        ("dp", "seq"),
        split_axis=0,
        concat_axis=0,
        tiled=True,
    )
    far_own = jnp.concatenate([expand_own, shrink_own.astype(BF).reshape(-1, units)], -1)
    affine_all, far_own, near.pieces, near.chains, travel.pieces = tie(
        (affine_all, far_own, near.pieces, near.chains, travel.pieces)
    )
    inputs, x_slots = travel.take(0, chips)
    near.forward()
    near.cross()
    affine_all = affine_all.reshape(devices, LAYERS, small).transpose(1, 0, 2)
    affine_all = affine_all.reshape(LAYERS, devices * small).astype(F32)
    vectors = [split_affine(affine_all[layer]) for layer in range(LAYERS)]
    vectors, inputs = near.hold(vectors, inputs)
    for step in range(3, outer - 1):
        near.forward()
        near.cross()
    while len(near.chains) < outer:
        near.cross()
    far = Gather(far_own)
    far.pieces[0], near.pieces, near.chains = tie((far.pieces[0], near.pieces, near.chains))
    far.forward()
    far.cross()
    pieces, slots = near.done()

    gain_one, shift_one, gain_two, shift_two = vectors[0][:4]
    normed, mixed, mixing, mixing_scaled, _ = mix(
        inputs,
        x_slots,
        cosine,
        sine,
        first=(gain_one, shift_one, mixing_part(vectors[0][4]), pieces, slots),
    )
    mixed, later_both, later_shrink, outputs, low_gradient = far.hold(
        mixed, later_both, shrink_weight[1], outputs, low_gradient
    )
    far.forward()
    far.cross()
    travel = SeqGather(low_gradient)
    later_both = seq_exchange(later_both)
    outputs = jnp.stack(
        [outputs[:, layer * width : (layer + 1) * width].reshape(parts, -1, D) for layer in (0, 1)],
        1,
    )
    attended, logs = [], []
    for half in range(halves):
        out, log_total = attend(mixed, half)
        attended.append(out)
        logs.append(log_total)
        if half == 0:
            mixed, out, later_both, outputs = far.hold(mixed, out, later_both, outputs)
            far.forward()
            far.cross()
            outputs = seq_exchange(outputs)
            later_both = later_both.reshape(parts * rows_d, -1)
            later_far = jnp.concatenate(
                [later_both[:, 3 * width :], later_shrink.astype(BF).reshape(-1, units)], -1
            )
            later_near = later_both[:, : 3 * width]
    attended, logs, later_far, later_near, outputs, travel.pieces = far.hold(
        attended, logs, later_far, later_near, outputs, travel.pieces
    )
    output, later_output = (settle_output(outputs[:, layer]) for layer in (0, 1))
    later_all = lax.all_gather(later_far, "dp", axis=0, tiled=True)
    while len(far.pieces) < outer:
        far.forward()
    while len(far.chains) < outer:
        far.cross()
    attended, logs, later_near, grads = far.hold(attended, logs, later_near, travel.done())
    near = Gather(later_near)
    near.forward()
    near.cross()
    pieces, slots = far.done()
    first = (gain_two, shift_two, expand_part(vectors[0][6]))
    if units == D:
        activated, slope, expand_scaled, expand_shift, expand, shrink, others = feed(
            False,
            normed,
            units,
            first=first + (pieces,),
            last=(None, output, attended),
            slots=slots,
        )
    else:
        far_all = assemble(pieces, slots)
        expand, shrink = far_all[:, :units], view(far_all, 1)[0]
        activated, slope, expand_scaled, expand_shift, others = feed(
            False,
            normed,
            units,
            first=first + ((expand, 0),),
            last=((shrink, 0), output, attended),
        )
    shrink = (shrink, 0)
    (others,) = near.hold(others)
    near.forward()
    near.cross()
    travel = SeqScatter(others)
    activated, slope = travel.hold(activated, slope)
    activated, slope, own = feed(
        True,
        normed,
        units,
        scaled=(expand_scaled, expand_shift),
        last=(shrink, output, attended),
        kept=(activated, slope),
    )
    (own,) = near.hold(own)
    for step in range(2, outer - 1):
        near.forward()
        near.cross()
    stored = [(own_normed, scale, normed, mixed, attended, logs, activated, slope)]
    weights = [(mixing, mixing_scaled, output, expand, expand_scaled, shrink)]
    total, (near.pieces, near.chains) = travel.done(own, (near.pieces, near.chains))
    while len(near.chains) < outer:
        near.cross()
    current = current + total + vectors[0][5] + vectors[0][7]

    own_normed, scale = normalize(current)
    travel = SeqGather(own_normed.astype(BF))
    pieces, slots = near.done()
    gain_one, shift_one, gain_two, shift_two = vectors[1][:4]
    inputs, x_slots = travel.take(0, 1)
    normed, mixed, mixing, mixing_scaled, mixing_shift = mix(
        inputs,
        x_slots,
        cosine,
        sine,
        first=(gain_one, shift_one, mixing_part(vectors[1][4]), pieces, slots),
    )
    normed, mixed = travel.hold(normed, mixed)
    inputs, x_slots = travel.take(1, chips)
    normed, mixed = mix(
        inputs,
        x_slots,
        cosine,
        sine,
        scaled=(mixing_scaled, mixing_shift),
        kept=(normed, mixed),
    )
    output = later_output
    attended, logs = [], []
    for half in range(halves):
        out, log_total = attend(mixed, half)
        attended.append(out)
        logs.append(log_total)
    attended, logs, later_all = tie((attended, logs, later_all))
    expand, shrink = later_all, view(later_all, 1)
    activated, slope, expand_scaled, expand_shift = feed(
        None,
        normed,
        units,
        first=(gain_two, shift_two, expand_part(vectors[1][6]), (later_all, 0)),
    )

    grads, attended, logs, activated = tie((grads, attended, logs, activated))

    def feed_grads(gain, shift, kept=()):
        output_grad, low_grads = tie((product(attended, grads), grads))
        output_grad = output_grad.reshape(copies // parts, parts, rows_d, D).transpose(1, 0, 2, 3)
        swap = SeqSwap(output_grad.reshape(parts, copies // parts * rows_d, D))
        made = feed_back(
            low_grads,
            shrink,
            slope,
            activated,
            normed,
            output,
            (expand, 0),
            gain,
            shift,
            kept if units == D else (),
        )
        made = swap.hold(*made)
        low, total, attended_grad, gain_grad, shift_grad = made[:5]
        output_grad = swap.done().reshape(-1, width)
        if units == D:
            joined = lax.dynamic_update_slice(made[5], output_grad, (0, 2 * units))
        else:
            joined = [made[5], made[6].reshape(-1, units), output_grad, *kept]
            joined = jnp.concatenate(joined, -1)
        return low, total, attended_grad, gain_grad, shift_grad, joined

    made = feed_grads(gain_two, shift_two)
    hidden_low, hidden_total, attended_grad, gain_two_grad, shift_two_grad, later_grad = made
    later_grad, attended_grad = tie((later_grad, attended_grad))
    later_first = lax.psum_scatter(later_grad, "dp", scatter_dimension=0, tiled=True)
    lows, totals = [], []
    for half in range(halves):
        low, total = attend_back(
            mixed, attended_grad, attended[half], logs[half], cosine, sine, half
        )
        lows.append(low)
        totals.append(total)
    mixed_total = jnp.concatenate(totals, -1)
    others = norm_grad(hidden_low, expand_scaled, lows, mixing_scaled, False)
    travel = SeqScatter(others)
    hidden_low, lows, activated = travel.hold(hidden_low, lows, activated)
    own = norm_grad(hidden_low, expand_scaled, lows, mixing_scaled, True)
    last = (shrink, output, attended)
    result_others = branch(False, activated, *last)
    result_own = branch(True, activated, *last)
    normed_grad, (result_others, result_own) = travel.done(own, (result_others, result_own))
    normed_grad, lows = tie((normed_grad, lows))
    gradient = norm_back(gradient, normed_grad, own_normed, scale)
    travel = SeqGather(gradient.astype(BF))
    lows, own_piece = tie((lows, travel.pieces[0]))
    wide = (3, 2 * units + 4 * width) if units == D else None
    later_mixing, gain_one_grad, shift_one_grad = weight_grad(
        normed, lows, (mixing, 0), gain_one, shift_one, mixed_total, wide
    )
    (later_mixing,) = travel.hold(later_mixing)
    grads = travel.done()
    output_sum = jnp.sum(cotangent.reshape(rows, D), 0)

    def small_grads(*pieces):
        gains, mixed_total, output_sum, hidden_total = pieces
        pieces = [piece[0] for piece in gains]
        pieces += [spread_mixing(mixed_total[0]), output_sum]
        return pieces + [spread_expand(hidden_total[0]), output_sum]

    gains = (gain_one_grad, shift_one_grad, gain_two_grad, shift_two_grad)
    later_pieces = small_grads(gains, mixed_total, output_sum, hidden_total)

    later_current, later_vectors = current, vectors[1]
    current = stream.reshape(rows, D)
    own_normed, scale, normed, mixed, attended, logs, activated, slope = stored[0]
    mixing, mixing_scaled, output, expand, expand_scaled, shrink = weights[0]
    gain_one, shift_one, gain_two, shift_two = vectors[0][:4]
    made = feed_grads(gain_two, shift_two, (later_mixing,))
    hidden_low, hidden_total, attended_grad, gain_two_grad, shift_two_grad, far_grad = made
    far_grad, attended_grad, result_others, later_pieces = tie(
        (far_grad, attended_grad, result_others, later_pieces)
    )
    far_grad = lax.psum_scatter(far_grad, "dp", scatter_dimension=0, tiled=True)
    travel = SeqScatter(result_others)
    lows, totals, mixing_grads, gain_grads, shift_grads = [], [], [], [], []
    for half in range(halves):
        low, total = attend_back(
            mixed, attended_grad, attended[half], logs[half], cosine, sine, half
        )
        if half == 0:
            mixed, low, later_first = tie((mixed, low, later_first))
            later_home = SeqSwap(later_first[:, :units].reshape(parts, rows_d, units))
        else:
            mixed, low = later_home.hold(mixed, low)
        mixing_grad, gain_one_grad, shift_one_grad = weight_grad(
            normed,
            [low],
            (mixing, half),
            gain_one,
            shift_one,
            total,
        )
        lows.append(low)
        totals.append(total)
        gain_grads.append(gain_one_grad)
        shift_grads.append(shift_one_grad)
        pieces = [later_pieces] if half == 0 else []
        if half == halves - 1:
            output_sum = jnp.sum(gradient, 0)
            gains = (sum(gain_grads), sum(shift_grads), gain_two_grad, shift_two_grad)
            pieces.append(
                small_grads(gains, jnp.concatenate(totals, -1), output_sum, hidden_total)
            )
        mixing_grad = beside(mixing_grad, *pieces) if pieces else mixing_grad
        if half == 0:
            result, (mixing_grad,) = travel.done(result_own, (mixing_grad,))
        mixing_grad, lows, mixed, attended_grad, mixing_grads = tie(
            (mixing_grad, lows, mixed, attended_grad, mixing_grads)
        )
        mixing_grads.append(sum_exchange(mixing_grad))
    result = later_current + result + later_vectors[5] + later_vectors[7]
    result = result.reshape(stream.shape)
    others = norm_grad(hidden_low, expand_scaled, lows, mixing_scaled, False)
    travel = SeqScatter(others)
    (lows,) = travel.hold(lows)
    own = norm_grad(hidden_low, expand_scaled, lows, mixing_scaled, True)
    normed_grad = travel.done(own)[0]
    gradient = norm_back(gradient, normed_grad, own_normed, scale)
    squares = sum_squares(later_first)
    mixing_grads[-1], gradient, result, squares = tie(
        (mixing_grads[-1], gradient, result, squares)
    )
    affine, parts_of_mixing = [], []
    for half in range(halves):
        count = (half == 0) + (half == halves - 1)
        summed, pieces = apart(mixing_grads[half], 3 * 128, count)
        parts_of_mixing.append(summed)
        affine += pieces
    affine_grad = jnp.stack(affine[::-1])
    squares = squares + sum_squares(*parts_of_mixing, affine_grad)
    mixing_grad = jnp.concatenate(parts_of_mixing, -1).astype(BF)
    far_grad, squares, mixing_grad = tie((far_grad, squares, mixing_grad))
    stream_grad = gradient.reshape(stream.shape)

    squares = squares + sum_squares(far_grad)
    squares = lax.all_to_all(
        jnp.broadcast_to(squares, (devices, 128)),
        ("dp", "seq"),
        split_axis=0,
        concat_axis=0,
        tiled=True,
    )
    home = jnp.concatenate([far_grad[:, :units], far_grad[:, 2 * units + width :]], -1)
    home = SeqSwap(home.reshape(parts, rows_d, units + 3 * width))
    output_grad = jnp.stack(
        [far_grad[:, 2 * units : 2 * units + width], later_first[:, 2 * units :]]
    ).reshape(LAYERS, rows_d, D)
    shrink_grad = jnp.stack(
        [far_grad[:, units : 2 * units], later_first[:, units : 2 * units]]
    ).reshape(LAYERS, rows_f, D)
    squares, output_grad, shrink_grad = home.hold(squares, output_grad, shrink_grad)
    home = home.done()
    expand_grad = jnp.stack([home[..., :units], later_home.done()])
    later_mixing = home[..., units:]
    gradient_norm = jnp.sqrt(jnp.sum(squares[:, 0]))
    clip_scale = jnp.minimum(1.0, CLIP_LIMIT / (gradient_norm + 1e-06))
    mixing_grad = jnp.stack([mixing_grad, later_mixing])
    if not aligned:
        mixing_grad = mixing_grad.reshape(LAYERS, parts, rows_d, halves, 3, 128)
        mixing_grad = mixing_grad.transpose(0, 2, 4, 1, 3, 5).reshape(LAYERS, 1, rows_d, 3 * D)
        expand_grad = expand_grad.reshape(LAYERS, parts, rows_d, copies, rows_f)
        expand_grad = expand_grad.transpose(0, 2, 3, 1, 4).reshape(LAYERS, 1, rows_d, FF)
        spans = ([(0, 0, 0, 3 * D)], [(0, 0, 0, FF)])
    states = (
        (mixing_weight, mixing_first, mixing_second, mixing_average)
        + (output_weight, output_first, output_second, output_average)
        + (expand_weight, expand_first, expand_second, expand_average)
        + (shrink_weight, shrink_first, shrink_second, shrink_average)
    )
    rates = (D ** (-0.5), (D * 32 // LEN) ** (-0.5), D ** (-0.5), FF ** (-0.5))
    updated = update(
        clip_scale.reshape(1), mixing_grad, expand_grad, output_grad, shrink_grad, states, spans, rates
    )
    affine_new = adam(
        affine_grad * clip_scale,
        affine_weight,
        affine_first,
        affine_second,
        affine_average,
        SMALL_RATE,
        0.0,
    )
    return (result, stream_grad, gradient_norm) + tuple(updated) + tuple(affine_new)


def solution(mesh):
    tokens = P("dp", "seq", None)
    matrix = P(None, ("dp", "seq"), None)
    vector = P(None, ("dp", "seq"))
    states = (matrix,) * 16 + (vector,) * 4
    return jax.shard_map(
        local,
        mesh=mesh,
        in_specs=(tokens, tokens, P("dp", "seq")) + states,
        out_specs=(tokens, tokens, P()) + states,
        check_vma=False,
    )
```

```python
from functools import partial
import math

import jax
import jax.numpy as jnp
from jax import lax
from jax.experimental import pallas as pl
from jax.experimental.pallas import tpu as pltpu
from jax.sharding import PartitionSpec as P

D = 1024
H = 16
HD = 64
ROT = 16
FF = 4096
LEN = 2048
LAYERS = 2
STEP = 3

NORM_EPS = 1e-05
CLIP_LIMIT = 1.0
BETA_FIRST = 0.5
BETA_SECOND = 0.5
ADAM_EPS = 1e-08
WEIGHT_DECAY = 0.01
EMA_DECAY = 0.999
SMALL_RATE = 0.1
MASK_VALUE = -1e30
ROWS = 256
BLOCK = 512
QUERY_SCALE = 1.0 / math.sqrt(HD)
BF = jnp.bfloat16
F32 = jnp.float32
VMEM_LIMIT = 60 * 1024 * 1024
LIGHT = pl.CostEstimate(flops=1000, bytes_accessed=1000, transcendentals=0)


def dp_parts():
    size = lax.axis_size("dp")
    outer = 4 if size % 4 == 0 else size
    return outer, size // outer


def outer_ring(value):
    outer, inner = dp_parts()
    size = outer * inner
    return lax.ppermute(value, "dp", [(i, (i + inner) % size) for i in range(size)])


def inner_ring(value):
    outer, inner = dp_parts()
    moves = [
        (a * inner + b, a * inner + (b + 1) % inner) for a in range(outer) for b in range(inner)
    ]
    return lax.ppermute(value, "dp", moves)


def chip_ring(value):
    size = lax.axis_size("seq")
    return lax.ppermute(value, "seq", [(i, (i + 2) % size) for i in range(size)])


def core_swap(value):
    size = lax.axis_size("seq")
    return lax.ppermute(value, "seq", [(i, i ^ 1) for i in range(size)])


def assemble_kernel(slots_ref, *refs):
    n = pl.program_id(0)
    for step, piece_ref in enumerate(refs[:-1]):

        @pl.when(n == step)
        def _(piece_ref=piece_ref):
            refs[-1][...] = piece_ref[...][None]


def assemble(pieces, slots):
    count, piece = len(pieces), pieces[0]
    total = pl.pallas_call(
        assemble_kernel,
        grid_spec=pltpu.PrefetchScalarGridSpec(
            num_scalar_prefetch=1,
            grid=(count,),
            in_specs=[pl.BlockSpec(memory_space=pltpu.VMEM)] * count,
            out_specs=pl.BlockSpec((1,) + piece.shape, lambda n, slots: (slots[n], 0, 0)),
        ),
        out_shape=jax.ShapeDtypeStruct((count,) + piece.shape, piece.dtype),
        compiler_params=pltpu.CompilerParams(vmem_limit_bytes=VMEM_LIMIT),
        cost_estimate=LIGHT,
        name="assemble",
    )(jnp.stack(slots).astype(jnp.int32), *pieces)
    return total.reshape((count * piece.shape[0],) + piece.shape[1:])


class Gather:
    def __init__(self, value):
        self.pieces = [value]
        self.chains = []

    def forward(self):
        self.pieces.append(outer_ring(self.pieces[-1]))

    def cross(self):
        chain = [self.pieces[len(self.chains)]]
        for turn in range(1, dp_parts()[1]):
            chain.append(inner_ring(chain[-1]))
        self.chains.append(chain)

    def hold(self, *values):
        held = lax.optimization_barrier((values, self.pieces, self.chains))
        self.pieces, self.chains = held[1], held[2]
        return held[0]

    def done(self):
        outer, inner = dp_parts()
        me = lax.axis_index("dp")
        a, b = me // inner, me % inner
        pieces, slots = [], []
        for step, chain in enumerate(self.chains):
            for turn, piece in enumerate(chain):
                pieces.append(piece)
                slots.append((a - step) % outer * inner + (b - turn) % inner)
        return pieces, slots


class SeqGather:
    def __init__(self, value):
        self.pieces = [value]
        for step in range(1, lax.axis_size("seq") // 2):
            self.pieces.append(chip_ring(self.pieces[-1]))

    def hold(self, *values):
        held = lax.optimization_barrier((values, self.pieces))
        self.pieces = held[1]
        return held[0]

    def take(self, start, stop):
        chips = lax.axis_size("seq") // 2
        me = lax.axis_index("seq")
        y, c = me // 2, me % 2
        pieces, slots = [], []
        for step in range(start, stop):
            at = (y - step) % chips
            pieces += [self.pieces[step], core_swap(self.pieces[step])]
            slots += [2 * at + c, 2 * at + 1 - c]
        return pieces, slots

    def done(self):
        return assemble(*self.take(0, len(self.pieces)))


class SeqScatter:
    def __init__(self, others):
        self.chips = lax.axis_size("seq") // 2
        self.core = lax.axis_index("seq") % 2
        rows = others.shape[0] // (2 * (self.chips - 1))
        others = others.reshape((self.chips - 1, 2, rows) + others.shape[1:])
        self.values = [others[n] for n in range(self.chips - 1)]
        self.sending = self.cores(self.values[0]).astype(BF)

    def cores(self, value):
        kept = lax.dynamic_index_in_dim(value, self.core, 0, keepdims=False)
        passed = lax.dynamic_index_in_dim(value, 1 - self.core, 0, keepdims=False)
        return kept.astype(F32) + core_swap(passed).astype(F32)

    def hold(self, *values):
        held = lax.optimization_barrier((values, self.sending))
        self.sending = held[1]
        return held[0]

    def done(self, own, others=()):
        own = own.reshape((2, own.shape[0] // 2) + own.shape[1:])
        for value in self.values[1:] + [own]:
            arrived = chip_ring(self.sending)
            arrived, value, others = lax.optimization_barrier((arrived, value, others))
            total = self.cores(value) + arrived.astype(F32)
            self.sending = total.astype(BF)
        return total, others


def sum_exchange(value):
    copies, parts = lax.axis_size("dp"), lax.axis_size("seq")
    rows = value.shape[0] // (copies * parts)
    value = value.reshape((copies * parts, rows) + value.shape[1:])
    value = lax.all_to_all(value, ("dp", "seq"), split_axis=0, concat_axis=0, tiled=True)
    return value.reshape((copies, parts) + value.shape[1:])


def flipped(values, index):
    bit = 1
    while bit < len(values):
        chosen = (index & bit) > 0
        values = [
            jnp.where(chosen, values[n ^ bit], values[n]) for n in range(len(values))
        ]
        bit *= 2
    return values


class SeqSwap:
    def __init__(self, value):
        size = lax.axis_size("seq")
        chunks = flipped([value[n] for n in range(size)], lax.axis_index("seq"))
        self.value = [
            lax.ppermute(chunk, "seq", [(i, i ^ n) for i in range(size)]) if n else chunk
            for n, chunk in enumerate(chunks)
        ]

    def hold(self, *values):
        held = lax.optimization_barrier((values, self.value))
        self.value = held[1]
        return held[0]

    def done(self):
        return jnp.stack(flipped(self.value, lax.axis_index("seq")))


def seq_exchange(value):
    return lax.all_to_all(value, "seq", split_axis=0, concat_axis=0, tiled=True)


def head_masks(width, dtype):
    lane = lax.broadcasted_iota(jnp.int32, (1, width), 1) // HD
    return [(lane == h).astype(F32).astype(dtype) for h in range(width // HD)]


def swap_halves(values):
    width = values.shape[1]
    lane = lax.broadcasted_iota(jnp.int32, values.shape, 1) % HD
    return jnp.where(
        lane < ROT // 2,
        pltpu.roll(values, width - ROT // 2, 1),
        pltpu.roll(values, ROT // 2, 1),
    )


def as_column(row):
    return jnp.broadcast_to(row, (128, row.shape[1])).T[:, :1]


def as_row(column):
    return jnp.broadcast_to(column, (column.shape[0], 128)).T[:1, :]


def matmul(left, right):
    return lax.dot_general(left, right, (((1,), (0,)), ((), ())), preferred_element_type=F32)


def matmul_nt(left, right):
    return lax.dot_general(left, right, (((1,), (1,)), ((), ())), preferred_element_type=F32)


def matmul_tn(left, right):
    return lax.dot_general(left, right, (((0,), (0,)), ((), ())), preferred_element_type=F32)


def mix_kernel(count, pieces, x_slots_ref, slots_ref, *refs):
    refs = list(refs)
    inputs = refs[:count]
    del refs[:count]
    cos_ref, sin_ref = refs[:2]
    i = pl.program_id(0)
    if pieces:
        gain_ref, low_ref, bias_ref = refs[2:5]
        normed_ref, out_ref, raw_ref, scaled_ref, shift_ref = refs[-5:]
        columns = scaled_ref.shape[1]

        @pl.when(i == 0)
        def _():
            for n, piece_ref in enumerate(refs[5 : 5 + pieces]):
                size = piece_ref.shape[0]
                rows = pl.ds(pl.multiple_of(slots_ref[n] * size, size), size)
                raw_ref[rows, :] = piece_ref[...]
            raw = raw_ref[...]
            scaled_ref[...] = (raw.astype(F32) * as_column(gain_ref[...])).astype(BF)
            low = jnp.broadcast_to(low_ref[...], (8, D)).astype(BF)
            shift_ref[...] = matmul(low, raw) + bias_ref[...]

    else:
        scaled_ref, shift_ref = refs[2:4]
        normed_ref, out_ref = refs[-2:]
        columns = scaled_ref.shape[1]
    for n, x_ref in enumerate(inputs):

        @pl.when(i == n)
        def _(x_ref=x_ref):
            normed_ref[...] = x_ref[...]

    mixed = matmul(normed_ref[...], scaled_ref[...]) + shift_ref[0:1, :]
    cosine, sine = cos_ref[...], sin_ref[...]
    for start in range(0, columns, 3 * 128):
        query = mixed[:, start : start + 128]
        key = mixed[:, start + 128 : start + 256]
        query = (query * cosine + swap_halves(query) * sine) * QUERY_SCALE
        key = key * cosine + swap_halves(key) * sine
        out_ref[:, start : start + 128] = query.astype(BF)
        out_ref[:, start + 128 : start + 256] = key.astype(BF)
        out_ref[:, start + 256 : start + 384] = mixed[:, start + 256 : start + 384].astype(BF)


def mix(inputs, x_slots, cosine, sine, first=None, scaled=None, kept=()):
    count, size, length = len(inputs), inputs[0].shape[0], cosine.shape[0]
    columns = (first[2].shape[0] if scaled is None else scaled[0].shape[1])

    def whole(shape):
        return pl.BlockSpec(shape, lambda i, *_: (0, 0))

    def rows(width):
        return pl.BlockSpec((size, width), lambda i, *_: (_[0][i], 0))

    held = pl.BlockSpec(memory_space=pltpu.VMEM)
    values = [*inputs, cosine, sine]
    specs = [held] * count + [rows(128), rows(128)]
    out_specs = [rows(D), rows(columns)]
    out_shape = [
        jax.ShapeDtypeStruct((length, D), BF),
        jax.ShapeDtypeStruct((length, columns), BF),
    ]
    pieces, slots = (), [jnp.int32(0)]
    if first is not None:
        gain, low, bias, pieces, slots = first
        values += [gain[None], low[None], bias[None], *pieces]
        specs += [whole((1, D)), whole((1, D)), whole((1, columns))] + [held] * len(pieces)
        out_specs += [whole((D, columns)), whole((D, columns)), whole((8, columns))]
        out_shape += [
            jax.ShapeDtypeStruct((D, columns), BF),
            jax.ShapeDtypeStruct((D, columns), BF),
            jax.ShapeDtypeStruct((8, columns), F32),
        ]
    else:
        values += list(scaled)
        specs += [whole((D, columns)), whole((8, columns))]
    aliases = {2 + len(values) + n: n for n in range(len(kept))}
    values += list(kept)
    specs += [pl.BlockSpec(memory_space=pl.ANY)] * len(kept)
    return pl.pallas_call(
        partial(mix_kernel, count, len(pieces)),
        grid_spec=pltpu.PrefetchScalarGridSpec(
            num_scalar_prefetch=2, grid=(count,), in_specs=specs, out_specs=out_specs
        ),
        out_shape=out_shape,
        input_output_aliases=aliases,
        compiler_params=pltpu.CompilerParams(vmem_limit_bytes=VMEM_LIMIT),
        cost_estimate=LIGHT,
        name="mix",
    )(jnp.stack(x_slots).astype(jnp.int32), jnp.stack(slots).astype(jnp.int32), *values)


def attend_kernel(q_ref, k_ref, v_ref, o_ref, lse_ref, acc_ref, turned_ref):
    block, width = q_ref.shape
    heads = width // HD
    i = pl.program_id(0)
    query = q_ref[...]
    queries = [query * mask for mask in head_masks(width, BF)]

    @pl.when(i == 0)
    def _():
        turned_ref[...] = v_ref[...].T

    acc_ref[...] = jnp.zeros(acc_ref.shape, F32)

    def tile(j, diagonal, carry):
        rows = pl.ds(pl.multiple_of(j * block, block), block)
        key = k_ref[rows, :]
        scores = [matmul_nt(key, queries[h]) for h in range(heads)]
        if diagonal:
            row = lax.broadcasted_iota(jnp.int32, (block, block), 0)
            column = lax.broadcasted_iota(jnp.int32, (block, block), 1)
            allowed = row <= column
            scores = [jnp.where(allowed, score, MASK_VALUE) for score in scores]
        highs = [
            jnp.maximum(carry[h][0], jnp.max(scores[h], 0, keepdims=True)) for h in range(heads)
        ]
        weights = [jnp.exp(scores[h] - highs[h]) for h in range(heads)]
        fades = [jnp.exp(carry[h][0] - highs[h]) for h in range(heads)]
        sums = [
            carry[h][1] * fades[h] + jnp.sum(weights[h], 0, keepdims=True) for h in range(heads)
        ]
        for h in range(heads):
            part = slice(h * HD, (h + 1) * HD)
            product = matmul(turned_ref[part, rows], weights[h].astype(BF))
            acc_ref[part, :] = acc_ref[part, :] * fades[h] + product
        return [(highs[h], sums[h]) for h in range(heads)]

    empty = (jnp.full((1, block), MASK_VALUE, F32), jnp.zeros((1, block), F32))
    carry = lax.fori_loop(0, i, lambda j, carry: tile(j, False, carry), [empty] * heads)
    carry = tile(i, True, carry)
    for h in range(heads):
        part = slice(h * HD, (h + 1) * HD)
        acc_ref[part, :] = acc_ref[part, :] / carry[h][1]
        lse_ref[h : h + 1, :] = carry[h][0] + jnp.log(carry[h][1])
    o_ref[...] = acc_ref[...].T.astype(BF)


def attend(mixed, half):
    length, width = mixed.shape[0], 128
    heads = width // HD
    block = min(BLOCK, length)
    return pl.pallas_call(
        attend_kernel,
        grid=(length // block,),
        in_specs=[
            pl.BlockSpec((block, width), lambda i: (i, 3 * half)),
            pl.BlockSpec((length, width), lambda i: (0, 3 * half + 1)),
            pl.BlockSpec((length, width), lambda i: (0, 3 * half + 2)),
        ],
        out_specs=[
            pl.BlockSpec((block, width), lambda i: (i, 0)),
            pl.BlockSpec((heads, block), lambda i: (0, i)),
        ],
        out_shape=[
            jax.ShapeDtypeStruct((length, width), BF),
            jax.ShapeDtypeStruct((heads, length), F32),
        ],
        scratch_shapes=[
            pltpu.VMEM((width, block), F32),
            pltpu.VMEM((width, length), BF),
        ],
        compiler_params=pltpu.CompilerParams(vmem_limit_bytes=VMEM_LIMIT),
        cost_estimate=LIGHT,
        name="attend",
    )(mixed, mixed, mixed)


def attend_back_kernel(
    q_ref,
    k_ref,
    v_ref,
    do_ref,
    o_ref,
    lse_ref,
    cos_ref,
    sin_ref,
    out_ref,
    total_ref,
    inner_ref,
    dq_ref,
    dk_ref,
    dv_ref,
):
    block, width = k_ref.shape
    length = q_ref.shape[0]
    heads = width // HD
    steps = length // block
    j = pl.program_id(0)
    masks = head_masks(width, BF)
    key = k_ref[...]
    value = v_ref[...]
    keys = [key * mask for mask in masks]
    values = [value * mask for mask in masks]

    @pl.when(j == 0)
    def _():
        dq_ref[...] = jnp.zeros(dq_ref.shape, F32)
        total_ref[...] = jnp.zeros(total_ref.shape, F32)
        product = do_ref[...].astype(F32) * o_ref[...].astype(F32)
        coarse = product.astype(BF)
        fine = (product - coarse.astype(F32)).astype(BF)
        row = lax.broadcasted_iota(jnp.int32, (8, width), 0)
        lane = lax.broadcasted_iota(jnp.int32, (8, width), 1) // HD
        chosen = (row == lane).astype(F32).astype(BF)
        inner_ref[...] = matmul_nt(chosen, coarse) + matmul_nt(chosen, fine)

    dk_ref[...] = jnp.zeros(dk_ref.shape, F32)
    dv_ref[...] = jnp.zeros(dv_ref.shape, F32)

    def tile(start, count, at, number, diagonal):
        rows = pl.ds(pl.multiple_of(start, count), count)
        part = slice(at, at + number)
        query = q_ref[rows, :]
        grad = do_ref[rows, :]
        log_total = lse_ref[:, rows]
        inner = inner_ref[:, rows]
        scores = [matmul_nt(keys[h][part, :], query) for h in range(heads)]
        weight_grads = [matmul_nt(values[h][part, :], grad) for h in range(heads)]
        if diagonal:
            row = lax.broadcasted_iota(jnp.int32, scores[0].shape, 0)
            column = lax.broadcasted_iota(jnp.int32, scores[0].shape, 1)
            allowed = row <= column
            scores = [jnp.where(allowed, score, MASK_VALUE) for score in scores]
        weights = [jnp.exp(scores[h] - log_total[h : h + 1, :]) for h in range(heads)]
        low = [weight.astype(BF) for weight in weights]
        score_grads = [
            (weights[h] * (weight_grads[h] - inner[h : h + 1, :])).astype(BF)
            for h in range(heads)
        ]
        dv_ref[part, :] += matmul(
            jnp.concatenate(low, 1), jnp.concatenate([grad * mask for mask in masks], 0)
        )
        dk_ref[part, :] += matmul(
            jnp.concatenate(score_grads, 1),
            jnp.concatenate([query * mask for mask in masks], 0),
        )
        dq_ref[rows, :] += matmul_tn(
            jnp.concatenate(score_grads, 0),
            jnp.concatenate([keys[h][part, :] for h in range(heads)], 0),
        )

    def step(i, carry):
        tile(i * block, block, 0, block, False)
        return carry

    part_size = block // 2
    tile(j * block, block, 0, part_size, True)
    tile(j * block + part_size, part_size, part_size, part_size, True)
    lax.fori_loop(j + 1, steps, step, 0)

    own = pl.ds(pl.multiple_of(j * block, block), block)
    cosine = cos_ref[own, :]
    sine = sin_ref[own, :]
    key_grad = dk_ref[...]
    key_grad = key_grad * cosine - swap_halves(key_grad) * sine
    value_grad = dv_ref[...]
    query_grad = dq_ref[own, :] * QUERY_SCALE
    query_grad = query_grad * cosine - swap_halves(query_grad) * sine
    out_ref[:, :width] = query_grad.astype(BF)
    out_ref[:, width : 2 * width] = key_grad.astype(BF)
    out_ref[:, 2 * width :] = value_grad.astype(BF)
    total_ref[:, :width] += jnp.sum(query_grad, 0, keepdims=True)
    total_ref[:, width : 2 * width] += jnp.sum(key_grad, 0, keepdims=True)
    total_ref[:, 2 * width :] += jnp.sum(value_grad, 0, keepdims=True)


def attend_back(mixed, grads, attended, log_total, cosine, sine, half):
    length, width = mixed.shape[0], 128
    heads = width // HD
    block = min(BLOCK, length)
    return pl.pallas_call(
        attend_back_kernel,
        grid=(length // block,),
        in_specs=[
            pl.BlockSpec((length, width), lambda j: (0, 3 * half)),
            pl.BlockSpec((block, width), lambda j: (j, 3 * half + 1)),
            pl.BlockSpec((block, width), lambda j: (j, 3 * half + 2)),
            pl.BlockSpec((length, width), lambda j: (0, half)),
            pl.BlockSpec((length, width), lambda j: (0, 0)),
            pl.BlockSpec((heads, length), lambda j: (0, 0)),
            pl.BlockSpec((length, 128), lambda j: (0, 0)),
            pl.BlockSpec((length, 128), lambda j: (0, 0)),
        ],
        out_specs=[
            pl.BlockSpec((block, 3 * width), lambda j: (j, 0)),
            pl.BlockSpec((1, 3 * width), lambda j: (0, 0)),
        ],
        out_shape=[
            jax.ShapeDtypeStruct((length, 3 * width), BF),
            jax.ShapeDtypeStruct((1, 3 * width), F32),
        ],
        scratch_shapes=[
            pltpu.VMEM((8, length), F32),
            pltpu.VMEM((length, width), F32),
            pltpu.VMEM((block, width), F32),
            pltpu.VMEM((block, width), F32),
        ],
        compiler_params=pltpu.CompilerParams(vmem_limit_bytes=VMEM_LIMIT),
        cost_estimate=LIGHT,
        name="attend_back",
    )(mixed, mixed, mixed, grads, attended, log_total, cosine, sine)


def gelu_pair(values):
    size = jnp.abs(values) * (1.0 / math.sqrt(2.0))
    bell = jnp.exp(-size * size)
    turn = 1.0 / (1.0 + 0.3275911 * size)
    series = turn * (
        0.254829592
        + turn * (-0.284496736 + turn * (1.421413741 + turn * (-1.453152027 + turn * 1.061405429)))
    )
    tail = 0.5 * series * bell
    below = jnp.where(values < 0.0, tail, 1.0 - tail)
    slope = below + values * bell * (1.0 / math.sqrt(2.0 * math.pi))
    return values * below, slope


def chip_rows(own, length, size=ROWS):
    chips = lax.axis_size("seq") // 2
    y = lax.axis_index("seq") // 2
    per = length // size // chips
    if own is None:
        return length // size, lambda i, y_ref: i, y
    if own:
        return per, lambda i, y_ref: y_ref[0] * per + i, y
    return (
        (chips - 1) * per,
        lambda i, y_ref: (y_ref[0] + chips - 1 - i // per) % chips * per + i % per,
        y,
    )


def feed_kernel(first, last, halves, count, y_ref, slots_ref, x_ref, *refs):
    refs = list(refs)
    if first:
        gain_ref, low_ref, bias_ref = refs[:3]
        del refs[:3]
        if count:
            pieces = refs[:count]
            del refs[:count]
        else:
            raw_ref = refs.pop(0)
    else:
        scaled_ref, shift_ref = refs[:2]
        del refs[:2]
    if last:
        out_ref = refs.pop()
        if count:
            shrink_ref = refs.pop()
        else:
            shrink_ref = refs.pop(0)
        output_ref = refs.pop(0)
        attended = refs[:halves]
    if first:
        if count:
            raw_ref = refs.pop()
        act_ref, slope_ref, scaled_ref, shift_ref = refs[-4:]
        units = scaled_ref.shape[1]

        @pl.when(pl.program_id(0) == 0)
        def _():
            if count:
                for n, piece_ref in enumerate(pieces):
                    size = piece_ref.shape[0]
                    rows = pl.ds(pl.multiple_of(slots_ref[n] * size, size), size)
                    raw_ref[rows, :] = piece_ref[:, :units]
                    shrink_ref[rows, :] = piece_ref[:, units:]
            raw = raw_ref[...]
            scaled_ref[...] = (raw.astype(F32) * as_column(gain_ref[...])).astype(BF)
            low = jnp.broadcast_to(low_ref[...], (8, D)).astype(BF)
            shift_ref[...] = matmul(low, raw) + bias_ref[...]

    else:
        act_ref, slope_ref = refs[-2:]
    size = x_ref.shape[0] // 4
    spans = [slice(n * size, (n + 1) * size) for n in range(4)]
    hidden = [matmul(x_ref[span, :], scaled_ref[...]) + shift_ref[0:1, :] for span in spans]
    for n, span in enumerate(spans):
        activated, slope = gelu_pair(hidden[n])
        act_ref[span, :] = activated.astype(BF)
        slope_ref[span, :] = slope.astype(BF)
    if last:
        for span in spans:
            out = matmul(act_ref[span, :], shrink_ref[...])
            for half, o_ref in enumerate(attended):
                weight = output_ref[half * 128 : (half + 1) * 128, :]
                out = out + matmul(o_ref[span, :], weight)
            out_ref[span, :] = out.astype(BF)


def feed(rows_of, x, units, first=None, scaled=None, last=None, kept=(), slots=None):
    length = x.shape[0]
    steps, row, y = chip_rows(rows_of, length, BLOCK)

    def rows(columns):
        return pl.BlockSpec((BLOCK, columns), lambda i, *_: (row(i, _[0]), 0))

    def whole(shape, column=0):
        return pl.BlockSpec(shape, lambda i, *_: (0, column))

    specs, values, halves, count = [rows(D)], [x], 0, 0
    out_specs = [rows(units), rows(units)]
    out_shape = [jax.ShapeDtypeStruct((length, units), BF)] * 2
    if first is not None:
        gain, low, bias, weight = first
        values += [gain[None], low[None], bias[None]]
        specs += [whole((1, D)), whole((1, D)), whole((1, units))]
        out_specs += [whole((D, units)), whole((8, units))]
        out_shape += [
            jax.ShapeDtypeStruct((D, units), BF),
            jax.ShapeDtypeStruct((8, units), F32),
        ]
        if slots is not None:
            count = len(weight)
            values += weight
            specs += [pl.BlockSpec(memory_space=pltpu.VMEM)] * count
            out_specs += [whole((D, units))]
            out_shape += [jax.ShapeDtypeStruct((D, units), BF)]
        else:
            values.append(weight[0])
            specs.append(whole((D, units), weight[1]))
    else:
        values += list(scaled)
        specs += [whole((D, units)), whole((8, units))]
    if last is not None:
        shrink, output, attended = last
        halves = len(attended)
        if count:
            out_specs.append(whole((units, D)))
            out_shape.append(jax.ShapeDtypeStruct((units, D), BF))
        else:
            values.append(shrink[0])
            specs.append(whole((units, D), shrink[1]))
        values += [output, *attended]
        specs += [whole(output.shape)] + [rows(128)] * halves
        out_specs.append(pl.BlockSpec((BLOCK, D), lambda i, *_: (i, 0)))
        out_shape.append(jax.ShapeDtypeStruct((steps * BLOCK, D), BF))
    aliases = {2 + len(values) + n: n for n in range(len(kept))}
    values += list(kept)
    specs += [pl.BlockSpec(memory_space=pl.ANY)] * len(kept)
    slots = jnp.zeros((1,), jnp.int32) if slots is None else jnp.stack(slots).astype(jnp.int32)
    return pl.pallas_call(
        partial(feed_kernel, first is not None, last is not None, halves, count),
        grid_spec=pltpu.PrefetchScalarGridSpec(
            num_scalar_prefetch=2, grid=(steps,), in_specs=specs, out_specs=out_specs
        ),
        out_shape=out_shape,
        input_output_aliases=aliases,
        compiler_params=pltpu.CompilerParams(vmem_limit_bytes=VMEM_LIMIT),
        cost_estimate=LIGHT,
        name="feed",
    )(y.reshape(1), slots, *values)


def branch_kernel(y_ref, act_ref, shrink_ref, output_ref, *refs):
    out = matmul(act_ref[...], shrink_ref[...])
    for half, o_ref in enumerate(refs[:-1]):
        out = out + matmul(o_ref[...], output_ref[half * 128 : (half + 1) * 128, :])
    refs[-1][...] = out.astype(BF)


def branch(rows_of, activated, shrink, output, attended):
    length, units = activated.shape
    steps, row, y = chip_rows(rows_of, length)

    def rows(columns):
        return pl.BlockSpec((ROWS, columns), lambda i, y_ref: (row(i, y_ref), 0))

    return pl.pallas_call(
        branch_kernel,
        grid_spec=pltpu.PrefetchScalarGridSpec(
            num_scalar_prefetch=1,
            grid=(steps,),
            in_specs=[
                rows(units),
                pl.BlockSpec((units, D), lambda i, y_ref: (0, shrink[1])),
                pl.BlockSpec(output.shape, lambda i, y_ref: (0, 0)),
            ]
            + [rows(128)] * len(attended),
            out_specs=pl.BlockSpec((ROWS, D), lambda i, y_ref: (i, 0)),
        ),
        out_shape=jax.ShapeDtypeStruct((steps * ROWS, D), BF),
        compiler_params=pltpu.CompilerParams(vmem_limit_bytes=VMEM_LIMIT),
        cost_estimate=LIGHT,
        name="branch",
    )(y.reshape(1), activated, shrink[0], output, *attended)


def norm_grad_kernel(y_ref, h_ref, wi_ref, wm_ref, *refs):
    out = matmul_nt(h_ref[...], wi_ref[...])
    for half, m_ref in enumerate(refs[:-1]):
        out = out + matmul_nt(m_ref[...], wm_ref[:, half * 384 : (half + 1) * 384])
    refs[-1][...] = out.astype(BF)


def norm_grad(hidden, expand, mixed, mixing, own):
    length, units, columns = hidden.shape[0], expand.shape[1], mixing.shape[1]
    steps, row, y = chip_rows(own, length)

    def rows(count):
        return pl.BlockSpec((ROWS, count), lambda i, y_ref: (row(i, y_ref), 0))

    def whole(shape):
        return pl.BlockSpec(shape, lambda i, y_ref: (0, 0))

    return pl.pallas_call(
        norm_grad_kernel,
        grid_spec=pltpu.PrefetchScalarGridSpec(
            num_scalar_prefetch=1,
            grid=(steps,),
            in_specs=[rows(units), whole((D, units)), whole((D, columns))]
            + [rows(384)] * len(mixed),
            out_specs=pl.BlockSpec((ROWS, D), lambda i, y_ref: (i, 0)),
        ),
        out_shape=jax.ShapeDtypeStruct((steps * ROWS, D), BF),
        compiler_params=pltpu.CompilerParams(vmem_limit_bytes=VMEM_LIMIT),
        cost_estimate=LIGHT,
        name="norm_grad",
    )(y.reshape(1), hidden, expand, mixing, *mixed)


def product_kernel(g_ref, *refs):
    for half, x_ref in enumerate(refs[:-1]):
        product = matmul_tn(x_ref[...], g_ref[...])
        refs[-1][half * 128 : (half + 1) * 128, :] = product.astype(BF)


def product(inputs, grads):
    rows = 128 * len(inputs)
    block = D // 2
    return pl.pallas_call(
        product_kernel,
        grid=(D // block,),
        in_specs=[pl.BlockSpec((grads.shape[0], block), lambda i: (0, i))]
        + [pl.BlockSpec(x.shape, lambda i: (0, 0)) for x in inputs],
        out_specs=pl.BlockSpec((rows, block), lambda i: (0, i)),
        out_shape=jax.ShapeDtypeStruct((rows, D), BF),
        compiler_params=pltpu.CompilerParams(vmem_limit_bytes=VMEM_LIMIT),
        cost_estimate=LIGHT,
        name="product",
    )(grads, *inputs)


def weight_grad_kernel(count, x_ref, weight_ref, gain_ref, shift_ref, total_ref, *refs):
    lows, (out_ref, gain_out_ref, shift_out_ref) = refs[:count], refs[-3:]
    gain, shift = as_column(gain_ref[...]), as_column(shift_ref[...])
    x = x_ref[...]
    start, gain_sum, shift_sum = 0, 0.0, 0.0
    for low_ref in lows:
        columns = slice(start, start + low_ref.shape[1])
        start += low_ref.shape[1]
        raw = matmul_tn(x, low_ref[...])
        weight = weight_ref[:, columns].astype(F32)
        total = total_ref[:, columns]
        out_ref[:, columns] = (raw * gain + shift * total).astype(BF)
        gain_sum = gain_sum + jnp.sum(raw * weight, 1, keepdims=True)
        shift_sum = shift_sum + jnp.sum(weight * total, 1, keepdims=True)
    gain_out_ref[...] = as_row(gain_sum)
    shift_out_ref[...] = as_row(shift_sum)


def weight_grad(x, lows, weight, gain, shift, total, wide=None):
    length, columns = x.shape[0], total.shape[1]
    array, column = weight
    wide = wide or (0, columns)
    row = pl.BlockSpec((1, ROWS), lambda i: (0, i))
    return pl.pallas_call(
        partial(weight_grad_kernel, len(lows)),
        grid=(D // ROWS,),
        in_specs=[
            pl.BlockSpec((length, ROWS), lambda i: (0, i)),
            pl.BlockSpec((ROWS, columns), lambda i: (i, column)),
            row,
            row,
            pl.BlockSpec((1, columns), lambda i: (0, 0)),
        ]
        + [pl.BlockSpec(low.shape, lambda i: (0, 0)) for low in lows],
        out_specs=[pl.BlockSpec((ROWS, columns), lambda i: (i, wide[0])), row, row],
        out_shape=[
            jax.ShapeDtypeStruct((D, wide[1]), BF),
            jax.ShapeDtypeStruct((1, D), F32),
            jax.ShapeDtypeStruct((1, D), F32),
        ],
        compiler_params=pltpu.CompilerParams(vmem_limit_bytes=VMEM_LIMIT),
        cost_estimate=LIGHT,
        name="weight_grad",
    )(x, array, gain[None], shift[None], total, *lows)


def pack_kernel(spans, split, mixing_ref, expand_ref, *refs):
    outs = refs[-2:] if split else (refs[-1], refs[-1])
    shift = split or 0
    for source_ref, part, out_ref, back in (
        (mixing_ref, spans[0], outs[0], 0),
        (expand_ref, spans[1], outs[1], shift),
    ):
        for p, start, at, count in part:
            columns = slice(start - back, start - back + count)
            out_ref[p, :, columns] = source_ref[0, :, at : at + count].astype(BF)
    for pair_ref in refs[: -2 if split else -1]:
        end = outs[1].shape[2] - pair_ref.shape[1]
        for p in range(outs[1].shape[0]):
            outs[1][p, :, end:] = pair_ref[...]


def pack(mixing, expand, layer, spans, columns, pair=(), split=0):
    parts, rows = lax.axis_size("seq"), mixing.shape[1]
    columns = columns + sum(value.shape[1] for value in pair)
    widths = [split, columns - split] if split else [columns]
    made = pl.pallas_call(
        partial(pack_kernel, spans, split),
        grid=(1,),
        in_specs=[
            pl.BlockSpec((1,) + mixing.shape[1:], lambda i: (layer, 0, 0)),
            pl.BlockSpec((1,) + expand.shape[1:], lambda i: (layer, 0, 0)),
        ]
        + [pl.BlockSpec(value.shape, lambda i: (0, 0)) for value in pair],
        out_specs=[pl.BlockSpec((parts, rows, w), lambda i: (0, 0, 0)) for w in widths],
        out_shape=[jax.ShapeDtypeStruct((parts, rows, w), BF) for w in widths],
        compiler_params=pltpu.CompilerParams(vmem_limit_bytes=VMEM_LIMIT),
        cost_estimate=LIGHT,
        name="pack",
    )(mixing, expand, *pair)
    return made if split else made[0]


def feed_back_kernel(joined, kept, *refs):
    grad_ref, shrink_ref, slope_ref, act_ref, x_ref, output_ref = refs[:6]
    weight_ref, gain_ref, shift_ref = refs[6:9]
    low_ref, total_ref, do_ref, gain_out_ref, shift_out_ref = refs[kept : kept + 5]
    outs = refs[kept + 5 : -2]
    expand_ref, shrink_acc_ref = refs[-2:]
    i = pl.program_id(0)

    @pl.when(i == 0)
    def _():
        total_ref[...] = jnp.zeros(total_ref.shape, F32)
        expand_ref[...] = jnp.zeros(expand_ref.shape, F32)
        shrink_acc_ref[...] = jnp.zeros(shrink_acc_ref.shape, F32)

    grads = grad_ref[...]
    hidden = matmul_nt(grads, shrink_ref[...]) * slope_ref[...].astype(F32)
    low = hidden.astype(BF)
    low_ref[...] = low
    total_ref[...] += jnp.sum(hidden, 0, keepdims=True)
    shrink_acc_ref[...] += matmul_tn(act_ref[...], grads)
    do_ref[...] = matmul_nt(grads, output_ref[...]).astype(BF)
    expand_ref[...] += matmul_tn(x_ref[...], low)

    @pl.when(i == pl.num_programs(0) - 1)
    def _():
        gain, shift, total = as_column(gain_ref[...]), as_column(shift_ref[...]), total_ref[...]
        units = total.shape[1]
        raw = expand_ref[...]
        weight = weight_ref[...].astype(F32)
        outs[0][:, :units] = (raw * gain + shift * total).astype(BF)
        if joined:
            outs[0][:, units:] = shrink_acc_ref[...].astype(BF)
        else:
            outs[1][...] = shrink_acc_ref[...].astype(BF)
        gain_out_ref[...] = as_row(jnp.sum(raw * weight, 1, keepdims=True))
        shift_out_ref[...] = as_row(jnp.sum(weight * total, 1, keepdims=True))


def feed_back(grads, shrink, slope, activated, x, output, weight, gain, shift, kept=()):
    length, units = slope.shape
    width, joined = output.shape[0], units == D

    def rows(count):
        return pl.BlockSpec((BLOCK, count), lambda i: (i, 0))

    def whole(shape, column=0):
        return pl.BlockSpec(shape, lambda i: (0, column))

    out_specs = [rows(units), whole((1, units)), rows(width), whole((1, D)), whole((1, D))]
    out_shape = [
        jax.ShapeDtypeStruct((length, units), BF),
        jax.ShapeDtypeStruct((1, units), F32),
        jax.ShapeDtypeStruct((length, width), BF),
        jax.ShapeDtypeStruct((1, D), F32),
        jax.ShapeDtypeStruct((1, D), F32),
    ]
    if joined:
        out_specs.append(whole((D, 2 * units)))
        wide = kept[0].shape[1] if kept else 2 * units + width
        out_shape.append(jax.ShapeDtypeStruct((D, wide), BF))
    else:
        out_specs += [whole((D, units)), whole((units, D))]
        out_shape += [
            jax.ShapeDtypeStruct((D, units), BF),
            jax.ShapeDtypeStruct((units, D), BF),
        ]
    return pl.pallas_call(
        partial(feed_back_kernel, joined, 9 + len(kept)),
        grid=(length // BLOCK,),
        in_specs=[
            rows(D),
            whole((units, D), shrink[1]),
            rows(units),
            rows(units),
            rows(D),
            whole((width, D)),
            whole((D, units), weight[1]),
            whole((1, D)),
            whole((1, D)),
        ]
        + [pl.BlockSpec(memory_space=pl.ANY)] * len(kept),
        out_specs=out_specs,
        out_shape=out_shape,
        input_output_aliases={9: 5} if kept else {},
        scratch_shapes=[
            pltpu.VMEM((D, units), F32),
            pltpu.VMEM((units, D), F32),
        ],
        compiler_params=pltpu.CompilerParams(vmem_limit_bytes=VMEM_LIMIT),
        cost_estimate=LIGHT,
        name="feed_back",
    )(
        grads,
        shrink[0],
        slope,
        activated,
        x,
        output,
        weight[0],
        gain[None],
        shift[None],
        *kept,
    )


def home_spans(parts, copies, width, units):
    mixing, expand = [], []
    size = units // copies
    for p in range(parts):
        for half in range(width // 128):
            for kind in range(3):
                at = kind * parts * width + p * width + half * 128
                mixing.append((p, half * 384 + kind * 128, at, 128))
        for d in range(copies):
            expand.append((p, 3 * width + d * size, (d * parts + p) * size, size))
    return mixing, expand


def adam(grad, weight, first, second, average, rate, decay):
    first_new = BETA_FIRST * first + (1.0 - BETA_FIRST) * grad
    second_new = BETA_SECOND * second + (1.0 - BETA_SECOND) * grad * grad
    first_hat = first_new / (1.0 - BETA_FIRST**STEP)
    second_hat = second_new / (1.0 - BETA_SECOND**STEP)
    weight_new = weight - rate * (
        first_hat / (jnp.sqrt(second_hat) + ADAM_EPS) + decay * weight
    )
    return weight_new, first_new, second_new, EMA_DECAY * average + (1.0 - EMA_DECAY) * weight_new


def adam_kernel(spans, rates, clip_ref, mixing_ref, expand_ref, output_ref, shrink_ref, *refs):
    clip = clip_ref[0]
    states, news = refs[:16], refs[16:]

    def step(kind, grad, columns):
        old = [ref[0, :, columns] for ref in states[4 * kind : 4 * kind + 4]]
        new = adam(grad.astype(F32) * clip, *old, rates[kind], WEIGHT_DECAY)
        for ref, value in zip(news[4 * kind : 4 * kind + 4], new):
            ref[0, :, columns] = value

    for kind, part, grad_ref in ((0, spans[0], mixing_ref), (2, spans[1], expand_ref)):
        back = part[0][1]
        for source, start, at, count in part:
            grad = grad_ref[0, source, :, start - back : start - back + count]
            step(kind, grad, slice(at, at + count))
    step(1, output_ref[0], slice(None))
    step(3, shrink_ref[0], slice(None))


def update(clip, mixing, expand, output, shrink, states, spans, rates):
    layers, parts, rows = mixing.shape[:3]
    chunk = 16 if rows % 16 == 0 else rows
    chunks = rows // chunk

    def block(array):
        size = array.shape[1] // chunks
        return pl.BlockSpec((1, size, array.shape[2]), lambda l, n: (l, n, 0))

    return pl.pallas_call(
        partial(adam_kernel, spans, rates),
        grid=(layers, chunks),
        in_specs=[
            pl.BlockSpec(memory_space=pltpu.SMEM),
            pl.BlockSpec((1, parts, chunk, mixing.shape[3]), lambda l, n: (l, 0, n, 0)),
            pl.BlockSpec((1, parts, chunk, expand.shape[3]), lambda l, n: (l, 0, n, 0)),
            block(output),
            block(shrink),
        ]
        + [block(state) for state in states],
        out_specs=[block(state) for state in states],
        out_shape=[jax.ShapeDtypeStruct(state.shape, F32) for state in states],
        compiler_params=pltpu.CompilerParams(vmem_limit_bytes=VMEM_LIMIT),
        cost_estimate=LIGHT,
        name="update",
    )(clip, mixing, expand, output, shrink, *states)


def rotary_tables(positions):
    half = ROT // 2
    steps_half = jnp.arange(half).astype(F32)
    frequency = 10000.0 ** (-2.0 * steps_half / ROT)
    angles = positions.astype(F32)[None, :] * frequency[:, None]
    cosine = jnp.concatenate([jnp.cos(angles), jnp.ones_like(angles)], 0)
    entry = jnp.arange(128)[None, :] % HD
    index = jnp.arange(half)[:, None]
    turning = (entry < ROT) & (entry % half == index)
    still = (entry >= ROT) & (index == 0)
    sign = jnp.where(entry < half, -1.0, 1.0)
    spread_cosine = jnp.concatenate([turning, still], 0).astype(F32)
    spread_sine = turning.astype(F32) * sign

    def lay(table, spread):
        return lax.dot_general(
            table, spread, (((0,), (0,)), ((), ())), precision=lax.Precision.HIGHEST
        )

    return lay(cosine, spread_cosine), lay(jnp.sin(angles), spread_sine)


def split_affine(affine):
    bounds = [D, D, D, D, 3 * D, D, FF, D]
    pieces = []
    offset = 0
    for length in bounds:
        pieces.append(affine[offset : offset + length])
        offset = offset + length
    return pieces


def normalize(values):
    centre = values - jnp.mean(values, -1, keepdims=True)
    spread = jnp.mean(centre * centre, -1, keepdims=True)
    scale = lax.rsqrt(spread + NORM_EPS)
    return centre * scale, scale


def local(
    stream,
    cotangent,
    positions,
    mixing_weight,
    mixing_first,
    mixing_second,
    mixing_average,
    output_weight,
    output_first,
    output_second,
    output_average,
    expand_weight,
    expand_first,
    expand_second,
    expand_average,
    shrink_weight,
    shrink_first,
    shrink_second,
    shrink_average,
    affine_weight,
    affine_first,
    affine_second,
    affine_average,
):
    parts = lax.axis_size("seq")
    copies = lax.axis_size("dp")
    devices = parts * copies
    part = lax.axis_index("seq")
    width = D // parts
    units = FF // parts
    rows_d = D // devices
    rows_f = FF // devices
    rows = stream.shape[0] * stream.shape[1]
    small = affine_weight.shape[1]

    halves = width // 128
    outer = dp_parts()[0]

    def mixing_part(vector):
        view = vector.reshape(3, parts, halves, 128)
        view = lax.dynamic_index_in_dim(view, part, 1, keepdims=False)
        return view.transpose(1, 0, 2).reshape(-1)

    def expand_part(vector):
        view = vector.reshape(copies, parts, -1)
        return lax.dynamic_index_in_dim(view, part, 1, keepdims=False).reshape(-1)

    def spread_mixing(vector):
        view = jnp.zeros((3, parts, width), F32)
        vector = vector.reshape(halves, 3, 128).transpose(1, 0, 2).reshape(3, 1, width)
        return lax.dynamic_update_slice(view, vector, (0, part, 0)).reshape(-1)

    def spread_expand(vector):
        view = jnp.zeros((copies, parts, rows_f), F32)
        return lax.dynamic_update_slice(view, vector.reshape(copies, 1, rows_f), (0, part, 0)).reshape(-1)

    spans = home_spans(parts, copies, width, units)
    aligned = rows_f % 128 == 0 and rows_d % 16 == 0

    def arrange(layer, mixing, expand, pair=(), split=False):
        if aligned:
            return pack(
                mixing, expand, layer, spans, 3 * width + units, pair, 3 * width * split
            )
        mixing = mixing[layer].astype(BF).reshape(rows_d, 3, parts, halves, 128)
        mixing = mixing.transpose(2, 0, 3, 1, 4).reshape(parts, rows_d, 3 * width)
        expand = expand[layer].astype(BF).reshape(rows_d, copies, parts, rows_f)
        expand = expand.transpose(2, 0, 1, 3).reshape(parts, rows_d, units)
        pair = [jnp.broadcast_to(value, (parts,) + value.shape) for value in pair]
        if split:
            return mixing, jnp.concatenate([expand] + pair, -1)
        return jnp.concatenate([mixing, expand] + pair, -1)

    def settle_output(exchanged):
        output = exchanged.reshape(parts, copies // parts, rows_d, D)
        return output.transpose(1, 0, 2, 3).reshape(width, D)

    def norm_back(gradient, normed_grad, own_normed, scale):
        projected = jnp.mean(normed_grad * own_normed, -1, keepdims=True)
        middle = jnp.mean(normed_grad, -1, keepdims=True)
        return gradient + scale * (normed_grad - middle - own_normed * projected)

    def beside(grads, *pieces):
        pieces = [jnp.concatenate(piece).reshape(devices, small) for piece in pieces]
        pieces = jnp.concatenate(pieces, -1)
        coarse = pieces.astype(BF)
        fine = (pieces - coarse.astype(F32)).astype(BF)
        pieces = jnp.concatenate([coarse, fine], -1)
        extra = 128 * pl.cdiv(pieces.shape[1], 128 * rows_d)
        pieces = jnp.pad(pieces, ((0, 0), (0, extra * rows_d - pieces.shape[1])))
        return jnp.concatenate([grads, pieces.reshape(D, extra)], -1)

    def apart(summed, columns, count):
        pieces = summed[..., columns:].reshape(devices, -1).astype(F32)
        size = count * small
        pieces = jnp.sum(pieces[:, :size] + pieces[:, size : 2 * size], 0).reshape(count, small)
        return jnp.sum(summed[..., :columns].astype(F32), 0), list(pieces)

    def sum_squares(*values):
        return sum(jnp.sum(value.astype(F32) * value.astype(F32)) for value in values)

    tie = lax.optimization_barrier
    chips = parts // 2
    current = stream.reshape(rows, D)
    gradient = cotangent.reshape(rows, D)

    def view(array, column):
        if units == D:
            return array, column
        return array[:, column * units : (column + 1) * units].reshape(-1, D), 0

    pair = jnp.stack([positions.reshape(-1) // 16, positions.reshape(-1) % 16]).astype(BF)
    pair = pair.reshape(rows_d, 2 * rows // rows_d)
    both = arrange(0, mixing_weight, expand_weight, (pair,))
    both, current = tie((both, current))
    both = seq_exchange(both)
    own_normed, scale = normalize(current)
    travel = SeqGather(own_normed.astype(BF))
    pair = both[..., 3 * width + units :].astype(F32).reshape(parts, 2, rows)
    places = (pair[:, 0] * 16.0 + pair[:, 1]).reshape(-1)
    both = both.reshape(parts * rows_d, -1)
    near = Gather(both[:, : 3 * width])
    places, affine_low, layer_mixing, layer_expand, first_output, later_output = near.hold(
        places,
        affine_weight,
        mixing_weight,
        expand_weight,
        output_weight[0],
        output_weight[1],
    )
    near.forward()
    outputs = jnp.concatenate(
        [value.astype(BF).reshape(-1, width) for value in (first_output, later_output)], -1
    )
    outputs = lax.all_gather(outputs, "dp", axis=0, tiled=True)
    cosine, sine = rotary_tables(places)
    later_both = arrange(1, layer_mixing, layer_expand)
    affine_low, cosine, sine, later_both, expand_own, shrink_own, low_gradient = near.hold(
        affine_low,
        cosine,
        sine,
        later_both,
        both[:, 3 * width : 3 * width + units],
        shrink_weight[0],
        gradient.astype(BF),
    )
    near.forward()
    near.cross()
    affine_low = affine_low.astype(BF).reshape(1, LAYERS * small)
    affine_all = lax.all_to_all(
        jnp.broadcast_to(affine_low, (devices, LAYERS * small)),
        ("dp", "seq"),
        split_axis=0,
        concat_axis=0,
        tiled=True,
    )
    far_own = jnp.concatenate([expand_own, shrink_own.astype(BF).reshape(-1, units)], -1)
    affine_all, far_own, near.pieces, near.chains, travel.pieces = tie(
        (affine_all, far_own, near.pieces, near.chains, travel.pieces)
    )
    inputs, x_slots = travel.take(0, chips)
    near.forward()
    near.cross()
    affine_all = affine_all.reshape(devices, LAYERS, small).transpose(1, 0, 2)
    affine_all = affine_all.reshape(LAYERS, devices * small).astype(F32)
    vectors = [split_affine(affine_all[layer]) for layer in range(LAYERS)]
    vectors, inputs = near.hold(vectors, inputs)
    for step in range(3, outer - 1):
        near.forward()
        near.cross()
    while len(near.chains) < outer:
        near.cross()
    far = Gather(far_own)
    far.pieces[0], near.pieces, near.chains = tie((far.pieces[0], near.pieces, near.chains))
    far.forward()
    far.cross()
    pieces, slots = near.done()

    gain_one, shift_one, gain_two, shift_two = vectors[0][:4]
    normed, mixed, mixing, mixing_scaled, _ = mix(
        inputs,
        x_slots,
        cosine,
        sine,
        first=(gain_one, shift_one, mixing_part(vectors[0][4]), pieces, slots),
    )
    mixed, later_both, later_shrink, outputs, low_gradient = far.hold(
        mixed, later_both, shrink_weight[1], outputs, low_gradient
    )
    far.forward()
    far.cross()
    travel = SeqGather(low_gradient)
    later_both = seq_exchange(later_both)
    outputs = jnp.stack(
        [outputs[:, layer * width : (layer + 1) * width].reshape(parts, -1, D) for layer in (0, 1)],
        1,
    )
    attended, logs = [], []
    for half in range(halves):
        out, log_total = attend(mixed, half)
        attended.append(out)
        logs.append(log_total)
        if half == 0:
            mixed, out, later_both, outputs = far.hold(mixed, out, later_both, outputs)
            far.forward()
            far.cross()
            outputs = seq_exchange(outputs)
            later_both = later_both.reshape(parts * rows_d, -1)
            later_far = jnp.concatenate(
                [later_both[:, 3 * width :], later_shrink.astype(BF).reshape(-1, units)], -1
            )
            later_near = later_both[:, : 3 * width]
    attended, logs, later_far, later_near, travel.pieces = far.hold(
        attended, logs, later_far, later_near, travel.pieces
    )
    later_all = lax.all_gather(later_far, "dp", axis=0, tiled=True)
    while len(far.pieces) < outer:
        far.forward()
    while len(far.chains) < outer:
        far.cross()
    attended, logs, later_near, grads, outputs = far.hold(
        attended, logs, later_near, travel.done(), outputs
    )
    output, later_output = (settle_output(outputs[:, layer]) for layer in (0, 1))
    near = Gather(later_near)
    near.forward()
    near.cross()
    pieces, slots = far.done()
    first = (gain_two, shift_two, expand_part(vectors[0][6]))
    if units == D:
        activated, slope, expand_scaled, expand_shift, expand, shrink, others = feed(
            False,
            normed,
            units,
            first=first + (pieces,),
            last=(None, output, attended),
            slots=slots,
        )
    else:
        far_all = assemble(pieces, slots)
        expand, shrink = far_all[:, :units], view(far_all, 1)[0]
        activated, slope, expand_scaled, expand_shift, others = feed(
            False,
            normed,
            units,
            first=first + ((expand, 0),),
            last=((shrink, 0), output, attended),
        )
    shrink = (shrink, 0)
    (others,) = near.hold(others)
    near.forward()
    near.cross()
    travel = SeqScatter(others)
    activated, slope = travel.hold(activated, slope)
    activated, slope, own = feed(
        True,
        normed,
        units,
        scaled=(expand_scaled, expand_shift),
        last=(shrink, output, attended),
        kept=(activated, slope),
    )
    (own,) = near.hold(own)
    for step in range(2, outer - 1):
        near.forward()
        near.cross()
    stored = [(own_normed, scale, normed, mixed, attended, logs, activated, slope)]
    weights = [(mixing, mixing_scaled, output, expand, expand_scaled, shrink)]
    total, (near.pieces, near.chains) = travel.done(own, (near.pieces, near.chains))
    while len(near.chains) < outer:
        near.cross()
    current = current + total + vectors[0][5] + vectors[0][7]

    own_normed, scale = normalize(current)
    travel = SeqGather(own_normed.astype(BF))
    pieces, slots = near.done()
    gain_one, shift_one, gain_two, shift_two = vectors[1][:4]
    inputs, x_slots = travel.take(0, 1)
    normed, mixed, mixing, mixing_scaled, mixing_shift = mix(
        inputs,
        x_slots,
        cosine,
        sine,
        first=(gain_one, shift_one, mixing_part(vectors[1][4]), pieces, slots),
    )
    normed, mixed = travel.hold(normed, mixed)
    inputs, x_slots = travel.take(1, chips)
    normed, mixed = mix(
        inputs,
        x_slots,
        cosine,
        sine,
        scaled=(mixing_scaled, mixing_shift),
        kept=(normed, mixed),
    )
    output = later_output
    attended, logs = [], []
    for half in range(halves):
        out, log_total = attend(mixed, half)
        attended.append(out)
        logs.append(log_total)
    attended, logs, later_all = tie((attended, logs, later_all))
    expand, shrink = later_all, view(later_all, 1)
    activated, slope, expand_scaled, expand_shift = feed(
        None,
        normed,
        units,
        first=(gain_two, shift_two, expand_part(vectors[1][6]), (later_all, 0)),
    )

    grads, attended, logs, activated = tie((grads, attended, logs, activated))

    def feed_grads(gain, shift, kept=()):
        output_grad, low_grads = tie((product(attended, grads), grads))
        output_grad = output_grad.reshape(copies // parts, parts, rows_d, D).transpose(1, 0, 2, 3)
        swap = SeqSwap(output_grad.reshape(parts, copies // parts * rows_d, D))
        made = feed_back(
            low_grads,
            shrink,
            slope,
            activated,
            normed,
            output,
            (expand, 0),
            gain,
            shift,
            kept if units == D else (),
        )
        made = swap.hold(*made)
        low, total, attended_grad, gain_grad, shift_grad = made[:5]
        output_grad = swap.done().reshape(-1, width)
        if units == D:
            joined = lax.dynamic_update_slice(made[5], output_grad, (0, 2 * units))
        else:
            joined = [made[5], made[6].reshape(-1, units), output_grad, *kept]
            joined = jnp.concatenate(joined, -1)
        return low, total, attended_grad, gain_grad, shift_grad, joined

    made = feed_grads(gain_two, shift_two)
    hidden_low, hidden_total, attended_grad, gain_two_grad, shift_two_grad, later_grad = made
    later_grad, attended_grad = tie((later_grad, attended_grad))
    later_first = lax.psum_scatter(later_grad, "dp", scatter_dimension=0, tiled=True)
    lows, totals = [], []
    for half in range(halves):
        low, total = attend_back(
            mixed, attended_grad, attended[half], logs[half], cosine, sine, half
        )
        lows.append(low)
        totals.append(total)
    mixed_total = jnp.concatenate(totals, -1)
    others = norm_grad(hidden_low, expand_scaled, lows, mixing_scaled, False)
    travel = SeqScatter(others)
    hidden_low, lows, activated = travel.hold(hidden_low, lows, activated)
    own = norm_grad(hidden_low, expand_scaled, lows, mixing_scaled, True)
    last = (shrink, output, attended)
    result_others = branch(False, activated, *last)
    result_own = branch(True, activated, *last)
    normed_grad, (result_others, result_own) = travel.done(own, (result_others, result_own))
    normed_grad, lows = tie((normed_grad, lows))
    gradient = norm_back(gradient, normed_grad, own_normed, scale)
    travel = SeqGather(gradient.astype(BF))
    lows, own_piece = tie((lows, travel.pieces[0]))
    wide = (3, 2 * units + 4 * width) if units == D else None
    later_mixing, gain_one_grad, shift_one_grad = weight_grad(
        normed, lows, (mixing, 0), gain_one, shift_one, mixed_total, wide
    )
    (later_mixing,) = travel.hold(later_mixing)
    grads = travel.done()
    output_sum = jnp.sum(cotangent.reshape(rows, D), 0)

    def small_grads(*pieces):
        gains, mixed_total, output_sum, hidden_total = pieces
        pieces = [piece[0] for piece in gains]
        pieces += [spread_mixing(mixed_total[0]), output_sum]
        return pieces + [spread_expand(hidden_total[0]), output_sum]

    gains = (gain_one_grad, shift_one_grad, gain_two_grad, shift_two_grad)
    later_pieces = small_grads(gains, mixed_total, output_sum, hidden_total)

    later_current, later_vectors = current, vectors[1]
    current = stream.reshape(rows, D)
    own_normed, scale, normed, mixed, attended, logs, activated, slope = stored[0]
    mixing, mixing_scaled, output, expand, expand_scaled, shrink = weights[0]
    gain_one, shift_one, gain_two, shift_two = vectors[0][:4]
    made = feed_grads(gain_two, shift_two, (later_mixing,))
    hidden_low, hidden_total, attended_grad, gain_two_grad, shift_two_grad, far_grad = made
    far_grad, attended_grad, result_others, later_pieces = tie(
        (far_grad, attended_grad, result_others, later_pieces)
    )
    far_grad = lax.psum_scatter(far_grad, "dp", scatter_dimension=0, tiled=True)
    travel = SeqScatter(result_others)
    lows, totals, mixing_grads, gain_grads, shift_grads = [], [], [], [], []
    for half in range(halves):
        low, total = attend_back(
            mixed, attended_grad, attended[half], logs[half], cosine, sine, half
        )
        if half == 0:
            mixed, low, later_first = tie((mixed, low, later_first))
            later_home = SeqSwap(later_first[:, :units].reshape(parts, rows_d, units))
        else:
            mixed, low = later_home.hold(mixed, low)
        if half == halves - 1:
            others = norm_grad(
                hidden_low, expand_scaled, lows + [low], mixing_scaled, False
            )
            others, low = tie((others, low))
            last_travel = SeqScatter(others)
        mixing_grad, gain_one_grad, shift_one_grad = weight_grad(
            normed,
            [low],
            (mixing, half),
            gain_one,
            shift_one,
            total,
        )
        lows.append(low)
        totals.append(total)
        gain_grads.append(gain_one_grad)
        shift_grads.append(shift_one_grad)
        pieces = [later_pieces] if half == 0 else []
        if half == halves - 1:
            output_sum = jnp.sum(gradient, 0)
            gains = (sum(gain_grads), sum(shift_grads), gain_two_grad, shift_two_grad)
            pieces.append(
                small_grads(gains, jnp.concatenate(totals, -1), output_sum, hidden_total)
            )
        mixing_grad = beside(mixing_grad, *pieces) if pieces else mixing_grad
        if half == 0:
            result, (mixing_grad,) = travel.done(result_own, (mixing_grad,))
        if half == halves - 1:
            (mixing_grad,) = last_travel.hold(mixing_grad)
        mixing_grad, lows, mixed, attended_grad, mixing_grads = tie(
            (mixing_grad, lows, mixed, attended_grad, mixing_grads)
        )
        mixing_grads.append(sum_exchange(mixing_grad))
    result = later_current + result + later_vectors[5] + later_vectors[7]
    result = result.reshape(stream.shape)
    own = norm_grad(hidden_low, expand_scaled, lows, mixing_scaled, True)
    normed_grad = last_travel.done(own)[0]
    gradient = norm_back(gradient, normed_grad, own_normed, scale)
    squares = sum_squares(later_first)
    mixing_grads[-1], gradient, result, squares = tie(
        (mixing_grads[-1], gradient, result, squares)
    )
    affine, parts_of_mixing = [], []
    for half in range(halves):
        count = (half == 0) + (half == halves - 1)
        summed, pieces = apart(mixing_grads[half], 3 * 128, count)
        parts_of_mixing.append(summed)
        affine += pieces
    affine_grad = jnp.stack(affine[::-1])
    squares = squares + sum_squares(*parts_of_mixing, affine_grad)
    mixing_grad = jnp.concatenate(parts_of_mixing, -1).astype(BF)
    far_grad, squares, mixing_grad = tie((far_grad, squares, mixing_grad))
    stream_grad = gradient.reshape(stream.shape)

    squares = squares + sum_squares(far_grad)
    squares = lax.all_to_all(
        jnp.broadcast_to(squares, (devices, 128)),
        ("dp", "seq"),
        split_axis=0,
        concat_axis=0,
        tiled=True,
    )
    home = jnp.concatenate([far_grad[:, :units], far_grad[:, 2 * units + width :]], -1)
    home = SeqSwap(home.reshape(parts, rows_d, units + 3 * width))
    output_grad = jnp.stack(
        [far_grad[:, 2 * units : 2 * units + width], later_first[:, 2 * units :]]
    ).reshape(LAYERS, rows_d, D)
    shrink_grad = jnp.stack(
        [far_grad[:, units : 2 * units], later_first[:, units : 2 * units]]
    ).reshape(LAYERS, rows_f, D)
    squares, output_grad, shrink_grad = home.hold(squares, output_grad, shrink_grad)
    home = home.done()
    expand_grad = jnp.stack([home[..., :units], later_home.done()])
    later_mixing = home[..., units:]
    gradient_norm = jnp.sqrt(jnp.sum(squares[:, 0]))
    clip_scale = jnp.minimum(1.0, CLIP_LIMIT / (gradient_norm + 1e-06))
    mixing_grad = jnp.stack([mixing_grad, later_mixing])
    if not aligned:
        mixing_grad = mixing_grad.reshape(LAYERS, parts, rows_d, halves, 3, 128)
        mixing_grad = mixing_grad.transpose(0, 2, 4, 1, 3, 5).reshape(LAYERS, 1, rows_d, 3 * D)
        expand_grad = expand_grad.reshape(LAYERS, parts, rows_d, copies, rows_f)
        expand_grad = expand_grad.transpose(0, 2, 3, 1, 4).reshape(LAYERS, 1, rows_d, FF)
        spans = ([(0, 0, 0, 3 * D)], [(0, 0, 0, FF)])
    states = (
        (mixing_weight, mixing_first, mixing_second, mixing_average)
        + (output_weight, output_first, output_second, output_average)
        + (expand_weight, expand_first, expand_second, expand_average)
        + (shrink_weight, shrink_first, shrink_second, shrink_average)
    )
    rates = (D ** (-0.5), (D * 32 // LEN) ** (-0.5), D ** (-0.5), FF ** (-0.5))
    updated = update(
        clip_scale.reshape(1), mixing_grad, expand_grad, output_grad, shrink_grad, states, spans, rates
    )
    affine_new = adam(
        affine_grad * clip_scale,
        affine_weight,
        affine_first,
        affine_second,
        affine_average,
        SMALL_RATE,
        0.0,
    )
    return (result, stream_grad, gradient_norm) + tuple(updated) + tuple(affine_new)


def solution(mesh):
    tokens = P("dp", "seq", None)
    matrix = P(None, ("dp", "seq"), None)
    vector = P(None, ("dp", "seq"))
    states = (matrix,) * 16 + (vector,) * 4
    return jax.shard_map(
        local,
        mesh=mesh,
        in_specs=(tokens, tokens, P("dp", "seq")) + states,
        out_specs=(tokens, tokens, P()) + states,
        check_vma=False,
    )
```

```python
from functools import partial
import math

import jax
import jax.numpy as jnp
from jax import lax
from jax.experimental import pallas as pl
from jax.experimental.pallas import tpu as pltpu
from jax.sharding import PartitionSpec as P

D = 1024
H = 16
HD = 64
ROT = 16
FF = 4096
LEN = 2048
LAYERS = 2
STEP = 3

NORM_EPS = 1e-05
CLIP_LIMIT = 1.0
BETA_FIRST = 0.5
BETA_SECOND = 0.5
ADAM_EPS = 1e-08
WEIGHT_DECAY = 0.01
EMA_DECAY = 0.999
SMALL_RATE = 0.1
MASK_VALUE = -1e30
ROWS = 256
BLOCK = 512
QUERY_SCALE = 1.0 / math.sqrt(HD)
BF = jnp.bfloat16
F32 = jnp.float32
VMEM_LIMIT = 62 * 1024 * 1024
LIGHT = pl.CostEstimate(flops=1000, bytes_accessed=1000, transcendentals=0)


def dp_parts():
    size = lax.axis_size("dp")
    outer = 4 if size % 4 == 0 else size
    return outer, size // outer


def outer_ring(value):
    outer, inner = dp_parts()
    size = outer * inner
    return lax.ppermute(value, "dp", [(i, (i + inner) % size) for i in range(size)])


def inner_ring(value):
    outer, inner = dp_parts()
    moves = [
        (a * inner + b, a * inner + (b + 1) % inner) for a in range(outer) for b in range(inner)
    ]
    return lax.ppermute(value, "dp", moves)


def chip_ring(value):
    size = lax.axis_size("seq")
    return lax.ppermute(value, "seq", [(i, (i + 2) % size) for i in range(size)])


def core_swap(value):
    size = lax.axis_size("seq")
    return lax.ppermute(value, "seq", [(i, i ^ 1) for i in range(size)])


def assemble_kernel(slots_ref, *refs):
    n = pl.program_id(0)
    for step, piece_ref in enumerate(refs[:-1]):

        @pl.when(n == step)
        def _(piece_ref=piece_ref):
            refs[-1][...] = piece_ref[...][None]


def assemble(pieces, slots):
    count, piece = len(pieces), pieces[0]
    total = pl.pallas_call(
        assemble_kernel,
        grid_spec=pltpu.PrefetchScalarGridSpec(
            num_scalar_prefetch=1,
            grid=(count,),
            in_specs=[pl.BlockSpec(memory_space=pltpu.VMEM)] * count,
            out_specs=pl.BlockSpec((1,) + piece.shape, lambda n, slots: (slots[n], 0, 0)),
        ),
        out_shape=jax.ShapeDtypeStruct((count,) + piece.shape, piece.dtype),
        compiler_params=pltpu.CompilerParams(vmem_limit_bytes=VMEM_LIMIT),
        cost_estimate=LIGHT,
        name="assemble",
    )(jnp.stack(slots).astype(jnp.int32), *pieces)
    return total.reshape((count * piece.shape[0],) + piece.shape[1:])


class Gather:
    def __init__(self, value):
        self.pieces = [value]
        self.chains = []

    def forward(self):
        self.pieces.append(outer_ring(self.pieces[-1]))

    def cross(self):
        chain = [self.pieces[len(self.chains)]]
        for turn in range(1, dp_parts()[1]):
            chain.append(inner_ring(chain[-1]))
        self.chains.append(chain)

    def hold(self, *values):
        held = lax.optimization_barrier((values, self.pieces, self.chains))
        self.pieces, self.chains = held[1], held[2]
        return held[0]

    def done(self):
        outer, inner = dp_parts()
        me = lax.axis_index("dp")
        a, b = me // inner, me % inner
        pieces, slots = [], []
        for step, chain in enumerate(self.chains):
            for turn, piece in enumerate(chain):
                pieces.append(piece)
                slots.append((a - step) % outer * inner + (b - turn) % inner)
        return pieces, slots


class SeqGather:
    def __init__(self, value):
        self.pieces = [value]
        for step in range(1, lax.axis_size("seq") // 2):
            self.pieces.append(chip_ring(self.pieces[-1]))

    def hold(self, *values):
        held = lax.optimization_barrier((values, self.pieces))
        self.pieces = held[1]
        return held[0]

    def take(self, start, stop):
        chips = lax.axis_size("seq") // 2
        me = lax.axis_index("seq")
        y, c = me // 2, me % 2
        pieces, slots = [], []
        for step in range(start, stop):
            at = (y - step) % chips
            pieces += [self.pieces[step], core_swap(self.pieces[step])]
            slots += [2 * at + c, 2 * at + 1 - c]
        return pieces, slots

    def done(self):
        return assemble(*self.take(0, len(self.pieces)))


class SeqScatter:
    def __init__(self, others):
        self.chips = lax.axis_size("seq") // 2
        self.core = lax.axis_index("seq") % 2
        rows = others.shape[0] // (2 * (self.chips - 1))
        others = others.reshape((self.chips - 1, 2, rows) + others.shape[1:])
        self.values = [others[n] for n in range(self.chips - 1)]
        self.sending = self.cores(self.values[0]).astype(BF)

    def cores(self, value):
        kept = lax.dynamic_index_in_dim(value, self.core, 0, keepdims=False)
        passed = lax.dynamic_index_in_dim(value, 1 - self.core, 0, keepdims=False)
        return kept.astype(F32) + core_swap(passed).astype(F32)

    def hold(self, *values):
        held = lax.optimization_barrier((values, self.sending))
        self.sending = held[1]
        return held[0]

    def done(self, own, others=()):
        own = own.reshape((2, own.shape[0] // 2) + own.shape[1:])
        for value in self.values[1:] + [own]:
            arrived = chip_ring(self.sending)
            arrived, value, others = lax.optimization_barrier((arrived, value, others))
            total = self.cores(value) + arrived.astype(F32)
            self.sending = total.astype(BF)
        return total, others


def sum_exchange(value):
    copies, parts = lax.axis_size("dp"), lax.axis_size("seq")
    rows = value.shape[0] // (copies * parts)
    value = value.reshape((copies * parts, rows) + value.shape[1:])
    value = lax.all_to_all(value, ("dp", "seq"), split_axis=0, concat_axis=0, tiled=True)
    return value.reshape((copies, parts) + value.shape[1:])


def flipped(values, index):
    bit = 1
    while bit < len(values):
        chosen = (index & bit) > 0
        values = [
            jnp.where(chosen, values[n ^ bit], values[n]) for n in range(len(values))
        ]
        bit *= 2
    return values


class SeqSwap:
    def __init__(self, value):
        size = lax.axis_size("seq")
        chunks = flipped([value[n] for n in range(size)], lax.axis_index("seq"))
        self.value = [
            lax.ppermute(chunk, "seq", [(i, i ^ n) for i in range(size)]) if n else chunk
            for n, chunk in enumerate(chunks)
        ]

    def hold(self, *values):
        held = lax.optimization_barrier((values, self.value))
        self.value = held[1]
        return held[0]

    def done(self):
        return jnp.stack(flipped(self.value, lax.axis_index("seq")))


def seq_exchange(value):
    return lax.all_to_all(value, "seq", split_axis=0, concat_axis=0, tiled=True)


def head_masks(width, dtype):
    lane = lax.broadcasted_iota(jnp.int32, (1, width), 1) // HD
    return [(lane == h).astype(F32).astype(dtype) for h in range(width // HD)]


def swap_halves(values):
    width = values.shape[1]
    lane = lax.broadcasted_iota(jnp.int32, values.shape, 1) % HD
    return jnp.where(
        lane < ROT // 2,
        pltpu.roll(values, width - ROT // 2, 1),
        pltpu.roll(values, ROT // 2, 1),
    )


def as_column(row):
    return jnp.broadcast_to(row, (128, row.shape[1])).T[:, :1]


def as_row(column):
    return jnp.broadcast_to(column, (column.shape[0], 128)).T[:1, :]


def matmul(left, right):
    return lax.dot_general(left, right, (((1,), (0,)), ((), ())), preferred_element_type=F32)


def matmul_nt(left, right):
    return lax.dot_general(left, right, (((1,), (1,)), ((), ())), preferred_element_type=F32)


def matmul_tn(left, right):
    return lax.dot_general(left, right, (((0,), (0,)), ((), ())), preferred_element_type=F32)


def mix_kernel(count, pieces, x_slots_ref, slots_ref, *refs):
    refs = list(refs)
    inputs = refs[:count]
    del refs[:count]
    cos_ref, sin_ref = refs[:2]
    i = pl.program_id(0)
    if pieces:
        gain_ref, low_ref, bias_ref = refs[2:5]
        normed_ref, out_ref, raw_ref, scaled_ref, shift_ref = refs[-5:]
        columns = scaled_ref.shape[1]

        @pl.when(i == 0)
        def _():
            for n, piece_ref in enumerate(refs[5 : 5 + pieces]):
                size = piece_ref.shape[0]
                rows = pl.ds(pl.multiple_of(slots_ref[n] * size, size), size)
                raw_ref[rows, :] = piece_ref[...]
            raw = raw_ref[...]
            scaled_ref[...] = (raw.astype(F32) * as_column(gain_ref[...])).astype(BF)
            low = jnp.broadcast_to(low_ref[...], (8, D)).astype(BF)
            shift_ref[...] = matmul(low, raw) + bias_ref[...]

    else:
        scaled_ref, shift_ref = refs[2:4]
        normed_ref, out_ref = refs[-2:]
        columns = scaled_ref.shape[1]
    for n, x_ref in enumerate(inputs):

        @pl.when(i == n)
        def _(x_ref=x_ref):
            normed_ref[...] = x_ref[...]

    mixed = matmul(normed_ref[...], scaled_ref[...]) + shift_ref[0:1, :]
    cosine, sine = cos_ref[...], sin_ref[...]
    for start in range(0, columns, 3 * 128):
        query = mixed[:, start : start + 128]
        key = mixed[:, start + 128 : start + 256]
        query = (query * cosine + swap_halves(query) * sine) * QUERY_SCALE
        key = key * cosine + swap_halves(key) * sine
        out_ref[:, start : start + 128] = query.astype(BF)
        out_ref[:, start + 128 : start + 256] = key.astype(BF)
        out_ref[:, start + 256 : start + 384] = mixed[:, start + 256 : start + 384].astype(BF)


def mix(inputs, x_slots, cosine, sine, first=None, scaled=None, kept=()):
    count, size, length = len(inputs), inputs[0].shape[0], cosine.shape[0]
    columns = (first[2].shape[0] if scaled is None else scaled[0].shape[1])

    def whole(shape):
        return pl.BlockSpec(shape, lambda i, *_: (0, 0))

    def rows(width):
        return pl.BlockSpec((size, width), lambda i, *_: (_[0][i], 0))

    held = pl.BlockSpec(memory_space=pltpu.VMEM)
    values = [*inputs, cosine, sine]
    specs = [held] * count + [rows(128), rows(128)]
    out_specs = [rows(D), rows(columns)]
    out_shape = [
        jax.ShapeDtypeStruct((length, D), BF),
        jax.ShapeDtypeStruct((length, columns), BF),
    ]
    pieces, slots = (), [jnp.int32(0)]
    if first is not None:
        gain, low, bias, pieces, slots = first
        values += [gain[None], low[None], bias[None], *pieces]
        specs += [whole((1, D)), whole((1, D)), whole((1, columns))] + [held] * len(pieces)
        out_specs += [whole((D, columns)), whole((D, columns)), whole((8, columns))]
        out_shape += [
            jax.ShapeDtypeStruct((D, columns), BF),
            jax.ShapeDtypeStruct((D, columns), BF),
            jax.ShapeDtypeStruct((8, columns), F32),
        ]
    else:
        values += list(scaled)
        specs += [whole((D, columns)), whole((8, columns))]
    aliases = {2 + len(values) + n: n for n in range(len(kept))}
    values += list(kept)
    specs += [pl.BlockSpec(memory_space=pl.ANY)] * len(kept)
    return pl.pallas_call(
        partial(mix_kernel, count, len(pieces)),
        grid_spec=pltpu.PrefetchScalarGridSpec(
            num_scalar_prefetch=2, grid=(count,), in_specs=specs, out_specs=out_specs
        ),
        out_shape=out_shape,
        input_output_aliases=aliases,
        compiler_params=pltpu.CompilerParams(vmem_limit_bytes=VMEM_LIMIT),
        cost_estimate=LIGHT,
        name="mix",
    )(jnp.stack(x_slots).astype(jnp.int32), jnp.stack(slots).astype(jnp.int32), *values)


def attend_kernel(q_ref, k_ref, v_ref, o_ref, lse_ref, acc_ref, turned_ref):
    block, width = q_ref.shape
    heads = width // HD
    i = pl.program_id(0)
    query = q_ref[...]
    queries = [query * mask for mask in head_masks(width, BF)]

    @pl.when(i == 0)
    def _():
        turned_ref[...] = v_ref[...].T

    acc_ref[...] = jnp.zeros(acc_ref.shape, F32)

    def tile(j, diagonal, carry):
        rows = pl.ds(pl.multiple_of(j * block, block), block)
        key = k_ref[rows, :]
        scores = [matmul_nt(key, queries[h]) for h in range(heads)]
        if diagonal:
            row = lax.broadcasted_iota(jnp.int32, (block, block), 0)
            column = lax.broadcasted_iota(jnp.int32, (block, block), 1)
            allowed = row <= column
            scores = [jnp.where(allowed, score, MASK_VALUE) for score in scores]
        highs = [
            jnp.maximum(carry[h][0], jnp.max(scores[h], 0, keepdims=True)) for h in range(heads)
        ]
        weights = [jnp.exp(scores[h] - highs[h]) for h in range(heads)]
        fades = [jnp.exp(carry[h][0] - highs[h]) for h in range(heads)]
        sums = [
            carry[h][1] * fades[h] + jnp.sum(weights[h], 0, keepdims=True) for h in range(heads)
        ]
        for h in range(heads):
            part = slice(h * HD, (h + 1) * HD)
            product = matmul(turned_ref[part, rows], weights[h].astype(BF))
            acc_ref[part, :] = acc_ref[part, :] * fades[h] + product
        return [(highs[h], sums[h]) for h in range(heads)]

    empty = (jnp.full((1, block), MASK_VALUE, F32), jnp.zeros((1, block), F32))
    carry = lax.fori_loop(0, i, lambda j, carry: tile(j, False, carry), [empty] * heads)
    carry = tile(i, True, carry)
    for h in range(heads):
        part = slice(h * HD, (h + 1) * HD)
        acc_ref[part, :] = acc_ref[part, :] / carry[h][1]
        lse_ref[h : h + 1, :] = carry[h][0] + jnp.log(carry[h][1])
    o_ref[...] = acc_ref[...].T.astype(BF)


def attend(mixed, half):
    length, width = mixed.shape[0], 128
    heads = width // HD
    block = min(BLOCK, length)
    return pl.pallas_call(
        attend_kernel,
        grid=(length // block,),
        in_specs=[
            pl.BlockSpec((block, width), lambda i: (i, 3 * half)),
            pl.BlockSpec((length, width), lambda i: (0, 3 * half + 1)),
            pl.BlockSpec((length, width), lambda i: (0, 3 * half + 2)),
        ],
        out_specs=[
            pl.BlockSpec((block, width), lambda i: (i, 0)),
            pl.BlockSpec((heads, block), lambda i: (0, i)),
        ],
        out_shape=[
            jax.ShapeDtypeStruct((length, width), BF),
            jax.ShapeDtypeStruct((heads, length), F32),
        ],
        scratch_shapes=[
            pltpu.VMEM((width, block), F32),
            pltpu.VMEM((width, length), BF),
        ],
        compiler_params=pltpu.CompilerParams(vmem_limit_bytes=VMEM_LIMIT),
        cost_estimate=LIGHT,
        name="attend",
    )(mixed, mixed, mixed)


def attend_back_kernel(
    q_ref,
    k_ref,
    v_ref,
    do_ref,
    o_ref,
    lse_ref,
    cos_ref,
    sin_ref,
    out_ref,
    total_ref,
    inner_ref,
    dq_ref,
    dk_ref,
    dv_ref,
):
    block, width = k_ref.shape
    length = q_ref.shape[0]
    heads = width // HD
    steps = length // block
    j = pl.program_id(0)
    masks = head_masks(width, BF)
    key = k_ref[...]
    value = v_ref[...]
    keys = [key * mask for mask in masks]
    values = [value * mask for mask in masks]

    @pl.when(j == 0)
    def _():
        dq_ref[...] = jnp.zeros(dq_ref.shape, F32)
        total_ref[...] = jnp.zeros(total_ref.shape, F32)
        product = do_ref[...].astype(F32) * o_ref[...].astype(F32)
        coarse = product.astype(BF)
        fine = (product - coarse.astype(F32)).astype(BF)
        row = lax.broadcasted_iota(jnp.int32, (8, width), 0)
        lane = lax.broadcasted_iota(jnp.int32, (8, width), 1) // HD
        chosen = (row == lane).astype(F32).astype(BF)
        inner_ref[...] = matmul_nt(chosen, coarse) + matmul_nt(chosen, fine)

    dk_ref[...] = jnp.zeros(dk_ref.shape, F32)
    dv_ref[...] = jnp.zeros(dv_ref.shape, F32)

    def tile(start, count, at, number, diagonal):
        rows = pl.ds(pl.multiple_of(start, count), count)
        part = slice(at, at + number)
        query = q_ref[rows, :]
        grad = do_ref[rows, :]
        log_total = lse_ref[:, rows]
        inner = inner_ref[:, rows]
        scores = [matmul_nt(keys[h][part, :], query) for h in range(heads)]
        weight_grads = [matmul_nt(values[h][part, :], grad) for h in range(heads)]
        if diagonal:
            row = lax.broadcasted_iota(jnp.int32, scores[0].shape, 0)
            column = lax.broadcasted_iota(jnp.int32, scores[0].shape, 1)
            allowed = row <= column
            scores = [jnp.where(allowed, score, MASK_VALUE) for score in scores]
        weights = [jnp.exp(scores[h] - log_total[h : h + 1, :]) for h in range(heads)]
        low = [weight.astype(BF) for weight in weights]
        score_grads = [
            (weights[h] * (weight_grads[h] - inner[h : h + 1, :])).astype(BF)
            for h in range(heads)
        ]
        dv_ref[part, :] += matmul(
            jnp.concatenate(low, 1), jnp.concatenate([grad * mask for mask in masks], 0)
        )
        dk_ref[part, :] += matmul(
            jnp.concatenate(score_grads, 1),
            jnp.concatenate([query * mask for mask in masks], 0),
        )
        dq_ref[rows, :] += matmul_tn(
            jnp.concatenate(score_grads, 0),
            jnp.concatenate([keys[h][part, :] for h in range(heads)], 0),
        )

    def step(i, carry):
        tile(i * block, block, 0, block, False)
        return carry

    part_size = block // 2
    tile(j * block, block, 0, part_size, True)
    tile(j * block + part_size, part_size, part_size, part_size, True)
    lax.fori_loop(j + 1, steps, step, 0)

    own = pl.ds(pl.multiple_of(j * block, block), block)
    cosine = cos_ref[own, :]
    sine = sin_ref[own, :]
    key_grad = dk_ref[...]
    key_grad = key_grad * cosine - swap_halves(key_grad) * sine
    value_grad = dv_ref[...]
    query_grad = dq_ref[own, :] * QUERY_SCALE
    query_grad = query_grad * cosine - swap_halves(query_grad) * sine
    out_ref[:, :width] = query_grad.astype(BF)
    out_ref[:, width : 2 * width] = key_grad.astype(BF)
    out_ref[:, 2 * width :] = value_grad.astype(BF)
    total_ref[:, :width] += jnp.sum(query_grad, 0, keepdims=True)
    total_ref[:, width : 2 * width] += jnp.sum(key_grad, 0, keepdims=True)
    total_ref[:, 2 * width :] += jnp.sum(value_grad, 0, keepdims=True)


def attend_back(mixed, grads, attended, log_total, cosine, sine, half):
    length, width = mixed.shape[0], 128
    heads = width // HD
    block = min(BLOCK, length)
    return pl.pallas_call(
        attend_back_kernel,
        grid=(length // block,),
        in_specs=[
            pl.BlockSpec((length, width), lambda j: (0, 3 * half)),
            pl.BlockSpec((block, width), lambda j: (j, 3 * half + 1)),
            pl.BlockSpec((block, width), lambda j: (j, 3 * half + 2)),
            pl.BlockSpec((length, width), lambda j: (0, half)),
            pl.BlockSpec((length, width), lambda j: (0, 0)),
            pl.BlockSpec((heads, length), lambda j: (0, 0)),
            pl.BlockSpec((length, 128), lambda j: (0, 0)),
            pl.BlockSpec((length, 128), lambda j: (0, 0)),
        ],
        out_specs=[
            pl.BlockSpec((block, 3 * width), lambda j: (j, 0)),
            pl.BlockSpec((1, 3 * width), lambda j: (0, 0)),
        ],
        out_shape=[
            jax.ShapeDtypeStruct((length, 3 * width), BF),
            jax.ShapeDtypeStruct((1, 3 * width), F32),
        ],
        scratch_shapes=[
            pltpu.VMEM((8, length), F32),
            pltpu.VMEM((length, width), F32),
            pltpu.VMEM((block, width), F32),
            pltpu.VMEM((block, width), F32),
        ],
        compiler_params=pltpu.CompilerParams(vmem_limit_bytes=VMEM_LIMIT),
        cost_estimate=LIGHT,
        name="attend_back",
    )(mixed, mixed, mixed, grads, attended, log_total, cosine, sine)


def gelu_pair(values):
    size = jnp.abs(values) * (1.0 / math.sqrt(2.0))
    bell = jnp.exp(-size * size)
    turn = 1.0 / (1.0 + 0.3275911 * size)
    series = turn * (
        0.254829592
        + turn * (-0.284496736 + turn * (1.421413741 + turn * (-1.453152027 + turn * 1.061405429)))
    )
    tail = 0.5 * series * bell
    below = jnp.where(values < 0.0, tail, 1.0 - tail)
    slope = below + values * bell * (1.0 / math.sqrt(2.0 * math.pi))
    return values * below, slope


def chip_rows(own, length, size=ROWS):
    chips = lax.axis_size("seq") // 2
    y = lax.axis_index("seq") // 2
    per = length // size // chips
    if own is None:
        return length // size, lambda i, y_ref: i, y
    if own:
        return per, lambda i, y_ref: y_ref[0] * per + i, y
    return (
        (chips - 1) * per,
        lambda i, y_ref: (y_ref[0] + chips - 1 - i // per) % chips * per + i % per,
        y,
    )


def feed_kernel(first, last, halves, count, y_ref, slots_ref, x_ref, *refs):
    refs = list(refs)
    if first:
        gain_ref, low_ref, bias_ref = refs[:3]
        del refs[:3]
        if count:
            pieces = refs[:count]
            del refs[:count]
        else:
            raw_ref = refs.pop(0)
    else:
        scaled_ref, shift_ref = refs[:2]
        del refs[:2]
    if last:
        out_ref = refs.pop()
        if count:
            shrink_ref = refs.pop()
        else:
            shrink_ref = refs.pop(0)
        output_ref = refs.pop(0)
        attended = refs[:halves]
    if first:
        if count:
            raw_ref = refs.pop()
        act_ref, slope_ref, scaled_ref, shift_ref = refs[-4:]
        units = scaled_ref.shape[1]

        @pl.when(pl.program_id(0) == 0)
        def _():
            if count:
                for n, piece_ref in enumerate(pieces):
                    size = piece_ref.shape[0]
                    rows = pl.ds(pl.multiple_of(slots_ref[n] * size, size), size)
                    raw_ref[rows, :] = piece_ref[:, :units]
                    shrink_ref[rows, :] = piece_ref[:, units:]
            raw = raw_ref[...]
            scaled_ref[...] = (raw.astype(F32) * as_column(gain_ref[...])).astype(BF)
            low = jnp.broadcast_to(low_ref[...], (8, D)).astype(BF)
            shift_ref[...] = matmul(low, raw) + bias_ref[...]

    else:
        act_ref, slope_ref = refs[-2:]
    size = x_ref.shape[0] // 4
    spans = [slice(n * size, (n + 1) * size) for n in range(4)]
    hidden = [matmul(x_ref[span, :], scaled_ref[...]) + shift_ref[0:1, :] for span in spans]
    for n, span in enumerate(spans):
        activated, slope = gelu_pair(hidden[n])
        act_ref[span, :] = activated.astype(BF)
        slope_ref[span, :] = slope.astype(BF)
    if last:
        for span in spans:
            out = matmul(act_ref[span, :], shrink_ref[...])
            for half, o_ref in enumerate(attended):
                weight = output_ref[half * 128 : (half + 1) * 128, :]
                out = out + matmul(o_ref[span, :], weight)
            out_ref[span, :] = out.astype(BF)


def feed(rows_of, x, units, first=None, scaled=None, last=None, kept=(), slots=None):
    length = x.shape[0]
    steps, row, y = chip_rows(rows_of, length, BLOCK)

    def rows(columns):
        return pl.BlockSpec((BLOCK, columns), lambda i, *_: (row(i, _[0]), 0))

    def whole(shape, column=0):
        return pl.BlockSpec(shape, lambda i, *_: (0, column))

    specs, values, halves, count = [rows(D)], [x], 0, 0
    out_specs = [rows(units), rows(units)]
    out_shape = [jax.ShapeDtypeStruct((length, units), BF)] * 2
    if first is not None:
        gain, low, bias, weight = first
        values += [gain[None], low[None], bias[None]]
        specs += [whole((1, D)), whole((1, D)), whole((1, units))]
        out_specs += [whole((D, units)), whole((8, units))]
        out_shape += [
            jax.ShapeDtypeStruct((D, units), BF),
            jax.ShapeDtypeStruct((8, units), F32),
        ]
        if slots is not None:
            count = len(weight)
            values += weight
            specs += [pl.BlockSpec(memory_space=pltpu.VMEM)] * count
            out_specs += [whole((D, units))]
            out_shape += [jax.ShapeDtypeStruct((D, units), BF)]
        else:
            values.append(weight[0])
            specs.append(whole((D, units), weight[1]))
    else:
        values += list(scaled)
        specs += [whole((D, units)), whole((8, units))]
    if last is not None:
        shrink, output, attended = last
        halves = len(attended)
        if count:
            out_specs.append(whole((units, D)))
            out_shape.append(jax.ShapeDtypeStruct((units, D), BF))
        else:
            values.append(shrink[0])
            specs.append(whole((units, D), shrink[1]))
        values += [output, *attended]
        specs += [whole(output.shape)] + [rows(128)] * halves
        out_specs.append(pl.BlockSpec((BLOCK, D), lambda i, *_: (i, 0)))
        out_shape.append(jax.ShapeDtypeStruct((steps * BLOCK, D), BF))
    aliases = {2 + len(values) + n: n for n in range(len(kept))}
    values += list(kept)
    specs += [pl.BlockSpec(memory_space=pl.ANY)] * len(kept)
    slots = jnp.zeros((1,), jnp.int32) if slots is None else jnp.stack(slots).astype(jnp.int32)
    return pl.pallas_call(
        partial(feed_kernel, first is not None, last is not None, halves, count),
        grid_spec=pltpu.PrefetchScalarGridSpec(
            num_scalar_prefetch=2, grid=(steps,), in_specs=specs, out_specs=out_specs
        ),
        out_shape=out_shape,
        input_output_aliases=aliases,
        compiler_params=pltpu.CompilerParams(vmem_limit_bytes=VMEM_LIMIT),
        cost_estimate=LIGHT,
        name="feed",
    )(y.reshape(1), slots, *values)


def branch_kernel(y_ref, act_ref, shrink_ref, output_ref, *refs):
    out = matmul(act_ref[...], shrink_ref[...])
    for half, o_ref in enumerate(refs[:-1]):
        out = out + matmul(o_ref[...], output_ref[half * 128 : (half + 1) * 128, :])
    refs[-1][...] = out.astype(BF)


def branch(rows_of, activated, shrink, output, attended):
    length, units = activated.shape
    steps, row, y = chip_rows(rows_of, length)

    def rows(columns):
        return pl.BlockSpec((ROWS, columns), lambda i, y_ref: (row(i, y_ref), 0))

    return pl.pallas_call(
        branch_kernel,
        grid_spec=pltpu.PrefetchScalarGridSpec(
            num_scalar_prefetch=1,
            grid=(steps,),
            in_specs=[
                rows(units),
                pl.BlockSpec((units, D), lambda i, y_ref: (0, shrink[1])),
                pl.BlockSpec(output.shape, lambda i, y_ref: (0, 0)),
            ]
            + [rows(128)] * len(attended),
            out_specs=pl.BlockSpec((ROWS, D), lambda i, y_ref: (i, 0)),
        ),
        out_shape=jax.ShapeDtypeStruct((steps * ROWS, D), BF),
        compiler_params=pltpu.CompilerParams(vmem_limit_bytes=VMEM_LIMIT),
        cost_estimate=LIGHT,
        name="branch",
    )(y.reshape(1), activated, shrink[0], output, *attended)


def norm_grad_kernel(y_ref, h_ref, wi_ref, wm_ref, *refs):
    out = matmul_nt(h_ref[...], wi_ref[...])
    for half, m_ref in enumerate(refs[:-1]):
        out = out + matmul_nt(m_ref[...], wm_ref[:, half * 384 : (half + 1) * 384])
    refs[-1][...] = out.astype(BF)


def norm_grad(hidden, expand, mixed, mixing, own):
    length, units, columns = hidden.shape[0], expand.shape[1], mixing.shape[1]
    steps, row, y = chip_rows(own, length)

    def rows(count):
        return pl.BlockSpec((ROWS, count), lambda i, y_ref: (row(i, y_ref), 0))

    def whole(shape):
        return pl.BlockSpec(shape, lambda i, y_ref: (0, 0))

    return pl.pallas_call(
        norm_grad_kernel,
        grid_spec=pltpu.PrefetchScalarGridSpec(
            num_scalar_prefetch=1,
            grid=(steps,),
            in_specs=[rows(units), whole((D, units)), whole((D, columns))]
            + [rows(384)] * len(mixed),
            out_specs=pl.BlockSpec((ROWS, D), lambda i, y_ref: (i, 0)),
        ),
        out_shape=jax.ShapeDtypeStruct((steps * ROWS, D), BF),
        compiler_params=pltpu.CompilerParams(vmem_limit_bytes=VMEM_LIMIT),
        cost_estimate=LIGHT,
        name="norm_grad",
    )(y.reshape(1), hidden, expand, mixing, *mixed)


def product_kernel(g_ref, *refs):
    for half, x_ref in enumerate(refs[:-1]):
        product = matmul_tn(x_ref[...], g_ref[...])
        refs[-1][half * 128 : (half + 1) * 128, :] = product.astype(BF)


def product(inputs, grads):
    rows = 128 * len(inputs)
    block = D // 2
    return pl.pallas_call(
        product_kernel,
        grid=(D // block,),
        in_specs=[pl.BlockSpec((grads.shape[0], block), lambda i: (0, i))]
        + [pl.BlockSpec(x.shape, lambda i: (0, 0)) for x in inputs],
        out_specs=pl.BlockSpec((rows, block), lambda i: (0, i)),
        out_shape=jax.ShapeDtypeStruct((rows, D), BF),
        compiler_params=pltpu.CompilerParams(vmem_limit_bytes=VMEM_LIMIT),
        cost_estimate=LIGHT,
        name="product",
    )(grads, *inputs)


def weight_grad_kernel(count, x_ref, weight_ref, gain_ref, shift_ref, total_ref, *refs):
    lows, (out_ref, gain_out_ref, shift_out_ref) = refs[:count], refs[-3:]
    gain, shift = as_column(gain_ref[...]), as_column(shift_ref[...])
    x = x_ref[...]
    start, gain_sum, shift_sum = 0, 0.0, 0.0
    for low_ref in lows:
        columns = slice(start, start + low_ref.shape[1])
        start += low_ref.shape[1]
        raw = matmul_tn(x, low_ref[...])
        weight = weight_ref[:, columns].astype(F32)
        total = total_ref[:, columns]
        out_ref[:, columns] = (raw * gain + shift * total).astype(BF)
        gain_sum = gain_sum + jnp.sum(raw * weight, 1, keepdims=True)
        shift_sum = shift_sum + jnp.sum(weight * total, 1, keepdims=True)
    gain_out_ref[...] = as_row(gain_sum)
    shift_out_ref[...] = as_row(shift_sum)


def weight_grad(x, lows, weight, gain, shift, total, wide=None):
    length, columns = x.shape[0], total.shape[1]
    array, column = weight
    wide = wide or (0, columns)
    row = pl.BlockSpec((1, ROWS), lambda i: (0, i))
    return pl.pallas_call(
        partial(weight_grad_kernel, len(lows)),
        grid=(D // ROWS,),
        in_specs=[
            pl.BlockSpec((length, ROWS), lambda i: (0, i)),
            pl.BlockSpec((ROWS, columns), lambda i: (i, column)),
            row,
            row,
            pl.BlockSpec((1, columns), lambda i: (0, 0)),
        ]
        + [pl.BlockSpec(low.shape, lambda i: (0, 0)) for low in lows],
        out_specs=[pl.BlockSpec((ROWS, columns), lambda i: (i, wide[0])), row, row],
        out_shape=[
            jax.ShapeDtypeStruct((D, wide[1]), BF),
            jax.ShapeDtypeStruct((1, D), F32),
            jax.ShapeDtypeStruct((1, D), F32),
        ],
        compiler_params=pltpu.CompilerParams(vmem_limit_bytes=VMEM_LIMIT),
        cost_estimate=LIGHT,
        name="weight_grad",
    )(x, array, gain[None], shift[None], total, *lows)


def pack_kernel(spans, split, mixing_ref, expand_ref, *refs):
    outs = refs[-2:] if split else (refs[-1], refs[-1])
    shift = split or 0
    for source_ref, part, out_ref, back in (
        (mixing_ref, spans[0], outs[0], 0),
        (expand_ref, spans[1], outs[1], shift),
    ):
        for p, start, at, count in part:
            columns = slice(start - back, start - back + count)
            out_ref[p, :, columns] = source_ref[0, :, at : at + count].astype(BF)
    for pair_ref in refs[: -2 if split else -1]:
        end = outs[1].shape[2] - pair_ref.shape[1]
        for p in range(outs[1].shape[0]):
            outs[1][p, :, end:] = pair_ref[...]


def pack(mixing, expand, layer, spans, columns, pair=(), split=0):
    parts, rows = lax.axis_size("seq"), mixing.shape[1]
    columns = columns + sum(value.shape[1] for value in pair)
    widths = [split, columns - split] if split else [columns]
    made = pl.pallas_call(
        partial(pack_kernel, spans, split),
        grid=(1,),
        in_specs=[
            pl.BlockSpec((1,) + mixing.shape[1:], lambda i: (layer, 0, 0)),
            pl.BlockSpec((1,) + expand.shape[1:], lambda i: (layer, 0, 0)),
        ]
        + [pl.BlockSpec(value.shape, lambda i: (0, 0)) for value in pair],
        out_specs=[pl.BlockSpec((parts, rows, w), lambda i: (0, 0, 0)) for w in widths],
        out_shape=[jax.ShapeDtypeStruct((parts, rows, w), BF) for w in widths],
        compiler_params=pltpu.CompilerParams(vmem_limit_bytes=VMEM_LIMIT),
        cost_estimate=LIGHT,
        name="pack",
    )(mixing, expand, *pair)
    return made if split else made[0]


def feed_back_kernel(joined, kept, *refs):
    grad_ref, shrink_ref, slope_ref, act_ref, x_ref, output_ref = refs[:6]
    weight_ref, gain_ref, shift_ref = refs[6:9]
    low_ref, total_ref, do_ref, gain_out_ref, shift_out_ref = refs[kept : kept + 5]
    outs = refs[kept + 5 : -2]
    expand_ref, shrink_acc_ref = refs[-2:]
    i = pl.program_id(0)

    @pl.when(i == 0)
    def _():
        total_ref[...] = jnp.zeros(total_ref.shape, F32)
        expand_ref[...] = jnp.zeros(expand_ref.shape, F32)
        shrink_acc_ref[...] = jnp.zeros(shrink_acc_ref.shape, F32)

    grads = grad_ref[...]
    hidden = matmul_nt(grads, shrink_ref[...]) * slope_ref[...].astype(F32)
    low = hidden.astype(BF)
    low_ref[...] = low
    total_ref[...] += jnp.sum(hidden, 0, keepdims=True)
    shrink_acc_ref[...] += matmul_tn(act_ref[...], grads)
    do_ref[...] = matmul_nt(grads, output_ref[...]).astype(BF)
    expand_ref[...] += matmul_tn(x_ref[...], low)

    @pl.when(i == pl.num_programs(0) - 1)
    def _():
        gain, shift, total = as_column(gain_ref[...]), as_column(shift_ref[...]), total_ref[...]
        units = total.shape[1]
        raw = expand_ref[...]
        weight = weight_ref[...].astype(F32)
        outs[0][:, :units] = (raw * gain + shift * total).astype(BF)
        if joined:
            outs[0][:, units:] = shrink_acc_ref[...].astype(BF)
        else:
            outs[1][...] = shrink_acc_ref[...].astype(BF)
        gain_out_ref[...] = as_row(jnp.sum(raw * weight, 1, keepdims=True))
        shift_out_ref[...] = as_row(jnp.sum(weight * total, 1, keepdims=True))


def feed_back(grads, shrink, slope, activated, x, output, weight, gain, shift, kept=()):
    length, units = slope.shape
    width, joined = output.shape[0], units == D

    def rows(count):
        return pl.BlockSpec((BLOCK, count), lambda i: (i, 0))

    def whole(shape, column=0):
        return pl.BlockSpec(shape, lambda i: (0, column))

    out_specs = [rows(units), whole((1, units)), rows(width), whole((1, D)), whole((1, D))]
    out_shape = [
        jax.ShapeDtypeStruct((length, units), BF),
        jax.ShapeDtypeStruct((1, units), F32),
        jax.ShapeDtypeStruct((length, width), BF),
        jax.ShapeDtypeStruct((1, D), F32),
        jax.ShapeDtypeStruct((1, D), F32),
    ]
    if joined:
        out_specs.append(whole((D, 2 * units)))
        wide = kept[0].shape[1] if kept else 2 * units + width
        out_shape.append(jax.ShapeDtypeStruct((D, wide), BF))
    else:
        out_specs += [whole((D, units)), whole((units, D))]
        out_shape += [
            jax.ShapeDtypeStruct((D, units), BF),
            jax.ShapeDtypeStruct((units, D), BF),
        ]
    return pl.pallas_call(
        partial(feed_back_kernel, joined, 9 + len(kept)),
        grid=(length // BLOCK,),
        in_specs=[
            rows(D),
            whole((units, D), shrink[1]),
            rows(units),
            rows(units),
            rows(D),
            whole((width, D)),
            whole((D, units), weight[1]),
            whole((1, D)),
            whole((1, D)),
        ]
        + [pl.BlockSpec(memory_space=pl.ANY)] * len(kept),
        out_specs=out_specs,
        out_shape=out_shape,
        input_output_aliases={9: 5} if kept else {},
        scratch_shapes=[
            pltpu.VMEM((D, units), F32),
            pltpu.VMEM((units, D), F32),
        ],
        compiler_params=pltpu.CompilerParams(vmem_limit_bytes=VMEM_LIMIT),
        cost_estimate=LIGHT,
        name="feed_back",
    )(
        grads,
        shrink[0],
        slope,
        activated,
        x,
        output,
        weight[0],
        gain[None],
        shift[None],
        *kept,
    )


def home_spans(parts, copies, width, units):
    mixing, expand = [], []
    size = units // copies
    for p in range(parts):
        for half in range(width // 128):
            for kind in range(3):
                at = kind * parts * width + p * width + half * 128
                mixing.append((p, half * 384 + kind * 128, at, 128))
        for d in range(copies):
            expand.append((p, 3 * width + d * size, (d * parts + p) * size, size))
    return mixing, expand


def adam(grad, weight, first, second, average, rate, decay):
    first_new = BETA_FIRST * first + (1.0 - BETA_FIRST) * grad
    second_new = BETA_SECOND * second + (1.0 - BETA_SECOND) * grad * grad
    first_hat = first_new / (1.0 - BETA_FIRST**STEP)
    second_hat = second_new / (1.0 - BETA_SECOND**STEP)
    weight_new = weight - rate * (
        first_hat / (jnp.sqrt(second_hat) + ADAM_EPS) + decay * weight
    )
    return weight_new, first_new, second_new, EMA_DECAY * average + (1.0 - EMA_DECAY) * weight_new


def adam_kernel(spans, rates, clip_ref, mixing_ref, expand_ref, output_ref, shrink_ref, *refs):
    clip = clip_ref[0]
    states, news = refs[:16], refs[16:]

    def step(kind, grad, columns):
        old = [ref[0, :, columns] for ref in states[4 * kind : 4 * kind + 4]]
        new = adam(grad.astype(F32) * clip, *old, rates[kind], WEIGHT_DECAY)
        for ref, value in zip(news[4 * kind : 4 * kind + 4], new):
            ref[0, :, columns] = value

    for kind, part, grad_ref in ((0, spans[0], mixing_ref), (2, spans[1], expand_ref)):
        back = part[0][1]
        for source, start, at, count in part:
            grad = grad_ref[0, source, :, start - back : start - back + count]
            step(kind, grad, slice(at, at + count))
    step(1, output_ref[0], slice(None))
    step(3, shrink_ref[0], slice(None))


def update(clip, mixing, expand, output, shrink, states, spans, rates):
    layers, parts, rows = mixing.shape[:3]
    chunk = 16 if rows % 16 == 0 else rows
    chunks = rows // chunk

    def block(array):
        size = array.shape[1] // chunks
        return pl.BlockSpec((1, size, array.shape[2]), lambda l, n: (l, n, 0))

    return pl.pallas_call(
        partial(adam_kernel, spans, rates),
        grid=(layers, chunks),
        in_specs=[
            pl.BlockSpec(memory_space=pltpu.SMEM),
            pl.BlockSpec((1, parts, chunk, mixing.shape[3]), lambda l, n: (l, 0, n, 0)),
            pl.BlockSpec((1, parts, chunk, expand.shape[3]), lambda l, n: (l, 0, n, 0)),
            block(output),
            block(shrink),
        ]
        + [block(state) for state in states],
        out_specs=[block(state) for state in states],
        out_shape=[jax.ShapeDtypeStruct(state.shape, F32) for state in states],
        compiler_params=pltpu.CompilerParams(vmem_limit_bytes=VMEM_LIMIT),
        cost_estimate=LIGHT,
        name="update",
    )(clip, mixing, expand, output, shrink, *states)


def rotary_tables(positions):
    half = ROT // 2
    steps_half = jnp.arange(half).astype(F32)
    frequency = 10000.0 ** (-2.0 * steps_half / ROT)
    angles = positions.astype(F32)[None, :] * frequency[:, None]
    cosine = jnp.concatenate([jnp.cos(angles), jnp.ones_like(angles)], 0)
    entry = jnp.arange(128)[None, :] % HD
    index = jnp.arange(half)[:, None]
    turning = (entry < ROT) & (entry % half == index)
    still = (entry >= ROT) & (index == 0)
    sign = jnp.where(entry < half, -1.0, 1.0)
    spread_cosine = jnp.concatenate([turning, still], 0).astype(F32)
    spread_sine = turning.astype(F32) * sign

    def lay(table, spread):
        return lax.dot_general(
            table, spread, (((0,), (0,)), ((), ())), precision=lax.Precision.HIGHEST
        )

    return lay(cosine, spread_cosine), lay(jnp.sin(angles), spread_sine)


def split_affine(affine):
    bounds = [D, D, D, D, 3 * D, D, FF, D]
    pieces = []
    offset = 0
    for length in bounds:
        pieces.append(affine[offset : offset + length])
        offset = offset + length
    return pieces


def normalize(values):
    centre = values - jnp.mean(values, -1, keepdims=True)
    spread = jnp.mean(centre * centre, -1, keepdims=True)
    scale = lax.rsqrt(spread + NORM_EPS)
    return centre * scale, scale


def local(
    stream,
    cotangent,
    positions,
    mixing_weight,
    mixing_first,
    mixing_second,
    mixing_average,
    output_weight,
    output_first,
    output_second,
    output_average,
    expand_weight,
    expand_first,
    expand_second,
    expand_average,
    shrink_weight,
    shrink_first,
    shrink_second,
    shrink_average,
    affine_weight,
    affine_first,
    affine_second,
    affine_average,
):
    parts = lax.axis_size("seq")
    copies = lax.axis_size("dp")
    devices = parts * copies
    part = lax.axis_index("seq")
    width = D // parts
    units = FF // parts
    rows_d = D // devices
    rows_f = FF // devices
    rows = stream.shape[0] * stream.shape[1]
    small = affine_weight.shape[1]

    halves = width // 128
    outer = dp_parts()[0]

    def mixing_part(vector):
        view = vector.reshape(3, parts, halves, 128)
        view = lax.dynamic_index_in_dim(view, part, 1, keepdims=False)
        return view.transpose(1, 0, 2).reshape(-1)

    def expand_part(vector):
        view = vector.reshape(copies, parts, -1)
        return lax.dynamic_index_in_dim(view, part, 1, keepdims=False).reshape(-1)

    def spread_mixing(vector):
        view = jnp.zeros((3, parts, width), F32)
        vector = vector.reshape(halves, 3, 128).transpose(1, 0, 2).reshape(3, 1, width)
        return lax.dynamic_update_slice(view, vector, (0, part, 0)).reshape(-1)

    def spread_expand(vector):
        view = jnp.zeros((copies, parts, rows_f), F32)
        return lax.dynamic_update_slice(view, vector.reshape(copies, 1, rows_f), (0, part, 0)).reshape(-1)

    spans = home_spans(parts, copies, width, units)
    aligned = rows_f % 128 == 0 and rows_d % 16 == 0

    def arrange(layer, mixing, expand, pair=(), split=False):
        if aligned:
            return pack(
                mixing, expand, layer, spans, 3 * width + units, pair, 3 * width * split
            )
        mixing = mixing[layer].astype(BF).reshape(rows_d, 3, parts, halves, 128)
        mixing = mixing.transpose(2, 0, 3, 1, 4).reshape(parts, rows_d, 3 * width)
        expand = expand[layer].astype(BF).reshape(rows_d, copies, parts, rows_f)
        expand = expand.transpose(2, 0, 1, 3).reshape(parts, rows_d, units)
        pair = [jnp.broadcast_to(value, (parts,) + value.shape) for value in pair]
        if split:
            return mixing, jnp.concatenate([expand] + pair, -1)
        return jnp.concatenate([mixing, expand] + pair, -1)

    def settle_output(exchanged):
        output = exchanged.reshape(parts, copies // parts, rows_d, D)
        return output.transpose(1, 0, 2, 3).reshape(width, D)

    def norm_back(gradient, normed_grad, own_normed, scale):
        projected = jnp.mean(normed_grad * own_normed, -1, keepdims=True)
        middle = jnp.mean(normed_grad, -1, keepdims=True)
        return gradient + scale * (normed_grad - middle - own_normed * projected)

    def beside(grads, *pieces):
        pieces = [jnp.concatenate(piece).reshape(devices, small) for piece in pieces]
        pieces = jnp.concatenate(pieces, -1)
        coarse = pieces.astype(BF)
        fine = (pieces - coarse.astype(F32)).astype(BF)
        pieces = jnp.concatenate([coarse, fine], -1)
        extra = 128 * pl.cdiv(pieces.shape[1], 128 * rows_d)
        pieces = jnp.pad(pieces, ((0, 0), (0, extra * rows_d - pieces.shape[1])))
        return jnp.concatenate([grads, pieces.reshape(D, extra)], -1)

    def apart(summed, columns, count):
        pieces = summed[..., columns:].reshape(devices, -1).astype(F32)
        size = count * small
        pieces = jnp.sum(pieces[:, :size] + pieces[:, size : 2 * size], 0).reshape(count, small)
        return jnp.sum(summed[..., :columns].astype(F32), 0), list(pieces)

    def sum_squares(*values):
        return sum(jnp.sum(value.astype(F32) * value.astype(F32)) for value in values)

    tie = lax.optimization_barrier
    chips = parts // 2
    current = stream.reshape(rows, D)
    gradient = cotangent.reshape(rows, D)

    def view(array, column):
        if units == D:
            return array, column
        return array[:, column * units : (column + 1) * units].reshape(-1, D), 0

    pair = jnp.stack([positions.reshape(-1) // 16, positions.reshape(-1) % 16]).astype(BF)
    pair = pair.reshape(rows_d, 2 * rows // rows_d)
    both = arrange(0, mixing_weight, expand_weight, (pair,))
    both, current = tie((both, current))
    both = seq_exchange(both)
    own_normed, scale = normalize(current)
    travel = SeqGather(own_normed.astype(BF))
    pair = both[..., 3 * width + units :].astype(F32).reshape(parts, 2, rows)
    places = (pair[:, 0] * 16.0 + pair[:, 1]).reshape(-1)
    both = both.reshape(parts * rows_d, -1)
    near = Gather(both[:, : 3 * width])
    places, affine_low, layer_mixing, layer_expand, first_output, later_output = near.hold(
        places,
        affine_weight,
        mixing_weight,
        expand_weight,
        output_weight[0],
        output_weight[1],
    )
    near.forward()
    outputs = jnp.concatenate(
        [value.astype(BF).reshape(-1, width) for value in (first_output, later_output)], -1
    )
    outputs = lax.all_gather(outputs, "dp", axis=0, tiled=True)
    cosine, sine = rotary_tables(places)
    later_both = arrange(1, layer_mixing, layer_expand)
    affine_low, cosine, sine, later_both, expand_own, shrink_own, low_gradient = near.hold(
        affine_low,
        cosine,
        sine,
        later_both,
        both[:, 3 * width : 3 * width + units],
        shrink_weight[0],
        gradient.astype(BF),
    )
    near.forward()
    near.cross()
    affine_low = affine_low.astype(BF).reshape(1, LAYERS * small)
    affine_all = lax.all_to_all(
        jnp.broadcast_to(affine_low, (devices, LAYERS * small)),
        ("dp", "seq"),
        split_axis=0,
        concat_axis=0,
        tiled=True,
    )
    far_own = jnp.concatenate([expand_own, shrink_own.astype(BF).reshape(-1, units)], -1)
    affine_all, far_own, near.pieces, near.chains, travel.pieces = tie(
        (affine_all, far_own, near.pieces, near.chains, travel.pieces)
    )
    inputs, x_slots = travel.take(0, chips)
    near.forward()
    near.cross()
    affine_all = affine_all.reshape(devices, LAYERS, small).transpose(1, 0, 2)
    affine_all = affine_all.reshape(LAYERS, devices * small).astype(F32)
    vectors = [split_affine(affine_all[layer]) for layer in range(LAYERS)]
    vectors, inputs = near.hold(vectors, inputs)
    for step in range(3, outer - 1):
        near.forward()
        near.cross()
    while len(near.chains) < outer:
        near.cross()
    far = Gather(far_own)
    far.pieces[0], near.pieces, near.chains = tie((far.pieces[0], near.pieces, near.chains))
    far.forward()
    far.cross()
    pieces, slots = near.done()

    gain_one, shift_one, gain_two, shift_two = vectors[0][:4]
    normed, mixed, mixing, mixing_scaled, _ = mix(
        inputs,
        x_slots,
        cosine,
        sine,
        first=(gain_one, shift_one, mixing_part(vectors[0][4]), pieces, slots),
    )
    mixed, later_both, later_shrink, outputs, low_gradient = far.hold(
        mixed, later_both, shrink_weight[1], outputs, low_gradient
    )
    far.forward()
    far.cross()
    travel = SeqGather(low_gradient)
    later_both = seq_exchange(later_both)
    outputs = jnp.stack(
        [outputs[:, layer * width : (layer + 1) * width].reshape(parts, -1, D) for layer in (0, 1)],
        1,
    )
    attended, logs = [], []
    for half in range(halves):
        out, log_total = attend(mixed, half)
        attended.append(out)
        logs.append(log_total)
        if half == 0:
            mixed, out, later_both, outputs = far.hold(mixed, out, later_both, outputs)
            far.forward()
            far.cross()
            outputs = seq_exchange(outputs)
            later_both = later_both.reshape(parts * rows_d, -1)
            later_far = jnp.concatenate(
                [later_both[:, 3 * width :], later_shrink.astype(BF).reshape(-1, units)], -1
            )
            later_near = later_both[:, : 3 * width]
    attended, logs, later_far, later_near, travel.pieces = far.hold(
        attended, logs, later_far, later_near, travel.pieces
    )
    later_all = lax.all_gather(later_far, "dp", axis=0, tiled=True)
    while len(far.pieces) < outer:
        far.forward()
    while len(far.chains) < outer:
        far.cross()
    attended, logs, later_near, grads, outputs = far.hold(
        attended, logs, later_near, travel.done(), outputs
    )
    output, later_output = (settle_output(outputs[:, layer]) for layer in (0, 1))
    near = Gather(later_near)
    near.forward()
    near.cross()
    pieces, slots = far.done()
    first = (gain_two, shift_two, expand_part(vectors[0][6]))
    if units == D:
        activated, slope, expand_scaled, expand_shift, expand, shrink, others = feed(
            False,
            normed,
            units,
            first=first + (pieces,),
            last=(None, output, attended),
            slots=slots,
        )
    else:
        far_all = assemble(pieces, slots)
        expand, shrink = far_all[:, :units], view(far_all, 1)[0]
        activated, slope, expand_scaled, expand_shift, others = feed(
            False,
            normed,
            units,
            first=first + ((expand, 0),),
            last=((shrink, 0), output, attended),
        )
    shrink = (shrink, 0)
    (others,) = near.hold(others)
    near.forward()
    near.cross()
    travel = SeqScatter(others)
    activated, slope = travel.hold(activated, slope)
    activated, slope, own = feed(
        True,
        normed,
        units,
        scaled=(expand_scaled, expand_shift),
        last=(shrink, output, attended),
        kept=(activated, slope),
    )
    (own,) = near.hold(own)
    for step in range(2, outer - 1):
        near.forward()
        near.cross()
    stored = [(own_normed, scale, normed, mixed, attended, logs, activated, slope)]
    weights = [(mixing, mixing_scaled, output, expand, expand_scaled, shrink)]
    total, (near.pieces, near.chains) = travel.done(own, (near.pieces, near.chains))
    while len(near.chains) < outer:
        near.cross()
    current = current + total + vectors[0][5] + vectors[0][7]

    own_normed, scale = normalize(current)
    travel = SeqGather(own_normed.astype(BF))
    pieces, slots = near.done()
    gain_one, shift_one, gain_two, shift_two = vectors[1][:4]
    inputs, x_slots = travel.take(0, 1)
    normed, mixed, mixing, mixing_scaled, mixing_shift = mix(
        inputs,
        x_slots,
        cosine,
        sine,
        first=(gain_one, shift_one, mixing_part(vectors[1][4]), pieces, slots),
    )
    normed, mixed = travel.hold(normed, mixed)
    inputs, x_slots = travel.take(1, chips)
    normed, mixed = mix(
        inputs,
        x_slots,
        cosine,
        sine,
        scaled=(mixing_scaled, mixing_shift),
        kept=(normed, mixed),
    )
    output = later_output
    attended, logs = [], []
    for half in range(halves):
        out, log_total = attend(mixed, half)
        attended.append(out)
        logs.append(log_total)
    attended, logs, later_all = tie((attended, logs, later_all))
    expand, shrink = later_all, view(later_all, 1)
    activated, slope, expand_scaled, expand_shift = feed(
        None,
        normed,
        units,
        first=(gain_two, shift_two, expand_part(vectors[1][6]), (later_all, 0)),
    )

    grads, attended, logs, activated = tie((grads, attended, logs, activated))

    def feed_grads(gain, shift, kept=()):
        output_grad, low_grads = tie((product(attended, grads), grads))
        output_grad = output_grad.reshape(copies // parts, parts, rows_d, D).transpose(1, 0, 2, 3)
        swap = SeqSwap(output_grad.reshape(parts, copies // parts * rows_d, D))
        made = feed_back(
            low_grads,
            shrink,
            slope,
            activated,
            normed,
            output,
            (expand, 0),
            gain,
            shift,
            kept if units == D else (),
        )
        made = swap.hold(*made)
        low, total, attended_grad, gain_grad, shift_grad = made[:5]
        output_grad = swap.done().reshape(-1, width)
        if units == D:
            joined = lax.dynamic_update_slice(made[5], output_grad, (0, 2 * units))
        else:
            joined = [made[5], made[6].reshape(-1, units), output_grad, *kept]
            joined = jnp.concatenate(joined, -1)
        return low, total, attended_grad, gain_grad, shift_grad, joined

    made = feed_grads(gain_two, shift_two)
    hidden_low, hidden_total, attended_grad, gain_two_grad, shift_two_grad, later_grad = made
    later_grad, attended_grad = tie((later_grad, attended_grad))
    later_first = lax.psum_scatter(later_grad, "dp", scatter_dimension=0, tiled=True)
    lows, totals = [], []
    for half in range(halves):
        low, total = attend_back(
            mixed, attended_grad, attended[half], logs[half], cosine, sine, half
        )
        lows.append(low)
        totals.append(total)
    mixed_total = jnp.concatenate(totals, -1)
    others = norm_grad(hidden_low, expand_scaled, lows, mixing_scaled, False)
    travel = SeqScatter(others)
    hidden_low, lows, activated = travel.hold(hidden_low, lows, activated)
    own = norm_grad(hidden_low, expand_scaled, lows, mixing_scaled, True)
    last = (shrink, output, attended)
    result_others = branch(False, activated, *last)
    result_own = branch(True, activated, *last)
    normed_grad, (result_others, result_own) = travel.done(own, (result_others, result_own))
    normed_grad, lows = tie((normed_grad, lows))
    gradient = norm_back(gradient, normed_grad, own_normed, scale)
    travel = SeqGather(gradient.astype(BF))
    lows, own_piece = tie((lows, travel.pieces[0]))
    wide = (3, 2 * units + 4 * width) if units == D else None
    later_mixing, gain_one_grad, shift_one_grad = weight_grad(
        normed, lows, (mixing, 0), gain_one, shift_one, mixed_total, wide
    )
    (later_mixing,) = travel.hold(later_mixing)
    grads = travel.done()
    output_sum = jnp.sum(cotangent.reshape(rows, D), 0)

    def small_grads(*pieces):
        gains, mixed_total, output_sum, hidden_total = pieces
        pieces = [piece[0] for piece in gains]
        pieces += [spread_mixing(mixed_total[0]), output_sum]
        return pieces + [spread_expand(hidden_total[0]), output_sum]

    gains = (gain_one_grad, shift_one_grad, gain_two_grad, shift_two_grad)
    later_pieces = small_grads(gains, mixed_total, output_sum, hidden_total)

    later_current, later_vectors = current, vectors[1]
    current = stream.reshape(rows, D)
    own_normed, scale, normed, mixed, attended, logs, activated, slope = stored[0]
    mixing, mixing_scaled, output, expand, expand_scaled, shrink = weights[0]
    gain_one, shift_one, gain_two, shift_two = vectors[0][:4]
    made = feed_grads(gain_two, shift_two, (later_mixing,))
    hidden_low, hidden_total, attended_grad, gain_two_grad, shift_two_grad, far_grad = made
    far_grad, attended_grad, result_others, later_pieces = tie(
        (far_grad, attended_grad, result_others, later_pieces)
    )
    far_grad = lax.psum_scatter(far_grad, "dp", scatter_dimension=0, tiled=True)
    travel = SeqScatter(result_others)
    lows, totals, mixing_grads, gain_grads, shift_grads = [], [], [], [], []
    for half in range(halves):
        low, total = attend_back(
            mixed, attended_grad, attended[half], logs[half], cosine, sine, half
        )
        if half == 0:
            mixed, low, later_first = tie((mixed, low, later_first))
            later_home = SeqSwap(later_first[:, :units].reshape(parts, rows_d, units))
        else:
            mixed, low = later_home.hold(mixed, low)
        if half == halves - 1:
            others = norm_grad(
                hidden_low, expand_scaled, lows + [low], mixing_scaled, False
            )
            others, low = tie((others, low))
            last_travel = SeqScatter(others)
        mixing_grad, gain_one_grad, shift_one_grad = weight_grad(
            normed,
            [low],
            (mixing, half),
            gain_one,
            shift_one,
            total,
        )
        lows.append(low)
        totals.append(total)
        gain_grads.append(gain_one_grad)
        shift_grads.append(shift_one_grad)
        pieces = [later_pieces] if half == 0 else []
        if half == halves - 1:
            output_sum = jnp.sum(gradient, 0)
            gains = (sum(gain_grads), sum(shift_grads), gain_two_grad, shift_two_grad)
            pieces.append(
                small_grads(gains, jnp.concatenate(totals, -1), output_sum, hidden_total)
            )
        mixing_grad = beside(mixing_grad, *pieces) if pieces else mixing_grad
        if half == 0:
            result, (mixing_grad,) = travel.done(result_own, (mixing_grad,))
        if half == halves - 1:
            (mixing_grad,) = last_travel.hold(mixing_grad)
        mixing_grad, lows, mixed, attended_grad, mixing_grads = tie(
            (mixing_grad, lows, mixed, attended_grad, mixing_grads)
        )
        mixing_grads.append(sum_exchange(mixing_grad))
    result = later_current + result + later_vectors[5] + later_vectors[7]
    result = result.reshape(stream.shape)
    own = norm_grad(hidden_low, expand_scaled, lows, mixing_scaled, True)
    normed_grad = last_travel.done(own)[0]
    gradient = norm_back(gradient, normed_grad, own_normed, scale)
    squares = sum_squares(later_first)
    mixing_grads[-1], gradient, result, squares = tie(
        (mixing_grads[-1], gradient, result, squares)
    )
    affine, parts_of_mixing = [], []
    for half in range(halves):
        count = (half == 0) + (half == halves - 1)
        summed, pieces = apart(mixing_grads[half], 3 * 128, count)
        parts_of_mixing.append(summed)
        affine += pieces
    affine_grad = jnp.stack(affine[::-1])
    squares = squares + sum_squares(*parts_of_mixing, affine_grad)
    mixing_grad = jnp.concatenate(parts_of_mixing, -1).astype(BF)
    far_grad, squares, mixing_grad = tie((far_grad, squares, mixing_grad))
    stream_grad = gradient.reshape(stream.shape)

    squares = squares + sum_squares(far_grad)
    squares = lax.all_to_all(
        jnp.broadcast_to(squares, (devices, 128)),
        ("dp", "seq"),
        split_axis=0,
        concat_axis=0,
        tiled=True,
    )
    home = jnp.concatenate([far_grad[:, :units], far_grad[:, 2 * units + width :]], -1)
    home = SeqSwap(home.reshape(parts, rows_d, units + 3 * width))
    output_grad = jnp.stack(
        [far_grad[:, 2 * units : 2 * units + width], later_first[:, 2 * units :]]
    ).reshape(LAYERS, rows_d, D)
    shrink_grad = jnp.stack(
        [far_grad[:, units : 2 * units], later_first[:, units : 2 * units]]
    ).reshape(LAYERS, rows_f, D)
    squares, output_grad, shrink_grad = home.hold(squares, output_grad, shrink_grad)
    home = home.done()
    expand_grad = jnp.stack([home[..., :units], later_home.done()])
    later_mixing = home[..., units:]
    gradient_norm = jnp.sqrt(jnp.sum(squares[:, 0]))
    clip_scale = jnp.minimum(1.0, CLIP_LIMIT / (gradient_norm + 1e-06))
    mixing_grad = jnp.stack([mixing_grad, later_mixing])
    if not aligned:
        mixing_grad = mixing_grad.reshape(LAYERS, parts, rows_d, halves, 3, 128)
        mixing_grad = mixing_grad.transpose(0, 2, 4, 1, 3, 5).reshape(LAYERS, 1, rows_d, 3 * D)
        expand_grad = expand_grad.reshape(LAYERS, parts, rows_d, copies, rows_f)
        expand_grad = expand_grad.transpose(0, 2, 3, 1, 4).reshape(LAYERS, 1, rows_d, FF)
        spans = ([(0, 0, 0, 3 * D)], [(0, 0, 0, FF)])
    states = (
        (mixing_weight, mixing_first, mixing_second, mixing_average)
        + (output_weight, output_first, output_second, output_average)
        + (expand_weight, expand_first, expand_second, expand_average)
        + (shrink_weight, shrink_first, shrink_second, shrink_average)
    )
    rates = (D ** (-0.5), (D * 32 // LEN) ** (-0.5), D ** (-0.5), FF ** (-0.5))
    updated = update(
        clip_scale.reshape(1), mixing_grad, expand_grad, output_grad, shrink_grad, states, spans, rates
    )
    affine_new = adam(
        affine_grad * clip_scale,
        affine_weight,
        affine_first,
        affine_second,
        affine_average,
        SMALL_RATE,
        0.0,
    )
    return (result, stream_grad, gradient_norm) + tuple(updated) + tuple(affine_new)


def solution(mesh):
    tokens = P("dp", "seq", None)
    matrix = P(None, ("dp", "seq"), None)
    vector = P(None, ("dp", "seq"))
    states = (matrix,) * 16 + (vector,) * 4
    return jax.shard_map(
        local,
        mesh=mesh,
        in_specs=(tokens, tokens, P("dp", "seq")) + states,
        out_specs=(tokens, tokens, P()) + states,
        check_vma=False,
    )
```
